32 devices in a mesh: seq: 8 (over y, x, core), fsdp: 4 (over z).
Axes of the slice: x: 2, y: 2, z: 4, core: 2. Of those that a mesh axis runs over, the one named last changes fastest.
Arguments:
- tokens: bfloat16 [4, 2048, 2048], P('fsdp', 'seq'), may hold values from -6 to 6
- segments: int32 [4, 2048], P('fsdp'), may hold values from 0 to 3, as said below
- routes: int32 [4, 2048, 8], P('fsdp', 'seq'), may hold values from 0 to 15, all different within a row; in each aligned block of 256 rows (0 to 255, 256 to 511, ..., all dimensions but the last counted through in order) at most 144 rows name the same one
- cotangent: bfloat16 [4, 2048, 2048], P('fsdp', 'seq'), may hold values from -6 to 6
- w_query: bfloat16 [2048, 2048], P(('seq', 'fsdp')), may hold values from -0.125 to 0.125
- w_key: bfloat16 [2048, 2048], P(('seq', 'fsdp')), may hold values from -0.125 to 0.125
- w_value: bfloat16 [2048, 2048], P(('seq', 'fsdp')), may hold values from -0.125 to 0.125
- w_output: bfloat16 [2048, 2048], P(('seq', 'fsdp')), may hold values from -4 to 4
- router: bfloat16 [2048, 16], P(('seq', 'fsdp')), may hold values from -0.0625 to 0.0625
- attn_gain: bfloat16 [2048], P(('seq', 'fsdp')), may hold values from 0.099609375 to 1.8984375
- moe_gain: bfloat16 [2048], P(('seq', 'fsdp')), may hold values from 0.099609375 to 1.8984375
- query_gain: bfloat16 [2048], P(('seq', 'fsdp')), may hold values from 0.099609375 to 1.8984375
- key_gain: bfloat16 [2048], P(('seq', 'fsdp')), may hold values from 0.099609375 to 1.8984375
- w_gate: bfloat16 [16, 2048, 1024], P('seq', 'fsdp'), may hold values from -0.125 to 0.125
- w_up: bfloat16 [16, 2048, 1024], P('seq', 'fsdp'), may hold values from -0.125 to 0.125
- w_down: bfloat16 [16, 1024, 2048], P('seq', 'fsdp'), may hold values from -1.5 to 1.5
Outputs:
- mixed: bfloat16 [4, 2048, 2048], P('fsdp', 'seq')
- grad_tokens: float32 [4, 2048, 2048], P('fsdp', 'seq')
- grad_query: float32 [2048, 2048], P(('seq', 'fsdp'))
- grad_key: float32 [2048, 2048], P(('seq', 'fsdp'))
- grad_value: float32 [2048, 2048], P(('seq', 'fsdp'))
- grad_output: float32 [2048, 2048], P(('seq', 'fsdp'))
- grad_router: float32 [2048, 16], P(('seq', 'fsdp'))
- grad_attn_gain: float32 [2048], P(('seq', 'fsdp'))
- grad_moe_gain: float32 [2048], P(('seq', 'fsdp'))
- grad_query_gain: float32 [2048], P(('seq', 'fsdp'))
- grad_key_gain: float32 [2048], P(('seq', 'fsdp'))
- grad_gate: float32 [16, 2048, 1024], P('seq', 'fsdp')
- grad_up: float32 [16, 2048, 1024], P('seq', 'fsdp')
- grad_down: float32 [16, 1024, 2048], P('seq', 'fsdp')
The draws below stay inside these ranges and needn't reach their ends.
Inputs may be any that keep to these rules, and one draw needn't show every extreme that they name: `segments`: along each sequence the document numbers never fall. `routes`: each token names 8 different experts; the tokens of one device name one expert 144 times at most.
All inputs are finite; a program needn't handle non-finite values.
Results may differ from the reference program's by a relative error of at most 0.018.
Values may be sent and summed in bfloat16 or wider, within the bound.
No kernel may reach another device: no remote copies, remote signals or barrier semaphores. Data moves between devices by JAX's collectives and lax.ppermute only.
A program may use at most 384 MiB of HBM per device.

```python
import math
import jax
import jax.numpy as jnp
import numpy as np
from jax import lax

D = 2048
H = 16
DH = 128
FF = 1024
TOPK = 8
E = 16
WINDOW = 1024
TOK_DEV = 256
SEQS = 4
LEN = 2048
CAP = 144


def draw_segments(key, part):
    key = jax.random.fold_in(key, 11)
    first_key, second_key, third_key = jax.random.split(key, 3)
    first_cut = jax.random.randint(first_key, (SEQS, 1), 1, TOK_DEV // 2)
    second_cut = jax.random.randint(second_key, (SEQS, 1), TOK_DEV // 2, TOK_DEV)
    third_cut = LEN - jax.random.randint(third_key, (SEQS, 1), 1, TOK_DEV // 2)
    places = jnp.arange(LEN, dtype=jnp.int32)[None, :]
    return ((places >= first_cut).astype(jnp.int32) + (places >= second_cut).astype(jnp.int32) + (places >= third_cut).astype(jnp.int32)).astype(jnp.int32)


def spiked(values, key, source, target, blocks, factor):
    owner, partner = [(jnp.arange(values.shape[dim]) // (values.shape[dim] // blocks)).reshape([-1 if axis == dim else 1 for axis in range(values.ndim)]) for dim in (source, target)]
    chosen = jax.random.permutation(key, blocks)[partner]
    strong = (owner == chosen) | (owner == (partner + blocks // 2) % blocks)
    return jnp.where(strong, factor * values, values)


def shard_levels(rng, extent, cuts, smallest, high):
    factor_of, own = 1.0, jax.random.fold_in(rng, 6)
    for dim, shards_of in cuts:
        heights = jnp.exp(jax.random.uniform(jax.random.fold_in(own, dim), (shards_of,), jnp.float32, smallest / len(cuts), high / len(cuts)))
        factor_of = factor_of * jnp.repeat(heights, extent[dim] // shards_of).reshape([-1 if axis == dim else 1 for axis in range(len(extent))])
    return factor_of


def assign_block(stream_key, own, number, rows, count, top, reach, slope):
    order = jax.random.permutation(stream_key, count)
    heavy_load, usual = load_shares(count, rows * top, reach, slope, True), load_shares(count, rows * top, reach, slope, False)
    places = jnp.arange(count)

    def named(sizes, offset_by):
        used = int((sizes > 0).sum())
        fixed = max(1, used // 4)
        passed = fixed + (places - fixed + offset_by * (used - fixed)) % max(1, count - fixed)
        return jnp.zeros((count,), jnp.int32).at[order[jnp.where(places < fixed, places, passed)]].set(jnp.asarray(sizes, jnp.int32))

    sizes = jnp.where(number % 4 == 0, named(heavy_load, number // 4), named(usual, number - number // 4 - 1))
    mixed = jax.random.permutation(jax.random.fold_in(own, 3), count)
    giver, sink = mixed[0:count // 2 * 2:2], mixed[1:count // 2 * 2:2]
    room = jnp.minimum(sizes[giver] - 1, reach - sizes[sink]) // 2
    room = jnp.where((giver == order[0]) | (sink == order[0]) | (sizes[sink] == 0), 0, jnp.maximum(room, 0))
    passed = jax.random.randint(jax.random.fold_in(own, 4), (count // 2,), 0, 1 << 20) % (room + 1)
    sizes = sizes.at[giver].add(-passed).at[sink].add(passed)
    members = jnp.searchsorted(jnp.cumsum(sizes), jnp.arange(rows * top), side="right").astype(jnp.int32)
    grid = members.reshape(top, rows).T
    grid = grid[jax.random.permutation(jax.random.fold_in(own, 1), rows)]
    offset_by = jax.random.randint(jax.random.fold_in(own, 2), (rows, 1), 0, top)
    return jnp.take_along_axis(grid, (jnp.arange(top)[None, :] + offset_by) % top, axis=1)


def load_shares(amount, total, reach, skew, full):
    portions = [(1 << 20) // math.isqrt(rank ** skew) + 1 for rank in range(1, amount + 1)]
    largest = reach if full else min(reach, max(-(-total // amount), total * portions[0] // sum(portions)))
    least = 1 if total - largest >= amount - 1 else 0
    given, spare = [largest] + [least] * (amount - 1), total - largest - least * (amount - 1)
    while spare > 0:
        movable = [i for i in range(1, amount) if given[i] < largest] or [i for i in range(1, amount) if given[i] < reach]
        mass, left = sum([portions[i] for i in movable]), spare
        for i in movable:
            more = min(reach - given[i], max(1, left * portions[i] // mass), spare)
            given[i] = given[i] + more
            spare = spare - more
    return np.array(given)


def normal_values(stream_key, dims, scale, most, cuts=(), held_as=jnp.bfloat16):
    level = shard_levels(stream_key, dims, cuts, -0.22, 0.18) if cuts else 1.0
    entries = jax.random.normal(stream_key, dims, jnp.float32) * scale * level
    return jnp.minimum(jnp.maximum(entries, -most), most).astype(held_as)


def gaussian_with(own_key, dims, spread, most, shards, heavy, kind=jnp.bfloat16):
    array = spread * jax.random.normal(own_key, dims, jnp.float32)
    if shards:
        array = array * shard_levels(own_key, dims, shards, -0.22, 0.18)
    return jnp.clip(spiked(array, jax.random.fold_in(own_key, 3), *heavy), -most, most).astype(kind)


def setup_inputs(seed: int = 0) -> dict:
    arg_keys = jax.random.split(jax.random.key(seed), 17)
    tokens = normal_values(arg_keys[0], (SEQS, LEN, D), 1.0, 6.0, ((0, 4), (1, 8)))
    segments = draw_segments(jax.random.fold_in(arg_keys[16], 71), 0)
    routes_keys = jax.random.split(jax.random.fold_in(arg_keys[2], 1), SEQS * LEN // TOK_DEV)
    routes_turns = jax.random.permutation(jax.random.fold_in(arg_keys[2], 3), SEQS * LEN // TOK_DEV)
    routes = jax.vmap(lambda own, number: assign_block(jax.random.fold_in(arg_keys[2], 2), own, number, TOK_DEV, E, TOPK, CAP, 1))(routes_keys, routes_turns).reshape((SEQS, LEN, TOPK))
    cotangent = gaussian_with(arg_keys[3], (SEQS, LEN, D), 1.0, 6.0, ((0, 4), (1, 8)), (1, 2, 8, 2.0))
    w_query = normal_values(arg_keys[4], (D, D), D ** -0.5, 0.125, ((0, 32),))
    w_key = normal_values(arg_keys[5], (D, D), D ** -0.5, 0.125, ((0, 32),))
    w_value = normal_values(arg_keys[6], (D, D), D ** -0.5, 0.125, ((0, 32),))
    w_output = normal_values(arg_keys[7], (D, D), (max(1, D // WINDOW)) ** -0.5, 4.0, ((0, 32),))
    router = normal_values(arg_keys[8], (D, E), (4 * D) ** -0.5, 0.0625, ((0, 32),))
    attn_gain = jnp.clip(1.0 + 0.18 * jax.random.normal(arg_keys[9], (D,), jnp.float32), 0.099609375, 1.8984375).astype(jnp.bfloat16)
    moe_gain = jnp.clip(1.0 + 0.18 * jax.random.normal(arg_keys[10], (D,), jnp.float32), 0.099609375, 1.8984375).astype(jnp.bfloat16)
    query_gain = jnp.clip(1.0 + 0.18 * jax.random.normal(arg_keys[11], (D,), jnp.float32), 0.099609375, 1.8984375).astype(jnp.bfloat16)
    key_gain = jnp.clip(1.0 + 0.18 * jax.random.normal(arg_keys[12], (D,), jnp.float32), 0.099609375, 1.8984375).astype(jnp.bfloat16)
    w_gate = normal_values(arg_keys[13], (E, D, FF), D ** -0.5, 0.125, ((0, 8), (1, 4)))
    w_up = normal_values(arg_keys[14], (E, D, FF), D ** -0.5, 0.125, ((0, 8), (1, 4)))
    w_down = normal_values(arg_keys[15], (E, FF, D), (max(1, FF // 64)) ** -0.5, 1.5, ((0, 8), (1, 4)))
    return {"tokens": tokens, "segments": segments, "routes": routes, "cotangent": cotangent, "w_query": w_query, "w_key": w_key, "w_value": w_value, "w_output": w_output, "router": router, "attn_gain": attn_gain, "moe_gain": moe_gain, "query_gain": query_gain, "key_gain": key_gain, "w_gate": w_gate, "w_up": w_up, "w_down": w_down}


EPSILON = 1e-06
ROPE_BASE = 50000.0
HIGHEST = lax.Precision.HIGHEST

@jax.custom_vjp
def low(v):
    return lax.optimization_barrier(v.astype(jnp.bfloat16)).astype(jnp.float32)

@jax.custom_vjp
def low_back(v):
    return v

def low_keep(v):
    return (low(v), None)

def low_pass(kept, grad):
    return (grad,)

def back_keep(v):
    return (v, None)

def back_low(kept, grad):
    return (low(grad),)
low.defvjp(low_keep, low_pass)
low_back.defvjp(back_keep, back_low)

def matmul(left, right):
    return jnp.dot(left, right, precision=HIGHEST, preferred_element_type=jnp.float32)

def rms_scale(values, gain):
    return values * lax.rsqrt(lax.optimization_barrier(jnp.mean(values * values, axis=-1, keepdims=True)) + EPSILON) * gain

def rotary(values, places):
    half_size = values.shape[-1] // 2
    freqs = ROPE_BASE ** (-(jnp.arange(half_size, dtype=jnp.float32) * 2.0 / values.shape[-1]))
    angles = places[:, None] * freqs[None, :]
    cosine = jnp.cos(angles)[:, None, :]
    sine = jnp.sin(angles)[:, None, :]
    first = values[..., :half_size]
    second = values[..., half_size:]
    return jnp.concatenate([first * cosine - second * sine, second * cosine + first * sine], axis=-1)

def prepare(projected, gain, places):
    normed = rms_scale(projected, gain)
    return rotary(normed.reshape(projected.shape[0], H, DH), places)

def attend(queries, key_all, value_all, seq_ids):
    length = queries.shape[0]
    block_rows = min(512, length)
    half_window = WINDOW // 2
    key_span = block_rows + 2 * half_window
    pad_rows = ((half_window, half_window), (0, 0), (0, 0))
    keys_pad = jnp.pad(key_all, pad_rows)
    values_pad = jnp.pad(value_all, pad_rows)
    segs_pad = jnp.pad(seq_ids, (half_window, half_window), constant_values=-1)

    def one_block(block_index):
        block_start = block_index * block_rows
        query_blk = lax.dynamic_slice_in_dim(queries, block_start, block_rows, 0)
        key_blk = lax.dynamic_slice_in_dim(keys_pad, block_start, key_span, 0)
        value_blk = lax.dynamic_slice_in_dim(values_pad, block_start, key_span, 0)
        seg_rows = lax.dynamic_slice_in_dim(seq_ids, block_start, block_rows, 0)
        seg_keys = lax.dynamic_slice_in_dim(segs_pad, block_start, key_span, 0)
        rows_at = block_start + jnp.arange(block_rows, dtype=jnp.int32)
        keys_at = block_start - half_window + jnp.arange(key_span, dtype=jnp.int32)
        allowed = (seg_rows[:, None] == seg_keys[None, :]) & (jnp.abs(rows_at[:, None] - keys_at[None, :]) <= half_window)
        scores = low_back(jnp.einsum('qhd,khd->hqk', query_blk, key_blk, precision=HIGHEST) * DH ** (-0.5))
        scores = jnp.where(allowed[None], scores, -1e+30)
        probs_low = low(jax.nn.softmax(scores, axis=-1))
        return jnp.einsum('hqk,khd->qhd', probs_low, value_blk, precision=HIGHEST)
    blocks_out = lax.map(jax.checkpoint(one_block), jnp.arange(length // block_rows, dtype=jnp.int32))
    return blocks_out.reshape(length, H, DH)

def layer(inputs, weights, seq_ids, route_ids):
    w_query, w_key, w_value, w_output, router, attn_gain, moe_gain, query_gain, key_gain, w_gate, w_up, w_down = weights
    length = inputs.shape[0]
    places = jnp.arange(length, dtype=jnp.int32).astype(jnp.float32)
    normed = low(rms_scale(inputs, attn_gain))
    query_pre = low_back(matmul(normed, w_query))
    key_pre = low_back(matmul(normed, w_key))
    value_all = low(low_back(matmul(normed, w_value))).reshape(length, H, DH)
    queries = low(low_back(prepare(query_pre, query_gain, places)))
    key_all = low(low_back(prepare(key_pre, key_gain, places)))
    attended = low(low_back(attend(queries, key_all, value_all, seq_ids))).reshape(length, H * DH)
    residual = inputs + low_back(matmul(attended, w_output))
    second = low(rms_scale(residual, moe_gain))
    router_probs = jax.nn.softmax(matmul(second, router), axis=-1)
    chosen = jnp.any(route_ids[:, :, None] == jnp.arange(E, dtype=jnp.int32)[None, None, :], axis=1)
    gate_all = jnp.where(chosen, router_probs, 0.0)

    def one_expert(running, pieces):
        gate_col, gate_weight, up_weight, down_weight = pieces
        expert_rows = low_back(second)
        gated = low_back(matmul(expert_rows, gate_weight))
        upward = low_back(matmul(expert_rows, up_weight))
        hidden = low(jax.nn.silu(gated) * upward)
        expert_out = low(low_back(matmul(hidden, down_weight)))
        return (running + gate_col[:, None] * expert_out, None)
    expert_sum = lax.scan(jax.checkpoint(one_expert), jnp.zeros_like(residual), (gate_all.T, w_gate, w_up, w_down))[0]
    return residual + expert_sum

def reference(tokens, segments, routes, cotangent, w_query, w_key, w_value, w_output, router, attn_gain, moe_gain, query_gain, key_gain, w_gate, w_up, w_down):
    weights = tuple((weight.astype(jnp.float32) for weight in (w_query, w_key, w_value, w_output, router, attn_gain, moe_gain, query_gain, key_gain, w_gate, w_up, w_down)))

    def per_sequence(totals, element):
        seq_tokens, seq_ids, route_ids, seq_grads = element

        def forward(inputs, *params):
            return layer(inputs, params, seq_ids, route_ids)
        output, pull = jax.vjp(forward, seq_tokens.astype(jnp.float32), *weights)
        grads = pull(seq_grads.astype(jnp.float32))
        totals = tuple((total_grad + new_grad for total_grad, new_grad in zip(totals, grads[1:])))
        return (totals, (output.astype(jnp.bfloat16), grads[0]))
    zeros_all = tuple((jnp.zeros_like(weight) for weight in weights))
    totals, results = lax.scan(per_sequence, zeros_all, (tokens, segments, routes, cotangent))
    return (results[0], results[1], totals[0], totals[1], totals[2], totals[3], totals[4], totals[5], totals[6], totals[7], totals[8], totals[9], totals[10], totals[11])
```

```python
from functools import partial

import jax
import jax.numpy as jnp
from jax import lax
from jax.experimental import pallas as pl
from jax.experimental.pallas import tpu as pltpu
from jax.sharding import PartitionSpec as P

D = 2048
H = 16
DH = 128
E = 16
WINDOW = 1024
CAP = 144

EPSILON = 1e-06
ROPE_BASE = 50000.0
HIGHEST = lax.Precision.HIGHEST
BF16 = jnp.bfloat16
F32 = jnp.float32
MIB = 1024 * 1024


def matmul(left, right):
    return jnp.dot(left, right, preferred_element_type=F32)


def matmul_t(left, right):
    return lax.dot_general(left, right, (((1,), (1,)), ((), ())), preferred_element_type=F32)


def t_matmul(left, right):
    return lax.dot_general(left, right, (((0,), (0,)), ((), ())), preferred_element_type=F32)


def rms_factor(values):
    return lax.rsqrt(jnp.mean(values * values, axis=-1, keepdims=True) + EPSILON)


def swap(values, axis, size, mask):
    return lax.ppermute(values, axis, [(i, i ^ mask) for i in range(size)])


def high_bit(number):
    return 1 << (number.bit_length() - 1)


def low_bit(number):
    return number & -number


def gather_pieces(values, axis, size):
    rows = values.shape[0] // 2
    pieces = {0: (values[:rows], values[rows:])}
    for r in range(2, size, 2):
        if r == low_bit(r):
            whole = swap(values, axis, size, r)
            pieces[r] = (whole[:rows], whole[rows:])
        else:
            up, down = high_bit(r), low_bit(r)
            pieces[r] = (
                swap(pieces[r ^ up][0], axis, size, up),
                swap(pieces[r ^ down][1], axis, size, down),
            )
    for r in range(0, size, 2):
        if r == low_bit(r) or r == 0:
            whole = swap(jnp.concatenate(pieces[r], 0), axis, size, 1)
            pieces[r + 1] = (whole[:rows], whole[rows:])
        else:
            pieces[r + 1] = tuple(swap(half, axis, size, 1) for half in pieces[r])
    return pieces


def place_pieces(pieces, me, size):
    half_rows, columns = pieces[0][0].shape
    whole = jnp.zeros((size * 2 * half_rows, columns), pieces[0][0].dtype)
    for r in range(size):
        for k in range(2):
            at = ((me ^ r) * 2 + k) * half_rows
            whole = lax.dynamic_update_slice_in_dim(whole, pieces[r][k], at, 0)
    return whole


def gather_seq(values, me, size):
    return place_pieces(gather_pieces(values, "seq", size), me, size)


def scatter_sum(chunk_of, axis, size):
    sums = {}
    for r in range(0, size, 2):
        sums[r] = chunk_of(r).astype(F32) + swap(chunk_of(r + 1), axis, size, 1).astype(F32)
    rows = sums[0].shape[0] // 2
    sums = {r: [value[:rows], value[rows:]] for r, value in sums.items()}
    for r in range(size - 2, 0, -2):
        if r == low_bit(r):
            whole = jnp.concatenate([half.astype(BF16) for half in sums[r]], 0)
            got = swap(whole, axis, size, r).astype(F32)
            sums[0] = [sums[0][0] + got[:rows], sums[0][1] + got[rows:]]
        else:
            up, down = high_bit(r), low_bit(r)
            sums[r ^ up][0] += swap(sums[r][0].astype(BF16), axis, size, up).astype(F32)
            sums[r ^ down][1] += swap(sums[r][1].astype(BF16), axis, size, down).astype(F32)
    return jnp.concatenate(sums[0], 0)


def sum_all(values, axis, size):
    mask = 1
    while mask < size:
        values = values + swap(values, axis, size, mask)
        mask *= 2
    return values


def gather_expert_cols(weight, me, size):
    experts, part, hidden = weight.shape
    half = size // 2
    mine = lax.dynamic_slice_in_dim(weight, (me // half) * (hidden // 2), hidden // 2, 2)
    theirs = lax.dynamic_slice_in_dim(weight, (1 - me // half) * (hidden // 2), hidden // 2, 2)
    pieces = {0: mine, half: swap(theirs, "fsdp", size, half)}
    for r in range(1, half):
        up = high_bit(r)
        for base in (0, half):
            pieces[r | base] = swap(pieces[(r ^ up) | base], "fsdp", size, up)
    whole = jnp.zeros((experts, size, part, hidden // 2), weight.dtype)
    for r in range(size):
        whole = lax.dynamic_update_slice_in_dim(whole, pieces[r][:, None], me ^ r, 1)
    return whole.reshape(experts, size * part, hidden // 2)


def gather_expert_rows(weight, me, size):
    experts, part, columns = weight.shape
    half = size // 2
    pieces = {0: weight}
    for r in range(1, half):
        up = high_bit(r)
        pieces[r] = swap(pieces[r ^ up], "fsdp", size, up)
    whole = jnp.zeros((experts, half, part, columns), weight.dtype)
    for r in range(half):
        whole = lax.dynamic_update_slice_in_dim(whole, pieces[r][:, None], (me ^ r) % half, 1)
    return whole.reshape(experts, half * part, columns)


def scatter_expert_cols(partial_sum, me, size):
    experts, depth, hidden_half = partial_sum.shape
    half = size // 2
    parts = partial_sum.reshape(experts, size, depth // size, hidden_half)

    def chunk(r):
        return lax.dynamic_index_in_dim(parts, me ^ r, 1, keepdims=False)

    sums = {r: chunk(r) for r in range(size)}
    for r in range(half - 1, 0, -1):
        up = high_bit(r)
        for base in (half, 0):
            got = swap(sums[r | base].astype(BF16), "fsdp", size, up)
            sums[(r ^ up) | base] += got.astype(F32)
    got = swap(sums[half].astype(BF16), "fsdp", size, half).astype(F32)
    first = me // half == 0
    return jnp.concatenate(
        [jnp.where(first, sums[0], got), jnp.where(first, got, sums[0])], axis=-1
    )


def scatter_expert_rows(partial_sum, me, size):
    experts, hidden_half, columns = partial_sum.shape
    half = size // 2
    parts = partial_sum.reshape(experts, half, hidden_half // half, columns)
    sums = {
        r: lax.dynamic_index_in_dim(parts, (me ^ r) % half, 1, keepdims=False) for r in range(half)
    }
    for r in range(half - 1, 0, -1):
        up = high_bit(r)
        sums[r ^ up] += swap(sums[r].astype(BF16), "fsdp", size, up).astype(F32)
    return sums[0]


def allowed_keys(seg_row, seg_col, first_query, first_key, rows, span, half_window):
    query_at = first_query + lax.broadcasted_iota(jnp.int32, (span, rows), 1)
    key_at = first_key + lax.broadcasted_iota(jnp.int32, (span, rows), 0)
    return (jnp.abs(query_at - key_at) <= half_window) & (seg_col == seg_row)


def first_key_of(block, rows, span, length):
    start = jnp.clip(block * rows - (span - rows) // 2, 0, length - span)
    return pl.multiple_of(start, rows)


def forward_kernel(span, q_ref, k_ref, v_ref, seg_row_ref, seg_col_ref, o_ref, lse_ref):
    block = pl.program_id(1)
    rows, length = q_ref.shape[0], k_ref.shape[0]
    first_key = first_key_of(block, rows, span, length)
    keys = k_ref[pl.ds(first_key, span), :]
    values = v_ref[pl.ds(first_key, span), :]
    scores = matmul_t(keys, q_ref[...]) * DH ** (-0.5)
    allowed = allowed_keys(
        seg_row_ref[...],
        seg_col_ref[pl.ds(first_key, span), :],
        block * rows,
        first_key,
        rows,
        span,
        WINDOW // 2,
    )
    scores = jnp.where(allowed, scores, -1e30)
    peak = jnp.max(scores, axis=0, keepdims=True)
    expos = jnp.exp(scores - peak)
    totals = jnp.sum(expos, axis=0, keepdims=True)
    probs = (expos * (1.0 / totals)).astype(BF16)
    o_ref[...] = t_matmul(values, probs).T.astype(BF16)
    lse_ref[...] = (peak + jnp.log(totals))[None]


def backward_kernel(
    span,
    q_ref,
    k_ref,
    v_ref,
    do_ref,
    lse_ref,
    seg_row_ref,
    seg_col_ref,
    dq_ref,
    dk_ref,
    dv_ref,
    dk_sum,
    dv_sum,
):
    block = pl.program_id(1)
    rows, length = q_ref.shape[0], k_ref.shape[0]

    @pl.when(block == 0)
    def _():
        dk_sum[...] = jnp.zeros_like(dk_sum)
        dv_sum[...] = jnp.zeros_like(dv_sum)

    first_key = first_key_of(block, rows, span, length)
    at = pl.ds(first_key, span)
    keys = k_ref[at, :]
    values = v_ref[at, :]
    queries = q_ref[...]
    grads = do_ref[...]
    scores = matmul_t(keys, queries) * DH ** (-0.5)
    allowed = allowed_keys(
        seg_row_ref[...],
        seg_col_ref[at, :],
        block * rows,
        first_key,
        rows,
        span,
        WINDOW // 2,
    )
    probs = jnp.where(allowed, jnp.exp(scores - lse_ref[0]), 0.0)
    dv_sum[at, :] += matmul(probs.astype(BF16), grads)
    prob_grads = matmul_t(values, grads)
    center = jnp.sum(probs * prob_grads, axis=0, keepdims=True)
    score_grads = (probs * (prob_grads - center)).astype(BF16)
    dk_sum[at, :] += matmul(score_grads, queries)
    dq_ref[...] = (t_matmul(keys, score_grads) * DH ** (-0.5)).T.astype(BF16)

    @pl.when(block == length // rows - 1)
    def _():
        dk_ref[...] = (dk_sum[...] * DH ** (-0.5)).astype(BF16)
        dv_ref[...] = dv_sum[...].astype(BF16)


def attention_sizes(length):
    rows = 256
    return rows, min(length, rows + WINDOW)


def attention_forward(queries, keys, values, seg_row, seg_col):
    length, columns = queries.shape
    heads = columns // DH
    rows, span = attention_sizes(length)
    block = pl.BlockSpec((rows, DH), lambda h, i: (i, h))
    whole = pl.BlockSpec((length, DH), lambda h, i: (0, h))
    return pl.pallas_call(
        partial(forward_kernel, span),
        grid=(heads, length // rows),
        in_specs=[
            block,
            whole,
            whole,
            pl.BlockSpec((1, rows), lambda h, i: (0, i)),
            pl.BlockSpec((length, 1), lambda h, i: (0, 0)),
        ],
        out_specs=[block, pl.BlockSpec((1, 1, rows), lambda h, i: (h, 0, i))],
        out_shape=[
            jax.ShapeDtypeStruct((length, columns), BF16),
            jax.ShapeDtypeStruct((heads, 1, length), F32),
        ],
        compiler_params=pltpu.CompilerParams(vmem_limit_bytes=48 * MIB),
        cost_estimate=pl.CostEstimate(
            flops=4 * heads * length * span * DH,
            bytes_accessed=8 * length * columns,
            transcendentals=heads * length * span,
        ),
        name="attend",
    )(queries, keys, values, seg_row, seg_col)


def attention_backward(queries, keys, values, grads, lse, seg_row, seg_col):
    length, columns = queries.shape
    heads = columns // DH
    rows, span = attention_sizes(length)
    block = pl.BlockSpec((rows, DH), lambda h, i: (i, h))
    whole = pl.BlockSpec((length, DH), lambda h, i: (0, h))
    shape = jax.ShapeDtypeStruct((length, columns), BF16)
    return pl.pallas_call(
        partial(backward_kernel, span),
        grid=(heads, length // rows),
        in_specs=[
            block,
            whole,
            whole,
            block,
            pl.BlockSpec((1, 1, rows), lambda h, i: (h, 0, i)),
            pl.BlockSpec((1, rows), lambda h, i: (0, i)),
            pl.BlockSpec((length, 1), lambda h, i: (0, 0)),
        ],
        out_specs=[block, whole, whole],
        out_shape=[shape, shape, shape],
        scratch_shapes=[pltpu.VMEM((length, DH), F32), pltpu.VMEM((length, DH), F32)],
        compiler_params=pltpu.CompilerParams(vmem_limit_bytes=48 * MIB),
        cost_estimate=pl.CostEstimate(
            flops=10 * heads * length * span * DH,
            bytes_accessed=14 * length * columns,
            transcendentals=heads * length * span,
        ),
        name="attend_back",
    )(queries, keys, values, grads, lse, seg_row, seg_col)


def rotate(values, cosine, sine, heads):
    half = DH // 2
    shaped = values.reshape(values.shape[0], heads, DH)
    first, second = shaped[..., :half], shaped[..., half:]
    cosine, sine = cosine[:, None, :], sine[:, None, :]
    return jnp.concatenate(
        [first * cosine - second * sine, second * cosine + first * sine], axis=-1
    ).reshape(values.shape)


def per_device(
    S,
    F,
    tokens,
    segments,
    routes,
    cotangent,
    w_query,
    w_key,
    w_value,
    w_output,
    router,
    attn_gain,
    moe_gain,
    query_gain,
    key_gain,
    w_gate,
    w_up,
    w_down,
):
    s = lax.axis_index("seq")
    f = lax.axis_index("fsdp")
    T = tokens.shape[1]
    L = S * T
    heads = H // S
    C = heads * DH
    experts = E // S
    part = w_query.shape[0]
    half_f = F // 2

    stacked = jnp.stack([w_query, w_key, w_value], 1).reshape(part, 3, S, C)
    stacked = stacked.transpose(2, 0, 1, 3).reshape(S, part, 3 * C)
    crossed = lax.all_to_all(stacked, "seq", split_axis=0, concat_axis=0, tiled=True)
    w_qkv = lax.all_gather(crossed, "fsdp", axis=1, tiled=True).reshape(D, 3 * C)
    small = jnp.concatenate(
        [router, attn_gain[:, None], moe_gain[:, None], query_gain[:, None], key_gain[:, None]], 1
    )
    small = lax.all_gather(small, ("seq", "fsdp"), axis=0, tiled=True)
    full_router = small[:, :E]
    gains = small[:, E:].astype(F32)
    gain_attn, gain_moe = gains[:, 0], gains[:, 1]
    gain_query = lax.dynamic_slice_in_dim(gains[:, 2], s * C, C, 0)
    gain_key = lax.dynamic_slice_in_dim(gains[:, 3], s * C, C, 0)

    tokens_low = tokens[0]
    inputs = tokens_low.astype(F32)
    tokens_all = gather_seq(tokens_low, s, S).astype(F32)
    normed_all = (tokens_all * rms_factor(tokens_all) * gain_attn).astype(BF16)

    full_output = lax.all_gather(w_output, ("seq", "fsdp"), axis=0, tiled=True)
    own_gate = gather_expert_cols(w_gate, f, F)
    own_up = gather_expert_cols(w_up, f, F)
    own_down = gather_expert_rows(w_down, f, F)
    routes_low = routes[0].reshape(1, -1)
    routes_both = jnp.concatenate([routes_low, swap(routes_low, "fsdp", F, half_f)], 0)
    routes_all = lax.all_gather(routes_both, "seq", axis=1).reshape(2 * S, T, -1)
    upstream_low = cotangent[0]
    upstream_all = jnp.stack(
        [
            lax.all_gather(upstream_low, "seq", axis=0),
            lax.all_gather(swap(upstream_low, "fsdp", F, half_f), "seq", axis=0),
        ],
        0,
    ).reshape(2 * S, T, D)

    places = jnp.arange(L, dtype=jnp.int32).astype(F32)
    freqs = ROPE_BASE ** (-(jnp.arange(DH // 2, dtype=F32) * 2.0 / DH))
    angles = places[:, None] * freqs[None, :]
    cosine, sine = jnp.cos(angles), jnp.sin(angles)
    query_pre = matmul(normed_all, w_qkv[:, :C])
    key_pre = matmul(normed_all, w_qkv[:, C : 2 * C])
    value_low = matmul(normed_all, w_qkv[:, 2 * C :]).astype(BF16)
    squares = jnp.stack([jnp.sum(query_pre**2, -1), jnp.sum(key_pre**2, -1)], 0)
    factors = lax.rsqrt(sum_all(squares, "seq", S) / D + EPSILON)
    query_n = query_pre * factors[0][:, None]
    key_n = key_pre * factors[1][:, None]
    query_low = rotate(query_n * gain_query, cosine, sine, heads).astype(BF16)
    key_low = rotate(key_n * gain_key, cosine, sine, heads).astype(BF16)
    seg_row = segments
    seg_col = segments.reshape(L, 1)
    attended, lse = attention_forward(query_low, key_low, value_low, seg_row, seg_col)
    attended_rows = (
        lax.all_to_all(attended.reshape(S, T, C), "seq", split_axis=0, concat_axis=0, tiled=True)
        .transpose(1, 0, 2)
        .reshape(T, D)
    )
    residual = inputs + matmul(attended_rows, full_output)

    moe_factor = rms_factor(residual)
    residual_n = residual * moe_factor
    second_low = (residual_n * gain_moe).astype(BF16)
    logits = matmul(second_low, full_router)
    router_probs = jax.nn.softmax(logits, axis=-1)
    partner_low = swap(second_low, "fsdp", F, half_f)
    second_all = jnp.stack(
        [gather_seq(second_low, s, S), gather_seq(partner_low, s, S)], 0
    ).reshape(2 * S, T, D)
    probs_all = jax.nn.softmax(matmul(second_all.reshape(2 * L, D), full_router), axis=-1)
    expert_ids = s * experts + jnp.arange(experts, dtype=jnp.int32)
    chosen = jnp.any(routes_all[None] == expert_ids[:, None, None, None], axis=-1)
    gates = lax.dynamic_slice_in_dim(probs_all, s * experts, experts, 1)
    gates = gates.T.reshape(experts, 2 * S, T)
    ranks = jnp.cumsum(chosen.astype(jnp.int32), axis=-1) - 1
    picked = chosen[:, :, None, :] & (
        ranks[:, :, None, :] == jnp.arange(CAP, dtype=jnp.int32)[None, None, :, None]
    )
    picks = picked.astype(BF16)
    slot_gate = jnp.sum(jnp.where(picked, gates[:, :, None, :], 0.0), axis=-1)
    out_sum = 0.0
    row_sum = 0.0
    gate_grad_parts = []
    down_terms, gate_terms, up_terms = [], [], []
    for e in range(experts):
        rows = jnp.einsum("bct,btd->bcd", picks[e], second_all, preferred_element_type=F32)
        rows = rows.astype(BF16).reshape(-1, D)
        ups = jnp.einsum("bct,btd->bcd", picks[e], upstream_all, preferred_element_type=F32)
        ups = ups.astype(BF16).reshape(-1, D)
        gate_col = slot_gate[e].reshape(-1, 1)
        gated = matmul(rows, own_gate[e])
        upward = matmul(rows, own_up[e])
        sig = jax.nn.sigmoid(gated)
        silu = gated * sig
        hidden = silu * upward
        hidden_gate = (hidden * gate_col).astype(BF16)
        hidden_pull = matmul_t(ups, own_down[e])
        slot_grads = jnp.sum(hidden * hidden_pull, axis=-1).reshape(2 * S, CAP)
        gate_grad_parts.append(
            jnp.sum(jnp.where(picked[e], slot_grads[:, :, None], 0.0), axis=1)
        )
        hidden_grads = hidden_pull * gate_col
        gated_low = (hidden_grads * upward * sig * (1.0 + gated * (1.0 - sig))).astype(BF16)
        upward_low = (hidden_grads * silu).astype(BF16)
        outs = matmul(hidden_gate, own_down[e]).astype(BF16).reshape(2 * S, CAP, D)
        out_sum += jnp.einsum("bct,bcd->btd", picks[e], outs, preferred_element_type=F32)
        backs = matmul_t(gated_low, own_gate[e]) + matmul_t(upward_low, own_up[e])
        backs = backs.astype(BF16).reshape(2 * S, CAP, D)
        row_sum += jnp.einsum("bct,bcd->btd", picks[e], backs, preferred_element_type=F32)
        down_terms.append(t_matmul(hidden_gate, ups))
        gate_terms.append(t_matmul(rows, gated_low))
        up_terms.append(t_matmul(rows, upward_low))
    row_sum = row_sum.astype(BF16).reshape(2, S, T, D)
    out_sum = out_sum.astype(BF16).reshape(2, S, T, D)

    def chunk(values, which):
        return lambda r: lax.dynamic_index_in_dim(values[which], s ^ r, 0, keepdims=False)

    def both(values):
        other = scatter_sum(chunk(values, 1), "seq", S).astype(BF16)
        own = scatter_sum(chunk(values, 0), "seq", S)
        return own + swap(other, "fsdp", F, half_f).astype(F32)

    gate_grads = jnp.stack(gate_grad_parts, -1).reshape(2, S, T, experts)
    gate_grads = lax.all_to_all(
        gate_grads.transpose(1, 0, 2, 3).reshape(S, -1), "seq", split_axis=0, concat_axis=0, tiled=True
    ).reshape(S, 2, T * experts)
    gate_grads = gate_grads[:, 0] + swap(gate_grads[:, 1], "fsdp", F, half_f)
    gate_grads = gate_grads.reshape(S, T, experts).transpose(1, 0, 2).reshape(T, E)
    row_grads = both(row_sum)
    mixed = (residual + both(out_sum)).astype(BF16)[None]
    grad_gate = scatter_expert_cols(jnp.stack(gate_terms, 0), f, F)
    grad_up = scatter_expert_cols(jnp.stack(up_terms, 0), f, F)
    grad_down = scatter_expert_rows(jnp.stack(down_terms, 0), f, F)

    upstream = upstream_low.astype(F32)
    logit_grads = router_probs * (
        gate_grads - jnp.sum(router_probs * gate_grads, axis=-1, keepdims=True)
    )
    router_wide = full_router.astype(F32)
    second_grads = row_grads + jnp.dot(logit_grads, router_wide.T, precision=HIGHEST)
    router_term = jnp.dot(second_low.astype(F32).T, logit_grads, precision=HIGHEST)
    moe_gain_term = jnp.sum(second_grads * residual_n, axis=0)
    pulled = second_grads * gain_moe
    residual_grads = upstream + moe_factor * (
        pulled - residual_n * jnp.mean(pulled * residual_n, axis=-1, keepdims=True)
    )
    branch_low = residual_grads.astype(BF16)

    branch_all = gather_seq(branch_low, s, S)
    own_output = lax.dynamic_slice_in_dim(full_output, s * C, C, 0)
    head_grads = matmul_t(branch_all, own_output).astype(BF16)
    output_term = t_matmul(attended, branch_all)
    query_back, key_back, value_back = attention_backward(
        query_low, key_low, value_low, head_grads, lse, seg_row, seg_col
    )
    query_turned = rotate(query_back.astype(F32), cosine, -sine, heads)
    key_turned = rotate(key_back.astype(F32), cosine, -sine, heads)
    query_gain_term = jnp.sum(query_turned * query_n, axis=0)
    key_gain_term = jnp.sum(key_turned * key_n, axis=0)
    query_pulled = query_turned * gain_query
    key_pulled = key_turned * gain_key
    means = jnp.stack([jnp.sum(query_pulled * query_n, -1), jnp.sum(key_pulled * key_n, -1)], 0)
    means = sum_all(means, "seq", S) / D
    query_pre_low = (factors[0][:, None] * (query_pulled - query_n * means[0][:, None])).astype(BF16)
    key_pre_low = (factors[1][:, None] * (key_pulled - key_n * means[1][:, None])).astype(BF16)
    pre_low = jnp.concatenate([query_pre_low, key_pre_low, value_back], 1)
    normed_parts = matmul_t(pre_low, w_qkv).astype(BF16).reshape(1, S, T, D)
    normed_grads = scatter_sum(chunk(normed_parts, 0), "seq", S)
    qkv_term = t_matmul(normed_all, pre_low).astype(BF16)
    qkv_term = lax.psum_scatter(
        qkv_term.reshape(S, F, part, 3 * C), "fsdp", scatter_dimension=1, tiled=True
    ).reshape(S, part, 3 * C)
    qkv_term = lax.all_to_all(qkv_term, "seq", split_axis=0, concat_axis=0, tiled=True)
    qkv_term = qkv_term.reshape(S, part, 3, C).transpose(2, 1, 0, 3).reshape(3, part, D).astype(F32)
    grad_output = lax.psum_scatter(
        output_term.astype(BF16), "fsdp", scatter_dimension=0, tiled=True
    ).astype(F32)
    head_gains = lax.psum_scatter(
        jnp.stack([query_gain_term, key_gain_term], 1), "fsdp", scatter_dimension=0, tiled=True
    )
    attn_factor = rms_factor(inputs)
    inputs_n = inputs * attn_factor
    attn_gain_term = jnp.sum(normed_grads * inputs_n, axis=0)
    attn_pulled = normed_grads * gain_attn
    grad_tokens = residual_grads + attn_factor * (
        attn_pulled - inputs_n * jnp.mean(attn_pulled * inputs_n, axis=-1, keepdims=True)
    )
    gain_terms = jnp.concatenate([router_term, moe_gain_term[:, None], attn_gain_term[:, None]], 1)
    gain_terms = lax.psum_scatter(gain_terms, ("seq", "fsdp"), scatter_dimension=0, tiled=True)
    return (
        mixed,
        grad_tokens[None],
        qkv_term[0],
        qkv_term[1],
        qkv_term[2],
        grad_output,
        gain_terms[:, :E],
        gain_terms[:, E + 1],
        gain_terms[:, E],
        head_gains[:, 0],
        head_gains[:, 1],
        grad_gate,
        grad_up,
        grad_down,
    )


def solution(mesh):
    tokens_spec = P("fsdp", "seq", None)
    rows_spec = P(("seq", "fsdp"), None)
    gain_spec = P(("seq", "fsdp"))
    expert_spec = P("seq", "fsdp", None)
    in_specs = (
        (tokens_spec, P("fsdp", None), tokens_spec, tokens_spec)
        + (rows_spec,) * 5
        + (gain_spec,) * 4
        + (expert_spec,) * 3
    )
    out_specs = (tokens_spec,) * 2 + (rows_spec,) * 5 + (gain_spec,) * 4 + (expert_spec,) * 3
    return jax.shard_map(
        partial(per_device, mesh.shape["seq"], mesh.shape["fsdp"]),
        mesh=mesh,
        in_specs=in_specs,
        out_specs=out_specs,
        check_vma=False,
    )
```

```python
from functools import partial

import jax
import jax.numpy as jnp
from jax import lax
from jax.experimental import pallas as pl
from jax.experimental.pallas import tpu as pltpu
from jax.sharding import PartitionSpec as P

D = 2048
H = 16
DH = 128
E = 16
WINDOW = 1024
CAP = 144

EPSILON = 1e-06
ROPE_BASE = 50000.0
HIGHEST = lax.Precision.HIGHEST
BF16 = jnp.bfloat16
F32 = jnp.float32
MIB = 1024 * 1024


def matmul(left, right):
    return jnp.dot(left, right, preferred_element_type=F32)


def matmul_t(left, right):
    return lax.dot_general(left, right, (((1,), (1,)), ((), ())), preferred_element_type=F32)


def t_matmul(left, right):
    return lax.dot_general(left, right, (((0,), (0,)), ((), ())), preferred_element_type=F32)


def rms_factor(values):
    return lax.rsqrt(jnp.mean(values * values, axis=-1, keepdims=True) + EPSILON)


def swap(values, axis, size, mask):
    return lax.ppermute(values, axis, [(i, i ^ mask) for i in range(size)])


def high_bit(number):
    return 1 << (number.bit_length() - 1)


def low_bit(number):
    return number & -number


def after(values, *others):
    return lax.optimization_barrier((values, others))[0]


def gather_seq(values, size):
    rows = values.shape[0] // 2
    pieces = {0: values}
    for r in range(2, size, 2):
        if r == low_bit(r):
            pieces[r] = swap(values, "seq", size, r)
        else:
            up, down = high_bit(r), low_bit(r)
            pieces[r] = jnp.concatenate(
                [
                    swap(pieces[r ^ up][:rows], "seq", size, up),
                    swap(pieces[r ^ down][rows:], "seq", size, down),
                ],
                0,
            )
    even = jnp.concatenate([pieces[r] for r in range(0, size, 2)], 0)
    return even, swap(even, "seq", size, 1)


def relative(blocks, me):
    size = blocks.shape[0]
    order = list(range(0, size, 2)) + list(range(1, size, 2))
    return jnp.concatenate([lax.dynamic_slice_in_dim(blocks, me ^ r, 1, 0) for r in order], 0)


def absolute(blocks, me):
    size = blocks.shape[0]
    places = [((me ^ j) // 2) + ((me ^ j) % 2) * (size // 2) for j in range(size)]
    return jnp.concatenate([lax.dynamic_slice_in_dim(blocks, at, 1, 0) for at in places], 0)


def scatter_sum(even, odd, size):
    got = swap(odd, "seq", size, 1)
    rows = even.shape[0] // (size // 2)
    half = rows // 2

    def part(r, first, count):
        at = slice(r // 2 * rows + first, r // 2 * rows + first + count)
        return even[at].astype(F32) + got[at].astype(F32)

    sums = {r: [part(r, 0, half), part(r, half, half)] for r in range(0, size, 2)}
    for r in range(size - 2, 0, -2):
        if r == low_bit(r):
            whole = jnp.concatenate([value.astype(BF16) for value in sums[r]], 0)
            come = swap(whole, "seq", size, r).astype(F32)
            sums[0] = [sums[0][0] + come[:half], sums[0][1] + come[half:]]
        else:
            up, down = high_bit(r), low_bit(r)
            sums[r ^ up][0] += swap(sums[r][0].astype(BF16), "seq", size, up).astype(F32)
            sums[r ^ down][1] += swap(sums[r][1].astype(BF16), "seq", size, down).astype(F32)
    return jnp.concatenate(sums[0], 0)


def sum_all(values, axis, size):
    mask = 1
    while mask < size:
        values = values + swap(values, axis, size, mask)
        mask *= 2
    return values


def ring_pieces(values, size):
    pieces = [values]
    for _ in range(1, size):
        pieces.append(lax.ppermute(pieces[-1], "fsdp", [(i, (i + 1) % size) for i in range(size)]))
    return pieces


def place_ring(pieces, me, axis):
    size = len(pieces)
    shape = pieces[0].shape
    whole = jnp.zeros(shape[:axis] + (size,) + shape[axis:], pieces[0].dtype)
    for k, piece in enumerate(pieces):
        at = lax.rem(me + size - k, size)
        whole = lax.dynamic_update_slice_in_dim(whole, jnp.expand_dims(piece, axis), at, axis)
    return whole


def near_swaps(pieces, base, size, dep):
    for r in range(1, size // 2):
        up = high_bit(r)
        pieces[base + r] = swap(after(pieces[base + (r ^ up)], dep), "fsdp", size, up)
        dep = pieces[base + r]
    return dep


def place_swapped(pieces, me, experts_first):
    size = len(pieces)
    experts, part, columns = pieces[0].shape
    whole = jnp.zeros((experts, size, part, columns), pieces[0].dtype)
    for r in range(size):
        at = (me ^ r) % size
        whole = lax.dynamic_update_slice_in_dim(whole, pieces[r][:, None], at, 1)
    return whole.reshape(experts, size * part, columns)


def scatter_expert_cols(partial_sum, me, size, dep):
    experts, depth, hidden_half = partial_sum.shape
    half = size // 2
    parts = partial_sum.reshape(experts, size, depth // size, hidden_half)
    sums = {
        r: lax.dynamic_index_in_dim(parts, me ^ r, 1, keepdims=False).astype(F32)
        for r in range(size)
    }
    for r in range(half - 1, 0, -1):
        up = high_bit(r)
        for base in (half, 0):
            got = swap(after(sums[r | base].astype(BF16), dep), "fsdp", size, up)
            sums[(r ^ up) | base] += got.astype(F32)
            dep = got
    got = swap(after(sums[half].astype(BF16), dep), "fsdp", size, half)
    dep, got = got, got.astype(F32)
    first = me // half == 0
    return jnp.concatenate(
        [jnp.where(first, sums[0], got), jnp.where(first, got, sums[0])], axis=-1
    ), dep


def scatter_expert_rows(partial_sum, me, size, dep):
    experts, hidden_half, columns = partial_sum.shape
    half = size // 2
    parts = partial_sum.reshape(experts, half, hidden_half // half, columns)
    sums = {
        r: lax.dynamic_index_in_dim(parts, (me ^ r) % half, 1, keepdims=False).astype(F32)
        for r in range(half)
    }
    for r in range(half - 1, 0, -1):
        up = high_bit(r)
        dep = swap(after(sums[r].astype(BF16), dep), "fsdp", size, up)
        sums[r ^ up] += dep.astype(F32)
    return sums[0], dep


def scatter_rows(partial_sum, me, size):
    sums = {
        r: lax.dynamic_index_in_dim(partial_sum, me ^ r, 0, keepdims=False).astype(F32)
        for r in range(size)
    }
    mask = 1
    while mask < size:
        stay = [r for r in sums if not r & mask]
        moved = jnp.stack([sums[r | mask].astype(BF16) for r in stay], 0)
        got = swap(moved, "fsdp", size, mask).astype(F32)
        sums = {r: sums[r] + got[i] for i, r in enumerate(stay)}
        mask *= 2
    return sums[0]


def allowed_keys(seg_row, seg_col, first_query, first_key, rows, span, half_window):
    query_at = first_query + lax.broadcasted_iota(jnp.int32, (span, rows), 1)
    key_at = first_key + lax.broadcasted_iota(jnp.int32, (span, rows), 0)
    return (jnp.abs(query_at - key_at) <= half_window) & (seg_col == seg_row)


def first_key_of(block, rows, span, length):
    start = jnp.clip(block * rows - (span - rows) // 2, 0, length - span)
    return pl.multiple_of(start, rows)


def forward_kernel(span, q_ref, k_ref, v_ref, seg_row_ref, seg_col_ref, o_ref, lse_ref):
    block = pl.program_id(1)
    rows, length = q_ref.shape[0], k_ref.shape[0]
    first_key = first_key_of(block, rows, span, length)
    keys = k_ref[pl.ds(first_key, span), :]
    values = v_ref[pl.ds(first_key, span), :]
    scores = matmul_t(keys, q_ref[...]) * DH ** (-0.5)
    allowed = allowed_keys(
        seg_row_ref[...],
        seg_col_ref[pl.ds(first_key, span), :],
        block * rows,
        first_key,
        rows,
        span,
        WINDOW // 2,
    )
    scores = jnp.where(allowed, scores, -1e30)
    peak = jnp.max(scores, axis=0, keepdims=True)
    expos = jnp.exp(scores - peak)
    totals = jnp.sum(expos, axis=0, keepdims=True)
    probs = (expos * (1.0 / totals)).astype(BF16)
    o_ref[...] = t_matmul(values, probs).T.astype(BF16)
    lse_ref[...] = (peak + jnp.log(totals))[None]


def backward_kernel(
    span,
    q_ref,
    k_ref,
    v_ref,
    do_ref,
    lse_ref,
    seg_row_ref,
    seg_col_ref,
    dq_ref,
    dk_ref,
    dv_ref,
    dk_sum,
    dv_sum,
):
    block = pl.program_id(1)
    rows, length = q_ref.shape[0], k_ref.shape[0]

    @pl.when(block == 0)
    def _():
        dk_sum[...] = jnp.zeros_like(dk_sum)
        dv_sum[...] = jnp.zeros_like(dv_sum)

    first_key = first_key_of(block, rows, span, length)
    at = pl.ds(first_key, span)
    keys = k_ref[at, :]
    values = v_ref[at, :]
    queries = q_ref[...]
    grads = do_ref[...]
    scores = matmul_t(keys, queries) * DH ** (-0.5)
    allowed = allowed_keys(
        seg_row_ref[...],
        seg_col_ref[at, :],
        block * rows,
        first_key,
        rows,
        span,
        WINDOW // 2,
    )
    probs = jnp.where(allowed, jnp.exp(scores - lse_ref[0]), 0.0)
    dv_sum[at, :] += matmul(probs.astype(BF16), grads)
    prob_grads = matmul_t(values, grads)
    center = jnp.sum(probs * prob_grads, axis=0, keepdims=True)
    score_grads = (probs * (prob_grads - center)).astype(BF16)
    dk_sum[at, :] += matmul(score_grads, queries)
    dq_ref[...] = (t_matmul(keys, score_grads) * DH ** (-0.5)).T.astype(BF16)

    @pl.when(block == length // rows - 1)
    def _():
        dk_ref[...] = (dk_sum[...] * DH ** (-0.5)).astype(BF16)
        dv_ref[...] = dv_sum[...].astype(BF16)


def attention_sizes(length):
    rows = 256
    return rows, min(length, rows + WINDOW)


def attention_forward(queries, keys, values, seg_row, seg_col):
    length, columns = queries.shape
    heads = columns // DH
    rows, span = attention_sizes(length)
    block = pl.BlockSpec((rows, DH), lambda h, i: (i, h))
    whole = pl.BlockSpec((length, DH), lambda h, i: (0, h))
    return pl.pallas_call(
        partial(forward_kernel, span),
        grid=(heads, length // rows),
        in_specs=[
            block,
            whole,
            whole,
            pl.BlockSpec((1, rows), lambda h, i: (0, i)),
            pl.BlockSpec((length, 1), lambda h, i: (0, 0)),
        ],
        out_specs=[block, pl.BlockSpec((1, 1, rows), lambda h, i: (h, 0, i))],
        out_shape=[
            jax.ShapeDtypeStruct((length, columns), BF16),
            jax.ShapeDtypeStruct((heads, 1, length), F32),
        ],
        compiler_params=pltpu.CompilerParams(vmem_limit_bytes=48 * MIB),
        cost_estimate=pl.CostEstimate(
            flops=4 * heads * length * span * DH,
            bytes_accessed=8 * length * columns,
            transcendentals=heads * length * span,
        ),
        name="attend",
    )(queries, keys, values, seg_row, seg_col)


def attention_backward(queries, keys, values, grads, lse, seg_row, seg_col):
    length, columns = queries.shape
    heads = columns // DH
    rows, span = attention_sizes(length)
    block = pl.BlockSpec((rows, DH), lambda h, i: (i, h))
    whole = pl.BlockSpec((length, DH), lambda h, i: (0, h))
    shape = jax.ShapeDtypeStruct((length, columns), BF16)
    return pl.pallas_call(
        partial(backward_kernel, span),
        grid=(heads, length // rows),
        in_specs=[
            block,
            whole,
            whole,
            block,
            pl.BlockSpec((1, 1, rows), lambda h, i: (h, 0, i)),
            pl.BlockSpec((1, rows), lambda h, i: (0, i)),
            pl.BlockSpec((length, 1), lambda h, i: (0, 0)),
        ],
        out_specs=[block, whole, whole],
        out_shape=[shape, shape, shape],
        scratch_shapes=[pltpu.VMEM((length, DH), F32), pltpu.VMEM((length, DH), F32)],
        compiler_params=pltpu.CompilerParams(vmem_limit_bytes=48 * MIB),
        cost_estimate=pl.CostEstimate(
            flops=10 * heads * length * span * DH,
            bytes_accessed=14 * length * columns,
            transcendentals=heads * length * span,
        ),
        name="attend_back",
    )(queries, keys, values, grads, lse, seg_row, seg_col)


def qkv_kernel(
    me_ref, even_ref, odd_ref, weight_ref, gain_ref, normed_ref, q_ref, k_ref, v_ref, square_ref
):
    turned = me_ref[0] % 2 == 1
    rows = even_ref.shape[0]
    columns = q_ref.shape[1]
    first, second = even_ref[...], odd_ref[...]
    blocks = (jnp.where(turned, second, first), jnp.where(turned, first, second))
    for k, block in enumerate(blocks):
        at = pl.ds(k * rows, rows)
        wide = block.astype(F32)
        normed = (wide * rms_factor(wide) * gain_ref[...]).astype(BF16)
        normed_ref[at, :] = normed
        pre = matmul(normed, weight_ref[...])
        q_ref[at, :] = pre[:, :columns]
        k_ref[at, :] = pre[:, columns : 2 * columns]
        v_ref[at, :] = pre[:, 2 * columns :].astype(BF16)
        for j in range(2):
            squares = 0.0
            for c in range(j * columns, (j + 1) * columns, DH):
                squares += pre[:, c : c + DH] * pre[:, c : c + DH]
            square_ref[j : j + 1, at] = jnp.sum(squares.T, axis=0, keepdims=True)


def project(even, odd, weight, gain, me, rows):
    pairs = even.shape[0] // rows
    length = 2 * even.shape[0]
    depth, columns = weight.shape[0], weight.shape[1] // 3
    token = pl.BlockSpec((rows, depth), lambda i, me: (i, 0))

    def placed(shape):
        return pl.BlockSpec(shape, lambda i, me: (i ^ (me[0] // 2), 0))

    head = jax.ShapeDtypeStruct((length, columns), F32)
    return pl.pallas_call(
        qkv_kernel,
        grid_spec=pltpu.PrefetchScalarGridSpec(
            num_scalar_prefetch=1,
            grid=(pairs,),
            in_specs=[
                token,
                token,
                pl.BlockSpec(weight.shape, lambda i, me: (0, 0)),
                pl.BlockSpec((1, depth), lambda i, me: (0, 0)),
            ],
            out_specs=[
                placed((2 * rows, depth)),
                placed((2 * rows, columns)),
                placed((2 * rows, columns)),
                placed((2 * rows, columns)),
                pl.BlockSpec((2, 2 * rows), lambda i, me: (0, i ^ (me[0] // 2))),
            ],
        ),
        out_shape=[
            jax.ShapeDtypeStruct((length, depth), BF16),
            head,
            head,
            jax.ShapeDtypeStruct((length, columns), BF16),
            jax.ShapeDtypeStruct((2, length), F32),
        ],
        compiler_params=pltpu.CompilerParams(vmem_limit_bytes=48 * MIB),
        cost_estimate=pl.CostEstimate(
            flops=6 * length * depth * columns,
            bytes_accessed=length * (4 * depth + 10 * columns) + 6 * depth * columns,
            transcendentals=length,
        ),
        name="project",
    )(me, even, odd, weight, gain)


def expert_kernel(
    first_ref,
    xa_ref,
    xb_ref,
    ua_ref,
    ub_ref,
    ra_ref,
    rb_ref,
    wg_ref,
    wu_ref,
    wd_ref,
    router_ref,
    *refs,
):
    ya_ref, yb_ref, za_ref, zb_ref, ga_ref, gb_ref, xc_ref, uc_ref, dg_ref, du_ref, hid_ref = refs[-11:]
    experts = wg_ref.shape[0]
    rows = xa_ref.shape[0]
    slot = lax.broadcasted_iota(jnp.int32, (CAP, rows), 0)
    blocks = (
        (xa_ref, ua_ref, ra_ref, ya_ref, za_ref, ga_ref),
        (xb_ref, ub_ref, rb_ref, yb_ref, zb_ref, gb_ref),
    )
    picks = []
    for k, (x_ref, u_ref, rank_ref, _, _, _) in enumerate(blocks):
        hits = jnp.concatenate([slot == rank_ref[0, e : e + 1, :] for e in range(experts)], 0)
        pick = hits.astype(F32).astype(BF16)
        picks.append(pick)
        x_rows = matmul(pick, x_ref[...]).astype(BF16)
        u_rows = matmul(pick, u_ref[...]).astype(BF16)
        for e in range(experts):
            xc_ref[e, k * CAP : (k + 1) * CAP, :] = x_rows[e * CAP : (e + 1) * CAP]
            uc_ref[e, k * CAP : (k + 1) * CAP, :] = u_rows[e * CAP : (e + 1) * CAP]
    outs, backs, gate_grads = [], [], []
    for e in range(experts):
        x_rows, u_rows = xc_ref[e], uc_ref[e]
        logits = matmul(x_rows, router_ref[...])
        lane = lax.broadcasted_iota(jnp.int32, logits.shape, 1)
        logits = jnp.where(lane < E, logits, -1e30)
        expos = jnp.exp(logits - jnp.max(logits, axis=-1, keepdims=True))
        own = jnp.sum(jnp.where(lane == first_ref[0] + e, expos, 0.0), axis=-1, keepdims=True)
        gate = own / jnp.sum(expos, axis=-1, keepdims=True)
        gated = matmul(x_rows, wg_ref[e])
        upward = matmul(x_rows, wu_ref[e])
        pulled = matmul_t(u_rows, wd_ref[e])
        sig = jax.nn.sigmoid(gated)
        silu = gated * sig
        hidden = silu * upward
        gate_grads.append(jnp.sum(hidden * pulled, axis=-1, keepdims=True))
        hidden_gate = (hidden * gate).astype(BF16)
        hidden_grads = pulled * gate
        gated_low = (hidden_grads * upward * sig * (1.0 + gated * (1.0 - sig))).astype(BF16)
        upward_low = (hidden_grads * silu).astype(BF16)
        hid_ref[e] = hidden_gate
        dg_ref[e] = gated_low
        du_ref[e] = upward_low
        outs.append(matmul(hidden_gate, wd_ref[e]).astype(BF16))
        backs.append(
            (matmul_t(gated_low, wg_ref[e]) + matmul_t(upward_low, wu_ref[e])).astype(BF16)
        )
    for k, (_, _, rank_ref, y_ref, z_ref, g_ref) in enumerate(blocks):
        at = slice(k * CAP, (k + 1) * CAP)
        y_ref[...] = t_matmul(picks[k], jnp.concatenate([v[at] for v in outs], 0)).astype(BF16)
        z_ref[...] = t_matmul(picks[k], jnp.concatenate([v[at] for v in backs], 0)).astype(BF16)
        for e in range(experts):
            hit = slot == rank_ref[0, e : e + 1, :]
            g_ref[0, e : e + 1, :] = jnp.sum(
                jnp.where(hit, gate_grads[e][at], 0.0), axis=0, keepdims=True
            )


def run_experts(x, u, ranks, weights, router, first, which, compact):
    experts, depth, hidden = weights[0].shape
    rows = ranks[0].shape[2]
    steps = x[0].shape[0] // rows
    token = pl.BlockSpec((rows, depth), lambda i: (i, 0))
    rank = pl.BlockSpec((1, experts, rows), lambda i: (i, 0, 0))

    def whole(array):
        return pl.BlockSpec(
            array.shape, lambda i: (0,) * array.ndim, pipeline_mode=pl.Buffered(1)
        )

    def slots(columns):
        return pl.BlockSpec((experts, 2 * CAP, columns), lambda i: (0, i + which * steps, 0))

    shape = jax.ShapeDtypeStruct
    tokens = shape(x[0].shape, BF16)
    gates = shape((steps, experts, rows), F32)
    count = 4 * steps * CAP
    wide = shape((experts, count, depth), BF16)
    narrow = shape((experts, count, hidden), BF16)
    inputs = [first, *x, *u, *ranks, *weights, router]
    return pl.pallas_call(
        expert_kernel,
        grid=(steps,),
        in_specs=[pl.BlockSpec(memory_space=pltpu.SMEM)]
        + [token] * 4
        + [rank] * 2
        + [whole(w) for w in weights]
        + [whole(router)]
        + [pl.BlockSpec(memory_space=pl.ANY)] * len(compact),
        out_specs=[token] * 4 + [rank] * 2 + [slots(depth)] * 2 + [slots(hidden)] * 3,
        out_shape=[tokens] * 4 + [gates] * 2 + [wide] * 2 + [narrow] * 3,
        input_output_aliases={len(inputs) + i: 6 + i for i in range(len(compact))},
        compiler_params=pltpu.CompilerParams(vmem_limit_bytes=60 * MIB),
        cost_estimate=pl.CostEstimate(
            flops=4 * steps * CAP * experts * depth * (7 * hidden + 2 * rows),
            bytes_accessed=40 * MIB,
            transcendentals=2 * steps * CAP * experts * hidden,
        ),
        name="experts",
    )(*inputs, *compact)


def rotate(values, cosine, sine, heads):
    half = DH // 2
    shaped = values.reshape(values.shape[0], heads, DH)
    first, second = shaped[..., :half], shaped[..., half:]
    cosine, sine = cosine[:, None, :], sine[:, None, :]
    return jnp.concatenate(
        [first * cosine - second * sine, second * cosine + first * sine], axis=-1
    ).reshape(values.shape)


def per_device(
    S,
    F,
    tokens,
    segments,
    routes,
    cotangent,
    w_query,
    w_key,
    w_value,
    w_output,
    router,
    attn_gain,
    moe_gain,
    query_gain,
    key_gain,
    w_gate,
    w_up,
    w_down,
):
    s = lax.axis_index("seq")
    f = lax.axis_index("fsdp")
    T = tokens.shape[1]
    L = S * T
    heads = H // S
    C = heads * DH
    experts = E // S
    part = w_query.shape[0]
    half_f = F // 2
    hidden_half = w_gate.shape[2] // 2

    tokens_low = tokens[0]
    inputs = tokens_low.astype(F32)
    small = jnp.concatenate(
        [
            router.reshape(-1),
            attn_gain,
            moe_gain,
            query_gain,
            key_gain,
            routes[0].astype(BF16).reshape(-1),
        ]
    )
    small = lax.all_gather(small, ("seq", "fsdp"), axis=0, tiled=False).reshape(S, F, -1)
    tokens_even, tokens_odd = gather_seq(tokens_low, S)

    stacked = jnp.stack([w_query, w_key, w_value], 1).reshape(part, 3, S, C)
    stacked = stacked.transpose(2, 0, 1, 3).reshape(S, part, 3 * C)
    crossed = lax.all_to_all(stacked, "seq", split_axis=0, concat_axis=0, tiled=True)
    output_ring = ring_pieces(w_output, F)
    own_output = place_ring(output_ring, f, 0).reshape(C, D)
    qkv_ring = ring_pieces(after(crossed, output_ring[-1]), F)
    w_qkv = place_ring(qkv_ring, f, 1).reshape(D, 3 * C)

    full_router = small[:, :, : part * E].reshape(D, E)
    gains = [
        small[:, :, part * (E + i) : part * (E + i + 1)].reshape(D).astype(F32) for i in range(4)
    ]
    gain_attn, gain_moe = gains[0], gains[1]
    gain_query = lax.dynamic_slice_in_dim(gains[2], s * C, C, 0)
    gain_key = lax.dynamic_slice_in_dim(gains[3], s * C, C, 0)
    route_part = small[:, :, part * (E + 4) :].reshape(S, F, T, -1)
    expert_ids = s * experts + jnp.arange(experts, dtype=jnp.int32)

    def ranks_of(index):
        named = lax.dynamic_index_in_dim(route_part, index, 1, keepdims=False)
        named = relative(named, s).astype(jnp.int32)
        chosen = jnp.any(named[:, None] == expert_ids[None, :, None, None], axis=-1)
        ranks = jnp.cumsum(chosen.astype(jnp.int32), axis=-1) - 1
        ranks = jnp.where(chosen, ranks, -1)
        return ranks[: S // 2], ranks[S // 2 :]

    def split_hidden(weight):
        mine = lax.dynamic_slice_in_dim(weight, (f // half_f) * hidden_half, hidden_half, 2)
        other = lax.dynamic_slice_in_dim(weight, (1 - f // half_f) * hidden_half, hidden_half, 2)
        return mine, other

    gate_pieces, up_pieces, down_pieces = {}, {}, {0: w_down}
    gate_pieces[0], gate_other = split_hidden(w_gate)
    up_pieces[0], up_other = split_hidden(w_up)
    gate_pieces[half_f] = swap(after(gate_other, qkv_ring[-2]), "fsdp", F, half_f)
    up_pieces[half_f] = swap(after(up_other, gate_pieces[half_f]), "fsdp", F, half_f)
    upstream_low = cotangent[0]
    partner_up = swap(after(upstream_low, up_pieces[half_f]), "fsdp", F, half_f)
    dep = near_swaps(gate_pieces, 0, F, qkv_ring[-1])
    dep = near_swaps(up_pieces, 0, F, dep)
    dep = near_swaps(gate_pieces, half_f, F, dep)
    dep = near_swaps(up_pieces, half_f, F, dep)
    dep = near_swaps(down_pieces, 0, F, dep)
    own_gate = place_swapped(gate_pieces, f, experts)
    own_up = place_swapped(up_pieces, f, experts)
    own_down = place_swapped(down_pieces, f, experts)

    own_up_even, own_up_odd = gather_seq(after(upstream_low, tokens_even), S)
    out_even, out_odd = gather_seq(after(own_output, own_up_even), S)
    other_up_even, other_up_odd = gather_seq(after(partner_up, out_even), S)

    me = s.reshape(1).astype(jnp.int32)
    normed_all, query_pre, key_pre, value_low, squares = project(
        tokens_even, tokens_odd, w_qkv, gain_attn[None], me, T
    )
    places = jnp.arange(L, dtype=jnp.int32).astype(F32)
    freqs = ROPE_BASE ** (-(jnp.arange(DH // 2, dtype=F32) * 2.0 / DH))
    angles = places[:, None] * freqs[None, :]
    cosine, sine = jnp.cos(angles), jnp.sin(angles)
    factors = lax.rsqrt(sum_all(squares, "seq", S) / D + EPSILON)
    query_n = query_pre * factors[0][:, None]
    key_n = key_pre * factors[1][:, None]
    query_low = rotate(query_n * gain_query, cosine, sine, heads).astype(BF16)
    key_low = rotate(key_n * gain_key, cosine, sine, heads).astype(BF16)
    seg_row = segments
    seg_col = segments.reshape(L, 1)
    attended, lse = attention_forward(query_low, key_low, value_low, seg_row, seg_col)
    attended_blocks = attended.reshape(S, T, C)
    come = lax.all_to_all(attended_blocks, "seq", split_axis=0, concat_axis=0, tiled=True)
    come = relative(come, s).transpose(1, 0, 2).reshape(T, D)
    residual = inputs + matmul(come[:, : D // 2], out_even) + matmul(come[:, D // 2 :], out_odd)

    moe_factor = rms_factor(residual)
    residual_n = residual * moe_factor
    second_low = (residual_n * gain_moe).astype(BF16)
    partner_low = swap(second_low, "fsdp", F, half_f)
    own_x = gather_seq(second_low, S)
    other_x = gather_seq(after(partner_low, own_x[0]), S)
    logits = matmul(second_low, full_router)
    router_probs = jax.nn.softmax(logits, axis=-1)
    expert_weights = (own_gate, own_up, own_down)
    wide_router = jnp.pad(full_router, ((0, 0), (0, 128 - E)))
    first = (s * experts).reshape(1).astype(jnp.int32)
    own_parts = run_experts(
        own_x, (own_up_even, own_up_odd), ranks_of(f), expert_weights, wide_router, first, 0, ()
    )
    other_parts = run_experts(
        other_x,
        (other_up_even, other_up_odd),
        ranks_of(f ^ half_f),
        expert_weights,
        wide_router,
        first,
        1,
        own_parts[6:],
    )
    x_rows, u_rows, gated_low, upward_low, hidden_gate = other_parts[6:]
    own_rows = scatter_sum(own_parts[2], own_parts[3], S)
    other_rows = scatter_sum(other_parts[2], other_parts[3], S).astype(BF16)
    back_rows = swap(other_rows, "fsdp", F, half_f)
    row_grads = own_rows + back_rows.astype(F32)

    def to_home(even, odd):
        return absolute(jnp.concatenate([even, odd], 0).transpose(0, 2, 1), s)

    gate_grads = jnp.stack(
        [to_home(own_parts[4], own_parts[5]), to_home(other_parts[4], other_parts[5])], 1
    )
    gate_grads = lax.all_to_all(
        gate_grads.reshape(S, -1), "seq", split_axis=0, concat_axis=0, tiled=True
    ).reshape(S, 2, T * experts)
    gate_grads = gate_grads[:, 0] + swap(gate_grads[:, 1], "fsdp", F, half_f)
    gate_grads = gate_grads.reshape(S, T, experts).transpose(1, 0, 2).reshape(T, E)

    down_term = jnp.stack([t_matmul(hidden_gate[e], u_rows[e]) for e in range(experts)], 0)
    gate_term = jnp.stack([t_matmul(x_rows[e], gated_low[e]) for e in range(experts)], 0)
    up_term = jnp.stack([t_matmul(x_rows[e], upward_low[e]) for e in range(experts)], 0)
    grad_down, dep = scatter_expert_rows(down_term.astype(BF16), f, F, own_rows)
    grad_gate, dep = scatter_expert_cols(gate_term.astype(BF16), f, F, back_rows)
    grad_up, dep = scatter_expert_cols(up_term.astype(BF16), f, F, dep)

    upstream = upstream_low.astype(F32)
    logit_grads = router_probs * (
        gate_grads - jnp.sum(router_probs * gate_grads, axis=-1, keepdims=True)
    )
    router_wide = full_router.astype(F32)
    second_grads = row_grads + jnp.dot(logit_grads, router_wide.T, precision=HIGHEST)
    router_term = jnp.dot(second_low.astype(F32).T, logit_grads, precision=HIGHEST)
    moe_gain_term = jnp.sum(second_grads * residual_n, axis=0)
    pulled = second_grads * gain_moe
    residual_grads = upstream + moe_factor * (
        pulled - residual_n * jnp.mean(pulled * residual_n, axis=-1, keepdims=True)
    )
    branch_low = residual_grads.astype(BF16)

    branch_even, branch_odd = gather_seq(branch_low, S)
    head_grads = jnp.concatenate(
        [matmul_t(branch_even, own_output), matmul_t(branch_odd, own_output)], 0
    ).astype(BF16)
    head_grads = absolute(head_grads.reshape(S, T, C), s).reshape(L, C)
    attended_rel = relative(attended_blocks, s).reshape(2, L // 2, C)
    output_term = t_matmul(attended_rel[0], branch_even) + t_matmul(attended_rel[1], branch_odd)
    query_back, key_back, value_back = attention_backward(
        query_low, key_low, value_low, head_grads, lse, seg_row, seg_col
    )
    own_outs = scatter_sum(own_parts[0], after(own_parts[1], branch_even), S)
    other_outs = scatter_sum(other_parts[0], after(other_parts[1], own_outs), S).astype(BF16)
    other_outs = swap(other_outs, "fsdp", F, half_f).astype(F32)
    mixed = (residual + own_outs + other_outs).astype(BF16)[None]
    query_turned = rotate(query_back.astype(F32), cosine, -sine, heads)
    key_turned = rotate(key_back.astype(F32), cosine, -sine, heads)
    query_gain_term = jnp.sum(query_turned * query_n, axis=0)
    key_gain_term = jnp.sum(key_turned * key_n, axis=0)
    query_pulled = query_turned * gain_query
    key_pulled = key_turned * gain_key
    means = jnp.stack([jnp.sum(query_pulled * query_n, -1), jnp.sum(key_pulled * key_n, -1)], 0)
    means = sum_all(means, "seq", S) / D
    query_pre_low = (factors[0][:, None] * (query_pulled - query_n * means[0][:, None])).astype(BF16)
    key_pre_low = (factors[1][:, None] * (key_pulled - key_n * means[1][:, None])).astype(BF16)
    pre_low = jnp.concatenate([query_pre_low, key_pre_low, value_back], 1)
    pre_rel = relative(pre_low.reshape(S, T, 3 * C), s).reshape(2, L // 2, 3 * C)
    normed_grads = scatter_sum(
        matmul_t(pre_rel[0], w_qkv).astype(BF16), matmul_t(pre_rel[1], w_qkv).astype(BF16), S
    )

    def weight_sum(grads):
        term = t_matmul(normed_all, grads).astype(BF16)
        term = term.reshape(S, F, part, -1).transpose(1, 0, 2, 3)
        return scatter_rows(term, f, F).astype(BF16)

    value_term = weight_sum(value_back)
    turned_term = weight_sum(pre_low[:, : 2 * C])
    qkv_term = jnp.concatenate([turned_term, value_term], -1)
    qkv_term = lax.all_to_all(qkv_term, "seq", split_axis=0, concat_axis=0, tiled=True)
    qkv_term = qkv_term.reshape(S, part, 3, C).transpose(2, 1, 0, 3).reshape(3, part, D).astype(F32)
    grad_output = scatter_rows(output_term.astype(BF16).reshape(F, part, D), f, F)
    head_gains = lax.psum_scatter(
        jnp.stack([query_gain_term, key_gain_term], 1), "fsdp", scatter_dimension=0, tiled=True
    )
    attn_factor = rms_factor(inputs)
    inputs_n = inputs * attn_factor
    attn_gain_term = jnp.sum(normed_grads * inputs_n, axis=0)
    attn_pulled = normed_grads * gain_attn
    grad_tokens = residual_grads + attn_factor * (
        attn_pulled - inputs_n * jnp.mean(attn_pulled * inputs_n, axis=-1, keepdims=True)
    )
    gain_terms = jnp.concatenate([router_term, moe_gain_term[:, None], attn_gain_term[:, None]], 1)
    gain_terms = lax.psum_scatter(gain_terms, ("seq", "fsdp"), scatter_dimension=0, tiled=True)
    return (
        mixed,
        grad_tokens[None],
        qkv_term[0],
        qkv_term[1],
        qkv_term[2],
        grad_output,
        gain_terms[:, :E],
        gain_terms[:, E + 1],
        gain_terms[:, E],
        head_gains[:, 0],
        head_gains[:, 1],
        grad_gate,
        grad_up,
        grad_down,
    )


def solution(mesh):
    tokens_spec = P("fsdp", "seq", None)
    rows_spec = P(("seq", "fsdp"), None)
    gain_spec = P(("seq", "fsdp"))
    expert_spec = P("seq", "fsdp", None)
    in_specs = (
        (tokens_spec, P("fsdp", None), tokens_spec, tokens_spec)
        + (rows_spec,) * 5
        + (gain_spec,) * 4
        + (expert_spec,) * 3
    )
    out_specs = (tokens_spec,) * 2 + (rows_spec,) * 5 + (gain_spec,) * 4 + (expert_spec,) * 3
    return jax.shard_map(
        partial(per_device, mesh.shape["seq"], mesh.shape["fsdp"]),
        mesh=mesh,
        in_specs=in_specs,
        out_specs=out_specs,
        check_vma=False,
    )
```

```python
from functools import partial

import jax
import jax.numpy as jnp
from jax import lax
from jax.experimental import pallas as pl
from jax.experimental.pallas import tpu as pltpu
from jax.sharding import PartitionSpec as P

D = 2048
H = 16
DH = 128
E = 16
WINDOW = 1024
CAP = 144

EPSILON = 1e-06
ROPE_BASE = 50000.0
HIGHEST = lax.Precision.HIGHEST
BF16 = jnp.bfloat16
F32 = jnp.float32
MIB = 1024 * 1024


def matmul(left, right):
    return jnp.dot(left, right, preferred_element_type=F32)


def matmul_t(left, right):
    return lax.dot_general(left, right, (((1,), (1,)), ((), ())), preferred_element_type=F32)


def t_matmul(left, right):
    return lax.dot_general(left, right, (((0,), (0,)), ((), ())), preferred_element_type=F32)


def rms_factor(values):
    return lax.rsqrt(jnp.mean(values * values, axis=-1, keepdims=True) + EPSILON)


def swap(values, axis, size, mask):
    return lax.ppermute(values, axis, [(i, i ^ mask) for i in range(size)])


def high_bit(number):
    return 1 << (number.bit_length() - 1)


def low_bit(number):
    return number & -number


def after(values, *others):
    return lax.optimization_barrier((values, others))[0]


def gather_seq(values, size):
    rows = values.shape[0] // 2
    pieces = {0: values}
    for r in range(2, size, 2):
        if r == low_bit(r):
            pieces[r] = swap(values, "seq", size, r)
        else:
            up, down = high_bit(r), low_bit(r)
            pieces[r] = jnp.concatenate(
                [
                    swap(pieces[r ^ up][:rows], "seq", size, up),
                    swap(pieces[r ^ down][rows:], "seq", size, down),
                ],
                0,
            )
    even = jnp.concatenate([pieces[r] for r in range(0, size, 2)], 0)
    return even, swap(even, "seq", size, 1)


def relative(blocks, me):
    size = blocks.shape[0]
    order = list(range(0, size, 2)) + list(range(1, size, 2))
    return jnp.concatenate([lax.dynamic_slice_in_dim(blocks, me ^ r, 1, 0) for r in order], 0)


def absolute(blocks, me):
    size = blocks.shape[0]
    places = [((me ^ j) // 2) + ((me ^ j) % 2) * (size // 2) for j in range(size)]
    return jnp.concatenate([lax.dynamic_slice_in_dim(blocks, at, 1, 0) for at in places], 0)


def scatter_sum(even, got, size):
    rows = even.shape[0] // (size // 2)
    half = rows // 2

    def part(r, first, count):
        at = slice(r // 2 * rows + first, r // 2 * rows + first + count)
        return even[at].astype(F32) + got[at].astype(F32)

    sums = {r: [part(r, 0, half), part(r, half, half)] for r in range(0, size, 2)}
    for r in range(size - 2, 0, -2):
        if r == low_bit(r):
            whole = jnp.concatenate([value.astype(BF16) for value in sums[r]], 0)
            come = swap(whole, "seq", size, r).astype(F32)
            sums[0] = [sums[0][0] + come[:half], sums[0][1] + come[half:]]
        else:
            up, down = high_bit(r), low_bit(r)
            sums[r ^ up][0] += swap(sums[r][0].astype(BF16), "seq", size, up).astype(F32)
            sums[r ^ down][1] += swap(sums[r][1].astype(BF16), "seq", size, down).astype(F32)
    return jnp.concatenate(sums[0], 0)


def sum_all(values, axis, size):
    mask = 1
    while mask < size:
        values = values + swap(values, axis, size, mask)
        mask *= 2
    return values


def ring_pieces(values, size):
    pieces = [values]
    for _ in range(1, size):
        pieces.append(lax.ppermute(pieces[-1], "fsdp", [(i, (i + 1) % size) for i in range(size)]))
    return pieces


def place_ring(pieces, me, axis):
    size = len(pieces)
    shape = pieces[0].shape
    whole = jnp.zeros(shape[:axis] + (size,) + shape[axis:], pieces[0].dtype)
    for k, piece in enumerate(pieces):
        at = lax.rem(me + size - k, size)
        whole = lax.dynamic_update_slice_in_dim(whole, jnp.expand_dims(piece, axis), at, axis)
    return whole


def near_swaps(pieces, base, size):
    for r in range(1, size // 2):
        up = high_bit(r)
        pieces[base + r] = swap(pieces[base + (r ^ up)], "fsdp", size, up)


def gather_small(values, seq_size, fsdp_size, s, f):
    count = seq_size * fsdp_size
    whole = values[None]
    for axis, size in (("seq", seq_size), ("fsdp", fsdp_size)):
        mask = 1
        while mask < size:
            whole = jnp.concatenate([whole, swap(whole, axis, size, mask)], 0)
            mask *= 2
    index = jnp.arange(count, dtype=jnp.int32)
    source = ((index % fsdp_size) ^ f) * seq_size + ((index // fsdp_size) ^ s)
    pick = (source[:, None] == index[None, :]).astype(values.dtype)
    return matmul(pick, whole).astype(values.dtype)


def sum_near(send, keep, size, dep):
    got = after(swap(send, "fsdp", size, 1), dep)
    sums = {2 * k: keep[k].astype(F32) + got[k].astype(F32) for k in range(size // 2)}
    mask = 2
    while mask < size // 2:
        stay = [r for r in sums if not r & mask]
        moved = jnp.stack([sums[r | mask].astype(BF16) for r in stay], 0)
        got = swap(moved, "fsdp", size, mask)
        sums = {r: sums[r] + got[i].astype(F32) for i, r in enumerate(stay)}
        mask *= 2
    return sums


def scatter_down(terms, half, size, dep):
    sums = {r: terms[r].astype(F32) for r in range(half)}
    mask = 1
    while mask < half:
        stay = [r for r in sums if not r & mask]
        moved = terms[1::2] if mask == 1 else jnp.stack([sums[r | mask].astype(BF16) for r in stay])
        got = after(swap(moved, "fsdp", size, mask), dep)
        sums = {r: sums[r] + got[i].astype(F32) for i, r in enumerate(stay)}
        mask *= 2
    return sums[0]


def scatter_rows(partial_sum, me, size):
    sums = {
        r: lax.dynamic_index_in_dim(partial_sum, me ^ r, 0, keepdims=False).astype(F32)
        for r in range(size)
    }
    mask = 1
    while mask < size:
        stay = [r for r in sums if not r & mask]
        moved = jnp.stack([sums[r | mask].astype(BF16) for r in stay], 0)
        got = swap(moved, "fsdp", size, mask).astype(F32)
        sums = {r: sums[r] + got[i] for i, r in enumerate(stay)}
        mask *= 2
    return sums[0]


def allowed_keys(seg_row, seg_col, first_query, first_key, rows, span, half_window):
    query_at = first_query + lax.broadcasted_iota(jnp.int32, (span, rows), 1)
    key_at = first_key + lax.broadcasted_iota(jnp.int32, (span, rows), 0)
    return (jnp.abs(query_at - key_at) <= half_window) & (seg_col == seg_row)


def first_key_of(block, rows, span, length):
    start = jnp.clip(block * rows - (span - rows) // 2, 0, length - span)
    return pl.multiple_of(start, rows)


def forward_kernel(span, q_ref, k_ref, v_ref, seg_row_ref, seg_col_ref, o_ref, lse_ref):
    block = pl.program_id(1)
    rows, length = q_ref.shape[0], k_ref.shape[0]
    first_key = first_key_of(block, rows, span, length)
    keys = k_ref[pl.ds(first_key, span), :]
    values = v_ref[pl.ds(first_key, span), :]
    scores = matmul_t(keys, q_ref[...]) * DH ** (-0.5)
    allowed = allowed_keys(
        seg_row_ref[...],
        seg_col_ref[pl.ds(first_key, span), :],
        block * rows,
        first_key,
        rows,
        span,
        WINDOW // 2,
    )
    scores = jnp.where(allowed, scores, -1e30)
    peak = jnp.max(scores, axis=0, keepdims=True)
    expos = jnp.exp(scores - peak)
    totals = jnp.sum(expos, axis=0, keepdims=True)
    probs = (expos * (1.0 / totals)).astype(BF16)
    o_ref[...] = t_matmul(values, probs).T.astype(BF16)
    lse_ref[...] = (peak + jnp.log(totals))[None]


def backward_kernel(
    span,
    q_ref,
    k_ref,
    v_ref,
    do_ref,
    lse_ref,
    seg_row_ref,
    seg_col_ref,
    dq_ref,
    dk_ref,
    dv_ref,
    dk_sum,
    dv_sum,
):
    block = pl.program_id(1)
    rows, length = q_ref.shape[0], k_ref.shape[0]

    @pl.when(block == 0)
    def _():
        dk_sum[...] = jnp.zeros_like(dk_sum)
        dv_sum[...] = jnp.zeros_like(dv_sum)

    first_key = first_key_of(block, rows, span, length)
    at = pl.ds(first_key, span)
    keys = k_ref[at, :]
    values = v_ref[at, :]
    queries = q_ref[...]
    grads = do_ref[...]
    scores = matmul_t(keys, queries) * DH ** (-0.5)
    allowed = allowed_keys(
        seg_row_ref[...],
        seg_col_ref[at, :],
        block * rows,
        first_key,
        rows,
        span,
        WINDOW // 2,
    )
    probs = jnp.where(allowed, jnp.exp(scores - lse_ref[0]), 0.0)
    dv_sum[at, :] += matmul(probs.astype(BF16), grads)
    prob_grads = matmul_t(values, grads)
    center = jnp.sum(probs * prob_grads, axis=0, keepdims=True)
    score_grads = (probs * (prob_grads - center)).astype(BF16)
    dk_sum[at, :] += matmul(score_grads, queries)
    dq_ref[...] = (t_matmul(keys, score_grads) * DH ** (-0.5)).T.astype(BF16)

    @pl.when(block == length // rows - 1)
    def _():
        dk_ref[...] = (dk_sum[...] * DH ** (-0.5)).astype(BF16)
        dv_ref[...] = dv_sum[...].astype(BF16)


def attention_sizes(length):
    rows = 256
    return rows, min(length, rows + WINDOW)


def attention_forward(queries, keys, values, seg_row, seg_col):
    length, columns = queries.shape
    heads = columns // DH
    rows, span = attention_sizes(length)
    block = pl.BlockSpec((rows, DH), lambda h, i: (i, h))
    whole = pl.BlockSpec((length, DH), lambda h, i: (0, h))
    return pl.pallas_call(
        partial(forward_kernel, span),
        grid=(heads, length // rows),
        in_specs=[
            block,
            whole,
            whole,
            pl.BlockSpec((1, rows), lambda h, i: (0, i)),
            pl.BlockSpec((length, 1), lambda h, i: (0, 0)),
        ],
        out_specs=[block, pl.BlockSpec((1, 1, rows), lambda h, i: (h, 0, i))],
        out_shape=[
            jax.ShapeDtypeStruct((length, columns), BF16),
            jax.ShapeDtypeStruct((heads, 1, length), F32),
        ],
        compiler_params=pltpu.CompilerParams(vmem_limit_bytes=48 * MIB),
        cost_estimate=pl.CostEstimate(
            flops=4 * heads * length * span * DH,
            bytes_accessed=8 * length * columns,
            transcendentals=heads * length * span,
        ),
        name="attend",
    )(queries, keys, values, seg_row, seg_col)


def attention_backward(queries, keys, values, grads, lse, seg_row, seg_col):
    length, columns = queries.shape
    heads = columns // DH
    rows, span = attention_sizes(length)
    block = pl.BlockSpec((rows, DH), lambda h, i: (i, h))
    whole = pl.BlockSpec((length, DH), lambda h, i: (0, h))
    shape = jax.ShapeDtypeStruct((length, columns), BF16)
    return pl.pallas_call(
        partial(backward_kernel, span),
        grid=(heads, length // rows),
        in_specs=[
            block,
            whole,
            whole,
            block,
            pl.BlockSpec((1, 1, rows), lambda h, i: (h, 0, i)),
            pl.BlockSpec((1, rows), lambda h, i: (0, i)),
            pl.BlockSpec((length, 1), lambda h, i: (0, 0)),
        ],
        out_specs=[block, whole, whole],
        out_shape=[shape, shape, shape],
        scratch_shapes=[pltpu.VMEM((length, DH), F32), pltpu.VMEM((length, DH), F32)],
        compiler_params=pltpu.CompilerParams(vmem_limit_bytes=48 * MIB),
        cost_estimate=pl.CostEstimate(
            flops=10 * heads * length * span * DH,
            bytes_accessed=14 * length * columns,
            transcendentals=heads * length * span,
        ),
        name="attend_back",
    )(queries, keys, values, grads, lse, seg_row, seg_col)


def qkv_kernel(
    me_ref, even_ref, odd_ref, weight_ref, gain_ref, normed_ref, q_ref, k_ref, v_ref, square_ref
):
    turned = me_ref[0] % 2 == 1
    rows = even_ref.shape[0]
    columns = q_ref.shape[1]
    first, second = even_ref[...], odd_ref[...]
    blocks = (jnp.where(turned, second, first), jnp.where(turned, first, second))
    for k, block in enumerate(blocks):
        at = pl.ds(k * rows, rows)
        wide = block.astype(F32)
        normed = (wide * rms_factor(wide) * gain_ref[...]).astype(BF16)
        normed_ref[at, :] = normed
        pre = matmul(normed, weight_ref[...])
        q_ref[at, :] = pre[:, :columns]
        k_ref[at, :] = pre[:, columns : 2 * columns]
        v_ref[at, :] = pre[:, 2 * columns :].astype(BF16)
        for j in range(2):
            squares = 0.0
            for c in range(j * columns, (j + 1) * columns, DH):
                squares += pre[:, c : c + DH] * pre[:, c : c + DH]
            square_ref[j : j + 1, at] = jnp.sum(squares.T, axis=0, keepdims=True)


def project(even, odd, weight, gain, me, rows):
    pairs = even.shape[0] // rows
    length = 2 * even.shape[0]
    depth, columns = weight.shape[0], weight.shape[1] // 3
    token = pl.BlockSpec((rows, depth), lambda i, me: (i, 0))

    def placed(shape):
        return pl.BlockSpec(shape, lambda i, me: (i ^ (me[0] // 2), 0))

    head = jax.ShapeDtypeStruct((length, columns), F32)
    return pl.pallas_call(
        qkv_kernel,
        grid_spec=pltpu.PrefetchScalarGridSpec(
            num_scalar_prefetch=1,
            grid=(pairs,),
            in_specs=[
                token,
                token,
                pl.BlockSpec(weight.shape, lambda i, me: (0, 0)),
                pl.BlockSpec((1, depth), lambda i, me: (0, 0)),
            ],
            out_specs=[
                placed((2 * rows, depth)),
                placed((2 * rows, columns)),
                placed((2 * rows, columns)),
                placed((2 * rows, columns)),
                pl.BlockSpec((2, 2 * rows), lambda i, me: (0, i ^ (me[0] // 2))),
            ],
        ),
        out_shape=[
            jax.ShapeDtypeStruct((length, depth), BF16),
            head,
            head,
            jax.ShapeDtypeStruct((length, columns), BF16),
            jax.ShapeDtypeStruct((2, length), F32),
        ],
        compiler_params=pltpu.CompilerParams(vmem_limit_bytes=48 * MIB),
        cost_estimate=pl.CostEstimate(
            flops=6 * length * depth * columns,
            bytes_accessed=length * (4 * depth + 10 * columns) + 6 * depth * columns,
            transcendentals=length,
        ),
        name="project",
    )(me, even, odd, weight, gain)


def expert_kernel(pieces, first_ref, xa_ref, xb_ref, ua_ref, ub_ref, ra_ref, rb_ref, router_ref, *refs):
    weight_refs = refs[: sum(pieces)]
    (ya_ref, yb_ref, za_ref, zb_ref, ga_ref, gb_ref, xc_ref, uc_ref, dg_ref, hid_ref) = refs[-13:-3]
    wi_ref, wd_ref, sems = refs[-3:]
    experts, _, hidden = hid_ref.shape
    rows = xa_ref.shape[0]

    @pl.when(pl.program_id(0) == 0)
    def _():
        copies = []
        for r, ref in enumerate(weight_refs[: pieces[0]]):
            part = ref.shape[1]
            at = pl.ds(pl.multiple_of((first_ref[1] ^ r) * part, part), part)
            copies.append(pltpu.make_async_copy(ref, wi_ref.at[:, at, :], sems.at[r]))
        for r, ref in enumerate(weight_refs[pieces[0] :]):
            part = ref.shape[1]
            place = lax.rem(first_ref[1] ^ r, pieces[1])
            at = pl.ds(pl.multiple_of(place * part, part), part)
            copies.append(pltpu.make_async_copy(ref, wd_ref.at[:, at, :], sems.at[pieces[0] + r]))
        for copy in copies:
            copy.start()
        for copy in copies:
            copy.wait()

    slot = lax.broadcasted_iota(jnp.int32, (CAP, rows), 0)
    blocks = (
        (xa_ref, ua_ref, ra_ref, ya_ref, za_ref, ga_ref),
        (xb_ref, ub_ref, rb_ref, yb_ref, zb_ref, gb_ref),
    )
    picks = []
    for k, (x_ref, u_ref, rank_ref, _, _, _) in enumerate(blocks):
        hits = jnp.concatenate([slot == rank_ref[0, e : e + 1, :] for e in range(experts)], 0)
        pick = hits.astype(F32).astype(BF16)
        picks.append(pick)
        x_rows = matmul(pick, x_ref[...]).astype(BF16)
        u_rows = matmul(pick, u_ref[...]).astype(BF16)
        for e in range(experts):
            xc_ref[e, k * CAP : (k + 1) * CAP, :] = x_rows[e * CAP : (e + 1) * CAP]
            uc_ref[e, k * CAP : (k + 1) * CAP, :] = u_rows[e * CAP : (e + 1) * CAP]
    outs, backs, gate_grads = [], [], []
    for e in range(experts):
        x_rows, u_rows = xc_ref[e], uc_ref[e]
        logits = matmul(x_rows, router_ref[...])
        lane = lax.broadcasted_iota(jnp.int32, logits.shape, 1)
        logits = jnp.where(lane < E, logits, -1e30)
        expos = jnp.exp(logits - jnp.max(logits, axis=-1, keepdims=True))
        own = jnp.sum(jnp.where(lane == first_ref[0] + e, expos, 0.0), axis=-1, keepdims=True)
        gate = own / jnp.sum(expos, axis=-1, keepdims=True)
        gated = matmul(x_rows, wi_ref[e, :, :hidden])
        upward = matmul(x_rows, wi_ref[e, :, hidden:])
        pulled = matmul_t(u_rows, wd_ref[e])
        sig = jax.nn.sigmoid(gated)
        silu = gated * sig
        acts = silu * upward
        gate_grads.append(jnp.sum(acts * pulled, axis=-1, keepdims=True))
        hidden_gate = (acts * gate).astype(BF16)
        hidden_grads = pulled * gate
        hid_ref[e] = hidden_gate
        dg_ref[e, :, :hidden] = (hidden_grads * upward * sig * (1.0 + gated * (1.0 - sig))).astype(BF16)
        dg_ref[e, :, hidden:] = (hidden_grads * silu).astype(BF16)
        outs.append(matmul(hidden_gate, wd_ref[e]).astype(BF16))
        backs.append(matmul_t(dg_ref[e], wi_ref[e]).astype(BF16))
    for k, (_, _, rank_ref, y_ref, z_ref, g_ref) in enumerate(blocks):
        at = slice(k * CAP, (k + 1) * CAP)
        y_ref[...] = t_matmul(picks[k], jnp.concatenate([v[at] for v in outs], 0)).astype(BF16)
        z_ref[...] = t_matmul(picks[k], jnp.concatenate([v[at] for v in backs], 0)).astype(BF16)
        for e in range(experts):
            hit = slot == rank_ref[0, e : e + 1, :]
            g_ref[0, e : e + 1, :] = jnp.sum(
                jnp.where(hit, gate_grads[e][at], 0.0), axis=0, keepdims=True
            )


def run_experts(x, u, ranks, in_pieces, down_pieces, router, places, which, compact):
    experts, part, hidden = in_pieces[0].shape
    hidden //= 2
    depth = part * len(in_pieces)
    rows = ranks[0].shape[2]
    steps = x[0].shape[0] // rows
    token = pl.BlockSpec((rows, depth), lambda i: (i, 0))
    rank = pl.BlockSpec((1, experts, rows), lambda i: (i, 0, 0))
    anywhere = pl.BlockSpec(memory_space=pl.ANY)

    def slots(columns):
        return pl.BlockSpec((experts, 2 * CAP, columns), lambda i: (0, i + which * steps, 0))

    shape = jax.ShapeDtypeStruct
    tokens = shape(x[0].shape, BF16)
    gates = shape((steps, experts, rows), F32)
    count = 4 * steps * CAP
    wide = shape((experts, count, depth), BF16)
    pieces = (len(in_pieces), len(down_pieces))
    inputs = [places, *x, *u, *ranks, router, *in_pieces, *down_pieces]
    return pl.pallas_call(
        partial(expert_kernel, pieces),
        grid=(steps,),
        in_specs=[pl.BlockSpec(memory_space=pltpu.SMEM)]
        + [token] * 4
        + [rank] * 2
        + [pl.BlockSpec(router.shape, lambda i: (0, 0), pipeline_mode=pl.Buffered(1))]
        + [anywhere] * (sum(pieces) + len(compact)),
        out_specs=[token] * 4 + [rank] * 2 + [slots(depth)] * 2 + [slots(2 * hidden), slots(hidden)],
        out_shape=[tokens] * 4
        + [gates] * 2
        + [wide] * 2
        + [shape((experts, count, 2 * hidden), BF16), shape((experts, count, hidden), BF16)],
        scratch_shapes=[
            pltpu.VMEM((experts, depth, 2 * hidden), BF16),
            pltpu.VMEM((experts, hidden, depth), BF16),
            pltpu.SemaphoreType.DMA((sum(pieces),)),
        ],
        input_output_aliases={len(inputs) + i: 6 + i for i in range(len(compact))},
        compiler_params=pltpu.CompilerParams(vmem_limit_bytes=60 * MIB),
        cost_estimate=pl.CostEstimate(
            flops=4 * steps * CAP * experts * depth * (7 * hidden + 2 * rows),
            bytes_accessed=60 * MIB,
            transcendentals=2 * steps * CAP * experts * hidden,
        ),
        name="experts",
    )(*inputs, *compact)


def product_kernel(me_ref, left_ref, right_ref, out_ref):
    out_ref[0, 0] = t_matmul(left_ref[0], right_ref[0]).astype(BF16)


def products(left, right, part, chosen, count, me, name):
    experts, rows, _ = left.shape
    columns = right.shape[2]
    wide = min(columns, 1024)
    start, step = chosen[0], chosen[1] - chosen[0] if len(chosen) > 1 else 1

    def place(e, k, j, me):
        return (e, 0, lax.rem(me[0] ^ (start + step * k), count))

    return pl.pallas_call(
        product_kernel,
        grid_spec=pltpu.PrefetchScalarGridSpec(
            num_scalar_prefetch=1,
            grid=(experts, len(chosen), columns // wide),
            in_specs=[
                pl.BlockSpec((1, rows, part), place),
                pl.BlockSpec((1, rows, wide), lambda e, k, j, me: (e, 0, j)),
            ],
            out_specs=pl.BlockSpec((1, 1, part, wide), lambda e, k, j, me: (k, e, 0, j)),
        ),
        out_shape=jax.ShapeDtypeStruct((len(chosen), experts, part, columns), BF16),
        compiler_params=pltpu.CompilerParams(vmem_limit_bytes=56 * MIB),
        cost_estimate=pl.CostEstimate(
            flops=2 * len(chosen) * experts * rows * part * columns,
            bytes_accessed=2 * experts * rows * (part * len(chosen) + columns),
            transcendentals=0,
        ),
        name=name,
    )(me, left, right)


def rotate(values, cosine, sine, heads):
    half = DH // 2
    shaped = values.reshape(values.shape[0], heads, DH)
    first, second = shaped[..., :half], shaped[..., half:]
    cosine, sine = cosine[:, None, :], sine[:, None, :]
    return jnp.concatenate(
        [first * cosine - second * sine, second * cosine + first * sine], axis=-1
    ).reshape(values.shape)


def per_device(
    S,
    F,
    tokens,
    segments,
    routes,
    cotangent,
    w_query,
    w_key,
    w_value,
    w_output,
    router,
    attn_gain,
    moe_gain,
    query_gain,
    key_gain,
    w_gate,
    w_up,
    w_down,
):
    s = lax.axis_index("seq")
    f = lax.axis_index("fsdp")
    T = tokens.shape[1]
    L = S * T
    heads = H // S
    C = heads * DH
    experts = E // S
    part = w_query.shape[0]
    half_f = F // 2
    hidden_half = w_gate.shape[2] // 2

    tokens_low = tokens[0]
    inputs = tokens_low.astype(F32)
    small = jnp.concatenate(
        [
            router.reshape(-1),
            attn_gain,
            moe_gain,
            query_gain,
            key_gain,
            routes[0].astype(BF16).reshape(-1),
        ]
    )
    tokens_even, tokens_odd = gather_seq(tokens_low, S)
    small = gather_small(small, S, F, s, f).reshape(S, F, -1)

    stacked = jnp.stack([w_query, w_key, w_value], 1).reshape(part, 3, S, C)
    stacked = stacked.transpose(2, 0, 1, 3).reshape(S, part, 3 * C)
    crossed = lax.all_to_all(stacked, "seq", split_axis=0, concat_axis=0, tiled=True)
    output_ring = ring_pieces(w_output, F)
    own_output = place_ring(output_ring, f, 0).reshape(C, D)
    qkv_ring = ring_pieces(after(crossed, output_ring[-1]), F)
    w_qkv = place_ring(qkv_ring, f, 1).reshape(D, 3 * C)

    full_router = small[:, :, : part * E].reshape(D, E)
    gains = [
        small[:, :, part * (E + i) : part * (E + i + 1)].reshape(D).astype(F32) for i in range(4)
    ]
    gain_attn, gain_moe = gains[0], gains[1]
    gain_query = lax.dynamic_slice_in_dim(gains[2], s * C, C, 0)
    gain_key = lax.dynamic_slice_in_dim(gains[3], s * C, C, 0)
    route_part = small[:, :, part * (E + 4) :].reshape(S, F, T, -1)
    expert_ids = s * experts + jnp.arange(experts, dtype=jnp.int32)

    def ranks_of(index):
        named = lax.dynamic_index_in_dim(route_part, index, 1, keepdims=False)
        named = relative(named, s).astype(jnp.int32)
        chosen = jnp.any(named[:, None] == expert_ids[None, :, None, None], axis=-1)
        ranks = jnp.cumsum(chosen.astype(jnp.int32), axis=-1) - 1
        ranks = jnp.where(chosen, ranks, -1)
        return ranks[: S // 2], ranks[S // 2 :]

    half_at = f // half_f

    def hidden_part(which):
        at = which * hidden_half
        return jnp.concatenate(
            [lax.dynamic_slice_in_dim(weight, at, hidden_half, 2) for weight in (w_gate, w_up)], 2
        )

    in_pieces = {0: hidden_part(half_at)}
    far_part = swap(after(hidden_part(1 - half_at), qkv_ring[-2]), "fsdp", F, half_f)
    in_pieces[0] = after(in_pieces[0], qkv_ring[-1])
    near_swaps(in_pieces, 0, F)

    upstream_low = cotangent[0]
    own_u = gather_seq(after(upstream_low, tokens_even), S)
    out_even, out_odd = gather_seq(after(own_output, own_u[0]), S)

    me = s.reshape(1).astype(jnp.int32)
    normed_all, query_pre, key_pre, value_low, squares = project(
        tokens_even, tokens_odd, w_qkv, gain_attn[None], me, T
    )
    places = jnp.arange(L, dtype=jnp.int32).astype(F32)
    freqs = ROPE_BASE ** (-(jnp.arange(DH // 2, dtype=F32) * 2.0 / DH))
    angles = places[:, None] * freqs[None, :]
    cosine, sine = jnp.cos(angles), jnp.sin(angles)
    factors = lax.rsqrt(sum_all(squares, "seq", S) / D + EPSILON)
    query_n = query_pre * factors[0][:, None]
    key_n = key_pre * factors[1][:, None]
    query_low = rotate(query_n * gain_query, cosine, sine, heads).astype(BF16)
    key_low = rotate(key_n * gain_key, cosine, sine, heads).astype(BF16)
    seg_row = segments
    seg_col = segments.reshape(L, 1)
    attended, lse = attention_forward(query_low, key_low, value_low, seg_row, seg_col)
    attended_blocks = attended.reshape(S, T, C)
    in_pieces[half_f] = after(far_part, attended)
    near_swaps(in_pieces, half_f, F)
    come = lax.all_to_all(attended_blocks, "seq", split_axis=0, concat_axis=0, tiled=True)
    come = relative(come, s).transpose(1, 0, 2).reshape(T, D)
    residual = inputs + matmul(come[:, : D // 2], out_even) + matmul(come[:, D // 2 :], out_odd)

    moe_factor = rms_factor(residual)
    residual_n = residual * moe_factor
    second_low = (residual_n * gain_moe).astype(BF16)
    partner_low = swap(second_low, "fsdp", F, half_f)
    own_x = gather_seq(second_low, S)
    down_pieces = {0: after(w_down, own_x[0])}
    near_swaps(down_pieces, 0, F)
    other_x = gather_seq(after(partner_low, own_x[0]), S)
    partner_up = swap(after(upstream_low, partner_low), "fsdp", F, half_f)
    other_u = gather_seq(after(partner_up, other_x[0]), S)
    logits = matmul(second_low, full_router)
    router_probs = jax.nn.softmax(logits, axis=-1)
    in_pieces = [in_pieces[r] for r in range(F)]
    down_pieces = [down_pieces[r] for r in range(half_f)]
    wide_router = jnp.pad(full_router, ((0, 0), (0, 128 - E)))
    expert_places = jnp.stack([s * experts, f]).astype(jnp.int32)
    own_parts = run_experts(
        own_x, own_u, ranks_of(f), in_pieces, down_pieces, wide_router, expert_places, 0, ()
    )
    other_parts = run_experts(
        other_x,
        other_u,
        ranks_of(f ^ half_f),
        in_pieces,
        down_pieces,
        wide_router,
        expert_places,
        1,
        own_parts[6:],
    )
    x_rows, u_rows, in_grads, hidden_gate = other_parts[6:]
    own_got = swap(own_parts[3], "seq", S, 1)
    other_got = swap(other_parts[3], "seq", S, 1)
    other_rows = scatter_sum(other_parts[2], other_got, S).astype(BF16)
    own_rows = scatter_sum(own_parts[2], after(own_got, other_rows), S)
    back_rows = swap(other_rows, "fsdp", F, half_f)
    row_grads = own_rows + back_rows.astype(F32)

    def to_home(even, odd):
        return absolute(jnp.concatenate([even, odd], 0).transpose(0, 2, 1), s)

    gate_grads = jnp.stack(
        [to_home(own_parts[4], own_parts[5]), to_home(other_parts[4], other_parts[5])], 1
    )
    gate_grads = lax.all_to_all(
        gate_grads.reshape(S, -1), "seq", split_axis=0, concat_axis=0, tiled=True
    ).reshape(S, 2, T * experts)
    gate_grads = gate_grads[:, 0] + swap(gate_grads[:, 1], "fsdp", F, half_f)
    gate_grads = gate_grads.reshape(S, T, experts).transpose(1, 0, 2).reshape(T, E)

    f_at = f.reshape(1).astype(jnp.int32)
    down_part = w_down.shape[1]
    in_part = w_gate.shape[1]
    hidden_gate = after(hidden_gate, other_got)
    down_terms = products(
        hidden_gate, u_rows, down_part, range(half_f), half_f, f_at, "down_products"
    )
    in_grads = after(in_grads, other_rows)
    in_send = products(x_rows, in_grads, in_part, range(1, F, 2), F, f_at, "in_products_sent")
    in_keep = products(x_rows, in_grads, in_part, range(0, F, 2), F, f_at, "in_products_kept")

    upstream = upstream_low.astype(F32)
    logit_grads = router_probs * (
        gate_grads - jnp.sum(router_probs * gate_grads, axis=-1, keepdims=True)
    )
    router_wide = full_router.astype(F32)
    second_grads = row_grads + jnp.dot(logit_grads, router_wide.T, precision=HIGHEST)
    router_term = jnp.dot(second_low.astype(F32).T, logit_grads, precision=HIGHEST)
    moe_gain_term = jnp.sum(second_grads * residual_n, axis=0)
    pulled = second_grads * gain_moe
    residual_grads = upstream + moe_factor * (
        pulled - residual_n * jnp.mean(pulled * residual_n, axis=-1, keepdims=True)
    )
    branch_low = residual_grads.astype(BF16)

    branch_even, branch_odd = gather_seq(branch_low, S)
    head_grads = jnp.concatenate(
        [matmul_t(branch_even, own_output), matmul_t(branch_odd, own_output)], 0
    ).astype(BF16)
    head_grads = absolute(head_grads.reshape(S, T, C), s).reshape(L, C)
    attended_rel = relative(attended_blocks, s).reshape(2, L // 2, C)
    query_back, key_back, value_back = attention_backward(
        query_low, key_low, value_low, head_grads, lse, seg_row, seg_col
    )
    attended_rel = after(attended_rel, query_back)
    output_term = t_matmul(attended_rel[0], branch_even) + t_matmul(attended_rel[1], branch_odd)
    own_out_got = after(swap(after(own_parts[1], branch_even), "seq", S, 1), query_back)
    other_out_got = after(swap(after(other_parts[1], own_out_got), "seq", S, 1), query_back)
    other_outs = scatter_sum(other_parts[0], other_out_got, S).astype(BF16)
    own_outs = scatter_sum(own_parts[0], after(own_out_got, other_outs), S)
    down_sums = scatter_down(down_terms, half_f, F, query_back)
    in_sums = sum_near(in_send, in_keep, F, query_back)
    far_sums = swap(in_sums[half_f].astype(BF16), "fsdp", F, half_f).astype(F32)
    first_half = half_at == 0
    lower = jnp.where(first_half, in_sums[0], far_sums)
    upper = jnp.where(first_half, far_sums, in_sums[0])
    grad_gate, grad_up = (
        jnp.concatenate([lower[..., at], upper[..., at]], axis=-1)
        for at in (slice(0, hidden_half), slice(hidden_half, 2 * hidden_half))
    )
    other_outs = swap(other_outs, "fsdp", F, half_f).astype(F32)
    mixed = (residual + own_outs + other_outs).astype(BF16)[None]
    query_turned = rotate(query_back.astype(F32), cosine, -sine, heads)
    key_turned = rotate(key_back.astype(F32), cosine, -sine, heads)
    query_gain_term = jnp.sum(query_turned * query_n, axis=0)
    key_gain_term = jnp.sum(key_turned * key_n, axis=0)
    query_pulled = query_turned * gain_query
    key_pulled = key_turned * gain_key
    means = jnp.stack([jnp.sum(query_pulled * query_n, -1), jnp.sum(key_pulled * key_n, -1)], 0)
    means = sum_all(means, "seq", S) / D
    query_pre_low = (factors[0][:, None] * (query_pulled - query_n * means[0][:, None])).astype(BF16)
    key_pre_low = (factors[1][:, None] * (key_pulled - key_n * means[1][:, None])).astype(BF16)
    pre_low = jnp.concatenate([query_pre_low, key_pre_low, value_back], 1)
    pre_rel = relative(pre_low.reshape(S, T, 3 * C), s).reshape(2, L // 2, 3 * C)
    normed_got = swap(matmul_t(pre_rel[1], w_qkv).astype(BF16), "seq", S, 1)
    normed_grads = scatter_sum(matmul_t(pre_rel[0], w_qkv).astype(BF16), normed_got, S)

    def weight_sum(grads):
        term = t_matmul(normed_all, grads).astype(BF16)
        term = term.reshape(S, F, part, -1).transpose(1, 0, 2, 3)
        return scatter_rows(term, f, F).astype(BF16)

    value_term = weight_sum(value_back)
    turned_term = weight_sum(pre_low[:, : 2 * C])
    qkv_term = jnp.concatenate([turned_term, value_term], -1)
    qkv_term = lax.all_to_all(qkv_term, "seq", split_axis=0, concat_axis=0, tiled=True)
    qkv_term = qkv_term.reshape(S, part, 3, C).transpose(2, 1, 0, 3).reshape(3, part, D).astype(F32)
    grad_output = scatter_rows(output_term.astype(BF16).reshape(F, part, D), f, F)
    head_gains = lax.psum_scatter(
        jnp.stack([query_gain_term, key_gain_term], 1), "fsdp", scatter_dimension=0, tiled=True
    )
    attn_factor = rms_factor(inputs)
    inputs_n = inputs * attn_factor
    attn_pulled = normed_grads * gain_attn
    grad_tokens = residual_grads + attn_factor * (
        attn_pulled - inputs_n * jnp.mean(attn_pulled * inputs_n, axis=-1, keepdims=True)
    )
    gain_terms = jnp.concatenate([router_term, moe_gain_term[:, None]], 1)
    gain_terms = lax.psum_scatter(gain_terms, ("seq", "fsdp"), scatter_dimension=0, tiled=True)
    own_weights = jnp.stack([w_query, w_key, w_value], 0).astype(F32)
    grad_attn_gain = jnp.sum(qkv_term * own_weights, axis=(0, 2)) / attn_gain.astype(F32)
    return (
        mixed,
        grad_tokens[None],
        qkv_term[0],
        qkv_term[1],
        qkv_term[2],
        grad_output,
        gain_terms[:, :E],
        grad_attn_gain,
        gain_terms[:, E],
        head_gains[:, 0],
        head_gains[:, 1],
        grad_gate,
        grad_up,
        down_sums,
    )


def solution(mesh):
    tokens_spec = P("fsdp", "seq", None)
    rows_spec = P(("seq", "fsdp"), None)
    gain_spec = P(("seq", "fsdp"))
    expert_spec = P("seq", "fsdp", None)
    in_specs = (
        (tokens_spec, P("fsdp", None), tokens_spec, tokens_spec)
        + (rows_spec,) * 5
        + (gain_spec,) * 4
        + (expert_spec,) * 3
    )
    out_specs = (tokens_spec,) * 2 + (rows_spec,) * 5 + (gain_spec,) * 4 + (expert_spec,) * 3
    return jax.shard_map(
        partial(per_device, mesh.shape["seq"], mesh.shape["fsdp"]),
        mesh=mesh,
        in_specs=in_specs,
        out_specs=out_specs,
        check_vma=False,
    )
```

```python
from functools import partial

import jax
import jax.numpy as jnp
from jax import lax
from jax.experimental import pallas as pl
from jax.experimental.pallas import tpu as pltpu
from jax.sharding import PartitionSpec as P

D = 2048
H = 16
DH = 128
E = 16
WINDOW = 1024
CAP = 144

EPSILON = 1e-06
ROPE_BASE = 50000.0
HIGHEST = lax.Precision.HIGHEST
BF16 = jnp.bfloat16
F32 = jnp.float32
MIB = 1024 * 1024


def matmul(left, right):
    return jnp.dot(left, right, preferred_element_type=F32)


def matmul_t(left, right):
    return lax.dot_general(left, right, (((1,), (1,)), ((), ())), preferred_element_type=F32)


def t_matmul(left, right):
    return lax.dot_general(left, right, (((0,), (0,)), ((), ())), preferred_element_type=F32)


def rms_factor(values):
    return lax.rsqrt(jnp.mean(values * values, axis=-1, keepdims=True) + EPSILON)


def swap(values, axis, size, mask):
    return lax.ppermute(values, axis, [(i, i ^ mask) for i in range(size)])


def high_bit(number):
    return 1 << (number.bit_length() - 1)


def low_bit(number):
    return number & -number


def after(values, *others):
    return lax.optimization_barrier((values, others))[0]


def tie(*values):
    return lax.optimization_barrier(values)


def gather_first(values, size):
    return {r: swap(values, "seq", size, r) for r in range(2, size, 2) if r == low_bit(r)}


def gather_more(values, first, size):
    rows = values.shape[0] // 2
    pieces = dict(first)
    for r in range(2, size, 2):
        if r not in pieces:
            up, down = high_bit(r), low_bit(r)
            upper, lower = pieces[r ^ up], pieces[r ^ down]
            upper = upper[0] if isinstance(upper, tuple) else upper[:rows]
            lower = lower[1] if isinstance(lower, tuple) else lower[rows:]
            pieces[r] = (swap(upper, "seq", size, up), swap(lower, "seq", size, down))
    return {r: piece for r, piece in pieces.items() if r not in first}


def gather_end(values, first, more, size):
    blocks = [values]
    for r in range(2, size, 2):
        blocks.extend([first[r]] if r in first else more[r])
    even = jnp.concatenate(blocks, 0)
    return even, swap(even, "seq", size, 1)


def relative(blocks, me):
    size = blocks.shape[0]
    order = list(range(0, size, 2)) + list(range(1, size, 2))
    return jnp.concatenate([lax.dynamic_slice_in_dim(blocks, me ^ r, 1, 0) for r in order], 0)


def absolute(blocks, me):
    size = blocks.shape[0]
    places = [((me ^ j) // 2) + ((me ^ j) % 2) * (size // 2) for j in range(size)]
    return jnp.concatenate([lax.dynamic_slice_in_dim(blocks, at, 1, 0) for at in places], 0)


def sum_first(even, got, size, dep=()):
    rows = even.shape[0] // (size // 2)
    half = rows // 2

    def part(r, first, count):
        at = slice(r // 2 * rows + first, r // 2 * rows + first + count)
        return even[at].astype(F32) + got[at].astype(F32)

    sums = {r: [part(r, 0, half), part(r, half, half)] for r in range(0, size, 2)}
    for r in range(size - 2, 0, -2):
        if r != low_bit(r):
            up, down = high_bit(r), low_bit(r)
            upper = after(swap(sums[r][0].astype(BF16), "seq", size, up), dep)
            lower = after(swap(sums[r][1].astype(BF16), "seq", size, down), dep)
            sums[r ^ up][0] += upper.astype(F32)
            sums[r ^ down][1] += lower.astype(F32)
            del sums[r]
    return {
        r: jnp.concatenate([v.astype(BF16) if r else v for v in value], 0)
        for r, value in sums.items()
    }


def sum_last(sums, size, dep=()):
    total = sums[0]
    for r in sums:
        if r:
            total += after(swap(sums[r], "seq", size, r), dep).astype(F32)
    return total


def sum_all(values, axis, size):
    mask = 1
    while mask < size:
        values = values + swap(values, axis, size, mask)
        mask *= 2
    return values


def fsdp_pieces(values, size):
    pieces = {0: values}
    for r in range(1, size):
        low = low_bit(r)
        pieces[r] = swap(pieces[r ^ low], "fsdp", size, low)
    return pieces


def place_fsdp(pieces, me, axis):
    size = len(pieces)
    shape = pieces[0].shape
    whole = jnp.zeros(shape[:axis] + (size,) + shape[axis:], pieces[0].dtype)
    for r, piece in pieces.items():
        whole = lax.dynamic_update_slice_in_dim(whole, jnp.expand_dims(piece, axis), me ^ r, axis)
    return whole


def near_pieces(values, size):
    pieces = {0: values}
    for r in range(1, size // 2):
        up = high_bit(r)
        pieces[r] = swap(pieces[r ^ up], "fsdp", size, up)
    return pieces


def gather_small(values, seq_size, fsdp_size, s, f):
    count = seq_size * fsdp_size
    whole = values[None]
    for axis, size in (("seq", seq_size), ("fsdp", fsdp_size)):
        mask = 1
        while mask < size:
            whole = jnp.concatenate([whole, swap(whole, axis, size, mask)], 0)
            mask *= 2
    index = jnp.arange(count, dtype=jnp.int32)
    source = ((index % fsdp_size) ^ f) * seq_size + ((index // fsdp_size) ^ s)
    pick = (source[:, None] == index[None, :]).astype(values.dtype)
    return matmul(pick, whole).astype(values.dtype)


def sum_small(values, axes):
    count = values.shape[0]
    index = jnp.arange(count, dtype=jnp.int32)
    source, stride = jnp.zeros_like(index), 1
    for _, size, me in reversed(axes):
        source += ((index // stride % size) ^ me) * stride
        stride *= size
    pick = (source[:, None] == index[None, :]).astype(F32)
    values = jnp.dot(pick, values, precision=HIGHEST)
    for name, size, _ in axes:
        mask = size // 2
        while mask:
            half = values.shape[0] // 2
            values = values[:half] + swap(values[half:], name, size, mask)
            mask //= 2
    return values[0]


def scatter_rows(partial_sum, me, size):
    sums = {
        r: lax.dynamic_index_in_dim(partial_sum, me ^ r, 0, keepdims=False).astype(F32)
        for r in range(size)
    }
    mask = 1
    while mask < size:
        stay = [r for r in sums if not r & mask]
        moved = jnp.stack([sums[r | mask].astype(BF16) for r in stay], 0)
        got = swap(moved, "fsdp", size, mask).astype(F32)
        sums = {r: sums[r] + got[i] for i, r in enumerate(stay)}
        mask *= 2
    return sums[0]


def allowed_keys(seg_row, seg_col, first_query, first_key, rows, span, half_window):
    query_at = first_query + lax.broadcasted_iota(jnp.int32, (span, rows), 1)
    key_at = first_key + lax.broadcasted_iota(jnp.int32, (span, rows), 0)
    return (jnp.abs(query_at - key_at) <= half_window) & (seg_col == seg_row)


def first_key_of(block, rows, span, length):
    start = jnp.clip(block * rows - (span - rows) // 2, 0, length - span)
    return pl.multiple_of(start, rows)


def forward_kernel(span, q_ref, k_ref, v_ref, seg_row_ref, seg_col_ref, o_ref, lse_ref):
    block = pl.program_id(1)
    rows, length = q_ref.shape[0], k_ref.shape[0]
    first_key = first_key_of(block, rows, span, length)
    keys = k_ref[pl.ds(first_key, span), :]
    values = v_ref[pl.ds(first_key, span), :]
    scores = matmul_t(keys, q_ref[...]) * DH ** (-0.5)
    allowed = allowed_keys(
        seg_row_ref[...],
        seg_col_ref[pl.ds(first_key, span), :],
        block * rows,
        first_key,
        rows,
        span,
        WINDOW // 2,
    )
    scores = jnp.where(allowed, scores, -1e30)
    peak = jnp.max(scores, axis=0, keepdims=True)
    expos = jnp.exp(scores - peak)
    totals = jnp.sum(expos, axis=0, keepdims=True)
    probs = (expos * (1.0 / totals)).astype(BF16)
    o_ref[...] = t_matmul(values, probs).T.astype(BF16)
    lse_ref[...] = (peak + jnp.log(totals))[None]


def backward_kernel(
    span,
    q_ref,
    k_ref,
    v_ref,
    do_ref,
    lse_ref,
    seg_row_ref,
    seg_col_ref,
    dq_ref,
    dk_ref,
    dv_ref,
    dk_sum,
    dv_sum,
):
    block = pl.program_id(1)
    rows, length = q_ref.shape[0], k_ref.shape[0]

    @pl.when(block == 0)
    def _():
        dk_sum[...] = jnp.zeros_like(dk_sum)
        dv_sum[...] = jnp.zeros_like(dv_sum)

    first_key = first_key_of(block, rows, span, length)
    at = pl.ds(first_key, span)
    keys = k_ref[at, :]
    values = v_ref[at, :]
    queries = q_ref[...]
    grads = do_ref[...]
    scores = matmul_t(keys, queries) * DH ** (-0.5)
    allowed = allowed_keys(
        seg_row_ref[...],
        seg_col_ref[at, :],
        block * rows,
        first_key,
        rows,
        span,
        WINDOW // 2,
    )
    probs = jnp.where(allowed, jnp.exp(scores - lse_ref[0]), 0.0)
    dv_sum[at, :] += matmul(probs.astype(BF16), grads)
    prob_grads = matmul_t(values, grads)
    center = jnp.sum(probs * prob_grads, axis=0, keepdims=True)
    score_grads = (probs * (prob_grads - center)).astype(BF16)
    dk_sum[at, :] += matmul(score_grads, queries)
    dq_ref[...] = (t_matmul(keys, score_grads) * DH ** (-0.5)).T.astype(BF16)

    @pl.when(block == length // rows - 1)
    def _():
        dk_ref[...] = (dk_sum[...] * DH ** (-0.5)).astype(BF16)
        dv_ref[...] = dv_sum[...].astype(BF16)


def attention_sizes(length):
    rows = 256
    return rows, min(length, rows + WINDOW)


def attention_forward(queries, keys, values, seg_row, seg_col):
    length, columns = queries.shape
    heads = columns // DH
    rows, span = attention_sizes(length)
    block = pl.BlockSpec((rows, DH), lambda h, i: (i, h))
    whole = pl.BlockSpec((length, DH), lambda h, i: (0, h))
    return pl.pallas_call(
        partial(forward_kernel, span),
        grid=(heads, length // rows),
        in_specs=[
            block,
            whole,
            whole,
            pl.BlockSpec((1, rows), lambda h, i: (0, i)),
            pl.BlockSpec((length, 1), lambda h, i: (0, 0)),
        ],
        out_specs=[block, pl.BlockSpec((1, 1, rows), lambda h, i: (h, 0, i))],
        out_shape=[
            jax.ShapeDtypeStruct((length, columns), BF16),
            jax.ShapeDtypeStruct((heads, 1, length), F32),
        ],
        compiler_params=pltpu.CompilerParams(vmem_limit_bytes=48 * MIB),
        cost_estimate=pl.CostEstimate(
            flops=4 * heads * length * span * DH,
            bytes_accessed=8 * length * columns,
            transcendentals=heads * length * span,
        ),
        name="attend",
    )(queries, keys, values, seg_row, seg_col)


def attention_backward(queries, keys, values, grads, lse, seg_row, seg_col):
    length, columns = queries.shape
    heads = columns // DH
    rows, span = attention_sizes(length)
    block = pl.BlockSpec((rows, DH), lambda h, i: (i, h))
    whole = pl.BlockSpec((length, DH), lambda h, i: (0, h))
    shape = jax.ShapeDtypeStruct((length, columns), BF16)
    return pl.pallas_call(
        partial(backward_kernel, span),
        grid=(heads, length // rows),
        in_specs=[
            block,
            whole,
            whole,
            block,
            pl.BlockSpec((1, 1, rows), lambda h, i: (h, 0, i)),
            pl.BlockSpec((1, rows), lambda h, i: (0, i)),
            pl.BlockSpec((length, 1), lambda h, i: (0, 0)),
        ],
        out_specs=[block, whole, whole],
        out_shape=[shape, shape, shape],
        scratch_shapes=[pltpu.VMEM((length, DH), F32), pltpu.VMEM((length, DH), F32)],
        compiler_params=pltpu.CompilerParams(vmem_limit_bytes=48 * MIB),
        cost_estimate=pl.CostEstimate(
            flops=10 * heads * length * span * DH,
            bytes_accessed=14 * length * columns,
            transcendentals=heads * length * span,
        ),
        name="attend_back",
    )(queries, keys, values, grads, lse, seg_row, seg_col)


def qkv_kernel(
    me_ref,
    even_ref,
    odd_ref,
    weight_ref,
    gain_ref,
    normed_even_ref,
    normed_odd_ref,
    q_ref,
    k_ref,
    v_ref,
    square_ref,
):
    turned = me_ref[0] % 2
    rows = even_ref.shape[0]
    columns = q_ref.shape[1]
    for k, (token_ref, normed_ref) in enumerate(
        ((even_ref, normed_even_ref), (odd_ref, normed_odd_ref))
    ):
        at = pl.ds(pl.multiple_of((turned ^ k) * rows, rows), rows)
        wide = token_ref[...].astype(F32)
        normed = (wide * rms_factor(wide) * gain_ref[...]).astype(BF16)
        normed_ref[...] = normed
        pre = matmul(normed, weight_ref[...])
        q_ref[at, :] = pre[:, :columns]
        k_ref[at, :] = pre[:, columns : 2 * columns]
        v_ref[at, :] = pre[:, 2 * columns :].astype(BF16)
        for j in range(2):
            squares = 0.0
            for c in range(j * columns, (j + 1) * columns, DH):
                squares += pre[:, c : c + DH] * pre[:, c : c + DH]
            square_ref[j : j + 1, at] = jnp.sum(squares.T, axis=0, keepdims=True)


def project(even, odd, weight, gain, me, rows):
    pairs = even.shape[0] // rows
    length = 2 * even.shape[0]
    depth, columns = weight.shape[0], weight.shape[1] // 3
    token = pl.BlockSpec((rows, depth), lambda i, me: (i, 0))

    def placed(shape):
        return pl.BlockSpec(shape, lambda i, me: (i ^ (me[0] // 2), 0))

    head = jax.ShapeDtypeStruct((length, columns), F32)
    return pl.pallas_call(
        qkv_kernel,
        grid_spec=pltpu.PrefetchScalarGridSpec(
            num_scalar_prefetch=1,
            grid=(pairs,),
            in_specs=[
                token,
                token,
                pl.BlockSpec(weight.shape, lambda i, me: (0, 0)),
                pl.BlockSpec((1, depth), lambda i, me: (0, 0)),
            ],
            out_specs=[
                token,
                token,
                placed((2 * rows, columns)),
                placed((2 * rows, columns)),
                placed((2 * rows, columns)),
                pl.BlockSpec((2, 2 * rows), lambda i, me: (0, i ^ (me[0] // 2))),
            ],
        ),
        out_shape=[
            jax.ShapeDtypeStruct((length // 2, depth), BF16),
            jax.ShapeDtypeStruct((length // 2, depth), BF16),
            head,
            head,
            jax.ShapeDtypeStruct((length, columns), BF16),
            jax.ShapeDtypeStruct((2, length), F32),
        ],
        compiler_params=pltpu.CompilerParams(vmem_limit_bytes=48 * MIB),
        cost_estimate=pl.CostEstimate(
            flops=6 * length * depth * columns,
            bytes_accessed=length * (4 * depth + 10 * columns) + 6 * depth * columns,
            transcendentals=length,
        ),
        name="project",
    )(me, even, odd, weight, gain)


def split_kernel(q_ref, k_ref, v_ref, out_ref):
    columns = q_ref.shape[1]
    for j, ref in enumerate((q_ref, k_ref, v_ref)):
        out_ref[0, :, j * columns : (j + 1) * columns] = ref[...]


def split_heads(w_query, w_key, w_value, parts):
    rows, columns = w_query.shape[0], w_query.shape[1] // parts
    block = pl.BlockSpec((rows, columns), lambda i: (0, i))
    return pl.pallas_call(
        split_kernel,
        grid=(parts,),
        in_specs=[block] * 3,
        out_specs=pl.BlockSpec((1, rows, 3 * columns), lambda i: (i, 0, 0)),
        out_shape=jax.ShapeDtypeStruct((parts, rows, 3 * columns), BF16),
        name="split_heads",
    )(w_query, w_key, w_value)


def spread(row, columns):
    return jnp.broadcast_to(row, (columns, row.shape[1])).T


def factor_of(square_row):
    return lax.rsqrt(square_row / D + EPSILON)


def turn(values, cosine, sine):
    return values * cosine + pltpu.roll(values, DH // 2, 1) * sine


def rope_kernel(q_ref, k_ref, square_ref, gain_ref, cos_ref, sin_ref, q_out, k_out):
    cosine, sine = cos_ref[...], sin_ref[...]
    for j, (pre_ref, out_ref) in enumerate(((q_ref, q_out), (k_ref, k_out))):
        factor = spread(factor_of(square_ref[j : j + 1, :]), DH)
        for c in range(0, pre_ref.shape[1], DH):
            at = slice(c, c + DH)
            normed = pre_ref[:, at] * factor * gain_ref[j : j + 1, at]
            out_ref[:, at] = turn(normed, cosine, sine).astype(BF16)


def rope(query_pre, key_pre, squares, gains, cosine, sine):
    length, columns = query_pre.shape
    rows = min(512, length)
    block = pl.BlockSpec((rows, columns), lambda i: (i, 0))
    table = pl.BlockSpec((rows, DH), lambda i: (i, 0))
    return pl.pallas_call(
        rope_kernel,
        grid=(length // rows,),
        in_specs=[
            block,
            block,
            pl.BlockSpec((2, rows), lambda i: (0, i)),
            pl.BlockSpec((2, columns), lambda i: (0, 0)),
            table,
            table,
        ],
        out_specs=[block, block],
        out_shape=[jax.ShapeDtypeStruct((length, columns), BF16)] * 2,
        compiler_params=pltpu.CompilerParams(vmem_limit_bytes=32 * MIB),
        name="rope",
    )(query_pre, key_pre, squares, gains, cosine, sine)


def pulled_of(grad_ref, pre_ref, factor, gain_ref, cosine, sine, j, at):
    turned = turn(grad_ref[:, at].astype(F32), cosine, -sine)
    return turned, turned * gain_ref[j : j + 1, at], pre_ref[:, at] * factor


def rope_mean_kernel(
    dq_ref, dk_ref, q_ref, k_ref, square_ref, gain_ref, cos_ref, sin_ref, mean_ref, term_ref
):
    @pl.when(pl.program_id(0) == 0)
    def _():
        term_ref[...] = jnp.zeros_like(term_ref)

    cosine, sine = cos_ref[...], sin_ref[...]
    for j, (grad_ref, pre_ref) in enumerate(((dq_ref, q_ref), (dk_ref, k_ref))):
        factor = spread(factor_of(square_ref[j : j + 1, :]), DH)
        total = 0.0
        for c in range(0, pre_ref.shape[1], DH):
            at = slice(c, c + DH)
            turned, pulled, normed = pulled_of(
                grad_ref, pre_ref, factor, gain_ref, cosine, sine, j, at
            )
            term_ref[j : j + 1, at] += jnp.sum(turned * normed, axis=0, keepdims=True)
            total += pulled * normed
        mean_ref[j : j + 1, :] = jnp.sum(total.T, axis=0, keepdims=True)


def rope_means(query_back, key_back, query_pre, key_pre, squares, gains, cosine, sine):
    length, columns = query_pre.shape
    rows = min(512, length)
    block = pl.BlockSpec((rows, columns), lambda i: (i, 0))
    table = pl.BlockSpec((rows, DH), lambda i: (i, 0))
    row = pl.BlockSpec((2, rows), lambda i: (0, i))
    fixed = pl.BlockSpec((2, columns), lambda i: (0, 0))
    return pl.pallas_call(
        rope_mean_kernel,
        grid=(length // rows,),
        in_specs=[block, block, block, block, row, fixed, table, table],
        out_specs=[row, fixed],
        out_shape=[
            jax.ShapeDtypeStruct((2, length), F32),
            jax.ShapeDtypeStruct((2, columns), F32),
        ],
        compiler_params=pltpu.CompilerParams(vmem_limit_bytes=32 * MIB),
        name="rope_means",
    )(query_back, key_back, query_pre, key_pre, squares, gains, cosine, sine)


def rope_back_kernel(
    me_ref,
    dq_ref,
    dk_ref,
    dv_ref,
    q_ref,
    k_ref,
    square_ref,
    mean_ref,
    gain_ref,
    cos_ref,
    sin_ref,
    out_ref,
):
    cosine, sine = cos_ref[...], sin_ref[...]
    columns = q_ref.shape[1]
    for j, (grad_ref, pre_ref) in enumerate(((dq_ref, q_ref), (dk_ref, k_ref))):
        factor = spread(factor_of(square_ref[j : j + 1, :]), DH)
        mean = spread(mean_ref[j : j + 1, :] / D, DH)
        for c in range(0, columns, DH):
            at = slice(c, c + DH)
            _, pulled, normed = pulled_of(grad_ref, pre_ref, factor, gain_ref, cosine, sine, j, at)
            out_ref[:, j * columns + c : j * columns + c + DH] = (
                factor * (pulled - normed * mean)
            ).astype(BF16)
    out_ref[:, 2 * columns :] = dv_ref[...]


def rope_back(grads, query_pre, key_pre, squares, means, gains, cosine, sine, me, rows):
    length, columns = query_pre.shape
    half = length // rows // 2

    def source(p, me):
        return me[0] ^ (p % half * 2 + p // half)

    block = pl.BlockSpec((rows, columns), lambda p, me: (source(p, me), 0))
    table = pl.BlockSpec((rows, DH), lambda p, me: (source(p, me), 0))
    row = pl.BlockSpec((2, rows), lambda p, me: (0, source(p, me)))
    return pl.pallas_call(
        rope_back_kernel,
        grid_spec=pltpu.PrefetchScalarGridSpec(
            num_scalar_prefetch=1,
            grid=(2 * half,),
            in_specs=[block] * 5
            + [row, row, pl.BlockSpec((2, columns), lambda p, me: (0, 0)), table, table],
            out_specs=pl.BlockSpec((rows, 3 * columns), lambda p, me: (p, 0)),
        ),
        out_shape=jax.ShapeDtypeStruct((length, 3 * columns), BF16),
        compiler_params=pltpu.CompilerParams(vmem_limit_bytes=32 * MIB),
        name="rope_back",
    )(me, *grads, query_pre, key_pre, squares, means, gains, cosine, sine)


def expert_kernel(pieces, first_ref, xa_ref, xb_ref, ua_ref, ub_ref, ra_ref, rb_ref, router_ref, *refs):
    weight_refs = refs[: sum(pieces)]
    (ya_ref, yb_ref, za_ref, zb_ref, ga_ref, gb_ref, xc_ref, uc_ref, dg_ref, hid_ref) = refs[-13:-3]
    wi_ref, wd_ref, sems = refs[-3:]
    experts, _, hidden = hid_ref.shape
    rows = xa_ref.shape[0]

    @pl.when(pl.program_id(0) == 0)
    def _():
        copies = []
        for n, ref in enumerate(weight_refs[: pieces[0]]):
            part = ref.shape[1]
            place = (first_ref[1] ^ (n // 2)) * 2 + n % 2
            at = pl.ds(pl.multiple_of(place * part, part), part)
            copies.append(pltpu.make_async_copy(ref, wi_ref.at[:, at, :], sems.at[n]))
        for r, ref in enumerate(weight_refs[pieces[0] :]):
            part = ref.shape[1]
            place = lax.rem(first_ref[1] ^ r, pieces[1])
            at = pl.ds(pl.multiple_of(place * part, part), part)
            copies.append(pltpu.make_async_copy(ref, wd_ref.at[:, at, :], sems.at[pieces[0] + r]))
        for copy in copies:
            copy.start()
        for copy in copies:
            copy.wait()

    slot = lax.broadcasted_iota(jnp.int32, (CAP, rows), 0)
    blocks = (
        (xa_ref, ua_ref, ra_ref, ya_ref, za_ref, ga_ref),
        (xb_ref, ub_ref, rb_ref, yb_ref, zb_ref, gb_ref),
    )
    picks = []
    for k, (x_ref, u_ref, rank_ref, _, _, _) in enumerate(blocks):
        hits = jnp.concatenate([slot == rank_ref[0, e : e + 1, :] for e in range(experts)], 0)
        pick = hits.astype(F32).astype(BF16)
        picks.append(pick)
        x_rows = matmul(pick, x_ref[...]).astype(BF16)
        u_rows = matmul(pick, u_ref[...]).astype(BF16)
        for e in range(experts):
            xc_ref[e, k * CAP : (k + 1) * CAP, :] = x_rows[e * CAP : (e + 1) * CAP]
            uc_ref[e, k * CAP : (k + 1) * CAP, :] = u_rows[e * CAP : (e + 1) * CAP]
    outs, backs, gate_grads = [], [], []
    for e in range(experts):
        x_rows, u_rows = xc_ref[e], uc_ref[e]
        logits = matmul(x_rows, router_ref[...])
        lane = lax.broadcasted_iota(jnp.int32, logits.shape, 1)
        logits = jnp.where(lane < E, logits, -1e30)
        expos = jnp.exp(logits - jnp.max(logits, axis=-1, keepdims=True))
        own = jnp.sum(jnp.where(lane == first_ref[0] + e, expos, 0.0), axis=-1, keepdims=True)
        gate = own / jnp.sum(expos, axis=-1, keepdims=True)
        gated = matmul(x_rows, wi_ref[e, :, :hidden])
        upward = matmul(x_rows, wi_ref[e, :, hidden:])
        pulled = matmul_t(u_rows, wd_ref[e])
        sig = jax.nn.sigmoid(gated)
        silu = gated * sig
        acts = silu * upward
        gate_grads.append(jnp.sum(acts * pulled, axis=-1, keepdims=True))
        hidden_gate = (acts * gate).astype(BF16)
        hidden_grads = pulled * gate
        hid_ref[e] = hidden_gate
        dg_ref[e, :, :hidden] = (hidden_grads * upward * sig * (1.0 + gated * (1.0 - sig))).astype(BF16)
        dg_ref[e, :, hidden:] = (hidden_grads * silu).astype(BF16)
        outs.append(matmul(hidden_gate, wd_ref[e]).astype(BF16))
        backs.append(matmul_t(dg_ref[e], wi_ref[e]).astype(BF16))
    for k, (_, _, rank_ref, y_ref, z_ref, g_ref) in enumerate(blocks):
        at = slice(k * CAP, (k + 1) * CAP)
        y_ref[...] = t_matmul(picks[k], jnp.concatenate([v[at] for v in outs], 0)).astype(BF16)
        z_ref[...] = t_matmul(picks[k], jnp.concatenate([v[at] for v in backs], 0)).astype(BF16)
        for e in range(experts):
            hit = slot == rank_ref[0, e : e + 1, :]
            g_ref[0, e : e + 1, :] = jnp.sum(
                jnp.where(hit, gate_grads[e][at], 0.0), axis=0, keepdims=True
            )


def run_experts(x, u, ranks, in_pieces, down_pieces, router, places, which, compact):
    experts, part, hidden = in_pieces[0].shape
    hidden = hidden // 2
    depth = part * len(in_pieces)
    rows = ranks[0].shape[2]
    steps = x[0].shape[0] // rows
    token = pl.BlockSpec((rows, depth), lambda i: (i, 0))
    rank = pl.BlockSpec((1, experts, rows), lambda i: (i, 0, 0))
    anywhere = pl.BlockSpec(memory_space=pl.ANY)

    def slots(columns):
        return pl.BlockSpec((experts, 2 * CAP, columns), lambda i: (0, i + which * steps, 0))

    shape = jax.ShapeDtypeStruct
    tokens = shape(x[0].shape, BF16)
    gates = shape((steps, experts, rows), F32)
    count = 4 * steps * CAP
    wide = shape((experts, count, depth), BF16)
    pieces = (len(in_pieces), len(down_pieces))
    inputs = [places, *x, *u, *ranks, router, *in_pieces, *down_pieces]
    return pl.pallas_call(
        partial(expert_kernel, pieces),
        grid=(steps,),
        in_specs=[pl.BlockSpec(memory_space=pltpu.SMEM)]
        + [token] * 4
        + [rank] * 2
        + [pl.BlockSpec(router.shape, lambda i: (0, 0), pipeline_mode=pl.Buffered(1))]
        + [anywhere] * (sum(pieces) + len(compact)),
        out_specs=[token] * 4 + [rank] * 2 + [slots(depth)] * 2 + [slots(2 * hidden), slots(hidden)],
        out_shape=[tokens] * 4
        + [gates] * 2
        + [wide] * 2
        + [shape((experts, count, 2 * hidden), BF16), shape((experts, count, hidden), BF16)],
        scratch_shapes=[
            pltpu.VMEM((experts, depth, 2 * hidden), BF16),
            pltpu.VMEM((experts, hidden, depth), BF16),
            pltpu.SemaphoreType.DMA((sum(pieces),)),
        ],
        input_output_aliases={len(inputs) + i: 6 + i for i in range(len(compact))},
        compiler_params=pltpu.CompilerParams(vmem_limit_bytes=60 * MIB),
        cost_estimate=pl.CostEstimate(
            flops=4 * steps * CAP * experts * depth * (7 * hidden + 2 * rows),
            bytes_accessed=60 * MIB,
            transcendentals=2 * steps * CAP * experts * hidden,
        ),
        name="experts",
    )(*inputs, *compact)


def product_kernel(me_ref, left_ref, right_ref, out_ref):
    out_ref[0] = t_matmul(left_ref[0], right_ref[0]).astype(BF16)


def products(left, right, part, r, count, me, name):
    experts, rows, _ = left.shape
    columns = right.shape[2]
    wide = min(columns, 1024)
    return pl.pallas_call(
        product_kernel,
        grid_spec=pltpu.PrefetchScalarGridSpec(
            num_scalar_prefetch=1,
            grid=(experts, columns // wide),
            in_specs=[
                pl.BlockSpec((1, rows, part), lambda e, j, me: (e, 0, lax.rem(me[0] ^ r, count))),
                pl.BlockSpec((1, rows, wide), lambda e, j, me: (e, 0, j)),
            ],
            out_specs=pl.BlockSpec((1, part, wide), lambda e, j, me: (e, 0, j)),
        ),
        out_shape=jax.ShapeDtypeStruct((experts, part, columns), BF16),
        compiler_params=pltpu.CompilerParams(vmem_limit_bytes=56 * MIB),
        cost_estimate=pl.CostEstimate(
            flops=2 * experts * rows * part * columns,
            bytes_accessed=2 * experts * rows * (part + columns),
            transcendentals=0,
        ),
        name=name,
    )(me, left, right)


def per_device(
    S,
    F,
    tokens,
    segments,
    routes,
    cotangent,
    w_query,
    w_key,
    w_value,
    w_output,
    router,
    attn_gain,
    moe_gain,
    query_gain,
    key_gain,
    w_gate,
    w_up,
    w_down,
):
    s = lax.axis_index("seq")
    f = lax.axis_index("fsdp")
    T = tokens.shape[1]
    L = S * T
    heads = H // S
    C = heads * DH
    experts = E // S
    part = w_query.shape[0]
    half_f = F // 2
    hidden_half = w_gate.shape[2] // 2

    me = s.reshape(1).astype(jnp.int32)
    f_at = f.reshape(1).astype(jnp.int32)
    tokens_low = tokens[0]
    upstream_low = cotangent[0]
    inputs = tokens_low.astype(F32)
    token_first = gather_first(tokens_low, S)
    crossed = split_heads(w_query, w_key, w_value, S)
    crossed = lax.all_to_all(crossed, "seq", split_axis=0, concat_axis=0, tiled=True)
    half_at = f // half_f
    quarter = w_gate.shape[1] // 4

    def hidden_part(which, first, count):
        return jnp.concatenate(
            [
                lax.dynamic_slice(
                    weight, (0, first, which * hidden_half), (experts, count, hidden_half)
                )
                for weight in (w_gate, w_up)
            ],
            2,
        )

    near = {}
    near[0, 0] = near_pieces(hidden_part(half_at, 0, 2 * quarter), F)
    out_pieces = fsdp_pieces(w_output, F)
    crossed, near[0, 0], out_pieces = tie(crossed, near[0, 0], out_pieces)
    own_output = place_fsdp(out_pieces, f, 0).reshape(C, D)
    small = jnp.concatenate(
        [
            router.reshape(-1),
            attn_gain,
            moe_gain,
            query_gain,
            key_gain,
            routes[0].astype(BF16).reshape(-1),
        ]
    )
    small = gather_small(small, S, F, s, f).reshape(S, F, -1)
    token_more = gather_more(tokens_low, token_first, S)
    tokens_even, tokens_odd = gather_end(tokens_low, token_first, token_more, S)
    qkv_pieces = fsdp_pieces(crossed, F)

    def far_part(n, dep):
        part = hidden_part(1 - half_at, n * quarter, quarter)
        return swap(after(part, dep), "fsdp", F, half_f)

    far = [far_part(0, qkv_pieces[half_f])]
    w_qkv = place_fsdp(qkv_pieces, f, 1).reshape(D, 3 * C)
    w_qkv, far[0] = tie(w_qkv, far[0])

    full_router = small[:, :, : part * E].reshape(D, E)
    gains = [
        small[:, :, part * (E + i) : part * (E + i + 1)].reshape(D).astype(F32) for i in range(4)
    ]
    gain_attn, gain_moe = gains[0], gains[1]
    head_gain = lax.dynamic_slice(jnp.stack(gains[2:], 0), (0, s * C), (2, C))
    route_part = small[:, :, part * (E + 4) :].reshape(S, F, T, -1)
    expert_ids = s * experts + jnp.arange(experts, dtype=jnp.int32)

    def ranks_of(index):
        named = lax.dynamic_index_in_dim(route_part, index, 1, keepdims=False)
        named = relative(named, s).astype(jnp.int32)
        chosen = jnp.any(named[:, None] == expert_ids[None, :, None, None], axis=-1)
        ranks = jnp.cumsum(chosen.astype(jnp.int32), axis=-1) - 1
        ranks = jnp.where(chosen, ranks, -1)
        return ranks[: S // 2], ranks[S // 2 :]

    places = jnp.arange(L, dtype=jnp.int32).astype(F32)
    freqs = ROPE_BASE ** (-(jnp.arange(DH // 2, dtype=F32) * 2.0 / DH))
    angles = places[:, None] * freqs[None, :]
    cosine, sine = jnp.cos(angles), jnp.sin(angles)
    cosine = jnp.concatenate([cosine, cosine], 1)
    sine = jnp.concatenate([-sine, sine], 1)

    out_first = gather_first(after(own_output, token_more), S)
    far.append(far_part(1, far[-1]))
    normed_even, normed_odd, query_pre, key_pre, value_low, squares = project(
        tokens_even, tokens_odd, w_qkv, gain_attn[None], me, T
    )
    squares, out_first, far[1] = tie(squares, out_first, far[1])
    squares = sum_all(squares, "seq", S)
    out_more = gather_more(own_output, out_first, S)
    far.append(far_part(2, far[-1]))
    query_low, key_low = rope(query_pre, key_pre, squares, head_gain, cosine, sine)
    query_low, out_more, far[2] = tie(query_low, out_more, far[2])
    seg_row = segments
    seg_col = segments.reshape(L, 1)
    own_up_first = gather_first(after(upstream_low, out_more), S)
    far.append(far_part(3, far[-1]))
    attended, lse = attention_forward(query_low, key_low, value_low, seg_row, seg_col)
    attended, own_up_first, far[3] = tie(attended, own_up_first, far[3])
    attended_blocks = attended.reshape(S, T, C)
    come = lax.all_to_all(attended_blocks, "seq", split_axis=0, concat_axis=0, tiled=True)
    come = relative(come, s).transpose(1, 0, 2).reshape(T, D)
    out_even, out_odd = gather_end(own_output, out_first, out_more, S)
    own_up_more = gather_more(upstream_low, own_up_first, S)
    near[0, 1] = near_pieces(after(hidden_part(half_at, 2 * quarter, 2 * quarter), far[3]), F)
    residual = inputs + matmul(come[:, : D // 2], out_even) + matmul(come[:, D // 2 :], out_odd)
    moe_factor = rms_factor(residual)
    residual_n = residual * moe_factor
    second_low = (residual_n * gain_moe).astype(BF16)
    second_low, own_up_more, near[0, 1] = tie(second_low, own_up_more, near[0, 1])

    own_u = gather_end(upstream_low, own_up_first, own_up_more, S)
    partner_low = swap(second_low, "fsdp", F, half_f)
    own_first = gather_first(second_low, S)
    near[1, 0] = near_pieces(after(jnp.concatenate(far[:2], 1), second_low), F)
    own_first, near[1, 0] = tie(own_first, near[1, 0])
    own_more = gather_more(second_low, own_first, S)
    near[1, 1] = near_pieces(after(jnp.concatenate(far[2:], 1), near[1, 0]), F)
    own_x = gather_end(second_low, own_first, own_more, S)
    partner_first = gather_first(after(partner_low, own_more), S)
    partner_first, near[1, 1] = tie(partner_first, near[1, 1])
    down_pieces = near_pieces(after(w_down, near[1, 1]), F)
    partner_up = swap(after(upstream_low, partner_low), "fsdp", F, half_f)
    partner_more = gather_more(partner_low, partner_first, S)
    other_x = gather_end(partner_low, partner_first, partner_more, S)
    partner_up_first = gather_first(after(partner_up, partner_more), S)
    partner_up_first, down_pieces, own_x, other_x = tie(
        partner_up_first, down_pieces, own_x, other_x
    )
    partner_up_more = gather_more(partner_up, partner_up_first, S)
    in_pieces = [
        near[r // half_f, k][r % half_f] for r in range(F) for k in range(2)
    ]
    down_pieces = [down_pieces[r] for r in range(half_f)]
    wide_router = jnp.pad(full_router, ((0, 0), (0, 128 - E)))
    expert_places = jnp.stack([s * experts, f]).astype(jnp.int32)
    own_parts = run_experts(
        own_x, own_u, ranks_of(f), in_pieces, down_pieces, wide_router, expert_places, 0, ()
    )
    own_parts, partner_up_more = tie(own_parts, partner_up_more)
    other_u = gather_end(partner_up, partner_up_first, partner_up_more, S)
    own_got = swap(own_parts[3], "seq", S, 1)
    own_out_got = swap(own_parts[1], "seq", S, 1)
    other_parts = run_experts(
        other_x,
        other_u,
        ranks_of(f ^ half_f),
        in_pieces,
        down_pieces,
        wide_router,
        expert_places,
        1,
        own_parts[6:],
    )
    other_parts, own_got, own_out_got = tie(other_parts, own_got, own_out_got)
    logits = matmul(second_low, full_router)
    router_probs = jax.nn.softmax(logits, axis=-1)

    x_rows, u_rows, in_grads, hidden_gate = other_parts[6:]
    down_part, in_part = w_down.shape[1], w_gate.shape[1]
    other_got = swap(other_parts[2 + 1], "seq", S, 1)
    other_sums = sum_first(other_parts[2], other_got, S)
    hidden_gate = after(hidden_gate, other_got)
    down_terms = {
        r: products(hidden_gate, u_rows, down_part, r, half_f, f_at, "down_products")
        for r in reversed(range(half_f))
    }
    other_out_got = swap(after(other_parts[1], other_got), "seq", S, 1)
    other_rows = sum_last(other_sums, S, (down_terms, other_out_got)).astype(BF16)
    half_rows = T // 2
    back_first = swap(other_rows[:half_rows], "fsdp", F, half_f)
    own_sums = sum_first(own_parts[2], after(own_got, other_rows), S, back_first)
    back_last = swap(after(other_rows[half_rows:], back_first), "fsdp", F, half_f)
    in_grads = after(in_grads, other_rows)
    order = [r for r in reversed(range(F)) if r & 1] + [r for r in reversed(range(F)) if not r & 1]
    in_terms = {
        r: products(x_rows, in_grads, in_part, r, F, f_at, "in_products") for r in order
    }
    own_rows = sum_last(own_sums, S, [in_terms[r] for r in order])
    row_grads = own_rows + jnp.concatenate([back_first, back_last], 0).astype(F32)

    def to_home(even, odd):
        return absolute(jnp.concatenate([even, odd], 0).transpose(0, 2, 1), s)

    gate_grads = jnp.stack(
        [to_home(own_parts[4], own_parts[5]), to_home(other_parts[4], other_parts[5])], 1
    )
    gate_grads = lax.all_to_all(
        gate_grads.reshape(S, -1), "seq", split_axis=0, concat_axis=0, tiled=True
    ).reshape(S, 2, T * experts)
    gate_grads = gate_grads[:, 0] + swap(gate_grads[:, 1], "fsdp", F, half_f)
    gate_grads = gate_grads.reshape(S, T, experts).transpose(1, 0, 2).reshape(T, E)

    upstream = upstream_low.astype(F32)
    logit_grads = router_probs * (
        gate_grads - jnp.sum(router_probs * gate_grads, axis=-1, keepdims=True)
    )
    router_wide = full_router.astype(F32)
    second_grads = row_grads + jnp.dot(logit_grads, router_wide.T, precision=HIGHEST)
    router_term = jnp.dot(second_low.astype(F32).T, logit_grads, precision=HIGHEST)
    moe_gain_term = jnp.sum(second_grads * residual_n, axis=0)
    pulled = second_grads * gain_moe
    residual_grads = upstream + moe_factor * (
        pulled - residual_n * jnp.mean(pulled * residual_n, axis=-1, keepdims=True)
    )
    branch_low = residual_grads.astype(BF16)

    def sum_near(terms, count, deps):
        terms = {r: value.astype(F32) for r, value in terms.items()}
        mask = 2
        while mask < half_f:
            stay = [r for r in terms if not r & mask]
            terms = {
                r: terms[r] + swap(terms[r | mask].astype(BF16), "fsdp", F, mask).astype(F32)
                for r in stay
            }
            mask *= 2
        return terms

    down_got = {r: swap(down_terms[r], "fsdp", F, 1) for r in range(1, half_f, 2)}
    branch_first = gather_first(branch_low, S)
    branch_first, down_got = tie(branch_first, down_got)
    odd = [r for r in range(F) if r & 1]
    far_odd = [r for r in odd if r & half_f]
    near_odd = [r for r in odd if not r & half_f]
    in_got = {r: swap(after(in_terms[r], down_got), "fsdp", F, 1) for r in far_odd}
    branch_more = gather_more(branch_low, branch_first, S)
    branch_even, branch_odd = gather_end(branch_low, branch_first, branch_more, S)

    head_grads = jnp.concatenate(
        [matmul_t(branch_even, own_output), matmul_t(branch_odd, own_output)], 0
    ).astype(BF16)
    head_grads = absolute(head_grads.reshape(S, T, C), s).reshape(L, C)
    head_grads, in_got = tie(head_grads, in_got)
    far_terms = {
        r ^ 1: in_terms[r ^ 1].astype(F32) + in_got[r].astype(F32) for r in far_odd
    }
    far_term = sum_near(far_terms, F, ())[half_f].astype(BF16)
    eighth = far_term.shape[1] // 4

    def far_sum(n, dep):
        return swap(
            after(far_term[:, n * eighth : (n + 1) * eighth], dep), "fsdp", F, half_f
        )

    far_sums = [far_sum(0, head_grads)]
    near_got = {r: swap(after(in_terms[r], in_got), "fsdp", F, 1) for r in near_odd}
    other_out_sums = sum_first(other_parts[0], after(other_out_got, branch_more), S)
    query_back, key_back, value_back = attention_backward(
        query_low, key_low, value_low, head_grads, lse, seg_row, seg_col
    )
    query_back, far_sums[0], near_got, other_out_sums = tie(
        query_back, far_sums[0], near_got, other_out_sums
    )
    value_rel = relative(value_back.reshape(S, T, C), s).reshape(2, L // 2, C)

    def weight_sum(even, odd):
        term = (t_matmul(normed_even, even) + t_matmul(normed_odd, odd)).astype(BF16)
        term = term.reshape(S, F, part, -1).transpose(1, 0, 2, 3)
        return scatter_rows(term, f, F).astype(BF16)

    far_sums.append(far_sum(1, far_sums[-1]))
    means, gain_term = rope_means(
        query_back, key_back, query_pre, key_pre, squares, head_gain, cosine, sine
    )
    other_outs = sum_last(other_out_sums, S).astype(BF16)
    means, far_sums[1], other_outs = tie(sum_all(means, "seq", S), far_sums[1], other_outs)
    far_sums.append(far_sum(2, far_sums[-1]))
    pre_rel = rope_back(
        (query_back, key_back, value_back),
        query_pre,
        key_pre,
        squares,
        means,
        head_gain,
        cosine,
        sine,
        me,
        T,
    ).reshape(2, L // 2, 3 * C)
    normed_got = swap(matmul_t(pre_rel[1], w_qkv).astype(BF16), "seq", S, 1)
    normed_kept = matmul_t(pre_rel[0], w_qkv).astype(BF16)
    value_term = weight_sum(value_rel[0], value_rel[1])
    normed_got, far_sums[2] = tie(normed_got, far_sums[2])
    normed_sums = sum_first(normed_kept, normed_got, S)
    far_sums.append(far_sum(3, far_sums[-1]))
    turned_term = weight_sum(pre_rel[0][:, : 2 * C], pre_rel[1][:, : 2 * C])
    normed_grads = sum_last(normed_sums, S)
    outs_back = swap(after(other_outs, far_sums[2]), "fsdp", F, half_f).astype(F32)
    own_out_sums = sum_first(own_parts[0], after(own_out_got, normed_sums), S)
    own_outs = sum_last(own_out_sums, S)
    mixed = (residual + own_outs + outs_back).astype(BF16)[None]

    qkv_term = jnp.concatenate([turned_term, value_term], -1)
    qkv_term = lax.all_to_all(qkv_term, "seq", split_axis=0, concat_axis=0, tiled=True)
    qkv_term = qkv_term.reshape(S, part, 3, C).transpose(2, 1, 0, 3).reshape(3, part, D).astype(F32)
    attended_rel = relative(after(attended_blocks, query_back), s).reshape(2, L // 2, C)
    output_term = t_matmul(attended_rel[0], branch_even) + t_matmul(attended_rel[1], branch_odd)
    grad_output = scatter_rows(output_term.astype(BF16).reshape(F, part, D), f, F)

    near_terms = {
        r ^ 1: in_terms[r ^ 1].astype(F32) + near_got[r].astype(F32) for r in near_odd
    }
    own_term = sum_near(near_terms, F, ())[0]
    far_term = jnp.concatenate(far_sums, 1).astype(F32)
    first_half = half_at == 0
    lower = jnp.where(first_half, own_term, far_term)
    upper = jnp.where(first_half, far_term, own_term)
    grad_gate, grad_up = (
        jnp.concatenate([lower[..., at], upper[..., at]], axis=-1)
        for at in (slice(0, hidden_half), slice(hidden_half, 2 * hidden_half))
    )
    down_sums = {
        r ^ 1: down_terms[r ^ 1].astype(F32) + down_got[r].astype(F32) for r in down_got
    }
    grad_down = sum_near(down_sums, half_f, ())[0]

    attn_factor = rms_factor(inputs)
    inputs_n = inputs * attn_factor
    attn_pulled = normed_grads * gain_attn
    grad_tokens = residual_grads + attn_factor * (
        attn_pulled - inputs_n * jnp.mean(attn_pulled * inputs_n, axis=-1, keepdims=True)
    )
    gain_terms = jnp.concatenate(
        [router_term.reshape(S * F, part * E), moe_gain_term.reshape(S * F, part)], 1
    )
    gain_terms = sum_small(after(gain_terms, query_back), (("seq", S, s), ("fsdp", F, f)))
    head_terms = gain_term.reshape(2, F, part).transpose(1, 0, 2).reshape(F, 2 * part)
    head_terms = sum_small(head_terms, (("fsdp", F, f),))
    own_weights = jnp.stack([w_query, w_key, w_value], 0).astype(F32)
    grad_attn_gain = jnp.sum(qkv_term * own_weights, axis=(0, 2)) / attn_gain.astype(F32)
    return (
        mixed,
        grad_tokens[None],
        qkv_term[0],
        qkv_term[1],
        qkv_term[2],
        grad_output,
        gain_terms[: part * E].reshape(part, E),
        grad_attn_gain,
        gain_terms[part * E :],
        head_terms[:part],
        head_terms[part:],
        grad_gate,
        grad_up,
        grad_down,
    )


def solution(mesh):
    tokens_spec = P("fsdp", "seq", None)
    rows_spec = P(("seq", "fsdp"), None)
    gain_spec = P(("seq", "fsdp"))
    expert_spec = P("seq", "fsdp", None)
    in_specs = (
        (tokens_spec, P("fsdp", None), tokens_spec, tokens_spec)
        + (rows_spec,) * 5
        + (gain_spec,) * 4
        + (expert_spec,) * 3
    )
    out_specs = (tokens_spec,) * 2 + (rows_spec,) * 5 + (gain_spec,) * 4 + (expert_spec,) * 3
    return jax.shard_map(
        partial(per_device, mesh.shape["seq"], mesh.shape["fsdp"]),
        mesh=mesh,
        in_specs=in_specs,
        out_specs=out_specs,
        check_vma=False,
    )
```

```python
from functools import partial

import jax
import jax.numpy as jnp
from jax import lax
from jax.experimental import pallas as pl
from jax.experimental.pallas import tpu as pltpu
from jax.sharding import PartitionSpec as P

D = 2048
H = 16
DH = 128
E = 16
WINDOW = 1024
CAP = 144

EPSILON = 1e-06
ROPE_BASE = 50000.0
HIGHEST = lax.Precision.HIGHEST
BF16 = jnp.bfloat16
F32 = jnp.float32
MIB = 1024 * 1024


def matmul(left, right):
    return jnp.dot(left, right, preferred_element_type=F32)


def matmul_t(left, right):
    return lax.dot_general(left, right, (((1,), (1,)), ((), ())), preferred_element_type=F32)


def t_matmul(left, right):
    return lax.dot_general(left, right, (((0,), (0,)), ((), ())), preferred_element_type=F32)


def rms_factor(values):
    return lax.rsqrt(jnp.mean(values * values, axis=-1, keepdims=True) + EPSILON)


def swap(values, axis, size, mask):
    return lax.ppermute(values, axis, [(i, i ^ mask) for i in range(size)])


def high_bit(number):
    return 1 << (number.bit_length() - 1)


def low_bit(number):
    return number & -number


def after(values, *others):
    return lax.optimization_barrier((values, others))[0]


def tie(*values):
    return lax.optimization_barrier(values)


def gather_first(values, size):
    return {r: swap(values, "seq", size, r) for r in range(2, size, 2) if r == low_bit(r)}


def gather_more(values, first, size):
    rows = values.shape[0] // 2
    pieces = dict(first)
    for r in range(2, size, 2):
        if r not in pieces:
            up, down = high_bit(r), low_bit(r)
            upper, lower = pieces[r ^ up], pieces[r ^ down]
            upper = upper[0] if isinstance(upper, tuple) else upper[:rows]
            lower = lower[1] if isinstance(lower, tuple) else lower[rows:]
            pieces[r] = (swap(upper, "seq", size, up), swap(lower, "seq", size, down))
    return {r: piece for r, piece in pieces.items() if r not in first}


def gather_end(values, first, more, size):
    blocks = [values]
    for r in range(2, size, 2):
        blocks.extend([first[r]] if r in first else more[r])
    even = jnp.concatenate(blocks, 0)
    return even, swap(even, "seq", size, 1)


def relative(blocks, me):
    size = blocks.shape[0]
    order = list(range(0, size, 2)) + list(range(1, size, 2))
    return jnp.concatenate([lax.dynamic_slice_in_dim(blocks, me ^ r, 1, 0) for r in order], 0)


def absolute(blocks, me):
    size = blocks.shape[0]
    places = [((me ^ j) // 2) + ((me ^ j) % 2) * (size // 2) for j in range(size)]
    return jnp.concatenate([lax.dynamic_slice_in_dim(blocks, at, 1, 0) for at in places], 0)


def sum_cores(even, got, size):
    rows = even.shape[0] // (size // 2)
    half = rows // 2

    def part(r, first):
        at = slice(r // 2 * rows + first, r // 2 * rows + first + half)
        return even[at].astype(F32) + got[at].astype(F32)

    return {r: [part(r, 0), part(r, half)] for r in range(0, size, 2)}


def sum_first(sums, size):
    sums = {r: list(value) for r, value in sums.items()}
    come = {}
    for r in range(size - 2, 0, -2):
        if r != low_bit(r):
            up, down = high_bit(r), low_bit(r)
            for (goal, k, _), piece in come.items():
                if goal == r:
                    sums[r][k] += piece.astype(F32)
            upper, lower = tie(sums[r][0].astype(BF16), sums[r][1].astype(BF16))
            come[r ^ up, 0, r] = swap(upper, "seq", size, up)
            come[r ^ down, 1, r] = swap(lower, "seq", size, down)
    return come


def sum_more(sums, come, size):
    sums = {r: list(value) for r, value in sums.items() if r == 0 or r == low_bit(r)}
    for (goal, k, _), piece in come.items():
        if goal in sums:
            sums[goal][k] += piece.astype(F32)
    singles = {
        r: jnp.concatenate([v.astype(BF16) for v in value], 0) for r, value in sums.items() if r
    }
    return tie(singles)[0], jnp.concatenate(sums[0], 0)


def sum_last(singles, size):
    return {r: swap(value, "seq", size, r) for r, value in singles.items()}


def add_all(total, pieces):
    for piece in pieces.values():
        total += piece.astype(F32)
    return total


def quarters(values, axis):
    step = values.shape[axis] // 4
    return [lax.slice_in_dim(values, k * step, (k + 1) * step, axis=axis) for k in range(4)]


def sum_all(values, axis, size):
    mask = 1
    while mask < size:
        values = values + swap(values, axis, size, mask)
        mask *= 2
    return values


def fsdp_pieces(values, size):
    pieces = {0: values}
    for r in range(1, size):
        low = low_bit(r)
        pieces[r] = swap(pieces[r ^ low], "fsdp", size, low)
    return pieces


def place_fsdp(pieces, me, axis):
    size = len(pieces)
    shape = pieces[0].shape
    whole = jnp.zeros(shape[:axis] + (size,) + shape[axis:], pieces[0].dtype)
    for r, piece in pieces.items():
        whole = lax.dynamic_update_slice_in_dim(whole, jnp.expand_dims(piece, axis), me ^ r, axis)
    return whole


def near_pieces(values, size):
    pieces = {0: values}
    for r in range(1, size // 2):
        up = high_bit(r)
        pieces[r] = swap(pieces[r ^ up], "fsdp", size, up)
    return pieces


def gather_small(values, seq_size, fsdp_size, s, f):
    count = seq_size * fsdp_size
    whole = values[None]
    for axis, size in (("seq", seq_size), ("fsdp", fsdp_size)):
        mask = 1
        while mask < size:
            whole = jnp.concatenate([whole, swap(whole, axis, size, mask)], 0)
            mask *= 2
    index = jnp.arange(count, dtype=jnp.int32)
    source = ((index % fsdp_size) ^ f) * seq_size + ((index // fsdp_size) ^ s)
    pick = (source[:, None] == index[None, :]).astype(values.dtype)
    return matmul(pick, whole).astype(values.dtype)


def sum_small(values, axes):
    count = values.shape[0]
    index = jnp.arange(count, dtype=jnp.int32)
    source, stride = jnp.zeros_like(index), 1
    for _, size, me in reversed(axes):
        source += ((index // stride % size) ^ me) * stride
        stride *= size
    pick = (source[:, None] == index[None, :]).astype(F32)
    values = jnp.dot(pick, values, precision=HIGHEST)
    for name, size, _ in axes:
        mask = size // 2
        while mask:
            half = values.shape[0] // 2
            values = values[:half] + swap(values[half:], name, size, mask)
            mask //= 2
    return values[0]


def by_index(partial_sum, me, size):
    order = [r for r in range(size) if r & 1] + [r for r in range(size) if not r & 1]
    return jnp.concatenate([lax.dynamic_slice_in_dim(partial_sum, me ^ r, 1, 0) for r in order], 0)


def sum_even(stacked, got, size):
    return (stacked[size // 2 :].astype(F32) + got.astype(F32)).astype(BF16)


def sum_rest(stacked, size):
    mask = 2
    values = stacked.astype(F32)
    while mask < size:
        count = values.shape[0] // 2
        pairs = values.reshape((count, 2) + values.shape[1:])
        got = swap(pairs[:, 1].astype(BF16), "fsdp", size, mask)
        values = pairs[:, 0] + got.astype(F32)
        mask *= 2
    return values[0]


def allowed_keys(seg_row, seg_col, first_query, first_key, rows, span, half_window):
    query_at = first_query + lax.broadcasted_iota(jnp.int32, (span, rows), 1)
    key_at = first_key + lax.broadcasted_iota(jnp.int32, (span, rows), 0)
    return (jnp.abs(query_at - key_at) <= half_window) & (seg_col == seg_row)


def first_key_of(block, rows, span, length):
    start = jnp.clip(block * rows - (span - rows) // 2, 0, length - span)
    return pl.multiple_of(start, rows)


def forward_kernel(span, q_ref, k_ref, v_ref, seg_row_ref, seg_col_ref, o_ref, lse_ref):
    block = pl.program_id(1)
    rows, length = q_ref.shape[0], k_ref.shape[0]
    first_key = first_key_of(block, rows, span, length)
    keys = k_ref[pl.ds(first_key, span), :]
    values = v_ref[pl.ds(first_key, span), :]
    scores = matmul_t(keys, q_ref[...]) * DH ** (-0.5)
    allowed = allowed_keys(
        seg_row_ref[...],
        seg_col_ref[pl.ds(first_key, span), :],
        block * rows,
        first_key,
        rows,
        span,
        WINDOW // 2,
    )
    scores = jnp.where(allowed, scores, -1e30)
    peak = jnp.max(scores, axis=0, keepdims=True)
    expos = jnp.exp(scores - peak)
    totals = jnp.sum(expos, axis=0, keepdims=True)
    probs = (expos * (1.0 / totals)).astype(BF16)
    o_ref[...] = t_matmul(values, probs).T.astype(BF16)
    lse_ref[...] = (peak + jnp.log(totals))[None]


def backward_kernel(
    span,
    q_ref,
    k_ref,
    v_ref,
    do_ref,
    lse_ref,
    seg_row_ref,
    seg_col_ref,
    dq_ref,
    dk_ref,
    dv_ref,
    dk_sum,
    dv_sum,
):
    block = pl.program_id(1)
    rows, length = q_ref.shape[0], k_ref.shape[0]

    @pl.when(block == 0)
    def _():
        dk_sum[...] = jnp.zeros_like(dk_sum)
        dv_sum[...] = jnp.zeros_like(dv_sum)

    first_key = first_key_of(block, rows, span, length)
    at = pl.ds(first_key, span)
    keys = k_ref[at, :]
    values = v_ref[at, :]
    queries = q_ref[...]
    grads = do_ref[...]
    scores = matmul_t(keys, queries) * DH ** (-0.5)
    allowed = allowed_keys(
        seg_row_ref[...],
        seg_col_ref[at, :],
        block * rows,
        first_key,
        rows,
        span,
        WINDOW // 2,
    )
    probs = jnp.where(allowed, jnp.exp(scores - lse_ref[0]), 0.0)
    dv_sum[at, :] += matmul(probs.astype(BF16), grads)
    prob_grads = matmul_t(values, grads)
    center = jnp.sum(probs * prob_grads, axis=0, keepdims=True)
    score_grads = (probs * (prob_grads - center)).astype(BF16)
    dk_sum[at, :] += matmul(score_grads, queries)
    dq_ref[...] = (t_matmul(keys, score_grads) * DH ** (-0.5)).T.astype(BF16)

    @pl.when(block == length // rows - 1)
    def _():
        dk_ref[...] = (dk_sum[...] * DH ** (-0.5)).astype(BF16)
        dv_ref[...] = dv_sum[...].astype(BF16)


def attention_sizes(length):
    rows = 256
    return rows, min(length, rows + WINDOW)


def attention_forward(queries, keys, values, seg_row, seg_col):
    length, columns = queries.shape
    heads = columns // DH
    rows, span = attention_sizes(length)
    block = pl.BlockSpec((rows, DH), lambda h, i: (i, h))
    whole = pl.BlockSpec((length, DH), lambda h, i: (0, h))
    return pl.pallas_call(
        partial(forward_kernel, span),
        grid=(heads, length // rows),
        in_specs=[
            block,
            whole,
            whole,
            pl.BlockSpec((1, rows), lambda h, i: (0, i)),
            pl.BlockSpec((length, 1), lambda h, i: (0, 0)),
        ],
        out_specs=[block, pl.BlockSpec((1, 1, rows), lambda h, i: (h, 0, i))],
        out_shape=[
            jax.ShapeDtypeStruct((length, columns), BF16),
            jax.ShapeDtypeStruct((heads, 1, length), F32),
        ],
        compiler_params=pltpu.CompilerParams(vmem_limit_bytes=48 * MIB),
        cost_estimate=pl.CostEstimate(
            flops=4 * heads * length * span * DH,
            bytes_accessed=8 * length * columns,
            transcendentals=heads * length * span,
        ),
        name="attend",
    )(queries, keys, values, seg_row, seg_col)


def attention_backward(queries, keys, values, grads, lse, seg_row, seg_col):
    length, columns = queries.shape
    heads = columns // DH
    rows, span = attention_sizes(length)
    block = pl.BlockSpec((rows, DH), lambda h, i: (i, h))
    whole = pl.BlockSpec((length, DH), lambda h, i: (0, h))
    shape = jax.ShapeDtypeStruct((length, columns), BF16)
    return pl.pallas_call(
        partial(backward_kernel, span),
        grid=(heads, length // rows),
        in_specs=[
            block,
            whole,
            whole,
            block,
            pl.BlockSpec((1, 1, rows), lambda h, i: (h, 0, i)),
            pl.BlockSpec((1, rows), lambda h, i: (0, i)),
            pl.BlockSpec((length, 1), lambda h, i: (0, 0)),
        ],
        out_specs=[block, whole, whole],
        out_shape=[shape, shape, shape],
        scratch_shapes=[pltpu.VMEM((length, DH), F32), pltpu.VMEM((length, DH), F32)],
        compiler_params=pltpu.CompilerParams(vmem_limit_bytes=48 * MIB),
        cost_estimate=pl.CostEstimate(
            flops=10 * heads * length * span * DH,
            bytes_accessed=14 * length * columns,
            transcendentals=heads * length * span,
        ),
        name="attend_back",
    )(queries, keys, values, grads, lse, seg_row, seg_col)


def qkv_kernel(
    me_ref,
    even_ref,
    odd_ref,
    weight_ref,
    gain_ref,
    normed_even_ref,
    normed_odd_ref,
    q_ref,
    k_ref,
    v_ref,
    square_ref,
):
    turned = me_ref[0] % 2
    rows = even_ref.shape[0]
    columns = q_ref.shape[1]
    for k, (token_ref, normed_ref) in enumerate(
        ((even_ref, normed_even_ref), (odd_ref, normed_odd_ref))
    ):
        at = pl.ds(pl.multiple_of((turned ^ k) * rows, rows), rows)
        wide = token_ref[...].astype(F32)
        normed = (wide * rms_factor(wide) * gain_ref[...]).astype(BF16)
        normed_ref[...] = normed
        pre = matmul(normed, weight_ref[...])
        q_ref[at, :] = pre[:, :columns]
        k_ref[at, :] = pre[:, columns : 2 * columns]
        v_ref[at, :] = pre[:, 2 * columns :].astype(BF16)
        for j in range(2):
            squares = 0.0
            for c in range(j * columns, (j + 1) * columns, DH):
                squares += pre[:, c : c + DH] * pre[:, c : c + DH]
            square_ref[j : j + 1, at] = jnp.sum(squares.T, axis=0, keepdims=True)


def project(even, odd, weight, gain, me, rows):
    pairs = even.shape[0] // rows
    length = 2 * even.shape[0]
    depth, columns = weight.shape[0], weight.shape[1] // 3
    token = pl.BlockSpec((rows, depth), lambda i, me: (i, 0))

    def placed(shape):
        return pl.BlockSpec(shape, lambda i, me: (i ^ (me[0] // 2), 0))

    head = jax.ShapeDtypeStruct((length, columns), F32)
    return pl.pallas_call(
        qkv_kernel,
        grid_spec=pltpu.PrefetchScalarGridSpec(
            num_scalar_prefetch=1,
            grid=(pairs,),
            in_specs=[
                token,
                token,
                pl.BlockSpec(weight.shape, lambda i, me: (0, 0)),
                pl.BlockSpec((1, depth), lambda i, me: (0, 0)),
            ],
            out_specs=[
                token,
                token,
                placed((2 * rows, columns)),
                placed((2 * rows, columns)),
                placed((2 * rows, columns)),
                pl.BlockSpec((2, 2 * rows), lambda i, me: (0, i ^ (me[0] // 2))),
            ],
        ),
        out_shape=[
            jax.ShapeDtypeStruct((length // 2, depth), BF16),
            jax.ShapeDtypeStruct((length // 2, depth), BF16),
            head,
            head,
            jax.ShapeDtypeStruct((length, columns), BF16),
            jax.ShapeDtypeStruct((2, length), F32),
        ],
        compiler_params=pltpu.CompilerParams(vmem_limit_bytes=48 * MIB),
        cost_estimate=pl.CostEstimate(
            flops=6 * length * depth * columns,
            bytes_accessed=length * (4 * depth + 10 * columns) + 6 * depth * columns,
            transcendentals=length,
        ),
        name="project",
    )(me, even, odd, weight, gain)


def split_kernel(q_ref, k_ref, v_ref, out_ref):
    columns = q_ref.shape[1]
    for j, ref in enumerate((q_ref, k_ref, v_ref)):
        out_ref[0, :, j * columns : (j + 1) * columns] = ref[...]


def split_heads(w_query, w_key, w_value, parts):
    rows, columns = w_query.shape[0], w_query.shape[1] // parts
    block = pl.BlockSpec((rows, columns), lambda i: (0, i))
    return pl.pallas_call(
        split_kernel,
        grid=(parts,),
        in_specs=[block] * 3,
        out_specs=pl.BlockSpec((1, rows, 3 * columns), lambda i: (i, 0, 0)),
        out_shape=jax.ShapeDtypeStruct((parts, rows, 3 * columns), BF16),
        name="split_heads",
    )(w_query, w_key, w_value)


def spread(row, columns):
    return jnp.broadcast_to(row, (columns, row.shape[1])).T


def factor_of(square_row):
    return lax.rsqrt(square_row / D + EPSILON)


def turn(values, cosine, sine):
    return values * cosine + pltpu.roll(values, DH // 2, 1) * sine


def rope_kernel(q_ref, k_ref, square_ref, gain_ref, cos_ref, sin_ref, q_out, k_out):
    cosine, sine = cos_ref[...], sin_ref[...]
    for j, (pre_ref, out_ref) in enumerate(((q_ref, q_out), (k_ref, k_out))):
        factor = spread(factor_of(square_ref[j : j + 1, :]), DH)
        for c in range(0, pre_ref.shape[1], DH):
            at = slice(c, c + DH)
            normed = pre_ref[:, at] * factor * gain_ref[j : j + 1, at]
            out_ref[:, at] = turn(normed, cosine, sine).astype(BF16)


def rope(query_pre, key_pre, squares, gains, cosine, sine):
    length, columns = query_pre.shape
    rows = min(512, length)
    block = pl.BlockSpec((rows, columns), lambda i: (i, 0))
    table = pl.BlockSpec((rows, DH), lambda i: (i, 0))
    return pl.pallas_call(
        rope_kernel,
        grid=(length // rows,),
        in_specs=[
            block,
            block,
            pl.BlockSpec((2, rows), lambda i: (0, i)),
            pl.BlockSpec((2, columns), lambda i: (0, 0)),
            table,
            table,
        ],
        out_specs=[block, block],
        out_shape=[jax.ShapeDtypeStruct((length, columns), BF16)] * 2,
        compiler_params=pltpu.CompilerParams(vmem_limit_bytes=32 * MIB),
        name="rope",
    )(query_pre, key_pre, squares, gains, cosine, sine)


def pulled_of(grad_ref, pre_ref, factor, gain_ref, cosine, sine, j, at):
    turned = turn(grad_ref[:, at].astype(F32), cosine, -sine)
    return turned, turned * gain_ref[j : j + 1, at], pre_ref[:, at] * factor


def rope_mean_kernel(
    dq_ref, dk_ref, q_ref, k_ref, square_ref, gain_ref, cos_ref, sin_ref, mean_ref, term_ref
):
    @pl.when(pl.program_id(0) == 0)
    def _():
        term_ref[...] = jnp.zeros_like(term_ref)

    cosine, sine = cos_ref[...], sin_ref[...]
    for j, (grad_ref, pre_ref) in enumerate(((dq_ref, q_ref), (dk_ref, k_ref))):
        factor = spread(factor_of(square_ref[j : j + 1, :]), DH)
        total = 0.0
        for c in range(0, pre_ref.shape[1], DH):
            at = slice(c, c + DH)
            turned, pulled, normed = pulled_of(
                grad_ref, pre_ref, factor, gain_ref, cosine, sine, j, at
            )
            term_ref[j : j + 1, at] += jnp.sum(turned * normed, axis=0, keepdims=True)
            total += pulled * normed
        mean_ref[j : j + 1, :] = jnp.sum(total.T, axis=0, keepdims=True)


def rope_means(query_back, key_back, query_pre, key_pre, squares, gains, cosine, sine):
    length, columns = query_pre.shape
    rows = min(512, length)
    block = pl.BlockSpec((rows, columns), lambda i: (i, 0))
    table = pl.BlockSpec((rows, DH), lambda i: (i, 0))
    row = pl.BlockSpec((2, rows), lambda i: (0, i))
    fixed = pl.BlockSpec((2, columns), lambda i: (0, 0))
    return pl.pallas_call(
        rope_mean_kernel,
        grid=(length // rows,),
        in_specs=[block, block, block, block, row, fixed, table, table],
        out_specs=[row, fixed],
        out_shape=[
            jax.ShapeDtypeStruct((2, length), F32),
            jax.ShapeDtypeStruct((2, columns), F32),
        ],
        compiler_params=pltpu.CompilerParams(vmem_limit_bytes=32 * MIB),
        name="rope_means",
    )(query_back, key_back, query_pre, key_pre, squares, gains, cosine, sine)


def rope_back_kernel(
    me_ref,
    dq_ref,
    dk_ref,
    dv_ref,
    q_ref,
    k_ref,
    square_ref,
    mean_ref,
    gain_ref,
    cos_ref,
    sin_ref,
    out_ref,
):
    cosine, sine = cos_ref[...], sin_ref[...]
    columns = q_ref.shape[1]
    for j, (grad_ref, pre_ref) in enumerate(((dq_ref, q_ref), (dk_ref, k_ref))):
        factor = spread(factor_of(square_ref[j : j + 1, :]), DH)
        mean = spread(mean_ref[j : j + 1, :] / D, DH)
        for c in range(0, columns, DH):
            at = slice(c, c + DH)
            _, pulled, normed = pulled_of(grad_ref, pre_ref, factor, gain_ref, cosine, sine, j, at)
            out_ref[:, j * columns + c : j * columns + c + DH] = (
                factor * (pulled - normed * mean)
            ).astype(BF16)
    out_ref[:, 2 * columns :] = dv_ref[...]


def rope_back(grads, query_pre, key_pre, squares, means, gains, cosine, sine, me, rows):
    length, columns = query_pre.shape
    half = length // rows // 2

    def source(p, me):
        return me[0] ^ (p % half * 2 + p // half)

    block = pl.BlockSpec((rows, columns), lambda p, me: (source(p, me), 0))
    table = pl.BlockSpec((rows, DH), lambda p, me: (source(p, me), 0))
    row = pl.BlockSpec((2, rows), lambda p, me: (0, source(p, me)))
    return pl.pallas_call(
        rope_back_kernel,
        grid_spec=pltpu.PrefetchScalarGridSpec(
            num_scalar_prefetch=1,
            grid=(2 * half,),
            in_specs=[block] * 5
            + [row, row, pl.BlockSpec((2, columns), lambda p, me: (0, 0)), table, table],
            out_specs=pl.BlockSpec((rows, 3 * columns), lambda p, me: (p, 0)),
        ),
        out_shape=jax.ShapeDtypeStruct((length, 3 * columns), BF16),
        compiler_params=pltpu.CompilerParams(vmem_limit_bytes=32 * MIB),
        name="rope_back",
    )(me, *grads, query_pre, key_pre, squares, means, gains, cosine, sine)


def expert_kernel(
    in_places, down_places, first_ref, xa_ref, xb_ref, ua_ref, ub_ref, ra_ref, rb_ref, router_ref, *refs
):
    weight_refs = refs[: len(in_places) + len(down_places)]
    (ya_ref, yb_ref, za_ref, zb_ref, ga_ref, gb_ref, xc_ref, uc_ref, dg_ref, hid_ref) = refs[-13:-3]
    wi_ref, wd_ref, sems = refs[-3:]
    experts, _, hidden = hid_ref.shape
    rows = xa_ref.shape[0]

    @pl.when(pl.program_id(0) == 0)
    def _():
        copies = []
        for n, (ref, (r, first, part)) in enumerate(zip(weight_refs, in_places + down_places)):
            goal = wi_ref if n < len(in_places) else wd_ref
            place = lax.rem(first_ref[1] ^ r, goal.shape[1] // part)
            at = pl.ds(pl.multiple_of(place * part + first, ref.shape[1]), ref.shape[1])
            copies.append(pltpu.make_async_copy(ref, goal.at[:, at, :], sems.at[n]))
        for copy in copies:
            copy.start()
        for copy in copies:
            copy.wait()

    slot = lax.broadcasted_iota(jnp.int32, (CAP, rows), 0)
    blocks = (
        (xa_ref, ua_ref, ra_ref, ya_ref, za_ref, ga_ref),
        (xb_ref, ub_ref, rb_ref, yb_ref, zb_ref, gb_ref),
    )
    picks = []
    for k, (x_ref, u_ref, rank_ref, _, _, _) in enumerate(blocks):
        hits = jnp.concatenate([slot == rank_ref[0, e : e + 1, :] for e in range(experts)], 0)
        pick = hits.astype(F32).astype(BF16)
        picks.append(pick)
        x_rows = matmul(pick, x_ref[...]).astype(BF16)
        u_rows = matmul(pick, u_ref[...]).astype(BF16)
        for e in range(experts):
            xc_ref[e, k * CAP : (k + 1) * CAP, :] = x_rows[e * CAP : (e + 1) * CAP]
            uc_ref[e, k * CAP : (k + 1) * CAP, :] = u_rows[e * CAP : (e + 1) * CAP]
    outs, backs, gate_grads = [], [], []
    for e in range(experts):
        x_rows, u_rows = xc_ref[e], uc_ref[e]
        logits = matmul(x_rows, router_ref[...])
        lane = lax.broadcasted_iota(jnp.int32, logits.shape, 1)
        logits = jnp.where(lane < E, logits, -1e30)
        expos = jnp.exp(logits - jnp.max(logits, axis=-1, keepdims=True))
        own = jnp.sum(jnp.where(lane == first_ref[0] + e, expos, 0.0), axis=-1, keepdims=True)
        gate = own / jnp.sum(expos, axis=-1, keepdims=True)
        gated = matmul(x_rows, wi_ref[e, :, :hidden])
        upward = matmul(x_rows, wi_ref[e, :, hidden:])
        pulled = matmul_t(u_rows, wd_ref[e])
        sig = jax.nn.sigmoid(gated)
        silu = gated * sig
        acts = silu * upward
        gate_grads.append(jnp.sum(acts * pulled, axis=-1, keepdims=True))
        hidden_gate = (acts * gate).astype(BF16)
        hidden_grads = pulled * gate
        hid_ref[e] = hidden_gate
        dg_ref[e, :, :hidden] = (hidden_grads * upward * sig * (1.0 + gated * (1.0 - sig))).astype(BF16)
        dg_ref[e, :, hidden:] = (hidden_grads * silu).astype(BF16)
        outs.append(matmul(hidden_gate, wd_ref[e]).astype(BF16))
        backs.append(matmul_t(dg_ref[e], wi_ref[e]).astype(BF16))
    for k, (_, _, rank_ref, y_ref, z_ref, g_ref) in enumerate(blocks):
        at = slice(k * CAP, (k + 1) * CAP)
        y_ref[...] = t_matmul(picks[k], jnp.concatenate([v[at] for v in outs], 0)).astype(BF16)
        z_ref[...] = t_matmul(picks[k], jnp.concatenate([v[at] for v in backs], 0)).astype(BF16)
        for e in range(experts):
            hit = slot == rank_ref[0, e : e + 1, :]
            g_ref[0, e : e + 1, :] = jnp.sum(
                jnp.where(hit, gate_grads[e][at], 0.0), axis=0, keepdims=True
            )


def run_experts(x, u, ranks, in_pieces, down_pieces, router, places, which, compact, parts):
    experts, _, hidden = in_pieces[0][2].shape
    hidden = hidden // 2
    depth = x[0].shape[1]
    in_places = [(r, at, parts[0]) for r, at, _ in in_pieces]
    down_places = [(r, at, parts[1]) for r, at, _ in down_pieces]
    pieces = [array for _, _, array in in_pieces + down_pieces]
    rows = ranks[0].shape[2]
    steps = x[0].shape[0] // rows
    token = pl.BlockSpec((rows, depth), lambda i: (i, 0))
    rank = pl.BlockSpec((1, experts, rows), lambda i: (i, 0, 0))
    anywhere = pl.BlockSpec(memory_space=pl.ANY)

    def slots(columns):
        return pl.BlockSpec((experts, 2 * CAP, columns), lambda i: (0, i + which * steps, 0))

    shape = jax.ShapeDtypeStruct
    tokens = shape(x[0].shape, BF16)
    gates = shape((steps, experts, rows), F32)
    count = 4 * steps * CAP
    wide = shape((experts, count, depth), BF16)
    inputs = [places, *x, *u, *ranks, router, *pieces]
    return pl.pallas_call(
        partial(expert_kernel, in_places, down_places),
        grid=(steps,),
        in_specs=[pl.BlockSpec(memory_space=pltpu.SMEM)]
        + [token] * 4
        + [rank] * 2
        + [pl.BlockSpec(router.shape, lambda i: (0, 0), pipeline_mode=pl.Buffered(1))]
        + [anywhere] * (len(pieces) + len(compact)),
        out_specs=[token] * 4 + [rank] * 2 + [slots(depth)] * 2 + [slots(2 * hidden), slots(hidden)],
        out_shape=[tokens] * 4
        + [gates] * 2
        + [wide] * 2
        + [shape((experts, count, 2 * hidden), BF16), shape((experts, count, hidden), BF16)],
        scratch_shapes=[
            pltpu.VMEM((experts, depth, 2 * hidden), BF16),
            pltpu.VMEM((experts, hidden, depth), BF16),
            pltpu.SemaphoreType.DMA((len(pieces),)),
        ],
        input_output_aliases={len(inputs) + i: 6 + i for i in range(len(compact))},
        compiler_params=pltpu.CompilerParams(vmem_limit_bytes=60 * MIB),
        cost_estimate=pl.CostEstimate(
            flops=4 * steps * CAP * experts * depth * (7 * hidden + 2 * rows),
            bytes_accessed=60 * MIB,
            transcendentals=2 * steps * CAP * experts * hidden,
        ),
        name="experts",
    )(*inputs, *compact)


def product_kernel(me_ref, left_ref, right_ref, out_ref):
    out_ref[0] = t_matmul(left_ref[0], right_ref[0]).astype(BF16)


def products(left, right, part, r, count, me, name):
    experts, rows, _ = left.shape
    columns = right.shape[2]
    wide = min(columns, 1024)
    return pl.pallas_call(
        product_kernel,
        grid_spec=pltpu.PrefetchScalarGridSpec(
            num_scalar_prefetch=1,
            grid=(experts, columns // wide),
            in_specs=[
                pl.BlockSpec((1, rows, part), lambda e, j, me: (e, 0, lax.rem(me[0] ^ r, count))),
                pl.BlockSpec((1, rows, wide), lambda e, j, me: (e, 0, j)),
            ],
            out_specs=pl.BlockSpec((1, part, wide), lambda e, j, me: (e, 0, j)),
        ),
        out_shape=jax.ShapeDtypeStruct((experts, part, columns), BF16),
        compiler_params=pltpu.CompilerParams(vmem_limit_bytes=56 * MIB),
        cost_estimate=pl.CostEstimate(
            flops=2 * experts * rows * part * columns,
            bytes_accessed=2 * experts * rows * (part + columns),
            transcendentals=0,
        ),
        name=name,
    )(me, left, right)


def per_device(
    S,
    F,
    tokens,
    segments,
    routes,
    cotangent,
    w_query,
    w_key,
    w_value,
    w_output,
    router,
    attn_gain,
    moe_gain,
    query_gain,
    key_gain,
    w_gate,
    w_up,
    w_down,
):
    s = lax.axis_index("seq")
    f = lax.axis_index("fsdp")
    T = tokens.shape[1]
    L = S * T
    heads = H // S
    C = heads * DH
    experts = E // S
    part = w_query.shape[0]
    half_f = F // 2
    hidden_half = w_gate.shape[2] // 2

    me = s.reshape(1).astype(jnp.int32)
    f_at = f.reshape(1).astype(jnp.int32)
    half_at = f // half_f
    tokens_low = tokens[0]
    upstream_low = cotangent[0]
    inputs = tokens_low.astype(F32)
    half_rows = T // 2
    in_part, down_part = w_gate.shape[1], w_down.shape[1]
    quarter = in_part // 4

    def hidden_part(which, first, count):
        return jnp.concatenate(
            [
                lax.dynamic_slice(
                    weight, (0, first, which * hidden_half), (experts, count, hidden_half)
                )
                for weight in (w_gate, w_up)
            ],
            2,
        )

    def far_swap(values, *dep):
        return swap(after(values, dep), "fsdp", F, half_f)

    def near_swap(values, *dep):
        return near_pieces(after(values, dep), F)

    token_first = gather_first(tokens_low, S)
    crossed = split_heads(w_query, w_key, w_value, S)
    crossed = lax.all_to_all(crossed, "seq", split_axis=0, concat_axis=0, tiled=True)
    near_own = [near_swap(hidden_part(half_at, 0, 2 * quarter))]
    crossed, near_own[0] = tie(crossed, near_own[0])

    token_more = gather_more(tokens_low, token_first, S)
    tokens_even, tokens_odd = gather_end(tokens_low, token_first, token_more, S)
    qkv_pieces = {0: crossed}
    for r in range(1, F):
        low = low_bit(r)
        qkv_pieces[r] = swap(qkv_pieces[r ^ low], "fsdp", F, low)
        if r == half_f:
            own_up_first = gather_first(after(upstream_low, token_more), S)
            qkv_pieces[r], own_up_first = tie(qkv_pieces[r], own_up_first)
            own_up_more = gather_more(upstream_low, own_up_first, S)
            partner_up = [far_swap(upstream_low[:half_rows], qkv_pieces[r])]
    small = jnp.concatenate(
        [
            router.reshape(-1),
            attn_gain,
            moe_gain,
            query_gain,
            key_gain,
            routes[0].astype(BF16).reshape(-1),
        ]
    )
    small = gather_small(after(small, qkv_pieces[half_f]), S, F, s, f).reshape(S, F, -1)
    w_qkv = place_fsdp(qkv_pieces, f, 1).reshape(D, 3 * C)
    w_qkv, partner_up[0], own_up_more, small = tie(w_qkv, partner_up[0], own_up_more, small)
    own_u = gather_end(upstream_low, own_up_first, own_up_more, S)

    full_router = small[:, :, : part * E].reshape(D, E)
    gains = [
        small[:, :, part * (E + i) : part * (E + i + 1)].reshape(D).astype(F32) for i in range(4)
    ]
    gain_attn, gain_moe = gains[0], gains[1]
    head_gain = lax.dynamic_slice(jnp.stack(gains[2:], 0), (0, s * C), (2, C))
    route_part = small[:, :, part * (E + 4) :].reshape(S, F, T, -1)
    expert_ids = s * experts + jnp.arange(experts, dtype=jnp.int32)

    def ranks_of(index):
        named = lax.dynamic_index_in_dim(route_part, index, 1, keepdims=False)
        named = relative(named, s).astype(jnp.int32)
        chosen = jnp.any(named[:, None] == expert_ids[None, :, None, None], axis=-1)
        ranks = jnp.cumsum(chosen.astype(jnp.int32), axis=-1) - 1
        ranks = jnp.where(chosen, ranks, -1)
        return ranks[: S // 2], ranks[S // 2 :]

    places = jnp.arange(L, dtype=jnp.int32).astype(F32)
    freqs = ROPE_BASE ** (-(jnp.arange(DH // 2, dtype=F32) * 2.0 / DH))
    angles = places[:, None] * freqs[None, :]
    cosine, sine = jnp.cos(angles), jnp.sin(angles)
    cosine = jnp.concatenate([cosine, cosine], 1)
    sine = jnp.concatenate([-sine, sine], 1)

    def far_part(n, *dep):
        return far_swap(hidden_part(1 - half_at, n * quarter, quarter), *dep)

    partner_up.append(far_swap(upstream_low[half_rows:], w_qkv))
    near_own.append(near_swap(hidden_part(half_at, 2 * quarter, quarter), w_qkv))
    out_pieces = fsdp_pieces(after(w_output, w_qkv), F)
    normed_even, normed_odd, query_pre, key_pre, value_low, squares = project(
        tokens_even, tokens_odd, w_qkv, gain_attn[None], me, T
    )
    squares, partner_up[1], near_own[1], out_pieces = tie(
        squares, partner_up[1], near_own[1], out_pieces
    )
    partner_up = jnp.concatenate(partner_up, 0)
    own_output = place_fsdp(out_pieces, f, 0).reshape(C, D)

    out_first = gather_first(own_output, S)
    far = [far_part(0, squares)]
    near_own.append(near_swap(hidden_part(half_at, 3 * quarter, quarter), squares))
    squares = sum_all(squares, "seq", S)
    query_low, key_low = rope(query_pre, key_pre, squares, head_gain, cosine, sine)
    query_low, out_first, far[0], near_own[2] = tie(query_low, out_first, far[0], near_own[2])

    seg_row = segments
    seg_col = segments.reshape(L, 1)
    out_more = gather_more(own_output, out_first, S)
    far.append(far_part(1, query_low))
    down_rows = quarters(w_down, 1)
    down = [near_swap(down_rows[0], query_low)]
    attended, lse = attention_forward(query_low, key_low, value_low, seg_row, seg_col)
    attended, out_more, far[1], down[0] = tie(attended, out_more, far[1], down[0])
    attended_blocks = attended.reshape(S, T, C)
    come = lax.all_to_all(attended_blocks, "seq", split_axis=0, concat_axis=0, tiled=True)
    out_even, out_odd = gather_end(own_output, out_first, out_more, S)
    far.append(far_part(2, attended))
    near_far = [near_swap(far[0], attended)]
    come, far[2], near_far[0] = tie(come, far[2], near_far[0])
    far.append(far_part(3, come))
    near_far.append(near_swap(far[1], come))
    partner_up_first = gather_first(after(partner_up, come), S)
    come = relative(come, s).transpose(1, 0, 2).reshape(T, D)
    residual = inputs + matmul(come[:, : D // 2], out_even) + matmul(come[:, D // 2 :], out_odd)
    moe_factor = rms_factor(residual)
    residual_n = residual * moe_factor
    second_low = (residual_n * gain_moe).astype(BF16)
    second_low, far[3], near_far[1], partner_up_first = tie(
        second_low, far[3], near_far[1], partner_up_first
    )

    own_first = gather_first(second_low, S)
    partner_low = [far_swap(second_low[:half_rows])]
    near_far.append(near_swap(far[2], second_low))
    own_first, partner_low[0], near_far[2] = tie(own_first, partner_low[0], near_far[2])
    own_more = gather_more(second_low, own_first, S)
    partner_low.append(far_swap(second_low[half_rows:], own_first))
    near_far.append(near_swap(far[3], own_first))
    own_more, partner_low[1], near_far[3] = tie(own_more, partner_low[1], near_far[3])
    partner_low = jnp.concatenate(partner_low, 0)
    own_x = gather_end(second_low, own_first, own_more, S)
    partner_first = gather_first(after(partner_low, own_more), S)
    down.append(near_swap(down_rows[1], own_more))
    down.append(near_swap(down_rows[2], own_more))
    partner_first, down[1], down[2], own_x = tie(partner_first, down[1], down[2], own_x)
    partner_more = gather_more(partner_low, partner_first, S)
    down.append(near_swap(down_rows[3], partner_first))
    partner_more, down[3] = tie(partner_more, down[3])
    partner_up_more = gather_more(after(partner_up, partner_more), partner_up_first, S)
    other_x = gather_end(partner_low, partner_first, partner_more, S)
    in_pieces = []
    for r in range(F):
        for n, rows in enumerate(near_own if r < half_f else near_far):
            first = (0, 2, 3)[n] if r < half_f else n
            in_pieces.append((r, first * quarter, rows[r % half_f]))
    down_pieces = [
        (r, n * (down_part // 4), down[n][r]) for r in range(half_f) for n in range(4)
    ]
    wide_router = jnp.pad(full_router, ((0, 0), (0, 128 - E)))
    expert_places = jnp.stack([s * experts, f]).astype(jnp.int32)
    parts = (in_part, down_part)
    own_ranks, other_ranks = ranks_of(f), ranks_of(f ^ half_f)
    own_x, other_x, partner_up_more, own_ranks, other_ranks = tie(
        own_x, other_x, partner_up_more, own_ranks, other_ranks
    )
    other_u = gather_end(partner_up, partner_up_first, partner_up_more, S)
    own_parts = run_experts(
        own_x, own_u, own_ranks, in_pieces, down_pieces, wide_router, expert_places, 0, (), parts
    )
    own_parts, other_u = tie(own_parts, other_u)
    own_got = swap(own_parts[3], "seq", S, 1)
    own_out_got = swap(own_parts[1], "seq", S, 1)
    other_parts = run_experts(
        other_x,
        other_u,
        other_ranks,
        in_pieces,
        down_pieces,
        wide_router,
        expert_places,
        1,
        own_parts[6:],
        parts,
    )
    other_parts, own_got, own_out_got = tie(other_parts, own_got, own_out_got)
    logits = matmul(second_low, full_router)
    router_probs = jax.nn.softmax(logits, axis=-1)

    x_rows, u_rows, in_grads, hidden_gate = other_parts[6:]
    in_terms, down_terms = {}, {}

    def in_products(r, *dep):
        in_terms[r] = products(
            x_rows, after(in_grads, dep), in_part, r, F, f_at, "in_products"
        )

    odd = [r for r in range(F) if r & 1]
    far_odd = [r for r in odd if r & half_f]
    near_odd = [r for r in odd if not r & half_f]

    def to_home(even, odd):
        return absolute(jnp.concatenate([even, odd], 0).transpose(0, 2, 1), s)

    gate_grads = jnp.stack(
        [to_home(own_parts[4], own_parts[5]), to_home(other_parts[4], other_parts[5])], 1
    ).reshape(S, -1)
    other_got = swap(other_parts[3], "seq", S, 1)
    for r in far_odd:
        in_products(r)
    gate_grads = lax.all_to_all(gate_grads, "seq", split_axis=0, concat_axis=0, tiled=True)
    other_got, in_terms, gate_grads = tie(other_got, in_terms, gate_grads)
    sent = {r: quarters(in_terms[r], 1) for r in far_odd}

    def send_in(n, *dep):
        return {r: swap(after(sent[r][n], dep), "fsdp", F, 1) for r in sent}

    other_sums = sum_cores(other_parts[2], other_got, S)
    come = sum_first(other_sums, S)
    far_got = [send_in(0, other_got)]
    other_out_got = swap(after(other_parts[1], other_got), "seq", S, 1)
    come, far_got[0], other_out_got = tie(come, far_got[0], other_out_got)
    gate_grads = gate_grads.reshape(S, 2, T * experts)
    partner_grads = far_swap(gate_grads[:, 1], come)
    singles, other_total = sum_more(other_sums, come, S)
    come = sum_last(singles, S)
    far_got.append(send_in(1, far_got[0]))
    far_got.append(send_in(2, far_got[0]))
    for r in range(half_f):
        down_terms[r] = products(
            after(hidden_gate, singles), u_rows, down_part, r, half_f, f_at, "down_products"
        )
    come, far_got[1], far_got[2], partner_grads, down_terms = tie(
        come, far_got[1], far_got[2], partner_grads, down_terms
    )
    other_rows = add_all(other_total, come).astype(BF16)
    gate_grads = gate_grads[:, 0] + partner_grads
    gate_grads = gate_grads.reshape(S, T, experts).transpose(1, 0, 2).reshape(T, E)
    back = [far_swap(other_rows[:half_rows])]
    own_sums = sum_cores(own_parts[2], after(own_got, other_rows), S)
    come = sum_first(own_sums, S)
    far_got.append(send_in(3, other_rows))
    for r in far_odd:
        in_products(r ^ 1, other_rows)
    come, back[0], far_got[3], in_terms = tie(come, back[0], far_got[3], in_terms)
    back.append(far_swap(other_rows[half_rows:], come))
    singles, own_total = sum_more(own_sums, come, S)
    come = sum_last(singles, S)
    down_sent = {r: quarters(down_terms[r], 1) for r in range(1, half_f, 2)}

    def send_down(n, *dep):
        return {r: swap(after(down_sent[r][n], dep), "fsdp", F, 1) for r in down_sent}

    down_got = [send_down(0, singles)]
    for r in near_odd:
        in_products(r, singles)
    come, back[1], down_got[0], in_terms = tie(come, back[1], down_got[0], in_terms)
    row_grads = add_all(own_total, come) + jnp.concatenate(back, 0).astype(F32)

    upstream = upstream_low.astype(F32)
    logit_grads = router_probs * (
        gate_grads - jnp.sum(router_probs * gate_grads, axis=-1, keepdims=True)
    )
    router_wide = full_router.astype(F32)
    second_grads = row_grads + jnp.dot(logit_grads, router_wide.T, precision=HIGHEST)
    pulled = second_grads * gain_moe
    residual_grads = upstream + moe_factor * (
        pulled - residual_n * jnp.mean(pulled * residual_n, axis=-1, keepdims=True)
    )
    branch_low = residual_grads.astype(BF16)

    def sum_near(terms):
        mask = 2
        while mask < half_f:
            terms = {
                r: terms[r] + swap(terms[r | mask].astype(BF16), "fsdp", F, mask).astype(F32)
                for r in terms
                if not r & mask
            }
            mask *= 2
        (total,) = terms.values()
        return total

    def far_sum(n, *dep):
        terms = {
            r ^ 1: quarters(in_terms[r ^ 1], 1)[n].astype(F32) + far_got[n][r].astype(F32)
            for r in far_odd
        }
        return far_swap(sum_near(terms).astype(BF16), *dep)

    branch_first = gather_first(branch_low, S)
    far_sums = [far_sum(0, branch_low)]
    down_got.append(send_down(1, branch_low))
    for r in near_odd:
        in_products(r ^ 1, branch_low)
    branch_first, far_sums[0], down_got[1], in_terms = tie(
        branch_first, far_sums[0], down_got[1], in_terms
    )
    branch_more = gather_more(branch_low, branch_first, S)
    far_sums.append(far_sum(1, branch_first))
    down_got.append(send_down(2, branch_first))
    branch_even, branch_odd = gather_end(branch_low, branch_first, branch_more, S)

    head_grads = jnp.concatenate(
        [matmul_t(branch_even, own_output), matmul_t(branch_odd, own_output)], 0
    ).astype(BF16)
    head_grads = absolute(head_grads.reshape(S, T, C), s).reshape(L, C)
    head_grads, far_sums[1], down_got[2] = tie(head_grads, far_sums[1], down_got[2])
    far_sums.append(far_sum(2, head_grads))
    down_got.append(send_down(3, head_grads))
    other_out_sums = sum_cores(other_parts[0], after(other_out_got, head_grads), S)
    come = sum_first(other_out_sums, S)
    query_back, key_back, value_back = attention_backward(
        query_low, key_low, value_low, head_grads, lse, seg_row, seg_col
    )
    query_back, far_sums[2], down_got[3], come = tie(query_back, far_sums[2], down_got[3], come)

    singles, other_total = sum_more(other_out_sums, come, S)
    come = sum_last(singles, S)
    far_sums.append(far_sum(3, query_back))
    attended_rel = relative(after(attended_blocks, singles), s).reshape(2, L // 2, C)
    output_term = t_matmul(attended_rel[0], branch_even) + t_matmul(attended_rel[1], branch_odd)
    output_term = by_index(output_term.astype(BF16).reshape(F, part, D), f, F)
    output_got = swap(output_term[: F // 2], "fsdp", F, 1)
    value_rel = relative(value_back.reshape(S, T, C), s).reshape(2, L // 2, C)

    def weight_term(even, odd):
        term = (t_matmul(normed_even, even) + t_matmul(normed_odd, odd)).astype(BF16)
        return by_index(term.reshape(S, F, part, -1).transpose(1, 0, 2, 3), f, F)

    means, gain_term = rope_means(
        query_back, key_back, query_pre, key_pre, squares, head_gain, cosine, sine
    )
    means = sum_all(means, "seq", S)
    value_term = weight_term(value_rel[0], value_rel[1])
    means, come, far_sums[3], output_got, value_term = tie(
        means, come, far_sums[3], output_got, value_term
    )
    other_outs = add_all(other_total, come).astype(BF16)
    outs_back = [far_swap(other_outs[:half_rows])]
    value_got = swap(value_term[: F // 2], "fsdp", F, 1)
    pre_rel = rope_back(
        (query_back, key_back, value_back),
        query_pre,
        key_pre,
        squares,
        means,
        head_gain,
        cosine,
        sine,
        me,
        T,
    ).reshape(2, L // 2, 3 * C)
    normed_got = swap(matmul_t(pre_rel[1], w_qkv).astype(BF16), "seq", S, 1)
    normed_kept = matmul_t(pre_rel[0], w_qkv).astype(BF16)
    normed_got, normed_kept, outs_back[0], value_got = tie(
        normed_got, normed_kept, outs_back[0], value_got
    )

    normed_sums = sum_cores(normed_kept, normed_got, S)
    come = sum_first(normed_sums, S)
    value_sum = sum_rest(sum_even(value_term, value_got, F), F)
    turned_term = weight_term(
        after(pre_rel[0][:, : 2 * C], normed_got), after(pre_rel[1][:, : 2 * C], normed_got)
    )
    come, turned_term, value_sum = tie(come, turned_term, value_sum)
    near_sent = {r: quarters(in_terms[r], 1) for r in near_odd}

    def send_near(n, *dep):
        return {r: swap(after(near_sent[r][n], dep), "fsdp", F, 1) for r in near_sent}

    turned_got = swap(turned_term[: F // 2], "fsdp", F, 1)
    singles, normed_total = sum_more(normed_sums, come, S)
    come = sum_last(singles, S)
    outs_back.append(far_swap(other_outs[half_rows:], turned_term))
    come, turned_got, outs_back[1] = tie(come, turned_got, outs_back[1])
    normed_grads = add_all(normed_total, come)
    turned_sum = sum_rest(sum_even(turned_term, turned_got, F), F)
    near_got = [send_near(0, turned_got), send_near(1, turned_got)]
    own_out_sums = sum_cores(own_parts[0], after(own_out_got, turned_got), S)
    come = sum_first(own_out_sums, S)
    turned_sum, come, near_got = tie(turned_sum, come, near_got)
    near_got.extend([send_near(2, turned_sum), send_near(3, turned_sum)])
    singles, own_total = sum_more(own_out_sums, come, S)
    own_outs = add_all(own_total, sum_last(singles, S))
    outs_back = jnp.concatenate(outs_back, 0).astype(F32)
    mixed = (residual + own_outs + outs_back).astype(BF16)[None]

    qkv_term = jnp.concatenate([turned_sum, value_sum], -1).astype(BF16)
    qkv_term = lax.all_to_all(qkv_term, "seq", split_axis=0, concat_axis=0, tiled=True)
    qkv_term = qkv_term.reshape(S, part, 3, C).transpose(2, 1, 0, 3).reshape(3, part, D).astype(F32)
    grad_output = sum_rest(sum_even(output_term, output_got, F), F)

    near_got = {r: jnp.concatenate([got[r] for got in near_got], 1) for r in near_odd}
    own_term = sum_near(
        {r ^ 1: in_terms[r ^ 1].astype(F32) + near_got[r].astype(F32) for r in near_odd}
    )
    far_term = jnp.concatenate(far_sums, 1).astype(F32)
    first_half = half_at == 0
    lower = jnp.where(first_half, own_term, far_term)
    upper = jnp.where(first_half, far_term, own_term)
    grad_gate, grad_up = (
        jnp.concatenate([lower[..., at], upper[..., at]], axis=-1)
        for at in (slice(0, hidden_half), slice(hidden_half, 2 * hidden_half))
    )
    down_got = {r: jnp.concatenate([got[r] for got in down_got], 1) for r in down_sent}
    grad_down = sum_near(
        {r ^ 1: down_terms[r ^ 1].astype(F32) + down_got[r].astype(F32) for r in down_sent}
    )

    attn_factor = rms_factor(inputs)
    inputs_n = inputs * attn_factor
    attn_pulled = normed_grads * gain_attn
    grad_tokens = residual_grads + attn_factor * (
        attn_pulled - inputs_n * jnp.mean(attn_pulled * inputs_n, axis=-1, keepdims=True)
    )
    late_grads, late_logits = after(second_grads, turned_got), after(logit_grads, turned_got)
    router_term = jnp.dot(second_low.astype(F32).T, late_logits, precision=HIGHEST)
    moe_gain_term = jnp.sum(late_grads * residual_n, axis=0)
    gain_terms = jnp.concatenate(
        [router_term.reshape(S * F, part * E), moe_gain_term.reshape(S * F, part)], 1
    )
    gain_terms = sum_small(gain_terms, (("seq", S, s), ("fsdp", F, f)))
    head_terms = gain_term.reshape(2, F, part).transpose(1, 0, 2).reshape(F, 2 * part)
    head_terms = sum_small(after(head_terms, turned_got), (("fsdp", F, f),))
    own_weights = jnp.stack([w_query, w_key, w_value], 0).astype(F32)
    grad_attn_gain = jnp.sum(qkv_term * own_weights, axis=(0, 2)) / attn_gain.astype(F32)
    return (
        mixed,
        grad_tokens[None],
        qkv_term[0],
        qkv_term[1],
        qkv_term[2],
        grad_output,
        gain_terms[: part * E].reshape(part, E),
        grad_attn_gain,
        gain_terms[part * E :],
        head_terms[:part],
        head_terms[part:],
        grad_gate,
        grad_up,
        grad_down,
    )


def solution(mesh):
    tokens_spec = P("fsdp", "seq", None)
    rows_spec = P(("seq", "fsdp"), None)
    gain_spec = P(("seq", "fsdp"))
    expert_spec = P("seq", "fsdp", None)
    in_specs = (
        (tokens_spec, P("fsdp", None), tokens_spec, tokens_spec)
        + (rows_spec,) * 5
        + (gain_spec,) * 4
        + (expert_spec,) * 3
    )
    out_specs = (tokens_spec,) * 2 + (rows_spec,) * 5 + (gain_spec,) * 4 + (expert_spec,) * 3
    return jax.shard_map(
        partial(per_device, mesh.shape["seq"], mesh.shape["fsdp"]),
        mesh=mesh,
        in_specs=in_specs,
        out_specs=out_specs,
        check_vma=False,
    )
```

```python
from functools import partial

import jax
import jax.numpy as jnp
from jax import lax
from jax.experimental import pallas as pl
from jax.experimental.pallas import tpu as pltpu
from jax.sharding import PartitionSpec as P

D = 2048
H = 16
DH = 128
E = 16
WINDOW = 1024
CAP = 144

EPSILON = 1e-06
ROPE_BASE = 50000.0
HIGHEST = lax.Precision.HIGHEST
BF16 = jnp.bfloat16
F32 = jnp.float32
MIB = 1024 * 1024


def matmul(left, right):
    return jnp.dot(left, right, preferred_element_type=F32)


def matmul_t(left, right):
    return lax.dot_general(left, right, (((1,), (1,)), ((), ())), preferred_element_type=F32)


def t_matmul(left, right):
    return lax.dot_general(left, right, (((0,), (0,)), ((), ())), preferred_element_type=F32)


def rms_factor(values):
    return lax.rsqrt(jnp.mean(values * values, axis=-1, keepdims=True) + EPSILON)


def swap(values, axis, size, mask):
    return lax.ppermute(values, axis, [(i, i ^ mask) for i in range(size)])


def high_bit(number):
    return 1 << (number.bit_length() - 1)


def low_bit(number):
    return number & -number


def after(values, *others):
    return lax.optimization_barrier((values, others))[0]


def tie(*values):
    return lax.optimization_barrier(values)


def gather_first(values, size):
    return {r: swap(values, "seq", size, r) for r in range(2, size, 2) if r == low_bit(r)}


def gather_more(values, first, size):
    rows = values.shape[0] // 2
    pieces = dict(first)
    for r in range(2, size, 2):
        if r not in pieces:
            up, down = high_bit(r), low_bit(r)
            upper, lower = pieces[r ^ up], pieces[r ^ down]
            upper = upper[0] if isinstance(upper, tuple) else upper[:rows]
            lower = lower[1] if isinstance(lower, tuple) else lower[rows:]
            pieces[r] = (swap(upper, "seq", size, up), swap(lower, "seq", size, down))
    return {r: piece for r, piece in pieces.items() if r not in first}


def gather_end(values, first, more, size):
    blocks = [values]
    for r in range(2, size, 2):
        blocks.extend([first[r]] if r in first else more[r])
    even = jnp.concatenate(blocks, 0)
    return even, swap(even, "seq", size, 1)


def relative(blocks, me):
    size = blocks.shape[0]
    order = list(range(0, size, 2)) + list(range(1, size, 2))
    return jnp.concatenate([lax.dynamic_slice_in_dim(blocks, me ^ r, 1, 0) for r in order], 0)


def absolute(blocks, me):
    size = blocks.shape[0]
    places = [((me ^ j) // 2) + ((me ^ j) % 2) * (size // 2) for j in range(size)]
    return jnp.concatenate([lax.dynamic_slice_in_dim(blocks, at, 1, 0) for at in places], 0)


def sum_cores(even, got, size):
    rows = even.shape[0] // (size // 2)
    half = rows // 2

    def part(r, first):
        at = slice(r // 2 * rows + first, r // 2 * rows + first + half)
        return even[at].astype(F32) + got[at].astype(F32)

    return {r: [part(r, 0), part(r, half)] for r in range(0, size, 2)}


def sum_first(sums, size):
    sums = {r: list(value) for r, value in sums.items()}
    come = {}
    for r in range(size - 2, 0, -2):
        if r != low_bit(r):
            up, down = high_bit(r), low_bit(r)
            for (goal, k, _), piece in come.items():
                if goal == r:
                    sums[r][k] += piece.astype(F32)
            upper, lower = tie(sums[r][0].astype(BF16), sums[r][1].astype(BF16))
            come[r ^ up, 0, r] = swap(upper, "seq", size, up)
            come[r ^ down, 1, r] = swap(lower, "seq", size, down)
    return come


def sum_more(sums, come, size):
    sums = {r: list(value) for r, value in sums.items() if r == 0 or r == low_bit(r)}
    for (goal, k, _), piece in come.items():
        if goal in sums:
            sums[goal][k] += piece.astype(F32)
    singles = {
        r: jnp.concatenate([v.astype(BF16) for v in value], 0) for r, value in sums.items() if r
    }
    return tie(singles)[0], jnp.concatenate(sums[0], 0)


def sum_last(singles, size):
    return {r: swap(value, "seq", size, r) for r, value in singles.items()}


def add_all(total, pieces):
    for piece in pieces.values():
        total += piece.astype(F32)
    return total


def quarters(values, axis):
    step = values.shape[axis] // 4
    return [lax.slice_in_dim(values, k * step, (k + 1) * step, axis=axis) for k in range(4)]


def sum_all(values, axis, size):
    mask = 1
    while mask < size:
        values = values + swap(values, axis, size, mask)
        mask *= 2
    return values


def fsdp_pieces(values, size):
    pieces = {0: values}
    for r in range(1, size):
        low = low_bit(r)
        pieces[r] = swap(pieces[r ^ low], "fsdp", size, low)
    return pieces


def place_fsdp(pieces, me, axis):
    size = len(pieces)
    shape = pieces[0].shape
    whole = jnp.zeros(shape[:axis] + (size,) + shape[axis:], pieces[0].dtype)
    for r, piece in pieces.items():
        whole = lax.dynamic_update_slice_in_dim(whole, jnp.expand_dims(piece, axis), me ^ r, axis)
    return whole


def near_pieces(values, size):
    pieces = {0: values}
    for r in range(1, size // 2):
        up = high_bit(r)
        pieces[r] = swap(pieces[r ^ up], "fsdp", size, up)
    return pieces


def double(values, axis, size):
    mask = 1
    while mask < size:
        values = jnp.concatenate([values, swap(values, axis, size, mask)], 0)
        mask *= 2
    return values


def halve(values, axis, size):
    mask = size // 2
    while mask:
        half = values.shape[0] // 2
        values = values[:half] + swap(values[half:], axis, size, mask)
        mask //= 2
    return values


def relative_pick(seq_size, fsdp_size, s, f):
    index = jnp.arange(seq_size * fsdp_size, dtype=jnp.int32)
    source = ((index // fsdp_size) ^ s) * fsdp_size + ((index % fsdp_size) ^ f)
    return source[:, None] == index[None, :]


def in_order(values, seq_size, fsdp_size, s, f):
    pick = relative_pick(seq_size, fsdp_size, s, f).astype(values.dtype)
    return matmul(pick, values).astype(values.dtype)


def in_relative(values, seq_size, fsdp_size, s, f):
    pick = relative_pick(seq_size, fsdp_size, s, f).astype(F32)
    return jnp.dot(pick, values, precision=HIGHEST)


def by_index(partial_sum, me, size):
    order = [r for r in range(size) if r & 1] + [r for r in range(size) if not r & 1]
    return jnp.concatenate([lax.dynamic_slice_in_dim(partial_sum, me ^ r, 1, 0) for r in order], 0)


def sum_even(stacked, got, size):
    return (stacked[size // 2 :].astype(F32) + got.astype(F32)).astype(BF16)


def sum_rest(stacked, size):
    mask = 2
    values = stacked.astype(F32)
    while mask < size:
        count = values.shape[0] // 2
        pairs = values.reshape((count, 2) + values.shape[1:])
        got = swap(pairs[:, 1].astype(BF16), "fsdp", size, mask)
        values = pairs[:, 0] + got.astype(F32)
        mask *= 2
    return values[0]


def allowed_keys(seg_row, seg_col, first_query, first_key, rows, span, half_window):
    query_at = first_query + lax.broadcasted_iota(jnp.int32, (span, rows), 1)
    key_at = first_key + lax.broadcasted_iota(jnp.int32, (span, rows), 0)
    return (jnp.abs(query_at - key_at) <= half_window) & (seg_col == seg_row)


def first_key_of(block, rows, span, length):
    start = jnp.clip(block * rows - (span - rows) // 2, 0, length - span)
    return pl.multiple_of(start, rows)


def forward_kernel(span, q_ref, k_ref, v_ref, seg_row_ref, seg_col_ref, o_ref, lse_ref):
    block = pl.program_id(1)
    rows, length = q_ref.shape[0], k_ref.shape[0]
    first_key = first_key_of(block, rows, span, length)
    keys = k_ref[pl.ds(first_key, span), :]
    values = v_ref[pl.ds(first_key, span), :]
    scores = matmul_t(keys, q_ref[...]) * DH ** (-0.5)
    allowed = allowed_keys(
        seg_row_ref[...],
        seg_col_ref[pl.ds(first_key, span), :],
        block * rows,
        first_key,
        rows,
        span,
        WINDOW // 2,
    )
    scores = jnp.where(allowed, scores, -1e30)
    peak = jnp.max(scores, axis=0, keepdims=True)
    expos = jnp.exp(scores - peak)
    totals = jnp.sum(expos, axis=0, keepdims=True)
    probs = (expos * (1.0 / totals)).astype(BF16)
    o_ref[...] = t_matmul(values, probs).T.astype(BF16)
    lse_ref[...] = (peak + jnp.log(totals))[None]


def backward_kernel(
    span,
    q_ref,
    k_ref,
    v_ref,
    do_ref,
    lse_ref,
    seg_row_ref,
    seg_col_ref,
    dq_ref,
    dk_ref,
    dv_ref,
    dk_sum,
    dv_sum,
):
    block = pl.program_id(1)
    rows, length = q_ref.shape[0], k_ref.shape[0]

    @pl.when(block == 0)
    def _():
        dk_sum[...] = jnp.zeros_like(dk_sum)
        dv_sum[...] = jnp.zeros_like(dv_sum)

    first_key = first_key_of(block, rows, span, length)
    at = pl.ds(first_key, span)
    keys = k_ref[at, :]
    values = v_ref[at, :]
    queries = q_ref[...]
    grads = do_ref[...]
    scores = matmul_t(keys, queries) * DH ** (-0.5)
    allowed = allowed_keys(
        seg_row_ref[...],
        seg_col_ref[at, :],
        block * rows,
        first_key,
        rows,
        span,
        WINDOW // 2,
    )
    probs = jnp.where(allowed, jnp.exp(scores - lse_ref[0]), 0.0)
    dv_sum[at, :] += matmul(probs.astype(BF16), grads)
    prob_grads = matmul_t(values, grads)
    center = jnp.sum(probs * prob_grads, axis=0, keepdims=True)
    score_grads = (probs * (prob_grads - center)).astype(BF16)
    dk_sum[at, :] += matmul(score_grads, queries)
    dq_ref[...] = (t_matmul(keys, score_grads) * DH ** (-0.5)).T.astype(BF16)

    @pl.when(block == length // rows - 1)
    def _():
        dk_ref[...] = (dk_sum[...] * DH ** (-0.5)).astype(BF16)
        dv_ref[...] = dv_sum[...].astype(BF16)


def attention_sizes(length):
    rows = 256
    return rows, min(length, rows + WINDOW)


def attention_forward(queries, keys, values, seg_row, seg_col):
    length, columns = queries.shape
    heads = columns // DH
    rows, span = attention_sizes(length)
    block = pl.BlockSpec((rows, DH), lambda h, i: (i, h))
    whole = pl.BlockSpec((length, DH), lambda h, i: (0, h))
    return pl.pallas_call(
        partial(forward_kernel, span),
        grid=(heads, length // rows),
        in_specs=[
            block,
            whole,
            whole,
            pl.BlockSpec((1, rows), lambda h, i: (0, i)),
            pl.BlockSpec((length, 1), lambda h, i: (0, 0)),
        ],
        out_specs=[block, pl.BlockSpec((1, 1, rows), lambda h, i: (h, 0, i))],
        out_shape=[
            jax.ShapeDtypeStruct((length, columns), BF16),
            jax.ShapeDtypeStruct((heads, 1, length), F32),
        ],
        compiler_params=pltpu.CompilerParams(vmem_limit_bytes=48 * MIB),
        cost_estimate=pl.CostEstimate(
            flops=4 * heads * length * span * DH,
            bytes_accessed=8 * length * columns,
            transcendentals=heads * length * span,
        ),
        name="attend",
    )(queries, keys, values, seg_row, seg_col)


def attention_backward(queries, keys, values, grads, lse, seg_row, seg_col):
    length, columns = queries.shape
    heads = columns // DH
    rows, span = attention_sizes(length)
    block = pl.BlockSpec((rows, DH), lambda h, i: (i, h))
    whole = pl.BlockSpec((length, DH), lambda h, i: (0, h))
    shape = jax.ShapeDtypeStruct((length, columns), BF16)
    return pl.pallas_call(
        partial(backward_kernel, span),
        grid=(heads, length // rows),
        in_specs=[
            block,
            whole,
            whole,
            block,
            pl.BlockSpec((1, 1, rows), lambda h, i: (h, 0, i)),
            pl.BlockSpec((1, rows), lambda h, i: (0, i)),
            pl.BlockSpec((length, 1), lambda h, i: (0, 0)),
        ],
        out_specs=[block, whole, whole],
        out_shape=[shape, shape, shape],
        scratch_shapes=[pltpu.VMEM((length, DH), F32), pltpu.VMEM((length, DH), F32)],
        compiler_params=pltpu.CompilerParams(vmem_limit_bytes=48 * MIB),
        cost_estimate=pl.CostEstimate(
            flops=10 * heads * length * span * DH,
            bytes_accessed=14 * length * columns,
            transcendentals=heads * length * span,
        ),
        name="attend_back",
    )(queries, keys, values, grads, lse, seg_row, seg_col)


def qkv_kernel(
    me_ref,
    even_ref,
    odd_ref,
    weight_ref,
    gain_ref,
    normed_even_ref,
    normed_odd_ref,
    q_ref,
    k_ref,
    v_ref,
    square_ref,
):
    turned = me_ref[0] % 2
    rows = even_ref.shape[0]
    columns = q_ref.shape[1]
    for k, (token_ref, normed_ref) in enumerate(
        ((even_ref, normed_even_ref), (odd_ref, normed_odd_ref))
    ):
        at = pl.ds(pl.multiple_of((turned ^ k) * rows, rows), rows)
        wide = token_ref[...].astype(F32)
        normed = (wide * rms_factor(wide) * gain_ref[...]).astype(BF16)
        normed_ref[...] = normed
        pre = matmul(normed, weight_ref[...])
        q_ref[at, :] = pre[:, :columns]
        k_ref[at, :] = pre[:, columns : 2 * columns]
        v_ref[at, :] = pre[:, 2 * columns :].astype(BF16)
        for j in range(2):
            squares = 0.0
            for c in range(j * columns, (j + 1) * columns, DH):
                squares += pre[:, c : c + DH] * pre[:, c : c + DH]
            square_ref[j : j + 1, at] = jnp.sum(squares.T, axis=0, keepdims=True)


def project(even, odd, weight, gain, me, rows):
    pairs = even.shape[0] // rows
    length = 2 * even.shape[0]
    depth, columns = weight.shape[0], weight.shape[1] // 3
    token = pl.BlockSpec((rows, depth), lambda i, me: (i, 0))

    def placed(shape):
        return pl.BlockSpec(shape, lambda i, me: (i ^ (me[0] // 2), 0))

    head = jax.ShapeDtypeStruct((length, columns), F32)
    return pl.pallas_call(
        qkv_kernel,
        grid_spec=pltpu.PrefetchScalarGridSpec(
            num_scalar_prefetch=1,
            grid=(pairs,),
            in_specs=[
                token,
                token,
                pl.BlockSpec(weight.shape, lambda i, me: (0, 0)),
                pl.BlockSpec((1, depth), lambda i, me: (0, 0)),
            ],
            out_specs=[
                token,
                token,
                placed((2 * rows, columns)),
                placed((2 * rows, columns)),
                placed((2 * rows, columns)),
                pl.BlockSpec((2, 2 * rows), lambda i, me: (0, i ^ (me[0] // 2))),
            ],
        ),
        out_shape=[
            jax.ShapeDtypeStruct((length // 2, depth), BF16),
            jax.ShapeDtypeStruct((length // 2, depth), BF16),
            head,
            head,
            jax.ShapeDtypeStruct((length, columns), BF16),
            jax.ShapeDtypeStruct((2, length), F32),
        ],
        compiler_params=pltpu.CompilerParams(vmem_limit_bytes=48 * MIB),
        cost_estimate=pl.CostEstimate(
            flops=6 * length * depth * columns,
            bytes_accessed=length * (4 * depth + 10 * columns) + 6 * depth * columns,
            transcendentals=length,
        ),
        name="project",
    )(me, even, odd, weight, gain)


def split_kernel(q_ref, k_ref, v_ref, out_ref):
    columns = q_ref.shape[1]
    for j, ref in enumerate((q_ref, k_ref, v_ref)):
        out_ref[0, :, j * columns : (j + 1) * columns] = ref[...]


def split_heads(w_query, w_key, w_value, parts):
    rows, columns = w_query.shape[0], w_query.shape[1] // parts
    block = pl.BlockSpec((rows, columns), lambda i: (0, i))
    return pl.pallas_call(
        split_kernel,
        grid=(parts,),
        in_specs=[block] * 3,
        out_specs=pl.BlockSpec((1, rows, 3 * columns), lambda i: (i, 0, 0)),
        out_shape=jax.ShapeDtypeStruct((parts, rows, 3 * columns), BF16),
        name="split_heads",
    )(w_query, w_key, w_value)


def spread(row, columns):
    return jnp.broadcast_to(row, (columns, row.shape[1])).T


def factor_of(square_row):
    return lax.rsqrt(square_row / D + EPSILON)


def turn(values, cosine, sine):
    return values * cosine + pltpu.roll(values, DH // 2, 1) * sine


def rope_kernel(q_ref, k_ref, square_ref, gain_ref, cos_ref, sin_ref, q_out, k_out):
    cosine, sine = cos_ref[...], sin_ref[...]
    for j, (pre_ref, out_ref) in enumerate(((q_ref, q_out), (k_ref, k_out))):
        factor = spread(factor_of(square_ref[j : j + 1, :]), DH)
        for c in range(0, pre_ref.shape[1], DH):
            at = slice(c, c + DH)
            normed = pre_ref[:, at] * factor * gain_ref[j : j + 1, at]
            out_ref[:, at] = turn(normed, cosine, sine).astype(BF16)


def rope(query_pre, key_pre, squares, gains, cosine, sine):
    length, columns = query_pre.shape
    rows = min(512, length)
    block = pl.BlockSpec((rows, columns), lambda i: (i, 0))
    table = pl.BlockSpec((rows, DH), lambda i: (i, 0))
    return pl.pallas_call(
        rope_kernel,
        grid=(length // rows,),
        in_specs=[
            block,
            block,
            pl.BlockSpec((2, rows), lambda i: (0, i)),
            pl.BlockSpec((2, columns), lambda i: (0, 0)),
            table,
            table,
        ],
        out_specs=[block, block],
        out_shape=[jax.ShapeDtypeStruct((length, columns), BF16)] * 2,
        compiler_params=pltpu.CompilerParams(vmem_limit_bytes=32 * MIB),
        name="rope",
    )(query_pre, key_pre, squares, gains, cosine, sine)


def pulled_of(grad_ref, pre_ref, factor, gain_ref, cosine, sine, j, at):
    turned = turn(grad_ref[:, at].astype(F32), cosine, -sine)
    return turned, turned * gain_ref[j : j + 1, at], pre_ref[:, at] * factor


def rope_mean_kernel(
    dq_ref, dk_ref, q_ref, k_ref, square_ref, gain_ref, cos_ref, sin_ref, mean_ref, term_ref
):
    @pl.when(pl.program_id(0) == 0)
    def _():
        term_ref[...] = jnp.zeros_like(term_ref)

    cosine, sine = cos_ref[...], sin_ref[...]
    for j, (grad_ref, pre_ref) in enumerate(((dq_ref, q_ref), (dk_ref, k_ref))):
        factor = spread(factor_of(square_ref[j : j + 1, :]), DH)
        total = 0.0
        for c in range(0, pre_ref.shape[1], DH):
            at = slice(c, c + DH)
            turned, pulled, normed = pulled_of(
                grad_ref, pre_ref, factor, gain_ref, cosine, sine, j, at
            )
            term_ref[j : j + 1, at] += jnp.sum(turned * normed, axis=0, keepdims=True)
            total += pulled * normed
        mean_ref[j : j + 1, :] = jnp.sum(total.T, axis=0, keepdims=True)


def rope_means(query_back, key_back, query_pre, key_pre, squares, gains, cosine, sine):
    length, columns = query_pre.shape
    rows = min(512, length)
    block = pl.BlockSpec((rows, columns), lambda i: (i, 0))
    table = pl.BlockSpec((rows, DH), lambda i: (i, 0))
    row = pl.BlockSpec((2, rows), lambda i: (0, i))
    fixed = pl.BlockSpec((2, columns), lambda i: (0, 0))
    return pl.pallas_call(
        rope_mean_kernel,
        grid=(length // rows,),
        in_specs=[block, block, block, block, row, fixed, table, table],
        out_specs=[row, fixed],
        out_shape=[
            jax.ShapeDtypeStruct((2, length), F32),
            jax.ShapeDtypeStruct((2, columns), F32),
        ],
        compiler_params=pltpu.CompilerParams(vmem_limit_bytes=32 * MIB),
        name="rope_means",
    )(query_back, key_back, query_pre, key_pre, squares, gains, cosine, sine)


def rope_back_kernel(
    me_ref,
    dq_ref,
    dk_ref,
    dv_ref,
    q_ref,
    k_ref,
    square_ref,
    mean_ref,
    gain_ref,
    cos_ref,
    sin_ref,
    out_ref,
):
    cosine, sine = cos_ref[...], sin_ref[...]
    columns = q_ref.shape[1]
    for j, (grad_ref, pre_ref) in enumerate(((dq_ref, q_ref), (dk_ref, k_ref))):
        factor = spread(factor_of(square_ref[j : j + 1, :]), DH)
        mean = spread(mean_ref[j : j + 1, :] / D, DH)
        for c in range(0, columns, DH):
            at = slice(c, c + DH)
            _, pulled, normed = pulled_of(grad_ref, pre_ref, factor, gain_ref, cosine, sine, j, at)
            out_ref[:, j * columns + c : j * columns + c + DH] = (
                factor * (pulled - normed * mean)
            ).astype(BF16)
    out_ref[:, 2 * columns :] = dv_ref[...]


def rope_back(grads, query_pre, key_pre, squares, means, gains, cosine, sine, me, rows):
    length, columns = query_pre.shape
    half = length // rows // 2

    def source(p, me):
        return me[0] ^ (p % half * 2 + p // half)

    block = pl.BlockSpec((rows, columns), lambda p, me: (source(p, me), 0))
    table = pl.BlockSpec((rows, DH), lambda p, me: (source(p, me), 0))
    row = pl.BlockSpec((2, rows), lambda p, me: (0, source(p, me)))
    return pl.pallas_call(
        rope_back_kernel,
        grid_spec=pltpu.PrefetchScalarGridSpec(
            num_scalar_prefetch=1,
            grid=(2 * half,),
            in_specs=[block] * 5
            + [row, row, pl.BlockSpec((2, columns), lambda p, me: (0, 0)), table, table],
            out_specs=pl.BlockSpec((rows, 3 * columns), lambda p, me: (p, 0)),
        ),
        out_shape=jax.ShapeDtypeStruct((length, 3 * columns), BF16),
        compiler_params=pltpu.CompilerParams(vmem_limit_bytes=32 * MIB),
        name="rope_back",
    )(me, *grads, query_pre, key_pre, squares, means, gains, cosine, sine)


def expert_kernel(
    in_places, down_places, first_ref, xa_ref, xb_ref, ua_ref, ub_ref, ra_ref, rb_ref, router_ref, *refs
):
    weight_refs = refs[: len(in_places) + len(down_places)]
    (ya_ref, yb_ref, za_ref, zb_ref, ga_ref, gb_ref, xc_ref, uc_ref, dg_ref, hid_ref) = refs[-13:-3]
    wi_ref, wd_ref, sems = refs[-3:]
    experts, _, hidden = hid_ref.shape
    rows = xa_ref.shape[0]

    @pl.when(pl.program_id(0) == 0)
    def _():
        copies = []
        for n, (ref, (r, first, part)) in enumerate(zip(weight_refs, in_places + down_places)):
            goal = wi_ref if n < len(in_places) else wd_ref
            place = lax.rem(first_ref[1] ^ r, goal.shape[1] // part)
            at = pl.ds(pl.multiple_of(place * part + first, ref.shape[1]), ref.shape[1])
            copies.append(pltpu.make_async_copy(ref, goal.at[:, at, :], sems.at[n]))
        for copy in copies:
            copy.start()
        for copy in copies:
            copy.wait()

    slot = lax.broadcasted_iota(jnp.int32, (CAP, rows), 0)
    blocks = (
        (xa_ref, ua_ref, ra_ref, ya_ref, za_ref, ga_ref),
        (xb_ref, ub_ref, rb_ref, yb_ref, zb_ref, gb_ref),
    )
    picks = []
    for k, (x_ref, u_ref, rank_ref, _, _, _) in enumerate(blocks):
        hits = jnp.concatenate([slot == rank_ref[0, e : e + 1, :] for e in range(experts)], 0)
        pick = hits.astype(F32).astype(BF16)
        picks.append(pick)
        x_rows = matmul(pick, x_ref[...]).astype(BF16)
        u_rows = matmul(pick, u_ref[...]).astype(BF16)
        for e in range(experts):
            xc_ref[e, k * CAP : (k + 1) * CAP, :] = x_rows[e * CAP : (e + 1) * CAP]
            uc_ref[e, k * CAP : (k + 1) * CAP, :] = u_rows[e * CAP : (e + 1) * CAP]
    outs, backs, gate_grads = [], [], []
    for e in range(experts):
        x_rows, u_rows = xc_ref[e], uc_ref[e]
        logits = matmul(x_rows, router_ref[...])
        lane = lax.broadcasted_iota(jnp.int32, logits.shape, 1)
        logits = jnp.where(lane < E, logits, -1e30)
        expos = jnp.exp(logits - jnp.max(logits, axis=-1, keepdims=True))
        own = jnp.sum(jnp.where(lane == first_ref[0] + e, expos, 0.0), axis=-1, keepdims=True)
        gate = own / jnp.sum(expos, axis=-1, keepdims=True)
        gated = matmul(x_rows, wi_ref[e, :, :hidden])
        upward = matmul(x_rows, wi_ref[e, :, hidden:])
        pulled = matmul_t(u_rows, wd_ref[e])
        sig = jax.nn.sigmoid(gated)
        silu = gated * sig
        acts = silu * upward
        gate_grads.append(jnp.sum(acts * pulled, axis=-1, keepdims=True))
        hidden_gate = (acts * gate).astype(BF16)
        hidden_grads = pulled * gate
        hid_ref[e] = hidden_gate
        dg_ref[e, :, :hidden] = (hidden_grads * upward * sig * (1.0 + gated * (1.0 - sig))).astype(BF16)
        dg_ref[e, :, hidden:] = (hidden_grads * silu).astype(BF16)
        outs.append(matmul(hidden_gate, wd_ref[e]).astype(BF16))
        backs.append(matmul_t(dg_ref[e], wi_ref[e]).astype(BF16))
    for k, (_, _, rank_ref, y_ref, z_ref, g_ref) in enumerate(blocks):
        at = slice(k * CAP, (k + 1) * CAP)
        y_ref[...] = t_matmul(picks[k], jnp.concatenate([v[at] for v in outs], 0)).astype(BF16)
        z_ref[...] = t_matmul(picks[k], jnp.concatenate([v[at] for v in backs], 0)).astype(BF16)
        for e in range(experts):
            hit = slot == rank_ref[0, e : e + 1, :]
            g_ref[0, e : e + 1, :] = jnp.sum(
                jnp.where(hit, gate_grads[e][at], 0.0), axis=0, keepdims=True
            )


def run_experts(x, u, ranks, in_pieces, down_pieces, router, places, which, compact, parts):
    experts, _, hidden = in_pieces[0][2].shape
    hidden = hidden // 2
    depth = x[0].shape[1]
    in_places = [(r, at, parts[0]) for r, at, _ in in_pieces]
    down_places = [(r, at, parts[1]) for r, at, _ in down_pieces]
    pieces = [array for _, _, array in in_pieces + down_pieces]
    rows = ranks[0].shape[2]
    steps = x[0].shape[0] // rows
    token = pl.BlockSpec((rows, depth), lambda i: (i, 0))
    rank = pl.BlockSpec((1, experts, rows), lambda i: (i, 0, 0))
    anywhere = pl.BlockSpec(memory_space=pl.ANY)

    def slots(columns):
        return pl.BlockSpec((experts, 2 * CAP, columns), lambda i: (0, i + which * steps, 0))

    shape = jax.ShapeDtypeStruct
    tokens = shape(x[0].shape, BF16)
    gates = shape((steps, experts, rows), F32)
    count = 4 * steps * CAP
    wide = shape((experts, count, depth), BF16)
    inputs = [places, *x, *u, *ranks, router, *pieces]
    return pl.pallas_call(
        partial(expert_kernel, in_places, down_places),
        grid=(steps,),
        in_specs=[pl.BlockSpec(memory_space=pltpu.SMEM)]
        + [token] * 4
        + [rank] * 2
        + [pl.BlockSpec(router.shape, lambda i: (0, 0), pipeline_mode=pl.Buffered(1))]
        + [anywhere] * (len(pieces) + len(compact)),
        out_specs=[token] * 4 + [rank] * 2 + [slots(depth)] * 2 + [slots(2 * hidden), slots(hidden)],
        out_shape=[tokens] * 4
        + [gates] * 2
        + [wide] * 2
        + [shape((experts, count, 2 * hidden), BF16), shape((experts, count, hidden), BF16)],
        scratch_shapes=[
            pltpu.VMEM((experts, depth, 2 * hidden), BF16),
            pltpu.VMEM((experts, hidden, depth), BF16),
            pltpu.SemaphoreType.DMA((len(pieces),)),
        ],
        input_output_aliases={len(inputs) + i: 6 + i for i in range(len(compact))},
        compiler_params=pltpu.CompilerParams(vmem_limit_bytes=60 * MIB),
        cost_estimate=pl.CostEstimate(
            flops=4 * steps * CAP * experts * depth * (7 * hidden + 2 * rows),
            bytes_accessed=60 * MIB,
            transcendentals=2 * steps * CAP * experts * hidden,
        ),
        name="experts",
    )(*inputs, *compact)


def product_kernel(me_ref, left_ref, right_ref, out_ref):
    out_ref[0] = t_matmul(left_ref[0], right_ref[0]).astype(BF16)


def products(left, right, part, r, count, me, name):
    experts, rows, _ = left.shape
    columns = right.shape[2]
    wide = min(columns, 1024)
    return pl.pallas_call(
        product_kernel,
        grid_spec=pltpu.PrefetchScalarGridSpec(
            num_scalar_prefetch=1,
            grid=(experts, columns // wide),
            in_specs=[
                pl.BlockSpec((1, rows, part), lambda e, j, me: (e, 0, lax.rem(me[0] ^ r, count))),
                pl.BlockSpec((1, rows, wide), lambda e, j, me: (e, 0, j)),
            ],
            out_specs=pl.BlockSpec((1, part, wide), lambda e, j, me: (e, 0, j)),
        ),
        out_shape=jax.ShapeDtypeStruct((experts, part, columns), BF16),
        compiler_params=pltpu.CompilerParams(vmem_limit_bytes=56 * MIB),
        cost_estimate=pl.CostEstimate(
            flops=2 * experts * rows * part * columns,
            bytes_accessed=2 * experts * rows * (part + columns),
            transcendentals=0,
        ),
        name=name,
    )(me, left, right)


def per_device(
    S,
    F,
    tokens,
    segments,
    routes,
    cotangent,
    w_query,
    w_key,
    w_value,
    w_output,
    router,
    attn_gain,
    moe_gain,
    query_gain,
    key_gain,
    w_gate,
    w_up,
    w_down,
):
    s = lax.axis_index("seq")
    f = lax.axis_index("fsdp")
    T = tokens.shape[1]
    L = S * T
    heads = H // S
    C = heads * DH
    experts = E // S
    part = w_query.shape[0]
    half_f = F // 2
    hidden_half = w_gate.shape[2] // 2

    me = s.reshape(1).astype(jnp.int32)
    f_at = f.reshape(1).astype(jnp.int32)
    half_at = f // half_f
    tokens_low = tokens[0]
    upstream_low = cotangent[0]
    inputs = tokens_low.astype(F32)
    half_rows = T // 2
    in_part, down_part = w_gate.shape[1], w_down.shape[1]
    quarter = in_part // 4

    def hidden_part(which, first, count):
        return jnp.concatenate(
            [
                lax.dynamic_slice(
                    weight, (0, first, which * hidden_half), (experts, count, hidden_half)
                )
                for weight in (w_gate, w_up)
            ],
            2,
        )

    def far_swap(values, *dep):
        return swap(after(values, dep), "fsdp", F, half_f)

    def near_swap(values, *dep):
        return near_pieces(after(values, dep), F)

    named = routes[0].T[None] == jnp.arange(E, dtype=jnp.int32)[:, None, None]
    chosen = jnp.any(named, axis=1)
    index = jnp.arange(T, dtype=jnp.int32)
    before = (index[:, None] <= index[None, :]).astype(BF16)
    ranks = jnp.where(chosen, matmul(chosen.astype(BF16), before) - 1.0, -1.0)
    small = jnp.concatenate(
        [
            router.reshape(-1),
            attn_gain,
            moe_gain,
            query_gain,
            key_gain,
            ranks.astype(BF16).reshape(-1),
        ]
    )[None]
    crossed = split_heads(w_query, w_key, w_value, S)
    small = double(after(small, crossed), "fsdp", F)
    crossed = lax.all_to_all(crossed, "seq", split_axis=0, concat_axis=0, tiled=True)
    near_own = [near_swap(hidden_part(half_at, 0, 2 * quarter), small)]
    small = double(small, "seq", S)
    crossed, near_own[0], small = tie(crossed, near_own[0], small)

    small = in_order(small, S, F, s, f).reshape(S, F, -1)
    token_first = gather_first(after(tokens_low, crossed), S)
    qkv_pieces = {0: crossed}
    for r in range(1, F):
        low = low_bit(r)
        qkv_pieces[r] = swap(qkv_pieces[r ^ low], "fsdp", F, low)
        if r == half_f:
            qkv_pieces, token_first = tie(qkv_pieces, token_first)
            partner_up = [far_swap(upstream_low[:half_rows], qkv_pieces[r])]
    token_more = gather_more(tokens_low, token_first, S)
    qkv_pieces, partner_up[0], token_more = tie(qkv_pieces, partner_up[0], token_more)
    tokens_even, tokens_odd = gather_end(tokens_low, token_first, token_more, S)
    w_qkv = place_fsdp(qkv_pieces, f, 1).reshape(D, 3 * C)

    full_router = small[:, :, : part * E].reshape(D, E)
    gains = [
        small[:, :, part * (E + i) : part * (E + i + 1)].reshape(D).astype(F32) for i in range(4)
    ]
    gain_attn, gain_moe = gains[0], gains[1]
    head_gain = lax.dynamic_slice(jnp.stack(gains[2:], 0), (0, s * C), (2, C))
    rank_part = small[:, :, part * (E + 4) :].reshape(S, F, E, T)

    def ranks_of(index):
        ranks = lax.dynamic_slice(rank_part, (0, index, s * experts, 0), (S, 1, experts, T))
        ranks = relative(ranks[:, 0], s).astype(jnp.int32)
        return ranks[: S // 2], ranks[S // 2 :]

    places = jnp.arange(L, dtype=jnp.int32).astype(F32)
    freqs = ROPE_BASE ** (-(jnp.arange(DH // 2, dtype=F32) * 2.0 / DH))
    angles = places[:, None] * freqs[None, :]
    cosine, sine = jnp.cos(angles), jnp.sin(angles)
    cosine = jnp.concatenate([cosine, cosine], 1)
    sine = jnp.concatenate([-sine, sine], 1)

    def far_part(n, *dep):
        return far_swap(hidden_part(1 - half_at, n * quarter, quarter), *dep)

    partner_up.append(far_swap(upstream_low[half_rows:], w_qkv))
    near_own.append(near_swap(hidden_part(half_at, 2 * quarter, quarter), w_qkv))
    out_pieces = fsdp_pieces(after(w_output, w_qkv), F)
    own_up_first = gather_first(after(upstream_low, w_qkv), S)
    normed_even, normed_odd, query_pre, key_pre, value_low, squares = project(
        tokens_even, tokens_odd, w_qkv, gain_attn[None], me, T
    )
    squares, partner_up[1], near_own[1], out_pieces, own_up_first = tie(
        squares, partner_up[1], near_own[1], out_pieces, own_up_first
    )
    partner_up = jnp.concatenate(partner_up, 0)
    own_output = place_fsdp(out_pieces, f, 0).reshape(C, D)

    out_first = gather_first(own_output, S)
    far = [far_part(0, squares)]
    near_own.append(near_swap(hidden_part(half_at, 3 * quarter, quarter), squares))
    squares = sum_all(squares, "seq", S)
    query_low, key_low = rope(query_pre, key_pre, squares, head_gain, cosine, sine)
    query_low, out_first, far[0], near_own[2] = tie(query_low, out_first, far[0], near_own[2])

    seg_row = segments
    seg_col = segments.reshape(L, 1)
    out_more = gather_more(own_output, out_first, S)
    far.append(far_part(1, query_low))
    down_rows = quarters(w_down, 1)
    down = [near_swap(down_rows[0], query_low)]
    attended, lse = attention_forward(query_low, key_low, value_low, seg_row, seg_col)
    attended, out_more, far[1], down[0] = tie(attended, out_more, far[1], down[0])
    attended_blocks = attended.reshape(S, T, C)
    come = lax.all_to_all(attended_blocks, "seq", split_axis=0, concat_axis=0, tiled=True)
    out_even, out_odd = gather_end(own_output, out_first, out_more, S)
    far.append(far_part(2, attended))
    near_far = [near_swap(far[0], attended)]
    own_up_more = gather_more(after(upstream_low, attended), own_up_first, S)
    come, far[2], near_far[0], own_up_more = tie(come, far[2], near_far[0], own_up_more)
    own_u = gather_end(upstream_low, own_up_first, own_up_more, S)
    far.append(far_part(3, come))
    near_far.append(near_swap(far[1], come))
    partner_up_first = gather_first(after(partner_up, come), S)
    come = relative(come, s).transpose(1, 0, 2).reshape(T, D)
    residual = inputs + matmul(come[:, : D // 2], out_even) + matmul(come[:, D // 2 :], out_odd)
    moe_factor = rms_factor(residual)
    residual_n = residual * moe_factor
    second_low = (residual_n * gain_moe).astype(BF16)
    second_low, far[3], near_far[1], partner_up_first = tie(
        second_low, far[3], near_far[1], partner_up_first
    )

    own_first = gather_first(second_low, S)
    partner_low = [far_swap(second_low[:half_rows])]
    near_far.append(near_swap(far[2], second_low))
    own_first, partner_low[0], near_far[2] = tie(own_first, partner_low[0], near_far[2])
    own_more = gather_more(second_low, own_first, S)
    partner_low.append(far_swap(second_low[half_rows:], own_first))
    near_far.append(near_swap(far[3], own_first))
    partner_up_more = gather_more(after(partner_up, own_first), partner_up_first, S)
    own_more, partner_low[1], near_far[3], partner_up_more = tie(
        own_more, partner_low[1], near_far[3], partner_up_more
    )
    partner_low = jnp.concatenate(partner_low, 0)
    own_x = gather_end(second_low, own_first, own_more, S)
    partner_first = gather_first(after(partner_low, own_more), S)
    down.append(near_swap(jnp.concatenate(down_rows[1:3], 1), own_more))
    own_ranks, other_ranks = ranks_of(f), ranks_of(f ^ half_f)
    partner_first, down[1], own_x, own_ranks, other_ranks = tie(
        partner_first, down[1], own_x, own_ranks, other_ranks
    )
    other_u = gather_end(partner_up, partner_up_first, partner_up_more, S)
    partner_more = gather_more(partner_low, partner_first, S)
    down.append(near_swap(down_rows[3], partner_first))
    partner_more, down[2], other_u = tie(partner_more, down[2], other_u)
    other_x = gather_end(partner_low, partner_first, partner_more, S)
    in_pieces = []
    for r in range(F):
        for n, rows in enumerate(near_own if r < half_f else near_far):
            first = (0, 2, 3)[n] if r < half_f else n
            in_pieces.append((r, first * quarter, rows[r % half_f]))
    down_pieces = [
        (r, (0, 1, 3)[n] * (down_part // 4), down[n][r]) for r in range(half_f) for n in range(3)
    ]
    wide_router = jnp.pad(full_router, ((0, 0), (0, 128 - E)))
    expert_places = jnp.stack([s * experts, f]).astype(jnp.int32)
    parts = (in_part, down_part)
    own_parts = run_experts(
        own_x, own_u, own_ranks, in_pieces, down_pieces, wide_router, expert_places, 0, (), parts
    )
    own_parts, other_x = tie(own_parts, other_x)
    own_got = swap(own_parts[3], "seq", S, 1)
    own_out_got = swap(own_parts[1], "seq", S, 1)
    other_parts = run_experts(
        other_x,
        other_u,
        other_ranks,
        in_pieces,
        down_pieces,
        wide_router,
        expert_places,
        1,
        own_parts[6:],
        parts,
    )
    other_parts, own_got, own_out_got = tie(other_parts, own_got, own_out_got)
    logits = matmul(second_low, full_router)
    router_probs = jax.nn.softmax(logits, axis=-1)

    x_rows, u_rows, in_grads, hidden_gate = other_parts[6:]
    in_terms, down_terms = {}, {}

    def in_products(r, *dep):
        in_terms[r] = products(
            x_rows, after(in_grads, dep), in_part, r, F, f_at, "in_products"
        )

    odd = [r for r in range(F) if r & 1]
    far_odd = [r for r in odd if r & half_f]
    near_odd = [r for r in odd if not r & half_f]

    def to_home(even, odd):
        return absolute(jnp.concatenate([even, odd], 0).transpose(0, 2, 1), s)

    gate_grads = jnp.stack(
        [to_home(own_parts[4], own_parts[5]), to_home(other_parts[4], other_parts[5])], 1
    ).reshape(S, -1)
    other_got = swap(other_parts[3], "seq", S, 1)
    for r in far_odd:
        in_products(r)
    gate_grads = lax.all_to_all(gate_grads, "seq", split_axis=0, concat_axis=0, tiled=True)
    other_got, in_terms, gate_grads = tie(other_got, in_terms, gate_grads)
    sent = {r: quarters(in_terms[r], 1) for r in far_odd}

    def send_in(n, *dep):
        return {r: swap(after(sent[r][n], dep), "fsdp", F, 1) for r in sent}

    other_sums = sum_cores(other_parts[2], other_got, S)
    come = sum_first(other_sums, S)
    far_got = [send_in(0, other_got)]
    other_out_got = swap(after(other_parts[1], other_got), "seq", S, 1)
    come, far_got[0], other_out_got = tie(come, far_got[0], other_out_got)
    gate_grads = gate_grads.reshape(S, 2, T * experts)
    partner_grads = far_swap(gate_grads[:, 1], come)
    singles, other_total = sum_more(other_sums, come, S)
    come = sum_last(singles, S)
    middle_sent = {r: jnp.concatenate(sent[r][1:3], 1) for r in sent}
    middle_got = {
        r: swap(after(middle_sent[r], far_got[0]), "fsdp", F, 1) for r in middle_sent
    }

    def down_products(r, dep):
        down_terms[r] = products(
            after(hidden_gate, dep), u_rows, down_part, r, half_f, f_at, "down_products"
        )

    for r in range(1, half_f, 2):
        down_products(r, singles)
    come, middle_got, partner_grads, down_terms = tie(
        come, middle_got, partner_grads, down_terms
    )
    for n in range(2):
        far_got.append({r: got[:, n * quarter : (n + 1) * quarter] for r, got in middle_got.items()})
    other_rows = add_all(other_total, come).astype(BF16)
    gate_grads = gate_grads[:, 0] + partner_grads
    gate_grads = gate_grads.reshape(S, T, experts).transpose(1, 0, 2).reshape(T, E)
    back = [far_swap(other_rows[:half_rows])]
    own_sums = sum_cores(own_parts[2], after(own_got, other_rows), S)
    come = sum_first(own_sums, S)
    far_got.append(send_in(3, other_rows))
    for r in far_odd:
        in_products(r ^ 1, other_rows)
    come, back[0], far_got[3], in_terms = tie(come, back[0], far_got[3], in_terms)
    back.append(far_swap(other_rows[half_rows:], come))
    singles, own_total = sum_more(own_sums, come, S)
    come = sum_last(singles, S)
    down_sent = {r: quarters(down_terms[r], 1) for r in range(1, half_f, 2)}

    def send_down(n, *dep):
        return {r: swap(after(down_sent[r][n], dep), "fsdp", F, 1) for r in down_sent}

    down_got = [send_down(0, singles)]
    for r in near_odd:
        in_products(r, singles)
    come, back[1], down_got[0], in_terms = tie(come, back[1], down_got[0], in_terms)
    row_grads = add_all(own_total, come) + jnp.concatenate(back, 0).astype(F32)

    upstream = upstream_low.astype(F32)
    logit_grads = router_probs * (
        gate_grads - jnp.sum(router_probs * gate_grads, axis=-1, keepdims=True)
    )
    router_wide = full_router.astype(F32)
    second_grads = row_grads + jnp.dot(logit_grads, router_wide.T, precision=HIGHEST)
    pulled = second_grads * gain_moe
    residual_grads = upstream + moe_factor * (
        pulled - residual_n * jnp.mean(pulled * residual_n, axis=-1, keepdims=True)
    )
    branch_low = residual_grads.astype(BF16)

    def sum_near(terms):
        mask = 2
        while mask < half_f:
            terms = {
                r: terms[r] + swap(terms[r | mask].astype(BF16), "fsdp", F, mask).astype(F32)
                for r in terms
                if not r & mask
            }
            mask *= 2
        (total,) = terms.values()
        return total

    def far_sum(n, *dep):
        terms = {
            r ^ 1: quarters(in_terms[r ^ 1], 1)[n].astype(F32) + far_got[n][r].astype(F32)
            for r in far_odd
        }
        return far_swap(sum_near(terms).astype(BF16), *dep)

    branch_first = gather_first(branch_low, S)
    far_sums = [far_sum(0, branch_low)]
    down_got.append(send_down(1, branch_low))
    for r in range(0, half_f, 2):
        down_products(r, branch_low)
    branch_first, far_sums[0], down_got[1], down_terms = tie(
        branch_first, far_sums[0], down_got[1], down_terms
    )
    branch_more = gather_more(branch_low, branch_first, S)
    far_sums.append(far_sum(1, branch_first))
    down_got.append(send_down(2, branch_first))
    branch_even, branch_odd = gather_end(branch_low, branch_first, branch_more, S)

    head_grads = jnp.concatenate(
        [matmul_t(branch_even, own_output), matmul_t(branch_odd, own_output)], 0
    ).astype(BF16)
    head_grads = absolute(head_grads.reshape(S, T, C), s).reshape(L, C)
    for r in near_odd:
        in_products(r ^ 1, branch_more)
    head_grads, far_sums[1], down_got[2], in_terms = tie(
        head_grads, far_sums[1], down_got[2], in_terms
    )
    far_sums.append(far_sum(2, head_grads))
    down_got.append(send_down(3, head_grads))
    other_out_sums = sum_cores(other_parts[0], after(other_out_got, head_grads), S)
    come = sum_first(other_out_sums, S)
    query_back, key_back, value_back = attention_backward(
        query_low, key_low, value_low, head_grads, lse, seg_row, seg_col
    )
    query_back, far_sums[2], down_got[3], come = tie(query_back, far_sums[2], down_got[3], come)

    singles, other_total = sum_more(other_out_sums, come, S)
    come = sum_last(singles, S)
    far_sums.append(far_sum(3, query_back))
    attended_rel = relative(after(attended_blocks, singles), s).reshape(2, L // 2, C)
    output_term = t_matmul(attended_rel[0], branch_even) + t_matmul(attended_rel[1], branch_odd)
    output_term = by_index(output_term.astype(BF16).reshape(F, part, D), f, F)
    output_got = swap(output_term[: F // 2], "fsdp", F, 1)
    value_rel = relative(value_back.reshape(S, T, C), s).reshape(2, L // 2, C)

    def weight_term(even, odd):
        term = (t_matmul(normed_even, even) + t_matmul(normed_odd, odd)).astype(BF16)
        return by_index(term.reshape(S, F, part, -1).transpose(1, 0, 2, 3), f, F)

    means, gain_term = rope_means(
        query_back, key_back, query_pre, key_pre, squares, head_gain, cosine, sine
    )
    means = sum_all(means, "seq", S)
    value_term = weight_term(value_rel[0], value_rel[1])
    means, come, far_sums[3], output_got, value_term = tie(
        means, come, far_sums[3], output_got, value_term
    )
    other_outs = add_all(other_total, come).astype(BF16)
    value_got = swap(value_term[: F // 2], "fsdp", F, 1)
    pre_rel = rope_back(
        (query_back, key_back, value_back),
        query_pre,
        key_pre,
        squares,
        means,
        head_gain,
        cosine,
        sine,
        me,
        T,
    ).reshape(2, L // 2, 3 * C)
    normed_got = swap(matmul_t(pre_rel[1], w_qkv).astype(BF16), "seq", S, 1)
    normed_kept = matmul_t(pre_rel[0], w_qkv).astype(BF16)
    normed_got, normed_kept, value_got = tie(normed_got, normed_kept, value_got)

    normed_sums = sum_cores(normed_kept, normed_got, S)
    come = sum_first(normed_sums, S)
    value_sum = sum_rest(sum_even(value_term, value_got, F), F)
    turned_term = weight_term(
        after(pre_rel[0][:, : 2 * C], normed_got), after(pre_rel[1][:, : 2 * C], normed_got)
    )
    come, turned_term, value_sum = tie(come, turned_term, value_sum)
    turned_got = swap(turned_term[: F // 2], "fsdp", F, 1)
    singles, normed_total = sum_more(normed_sums, come, S)
    come = sum_last(singles, S)
    outs_back = [far_swap(other_outs[:half_rows], turned_term)]
    late_grads, late_logits = after(second_grads, turned_term), after(logit_grads, turned_term)
    router_term = jnp.dot(second_low.astype(F32).T, late_logits, precision=HIGHEST)
    moe_gain_term = jnp.sum(late_grads * residual_n, axis=0)
    gain_terms = jnp.concatenate(
        [router_term.reshape(S * F, part * E), moe_gain_term.reshape(S * F, part)], 1
    )
    gain_terms = in_relative(gain_terms, S, F, s, f)
    head_terms = gain_term.reshape(2, F, part).transpose(1, 0, 2).reshape(F, 2 * part)
    head_terms = in_relative(head_terms, 1, F, 0, f)
    come, turned_got, outs_back[0], gain_terms, head_terms = tie(
        come, turned_got, outs_back[0], gain_terms, head_terms
    )
    normed_grads = add_all(normed_total, come)
    turned_sum = sum_rest(sum_even(turned_term, turned_got, F), F)
    middle = in_part // 2

    def send_near(first, dep):
        return {
            r: swap(after(in_terms[r][:, first : first + middle], dep), "fsdp", F, 1)
            for r in near_odd
        }

    near_got = [send_near(0, turned_got)]
    own_out_sums = sum_cores(own_parts[0], after(own_out_got, turned_got), S)
    come = sum_first(own_out_sums, S)
    turned_sum, come, near_got[0] = tie(turned_sum, come, near_got[0])
    near_got.append(send_near(middle, turned_sum))
    outs_back.append(far_swap(other_outs[half_rows:], turned_sum))
    gain_terms = halve(after(gain_terms, turned_sum), "seq", S)
    gain_terms = halve(jnp.concatenate([gain_terms, head_terms], 1), "fsdp", F)[0]
    head_terms = gain_terms[part * (E + 1) :]
    singles, own_total = sum_more(own_out_sums, come, S)
    own_outs = add_all(own_total, sum_last(singles, S))
    outs_back = jnp.concatenate(outs_back, 0).astype(F32)
    mixed = (residual + own_outs + outs_back).astype(BF16)[None]

    qkv_term = jnp.concatenate([turned_sum, value_sum], -1).astype(BF16)
    qkv_term = lax.all_to_all(qkv_term, "seq", split_axis=0, concat_axis=0, tiled=True)
    qkv_term = qkv_term.reshape(S, part, 3, C).transpose(2, 1, 0, 3).reshape(3, part, D).astype(F32)
    grad_output = sum_rest(sum_even(output_term, output_got, F), F)

    near_got = {r: jnp.concatenate([got[r] for got in near_got], 1) for r in near_odd}
    own_term = sum_near(
        {r ^ 1: in_terms[r ^ 1].astype(F32) + near_got[r].astype(F32) for r in near_odd}
    )
    far_term = jnp.concatenate(far_sums, 1).astype(F32)
    first_half = half_at == 0
    lower = jnp.where(first_half, own_term, far_term)
    upper = jnp.where(first_half, far_term, own_term)
    grad_gate, grad_up = (
        jnp.concatenate([lower[..., at], upper[..., at]], axis=-1)
        for at in (slice(0, hidden_half), slice(hidden_half, 2 * hidden_half))
    )
    down_got = {r: jnp.concatenate([got[r] for got in down_got], 1) for r in down_sent}
    grad_down = sum_near(
        {r ^ 1: down_terms[r ^ 1].astype(F32) + down_got[r].astype(F32) for r in down_sent}
    )

    attn_factor = rms_factor(inputs)
    inputs_n = inputs * attn_factor
    attn_pulled = normed_grads * gain_attn
    grad_tokens = residual_grads + attn_factor * (
        attn_pulled - inputs_n * jnp.mean(attn_pulled * inputs_n, axis=-1, keepdims=True)
    )
    own_weights = jnp.stack([w_query, w_key, w_value], 0).astype(F32)
    grad_attn_gain = jnp.sum(qkv_term * own_weights, axis=(0, 2)) / attn_gain.astype(F32)
    return (
        mixed,
        grad_tokens[None],
        qkv_term[0],
        qkv_term[1],
        qkv_term[2],
        grad_output,
        gain_terms[: part * E].reshape(part, E),
        grad_attn_gain,
        gain_terms[part * E : part * (E + 1)],
        head_terms[:part],
        head_terms[part:],
        grad_gate,
        grad_up,
        grad_down,
    )


def solution(mesh):
    tokens_spec = P("fsdp", "seq", None)
    rows_spec = P(("seq", "fsdp"), None)
    gain_spec = P(("seq", "fsdp"))
    expert_spec = P("seq", "fsdp", None)
    in_specs = (
        (tokens_spec, P("fsdp", None), tokens_spec, tokens_spec)
        + (rows_spec,) * 5
        + (gain_spec,) * 4
        + (expert_spec,) * 3
    )
    out_specs = (tokens_spec,) * 2 + (rows_spec,) * 5 + (gain_spec,) * 4 + (expert_spec,) * 3
    return jax.shard_map(
        partial(per_device, mesh.shape["seq"], mesh.shape["fsdp"]),
        mesh=mesh,
        in_specs=in_specs,
        out_specs=out_specs,
        check_vma=False,
    )
```

```python
from functools import partial

import jax
import jax.numpy as jnp
from jax import lax
from jax.experimental import pallas as pl
from jax.experimental.pallas import tpu as pltpu
from jax.sharding import PartitionSpec as P

D = 2048
H = 16
DH = 128
E = 16
WINDOW = 1024
CAP = 144

EPSILON = 1e-06
ROPE_BASE = 50000.0
HIGHEST = lax.Precision.HIGHEST
BF16 = jnp.bfloat16
F32 = jnp.float32
MIB = 1024 * 1024


def matmul(left, right):
    return jnp.dot(left, right, preferred_element_type=F32)


def matmul_t(left, right):
    return lax.dot_general(left, right, (((1,), (1,)), ((), ())), preferred_element_type=F32)


def t_matmul(left, right):
    return lax.dot_general(left, right, (((0,), (0,)), ((), ())), preferred_element_type=F32)


def rms_factor(values):
    return lax.rsqrt(jnp.mean(values * values, axis=-1, keepdims=True) + EPSILON)


def swap(values, axis, size, mask):
    return lax.ppermute(values, axis, [(i, i ^ mask) for i in range(size)])


def high_bit(number):
    return 1 << (number.bit_length() - 1)


def low_bit(number):
    return number & -number


def after(values, *others):
    return lax.optimization_barrier((values, others))[0]


def tie(*values):
    return lax.optimization_barrier(values)


def gather_first(values, size):
    return {r: swap(values, "seq", size, r) for r in range(2, size, 2) if r == low_bit(r)}


def gather_more(values, first, size):
    rows = values.shape[0] // 2
    pieces = dict(first)
    for r in range(2, size, 2):
        if r not in pieces:
            up, down = high_bit(r), low_bit(r)
            upper, lower = pieces[r ^ up], pieces[r ^ down]
            upper = upper[0] if isinstance(upper, tuple) else upper[:rows]
            lower = lower[1] if isinstance(lower, tuple) else lower[rows:]
            pieces[r] = (swap(upper, "seq", size, up), swap(lower, "seq", size, down))
    return {r: piece for r, piece in pieces.items() if r not in first}


def gather_end(values, first, more, size):
    blocks = [values]
    for r in range(2, size, 2):
        blocks.extend([first[r]] if r in first else more[r])
    even = jnp.concatenate(blocks, 0)
    return even, swap(even, "seq", size, 1)


def relative(blocks, me):
    size = blocks.shape[0]
    order = list(range(0, size, 2)) + list(range(1, size, 2))
    return jnp.concatenate([lax.dynamic_slice_in_dim(blocks, me ^ r, 1, 0) for r in order], 0)


def absolute(blocks, me):
    size = blocks.shape[0]
    places = [((me ^ j) // 2) + ((me ^ j) % 2) * (size // 2) for j in range(size)]
    return jnp.concatenate([lax.dynamic_slice_in_dim(blocks, at, 1, 0) for at in places], 0)


def sum_cores(even, got, size):
    rows = even.shape[0] // (size // 2)
    half = rows // 2

    def part(r, first):
        at = slice(r // 2 * rows + first, r // 2 * rows + first + half)
        return even[at].astype(F32) + got[at].astype(F32)

    return {r: [part(r, 0), part(r, half)] for r in range(0, size, 2)}


def sum_first(sums, size):
    sums = {r: list(value) for r, value in sums.items()}
    come = {}
    for r in range(size - 2, 0, -2):
        if r != low_bit(r):
            up, down = high_bit(r), low_bit(r)
            for (goal, k, _), piece in come.items():
                if goal == r:
                    sums[r][k] += piece.astype(F32)
            upper, lower = tie(sums[r][0].astype(BF16), sums[r][1].astype(BF16))
            come[r ^ up, 0, r] = swap(upper, "seq", size, up)
            come[r ^ down, 1, r] = swap(lower, "seq", size, down)
    return come


def sum_more(sums, come, size):
    sums = {r: list(value) for r, value in sums.items() if r == 0 or r == low_bit(r)}
    for (goal, k, _), piece in come.items():
        if goal in sums:
            sums[goal][k] += piece.astype(F32)
    singles = {
        r: jnp.concatenate([v.astype(BF16) for v in value], 0) for r, value in sums.items() if r
    }
    return tie(singles)[0], jnp.concatenate(sums[0], 0)


def sum_last(singles, size):
    return {r: swap(value, "seq", size, r) for r, value in singles.items()}


def add_all(total, pieces):
    for piece in pieces.values():
        total += piece.astype(F32)
    return total


def quarters(values, axis):
    step = values.shape[axis] // 4
    return [lax.slice_in_dim(values, k * step, (k + 1) * step, axis=axis) for k in range(4)]


def sum_all(values, axis, size):
    mask = 1
    while mask < size:
        values = values + swap(values, axis, size, mask)
        mask *= 2
    return values


def fsdp_pieces(values, size):
    pieces = {0: values}
    for r in range(1, size):
        low = low_bit(r)
        pieces[r] = swap(pieces[r ^ low], "fsdp", size, low)
    return pieces


def place_fsdp(pieces, me, axis):
    size = len(pieces)
    shape = pieces[0].shape
    whole = jnp.zeros(shape[:axis] + (size,) + shape[axis:], pieces[0].dtype)
    for r, piece in pieces.items():
        whole = lax.dynamic_update_slice_in_dim(whole, jnp.expand_dims(piece, axis), me ^ r, axis)
    return whole


def near_pieces(values, size):
    pieces = {0: values}
    for r in range(1, size // 2):
        up = high_bit(r)
        pieces[r] = swap(pieces[r ^ up], "fsdp", size, up)
    return pieces


def double(values, axis, size):
    mask = 1
    while mask < size:
        values = jnp.concatenate([values, swap(values, axis, size, mask)], 0)
        mask *= 2
    return values


def halve(values, axis, size, mask):
    while mask:
        half = values.shape[0] // 2
        values = values[:half] + swap(values[half:], axis, size, mask)
        mask //= 2
    return values


def relative_pick(seq_size, fsdp_size, s, f):
    index = jnp.arange(seq_size * fsdp_size, dtype=jnp.int32)
    source = ((index // fsdp_size) ^ s) * fsdp_size + ((index % fsdp_size) ^ f)
    return source[:, None] == index[None, :]


def in_order(values, seq_size, fsdp_size, s, f):
    pick = relative_pick(seq_size, fsdp_size, s, f).astype(values.dtype)
    return matmul(pick, values).astype(values.dtype)


def in_relative(values, seq_size, fsdp_size, s, f):
    pick = relative_pick(seq_size, fsdp_size, s, f).astype(F32)
    return jnp.dot(pick, values, precision=HIGHEST)


def by_index(partial_sum, me, size):
    order = [r for r in range(size) if r & 1] + [r for r in range(size) if not r & 1]
    return jnp.concatenate([lax.dynamic_slice_in_dim(partial_sum, me ^ r, 1, 0) for r in order], 0)


def sum_even(stacked, got, size):
    return (stacked[size // 2 :].astype(F32) + got.astype(F32)).astype(BF16)


def sum_rest(stacked, size):
    mask = 2
    values = stacked.astype(F32)
    while mask < size:
        count = values.shape[0] // 2
        pairs = values.reshape((count, 2) + values.shape[1:])
        got = swap(pairs[:, 1].astype(BF16), "fsdp", size, mask)
        values = pairs[:, 0] + got.astype(F32)
        mask *= 2
    return values[0]


def allowed_keys(seg_row, seg_col, first_query, first_key, rows, span, half_window):
    query_at = first_query + lax.broadcasted_iota(jnp.int32, (span, rows), 1)
    key_at = first_key + lax.broadcasted_iota(jnp.int32, (span, rows), 0)
    return (jnp.abs(query_at - key_at) <= half_window) & (seg_col == seg_row)


def first_key_of(block, rows, span, length):
    start = jnp.clip(block * rows - (span - rows) // 2, 0, length - span)
    return pl.multiple_of(start, rows)


def forward_kernel(span, q_ref, k_ref, v_ref, seg_row_ref, seg_col_ref, o_ref, lse_ref):
    block = pl.program_id(1)
    rows, length = q_ref.shape[0], k_ref.shape[0]
    first_key = first_key_of(block, rows, span, length)
    keys = k_ref[pl.ds(first_key, span), :]
    values = v_ref[pl.ds(first_key, span), :]
    scores = matmul_t(keys, q_ref[...]) * DH ** (-0.5)
    allowed = allowed_keys(
        seg_row_ref[...],
        seg_col_ref[pl.ds(first_key, span), :],
        block * rows,
        first_key,
        rows,
        span,
        WINDOW // 2,
    )
    scores = jnp.where(allowed, scores, -1e30)
    peak = jnp.max(scores, axis=0, keepdims=True)
    expos = jnp.exp(scores - peak)
    totals = jnp.sum(expos, axis=0, keepdims=True)
    probs = (expos * (1.0 / totals)).astype(BF16)
    o_ref[...] = t_matmul(values, probs).T.astype(BF16)
    lse_ref[...] = (peak + jnp.log(totals))[None]


def backward_kernel(
    span,
    q_ref,
    k_ref,
    v_ref,
    do_ref,
    lse_ref,
    seg_row_ref,
    seg_col_ref,
    dq_ref,
    dk_ref,
    dv_ref,
    dk_sum,
    dv_sum,
):
    block = pl.program_id(1)
    rows, length = q_ref.shape[0], k_ref.shape[0]

    @pl.when(block == 0)
    def _():
        dk_sum[...] = jnp.zeros_like(dk_sum)
        dv_sum[...] = jnp.zeros_like(dv_sum)

    first_key = first_key_of(block, rows, span, length)
    at = pl.ds(first_key, span)
    keys = k_ref[at, :]
    values = v_ref[at, :]
    queries = q_ref[...]
    grads = do_ref[...]
    scores = matmul_t(keys, queries) * DH ** (-0.5)
    allowed = allowed_keys(
        seg_row_ref[...],
        seg_col_ref[at, :],
        block * rows,
        first_key,
        rows,
        span,
        WINDOW // 2,
    )
    probs = jnp.where(allowed, jnp.exp(scores - lse_ref[0]), 0.0)
    dv_sum[at, :] += matmul(probs.astype(BF16), grads)
    prob_grads = matmul_t(values, grads)
    center = jnp.sum(probs * prob_grads, axis=0, keepdims=True)
    score_grads = (probs * (prob_grads - center)).astype(BF16)
    dk_sum[at, :] += matmul(score_grads, queries)
    dq_ref[...] = (t_matmul(keys, score_grads) * DH ** (-0.5)).T.astype(BF16)

    @pl.when(block == length // rows - 1)
    def _():
        dk_ref[...] = (dk_sum[...] * DH ** (-0.5)).astype(BF16)
        dv_ref[...] = dv_sum[...].astype(BF16)


def attention_sizes(length):
    rows = 256
    return rows, min(length, rows + WINDOW)


def attention_forward(queries, keys, values, seg_row, seg_col):
    length, columns = queries.shape
    heads = columns // DH
    rows, span = attention_sizes(length)
    block = pl.BlockSpec((rows, DH), lambda h, i: (i, h))
    whole = pl.BlockSpec((length, DH), lambda h, i: (0, h))
    return pl.pallas_call(
        partial(forward_kernel, span),
        grid=(heads, length // rows),
        in_specs=[
            block,
            whole,
            whole,
            pl.BlockSpec((1, rows), lambda h, i: (0, i)),
            pl.BlockSpec((length, 1), lambda h, i: (0, 0)),
        ],
        out_specs=[block, pl.BlockSpec((1, 1, rows), lambda h, i: (h, 0, i))],
        out_shape=[
            jax.ShapeDtypeStruct((length, columns), BF16),
            jax.ShapeDtypeStruct((heads, 1, length), F32),
        ],
        compiler_params=pltpu.CompilerParams(vmem_limit_bytes=48 * MIB),
        cost_estimate=pl.CostEstimate(
            flops=4 * heads * length * span * DH,
            bytes_accessed=8 * length * columns,
            transcendentals=heads * length * span,
        ),
        name="attend",
    )(queries, keys, values, seg_row, seg_col)


def attention_backward(queries, keys, values, grads, lse, seg_row, seg_col):
    length, columns = queries.shape
    heads = columns // DH
    rows, span = attention_sizes(length)
    block = pl.BlockSpec((rows, DH), lambda h, i: (i, h))
    whole = pl.BlockSpec((length, DH), lambda h, i: (0, h))
    shape = jax.ShapeDtypeStruct((length, columns), BF16)
    return pl.pallas_call(
        partial(backward_kernel, span),
        grid=(heads, length // rows),
        in_specs=[
            block,
            whole,
            whole,
            block,
            pl.BlockSpec((1, 1, rows), lambda h, i: (h, 0, i)),
            pl.BlockSpec((1, rows), lambda h, i: (0, i)),
            pl.BlockSpec((length, 1), lambda h, i: (0, 0)),
        ],
        out_specs=[block, whole, whole],
        out_shape=[shape, shape, shape],
        scratch_shapes=[pltpu.VMEM((length, DH), F32), pltpu.VMEM((length, DH), F32)],
        compiler_params=pltpu.CompilerParams(vmem_limit_bytes=48 * MIB),
        cost_estimate=pl.CostEstimate(
            flops=10 * heads * length * span * DH,
            bytes_accessed=14 * length * columns,
            transcendentals=heads * length * span,
        ),
        name="attend_back",
    )(queries, keys, values, grads, lse, seg_row, seg_col)


def qkv_kernel(
    me_ref,
    even_ref,
    odd_ref,
    weight_ref,
    gain_ref,
    normed_even_ref,
    normed_odd_ref,
    q_ref,
    k_ref,
    v_ref,
    square_ref,
):
    turned = me_ref[0] % 2
    rows = even_ref.shape[0]
    columns = q_ref.shape[1]
    for k, (token_ref, normed_ref) in enumerate(
        ((even_ref, normed_even_ref), (odd_ref, normed_odd_ref))
    ):
        at = pl.ds(pl.multiple_of((turned ^ k) * rows, rows), rows)
        wide = token_ref[...].astype(F32)
        normed = (wide * rms_factor(wide) * gain_ref[...]).astype(BF16)
        normed_ref[...] = normed
        pre = matmul(normed, weight_ref[...])
        q_ref[at, :] = pre[:, :columns]
        k_ref[at, :] = pre[:, columns : 2 * columns]
        v_ref[at, :] = pre[:, 2 * columns :].astype(BF16)
        for j in range(2):
            squares = 0.0
            for c in range(j * columns, (j + 1) * columns, DH):
                squares += pre[:, c : c + DH] * pre[:, c : c + DH]
            square_ref[j : j + 1, at] = jnp.sum(squares.T, axis=0, keepdims=True)


def project(even, odd, weight, gain, me, rows):
    pairs = even.shape[0] // rows
    length = 2 * even.shape[0]
    depth, columns = weight.shape[0], weight.shape[1] // 3
    token = pl.BlockSpec((rows, depth), lambda i, me: (i, 0))

    def placed(shape):
        return pl.BlockSpec(shape, lambda i, me: (i ^ (me[0] // 2), 0))

    head = jax.ShapeDtypeStruct((length, columns), F32)
    return pl.pallas_call(
        qkv_kernel,
        grid_spec=pltpu.PrefetchScalarGridSpec(
            num_scalar_prefetch=1,
            grid=(pairs,),
            in_specs=[
                token,
                token,
                pl.BlockSpec(weight.shape, lambda i, me: (0, 0)),
                pl.BlockSpec((1, depth), lambda i, me: (0, 0)),
            ],
            out_specs=[
                token,
                token,
                placed((2 * rows, columns)),
                placed((2 * rows, columns)),
                placed((2 * rows, columns)),
                pl.BlockSpec((2, 2 * rows), lambda i, me: (0, i ^ (me[0] // 2))),
            ],
        ),
        out_shape=[
            jax.ShapeDtypeStruct((length // 2, depth), BF16),
            jax.ShapeDtypeStruct((length // 2, depth), BF16),
            head,
            head,
            jax.ShapeDtypeStruct((length, columns), BF16),
            jax.ShapeDtypeStruct((2, length), F32),
        ],
        compiler_params=pltpu.CompilerParams(vmem_limit_bytes=48 * MIB),
        cost_estimate=pl.CostEstimate(
            flops=6 * length * depth * columns,
            bytes_accessed=length * (4 * depth + 10 * columns) + 6 * depth * columns,
            transcendentals=length,
        ),
        name="project",
    )(me, even, odd, weight, gain)


def split_kernel(q_ref, k_ref, v_ref, out_ref):
    columns = q_ref.shape[1]
    for j, ref in enumerate((q_ref, k_ref, v_ref)):
        out_ref[0, :, j * columns : (j + 1) * columns] = ref[...]


def split_heads(w_query, w_key, w_value, parts):
    rows, columns = w_query.shape[0], w_query.shape[1] // parts
    block = pl.BlockSpec((rows, columns), lambda i: (0, i))
    return pl.pallas_call(
        split_kernel,
        grid=(parts,),
        in_specs=[block] * 3,
        out_specs=pl.BlockSpec((1, rows, 3 * columns), lambda i: (i, 0, 0)),
        out_shape=jax.ShapeDtypeStruct((parts, rows, 3 * columns), BF16),
        name="split_heads",
    )(w_query, w_key, w_value)


def spread(row, columns):
    return jnp.broadcast_to(row, (columns, row.shape[1])).T


def factor_of(square_row):
    return lax.rsqrt(square_row / D + EPSILON)


def turn(values, cosine, sine):
    return values * cosine + pltpu.roll(values, DH // 2, 1) * sine


def rope_kernel(q_ref, k_ref, square_ref, gain_ref, cos_ref, sin_ref, q_out, k_out):
    cosine, sine = cos_ref[...], sin_ref[...]
    for j, (pre_ref, out_ref) in enumerate(((q_ref, q_out), (k_ref, k_out))):
        factor = spread(factor_of(square_ref[j : j + 1, :]), DH)
        for c in range(0, pre_ref.shape[1], DH):
            at = slice(c, c + DH)
            normed = pre_ref[:, at] * factor * gain_ref[j : j + 1, at]
            out_ref[:, at] = turn(normed, cosine, sine).astype(BF16)


def rope(query_pre, key_pre, squares, gains, cosine, sine):
    length, columns = query_pre.shape
    rows = min(512, length)
    block = pl.BlockSpec((rows, columns), lambda i: (i, 0))
    table = pl.BlockSpec((rows, DH), lambda i: (i, 0))
    return pl.pallas_call(
        rope_kernel,
        grid=(length // rows,),
        in_specs=[
            block,
            block,
            pl.BlockSpec((2, rows), lambda i: (0, i)),
            pl.BlockSpec((2, columns), lambda i: (0, 0)),
            table,
            table,
        ],
        out_specs=[block, block],
        out_shape=[jax.ShapeDtypeStruct((length, columns), BF16)] * 2,
        compiler_params=pltpu.CompilerParams(vmem_limit_bytes=32 * MIB),
        name="rope",
    )(query_pre, key_pre, squares, gains, cosine, sine)


def pulled_of(grad_ref, pre_ref, factor, gain_ref, cosine, sine, j, at):
    turned = turn(grad_ref[:, at].astype(F32), cosine, -sine)
    return turned, turned * gain_ref[j : j + 1, at], pre_ref[:, at] * factor


def rope_mean_kernel(
    dq_ref, dk_ref, q_ref, k_ref, square_ref, gain_ref, cos_ref, sin_ref, mean_ref, term_ref
):
    @pl.when(pl.program_id(0) == 0)
    def _():
        term_ref[...] = jnp.zeros_like(term_ref)

    cosine, sine = cos_ref[...], sin_ref[...]
    for j, (grad_ref, pre_ref) in enumerate(((dq_ref, q_ref), (dk_ref, k_ref))):
        factor = spread(factor_of(square_ref[j : j + 1, :]), DH)
        total = 0.0
        for c in range(0, pre_ref.shape[1], DH):
            at = slice(c, c + DH)
            turned, pulled, normed = pulled_of(
                grad_ref, pre_ref, factor, gain_ref, cosine, sine, j, at
            )
            term_ref[j : j + 1, at] += jnp.sum(turned * normed, axis=0, keepdims=True)
            total += pulled * normed
        mean_ref[j : j + 1, :] = jnp.sum(total.T, axis=0, keepdims=True)


def rope_means(query_back, key_back, query_pre, key_pre, squares, gains, cosine, sine):
    length, columns = query_pre.shape
    rows = min(512, length)
    block = pl.BlockSpec((rows, columns), lambda i: (i, 0))
    table = pl.BlockSpec((rows, DH), lambda i: (i, 0))
    row = pl.BlockSpec((2, rows), lambda i: (0, i))
    fixed = pl.BlockSpec((2, columns), lambda i: (0, 0))
    return pl.pallas_call(
        rope_mean_kernel,
        grid=(length // rows,),
        in_specs=[block, block, block, block, row, fixed, table, table],
        out_specs=[row, fixed],
        out_shape=[
            jax.ShapeDtypeStruct((2, length), F32),
            jax.ShapeDtypeStruct((2, columns), F32),
        ],
        compiler_params=pltpu.CompilerParams(vmem_limit_bytes=32 * MIB),
        name="rope_means",
    )(query_back, key_back, query_pre, key_pre, squares, gains, cosine, sine)


def rope_back_kernel(
    me_ref,
    dq_ref,
    dk_ref,
    dv_ref,
    q_ref,
    k_ref,
    square_ref,
    mean_ref,
    gain_ref,
    cos_ref,
    sin_ref,
    out_ref,
):
    cosine, sine = cos_ref[...], sin_ref[...]
    columns = q_ref.shape[1]
    for j, (grad_ref, pre_ref) in enumerate(((dq_ref, q_ref), (dk_ref, k_ref))):
        factor = spread(factor_of(square_ref[j : j + 1, :]), DH)
        mean = spread(mean_ref[j : j + 1, :] / D, DH)
        for c in range(0, columns, DH):
            at = slice(c, c + DH)
            _, pulled, normed = pulled_of(grad_ref, pre_ref, factor, gain_ref, cosine, sine, j, at)
            out_ref[:, j * columns + c : j * columns + c + DH] = (
                factor * (pulled - normed * mean)
            ).astype(BF16)
    out_ref[:, 2 * columns :] = dv_ref[...]


def rope_back(grads, query_pre, key_pre, squares, means, gains, cosine, sine, me, rows):
    length, columns = query_pre.shape
    half = length // rows // 2

    def source(p, me):
        return me[0] ^ (p % half * 2 + p // half)

    block = pl.BlockSpec((rows, columns), lambda p, me: (source(p, me), 0))
    table = pl.BlockSpec((rows, DH), lambda p, me: (source(p, me), 0))
    row = pl.BlockSpec((2, rows), lambda p, me: (0, source(p, me)))
    return pl.pallas_call(
        rope_back_kernel,
        grid_spec=pltpu.PrefetchScalarGridSpec(
            num_scalar_prefetch=1,
            grid=(2 * half,),
            in_specs=[block] * 5
            + [row, row, pl.BlockSpec((2, columns), lambda p, me: (0, 0)), table, table],
            out_specs=pl.BlockSpec((rows, 3 * columns), lambda p, me: (p, 0)),
        ),
        out_shape=jax.ShapeDtypeStruct((length, 3 * columns), BF16),
        compiler_params=pltpu.CompilerParams(vmem_limit_bytes=32 * MIB),
        name="rope_back",
    )(me, *grads, query_pre, key_pre, squares, means, gains, cosine, sine)


def expert_kernel(
    in_places, down_places, first_ref, xa_ref, xb_ref, ua_ref, ub_ref, ra_ref, rb_ref, router_ref, *refs
):
    weight_refs = refs[: len(in_places) + len(down_places)]
    (ya_ref, yb_ref, za_ref, zb_ref, ga_ref, gb_ref, xc_ref, uc_ref, dg_ref, hid_ref) = refs[-13:-3]
    wi_ref, wd_ref, sems = refs[-3:]
    experts, _, hidden = hid_ref.shape
    rows = xa_ref.shape[0]

    @pl.when(pl.program_id(0) == 0)
    def _():
        copies = []
        for n, (ref, (r, first, part)) in enumerate(zip(weight_refs, in_places + down_places)):
            goal = wi_ref if n < len(in_places) else wd_ref
            place = lax.rem(first_ref[1] ^ r, goal.shape[1] // part)
            at = pl.ds(pl.multiple_of(place * part + first, ref.shape[1]), ref.shape[1])
            copies.append(pltpu.make_async_copy(ref, goal.at[:, at, :], sems.at[n]))
        for copy in copies:
            copy.start()
        for copy in copies:
            copy.wait()

    slot = lax.broadcasted_iota(jnp.int32, (CAP, rows), 0)
    blocks = (
        (xa_ref, ua_ref, ra_ref, ya_ref, za_ref, ga_ref),
        (xb_ref, ub_ref, rb_ref, yb_ref, zb_ref, gb_ref),
    )
    picks = []
    for k, (x_ref, u_ref, rank_ref, _, _, _) in enumerate(blocks):
        hits = jnp.concatenate([slot == rank_ref[0, e : e + 1, :] for e in range(experts)], 0)
        pick = hits.astype(F32).astype(BF16)
        picks.append(pick)
        x_rows = matmul(pick, x_ref[...]).astype(BF16)
        u_rows = matmul(pick, u_ref[...]).astype(BF16)
        for e in range(experts):
            xc_ref[e, k * CAP : (k + 1) * CAP, :] = x_rows[e * CAP : (e + 1) * CAP]
            uc_ref[e, k * CAP : (k + 1) * CAP, :] = u_rows[e * CAP : (e + 1) * CAP]
    outs, backs, gate_grads = [], [], []
    for e in range(experts):
        x_rows, u_rows = xc_ref[e], uc_ref[e]
        logits = matmul(x_rows, router_ref[...])
        lane = lax.broadcasted_iota(jnp.int32, logits.shape, 1)
        logits = jnp.where(lane < E, logits, -1e30)
        expos = jnp.exp(logits - jnp.max(logits, axis=-1, keepdims=True))
        own = jnp.sum(jnp.where(lane == first_ref[0] + e, expos, 0.0), axis=-1, keepdims=True)
        gate = own / jnp.sum(expos, axis=-1, keepdims=True)
        gated = matmul(x_rows, wi_ref[e, :, :hidden])
        upward = matmul(x_rows, wi_ref[e, :, hidden:])
        pulled = matmul_t(u_rows, wd_ref[e])
        sig = jax.nn.sigmoid(gated)
        silu = gated * sig
        acts = silu * upward
        gate_grads.append(jnp.sum(acts * pulled, axis=-1, keepdims=True))
        hidden_gate = (acts * gate).astype(BF16)
        hidden_grads = pulled * gate
        hid_ref[e] = hidden_gate
        dg_ref[e, :, :hidden] = (hidden_grads * upward * sig * (1.0 + gated * (1.0 - sig))).astype(BF16)
        dg_ref[e, :, hidden:] = (hidden_grads * silu).astype(BF16)
        outs.append(matmul(hidden_gate, wd_ref[e]).astype(BF16))
        backs.append(matmul_t(dg_ref[e], wi_ref[e]).astype(BF16))
    for k, (_, _, rank_ref, y_ref, z_ref, g_ref) in enumerate(blocks):
        at = slice(k * CAP, (k + 1) * CAP)
        y_ref[...] = t_matmul(picks[k], jnp.concatenate([v[at] for v in outs], 0)).astype(BF16)
        z_ref[...] = t_matmul(picks[k], jnp.concatenate([v[at] for v in backs], 0)).astype(BF16)
        for e in range(experts):
            hit = slot == rank_ref[0, e : e + 1, :]
            g_ref[0, e : e + 1, :] = jnp.sum(
                jnp.where(hit, gate_grads[e][at], 0.0), axis=0, keepdims=True
            )


def run_experts(x, u, ranks, in_pieces, down_pieces, router, places, which, compact, parts):
    experts, _, hidden = in_pieces[0][2].shape
    hidden = hidden // 2
    depth = x[0].shape[1]
    in_places = [(r, at, parts[0]) for r, at, _ in in_pieces]
    down_places = [(r, at, parts[1]) for r, at, _ in down_pieces]
    pieces = [array for _, _, array in in_pieces + down_pieces]
    rows = ranks[0].shape[2]
    steps = x[0].shape[0] // rows
    token = pl.BlockSpec((rows, depth), lambda i: (i, 0))
    rank = pl.BlockSpec((1, experts, rows), lambda i: (i, 0, 0))
    anywhere = pl.BlockSpec(memory_space=pl.ANY)

    def slots(columns):
        return pl.BlockSpec((experts, 2 * CAP, columns), lambda i: (0, i + which * steps, 0))

    shape = jax.ShapeDtypeStruct
    tokens = shape(x[0].shape, BF16)
    gates = shape((steps, experts, rows), F32)
    count = 4 * steps * CAP
    wide = shape((experts, count, depth), BF16)
    inputs = [places, *x, *u, *ranks, router, *pieces]
    return pl.pallas_call(
        partial(expert_kernel, in_places, down_places),
        grid=(steps,),
        in_specs=[pl.BlockSpec(memory_space=pltpu.SMEM)]
        + [token] * 4
        + [rank] * 2
        + [pl.BlockSpec(router.shape, lambda i: (0, 0), pipeline_mode=pl.Buffered(1))]
        + [anywhere] * (len(pieces) + len(compact)),
        out_specs=[token] * 4 + [rank] * 2 + [slots(depth)] * 2 + [slots(2 * hidden), slots(hidden)],
        out_shape=[tokens] * 4
        + [gates] * 2
        + [wide] * 2
        + [shape((experts, count, 2 * hidden), BF16), shape((experts, count, hidden), BF16)],
        scratch_shapes=[
            pltpu.VMEM((experts, depth, 2 * hidden), BF16),
            pltpu.VMEM((experts, hidden, depth), BF16),
            pltpu.SemaphoreType.DMA((len(pieces),)),
        ],
        input_output_aliases={len(inputs) + i: 6 + i for i in range(len(compact))},
        compiler_params=pltpu.CompilerParams(vmem_limit_bytes=60 * MIB),
        cost_estimate=pl.CostEstimate(
            flops=4 * steps * CAP * experts * depth * (7 * hidden + 2 * rows),
            bytes_accessed=60 * MIB,
            transcendentals=2 * steps * CAP * experts * hidden,
        ),
        name="experts",
    )(*inputs, *compact)


def product_kernel(me_ref, left_ref, right_ref, out_ref):
    out_ref[0] = t_matmul(left_ref[0], right_ref[0]).astype(BF16)


def products(left, right, part, r, count, me, name):
    experts, rows, _ = left.shape
    columns = right.shape[2]
    wide = min(columns, 1024)
    return pl.pallas_call(
        product_kernel,
        grid_spec=pltpu.PrefetchScalarGridSpec(
            num_scalar_prefetch=1,
            grid=(experts, columns // wide),
            in_specs=[
                pl.BlockSpec((1, rows, part), lambda e, j, me: (e, 0, lax.rem(me[0] ^ r, count))),
                pl.BlockSpec((1, rows, wide), lambda e, j, me: (e, 0, j)),
            ],
            out_specs=pl.BlockSpec((1, part, wide), lambda e, j, me: (e, 0, j)),
        ),
        out_shape=jax.ShapeDtypeStruct((experts, part, columns), BF16),
        compiler_params=pltpu.CompilerParams(vmem_limit_bytes=56 * MIB),
        cost_estimate=pl.CostEstimate(
            flops=2 * experts * rows * part * columns,
            bytes_accessed=2 * experts * rows * (part + columns),
            transcendentals=0,
        ),
        name=name,
    )(me, left, right)


def per_device(
    S,
    F,
    tokens,
    segments,
    routes,
    cotangent,
    w_query,
    w_key,
    w_value,
    w_output,
    router,
    attn_gain,
    moe_gain,
    query_gain,
    key_gain,
    w_gate,
    w_up,
    w_down,
):
    s = lax.axis_index("seq")
    f = lax.axis_index("fsdp")
    T = tokens.shape[1]
    L = S * T
    heads = H // S
    C = heads * DH
    experts = E // S
    part = w_query.shape[0]
    half_f = F // 2
    hidden_half = w_gate.shape[2] // 2

    me = s.reshape(1).astype(jnp.int32)
    f_at = f.reshape(1).astype(jnp.int32)
    half_at = f // half_f
    tokens_low = tokens[0]
    upstream_low = cotangent[0]
    inputs = tokens_low.astype(F32)
    half_rows = T // 2
    in_part, down_part = w_gate.shape[1], w_down.shape[1]
    quarter = in_part // 4

    def hidden_part(which, first, count):
        return jnp.concatenate(
            [
                lax.dynamic_slice(
                    weight, (0, first, which * hidden_half), (experts, count, hidden_half)
                )
                for weight in (w_gate, w_up)
            ],
            2,
        )

    def far_swap(values, *dep):
        return swap(after(values, dep), "fsdp", F, half_f)

    def near_swap(values, *dep):
        return near_pieces(after(values, dep), F)

    named = routes[0].T[None] == jnp.arange(E, dtype=jnp.int32)[:, None, None]
    chosen = jnp.any(named, axis=1)
    index = jnp.arange(T, dtype=jnp.int32)
    before = (index[:, None] <= index[None, :]).astype(BF16)
    ranks = jnp.where(chosen, matmul(chosen.astype(BF16), before) - 1.0, -1.0)
    small = jnp.concatenate(
        [
            router.reshape(-1),
            attn_gain,
            moe_gain,
            query_gain,
            key_gain,
            ranks.astype(BF16).reshape(-1),
        ]
    )[None]
    crossed = split_heads(w_query, w_key, w_value, S)
    small = double(after(small, crossed), "fsdp", F)
    crossed = lax.all_to_all(crossed, "seq", split_axis=0, concat_axis=0, tiled=True)
    near_own = {0: near_swap(hidden_part(half_at, 0, quarter), small)}
    out_pieces = fsdp_pieces(after(w_output, small), F)
    small = double(small, "seq", S)
    crossed, near_own[0], out_pieces, small = tie(crossed, near_own[0], out_pieces, small)

    own_parts = {n: hidden_part(half_at, n * quarter, quarter) for n in range(1, 4)}
    other_parts = [hidden_part(1 - half_at, n * quarter, quarter) for n in range(4)]
    down_rows = quarters(w_down, 1)
    down_rows = [down_rows[0], jnp.concatenate(down_rows[1:3], 1), down_rows[3]]
    upstream_halves = [upstream_low[:half_rows], upstream_low[half_rows:]]
    own_output = place_fsdp(out_pieces, f, 0).reshape(C, D)
    places = jnp.arange(L, dtype=jnp.int32).astype(F32)
    freqs = ROPE_BASE ** (-(jnp.arange(DH // 2, dtype=F32) * 2.0 / DH))
    angles = places[:, None] * freqs[None, :]
    cosine, sine = jnp.cos(angles), jnp.sin(angles)
    cosine = jnp.concatenate([cosine, cosine], 1)
    sine = jnp.concatenate([-sine, sine], 1)
    seg_row, seg_col = segments, segments.reshape(L, 1)
    prepared = (
        own_parts, other_parts, down_rows, upstream_halves, own_output, cosine, sine, seg_col
    )
    token_first = gather_first(after(tokens_low, crossed), S)
    qkv_pieces = {0: crossed}
    for r in range(1, F):
        low = low_bit(r)
        qkv_pieces[r] = swap(qkv_pieces[r ^ low], "fsdp", F, low)
        if r == half_f:
            qkv_pieces, token_first, prepared = tie(qkv_pieces, token_first, prepared)
    own_parts, other_parts, down_rows, upstream_halves, own_output, cosine, sine, seg_col = prepared
    partner_up = [far_swap(upstream_halves[0])]
    token_more = gather_more(tokens_low, token_first, S)
    out_first = gather_first(own_output, S)
    small = in_order(small, S, F, s, f).reshape(S, F, -1)
    qkv_pieces, partner_up[0], token_more, out_first, small = tie(
        qkv_pieces, partner_up[0], token_more, out_first, small
    )
    tokens_even, tokens_odd = gather_end(tokens_low, token_first, token_more, S)
    w_qkv = place_fsdp(qkv_pieces, f, 1).reshape(D, 3 * C)

    full_router = small[:, :, : part * E].reshape(D, E)
    gains = [
        small[:, :, part * (E + i) : part * (E + i + 1)].reshape(D).astype(F32) for i in range(4)
    ]
    gain_attn, gain_moe = gains[0], gains[1]
    head_gain = lax.dynamic_slice(jnp.stack(gains[2:], 0), (0, s * C), (2, C))
    rank_part = small[:, :, part * (E + 4) :].reshape(S, F, E, T)

    def ranks_of(index):
        ranks = lax.dynamic_slice(rank_part, (0, index, s * experts, 0), (S, 1, experts, T))
        ranks = relative(ranks[:, 0], s).astype(jnp.int32)
        return ranks[: S // 2], ranks[S // 2 :]

    def far_part(n, *dep):
        return far_swap(other_parts[n], *dep)

    partner_up.append(far_swap(upstream_halves[1], w_qkv))
    near_own[2] = near_swap(own_parts[2], w_qkv)
    out_more = gather_more(after(own_output, w_qkv), out_first, S)
    normed_even, normed_odd, query_pre, key_pre, value_low, squares = project(
        tokens_even, tokens_odd, w_qkv, gain_attn[None], me, T
    )
    squares, partner_up[1], near_own[2], out_more = tie(
        squares, partner_up[1], near_own[2], out_more
    )

    out_even, out_odd = gather_end(own_output, out_first, out_more, S)
    own_up_first = gather_first(after(upstream_low, squares), S)
    far = [far_part(0, squares)]
    near_own[3] = near_swap(own_parts[3], squares)
    squares = sum_all(squares, "seq", S)
    query_low, key_low = rope(query_pre, key_pre, squares, head_gain, cosine, sine)
    query_low, own_up_first, far[0], near_own[3], out_even, out_odd = tie(
        query_low, own_up_first, far[0], near_own[3], out_even, out_odd
    )

    own_up_more = gather_more(after(upstream_low, query_low), own_up_first, S)
    far.append(far_part(1, query_low))
    down = [near_swap(down_rows[0], query_low)]
    attended, lse = attention_forward(query_low, key_low, value_low, seg_row, seg_col)
    attended, own_up_more, far[1], down[0] = tie(attended, own_up_more, far[1], down[0])
    attended_blocks = attended.reshape(S, T, C)
    come = lax.all_to_all(attended_blocks, "seq", split_axis=0, concat_axis=0, tiled=True)
    partner_up = after(jnp.concatenate(partner_up, 0), attended)
    near_own[1] = near_swap(own_parts[1], attended)
    far.append(far_part(2, attended))
    near_far = [near_swap(far[0], attended)]
    come, far[2], near_far[0], near_own[1], partner_up = tie(
        come, far[2], near_far[0], near_own[1], partner_up
    )
    own_u = gather_end(upstream_low, own_up_first, own_up_more, S)
    far.append(far_part(3, come))
    near_far.append(near_swap(far[1], come))
    partner_up_first = gather_first(after(partner_up, come), S)
    come = relative(come, s).transpose(1, 0, 2).reshape(T, D)
    residual = inputs + matmul(come[:, : D // 2], out_even) + matmul(come[:, D // 2 :], out_odd)
    moe_factor = rms_factor(residual)
    residual_n = residual * moe_factor
    second_low = (residual_n * gain_moe).astype(BF16)
    second_low, far[3], near_far[1], partner_up_first, own_u = tie(
        second_low, far[3], near_far[1], partner_up_first, own_u
    )

    own_first = gather_first(second_low, S)
    partner_low = [far_swap(second_low[:half_rows])]
    near_far.append(near_swap(far[2], second_low))
    own_ranks, other_ranks = ranks_of(f), ranks_of(f ^ half_f)
    own_first, partner_low[0], near_far[2], own_ranks, other_ranks = tie(
        own_first, partner_low[0], near_far[2], own_ranks, other_ranks
    )
    own_more = gather_more(second_low, own_first, S)
    partner_low.append(far_swap(second_low[half_rows:], own_first))
    near_far.append(near_swap(far[3], own_first))
    partner_up_more = gather_more(after(partner_up, own_first), partner_up_first, S)
    own_more, partner_low[1], near_far[3], partner_up_more = tie(
        own_more, partner_low[1], near_far[3], partner_up_more
    )
    partner_low = jnp.concatenate(partner_low, 0)
    own_x = gather_end(second_low, own_first, own_more, S)
    partner_first = gather_first(after(partner_low, own_more), S)
    down.append(near_swap(down_rows[1], own_more))
    partner_first, down[1], own_x = tie(partner_first, down[1], own_x)
    other_u = gather_end(after(partner_up, partner_first), partner_up_first, partner_up_more, S)
    partner_more = gather_more(partner_low, partner_first, S)
    down.append(near_swap(down_rows[2], partner_first))
    partner_more, down[2], other_u = tie(partner_more, down[2], other_u)
    other_x = gather_end(partner_low, partner_first, partner_more, S)
    in_pieces = []
    for r in range(F):
        for n in range(4):
            rows = near_own[n] if r < half_f else near_far[n]
            in_pieces.append((r, n * quarter, rows[r % half_f]))
    down_pieces = [
        (r, (0, 1, 3)[n] * (down_part // 4), down[n][r]) for r in range(half_f) for n in range(3)
    ]
    wide_router = jnp.pad(full_router, ((0, 0), (0, 128 - E)))
    expert_places = jnp.stack([s * experts, f]).astype(jnp.int32)
    parts = (in_part, down_part)
    own_parts = run_experts(
        own_x, own_u, own_ranks, in_pieces, down_pieces, wide_router, expert_places, 0, (), parts
    )
    own_parts, other_x = tie(own_parts, other_x)
    own_got = swap(own_parts[3], "seq", S, 1)
    own_out_got = swap(own_parts[1], "seq", S, 1)
    other_parts = run_experts(
        other_x,
        other_u,
        other_ranks,
        in_pieces,
        down_pieces,
        wide_router,
        expert_places,
        1,
        own_parts[6:],
        parts,
    )
    other_parts, own_got, own_out_got = tie(other_parts, own_got, own_out_got)
    logits = matmul(second_low, full_router)
    router_probs = jax.nn.softmax(logits, axis=-1)

    x_rows, u_rows, in_grads, hidden_gate = other_parts[6:]
    in_terms, down_terms = {}, {}

    def in_products(r, *dep):
        in_terms[r] = products(
            x_rows, after(in_grads, dep), in_part, r, F, f_at, "in_products"
        )

    odd = [r for r in range(F) if r & 1]
    far_odd = [r for r in odd if r & half_f]
    near_odd = [r for r in odd if not r & half_f]

    def to_home(even, odd):
        return absolute(jnp.concatenate([even, odd], 0).transpose(0, 2, 1), s)

    gate_grads = jnp.stack(
        [to_home(own_parts[4], own_parts[5]), to_home(other_parts[4], other_parts[5])], 1
    ).reshape(S, -1)
    other_got = swap(other_parts[3], "seq", S, 1)
    for r in far_odd:
        in_products(r)
    gate_grads = lax.all_to_all(gate_grads, "seq", split_axis=0, concat_axis=0, tiled=True)
    other_got, in_terms, gate_grads = tie(other_got, in_terms, gate_grads)
    sent = {r: quarters(in_terms[r], 1) for r in far_odd}

    def send_in(n, *dep):
        return {r: swap(after(sent[r][n], dep), "fsdp", F, 1) for r in sent}

    other_sums = sum_cores(other_parts[2], other_got, S)
    come = sum_first(other_sums, S)
    far_got = [send_in(0, other_got)]
    other_out_got = swap(after(other_parts[1], other_got), "seq", S, 1)
    come, far_got[0], other_out_got = tie(come, far_got[0], other_out_got)
    gate_grads = gate_grads.reshape(S, 2, T * experts)
    partner_grads = far_swap(gate_grads[:, 1], come)
    singles, other_total = sum_more(other_sums, come, S)
    come = sum_last(singles, S)
    middle_sent = {r: jnp.concatenate(sent[r][1:3], 1) for r in sent}
    middle_got = {
        r: swap(after(middle_sent[r], far_got[0]), "fsdp", F, 1) for r in middle_sent
    }

    def down_products(r, dep):
        down_terms[r] = products(
            after(hidden_gate, dep), u_rows, down_part, r, half_f, f_at, "down_products"
        )

    for r in range(1, half_f, 2):
        down_products(r, singles)
    come, middle_got, partner_grads, down_terms = tie(
        come, middle_got, partner_grads, down_terms
    )
    for n in range(2):
        far_got.append({r: got[:, n * quarter : (n + 1) * quarter] for r, got in middle_got.items()})
    other_rows = add_all(other_total, come).astype(BF16)
    gate_grads = gate_grads[:, 0] + partner_grads
    gate_grads = gate_grads.reshape(S, T, experts).transpose(1, 0, 2).reshape(T, E)
    back = [far_swap(other_rows[:half_rows])]
    own_sums = sum_cores(own_parts[2], after(own_got, other_rows), S)
    come = sum_first(own_sums, S)
    far_got.append(send_in(3, other_rows))
    for r in far_odd:
        in_products(r ^ 1, other_rows)
    come, back[0], far_got[3], in_terms = tie(come, back[0], far_got[3], in_terms)
    back.append(far_swap(other_rows[half_rows:], come))
    singles, own_total = sum_more(own_sums, come, S)
    come = sum_last(singles, S)
    down_sent = {r: quarters(down_terms[r], 1) for r in range(1, half_f, 2)}

    def send_down(n, *dep):
        return {r: swap(after(down_sent[r][n], dep), "fsdp", F, 1) for r in down_sent}

    down_got = [send_down(0, singles)]
    for r in near_odd:
        in_products(r, singles)
    come, back[1], down_got[0], in_terms = tie(come, back[1], down_got[0], in_terms)
    row_grads = add_all(own_total, come) + jnp.concatenate(back, 0).astype(F32)

    upstream = upstream_low.astype(F32)
    logit_grads = router_probs * (
        gate_grads - jnp.sum(router_probs * gate_grads, axis=-1, keepdims=True)
    )
    router_wide = full_router.astype(F32)
    second_grads = row_grads + jnp.dot(logit_grads, router_wide.T, precision=HIGHEST)
    pulled = second_grads * gain_moe
    residual_grads = upstream + moe_factor * (
        pulled - residual_n * jnp.mean(pulled * residual_n, axis=-1, keepdims=True)
    )
    branch_low = residual_grads.astype(BF16)

    def sum_near(terms):
        mask = 2
        while mask < half_f:
            terms = {
                r: terms[r] + swap(terms[r | mask].astype(BF16), "fsdp", F, mask).astype(F32)
                for r in terms
                if not r & mask
            }
            mask *= 2
        (total,) = terms.values()
        return total

    def far_sum(n, *dep):
        terms = {
            r ^ 1: quarters(in_terms[r ^ 1], 1)[n].astype(F32) + far_got[n][r].astype(F32)
            for r in far_odd
        }
        return far_swap(sum_near(terms).astype(BF16), *dep)

    branch_first = gather_first(branch_low, S)
    far_sums = [far_sum(0, branch_low)]
    down_got.append(send_down(1, branch_low))
    for r in range(0, half_f, 2):
        down_products(r, branch_low)
    branch_first, far_sums[0], down_got[1], down_terms = tie(
        branch_first, far_sums[0], down_got[1], down_terms
    )
    branch_more = gather_more(branch_low, branch_first, S)
    far_sums.append(far_sum(1, branch_first))
    down_got.append(send_down(2, branch_first))
    branch_even, branch_odd = gather_end(branch_low, branch_first, branch_more, S)

    head_grads = jnp.concatenate(
        [matmul_t(branch_even, own_output), matmul_t(branch_odd, own_output)], 0
    ).astype(BF16)
    head_grads = absolute(head_grads.reshape(S, T, C), s).reshape(L, C)
    head_grads, far_sums[1], down_got[2] = tie(head_grads, far_sums[1], down_got[2])
    far_sums.append(far_sum(2, head_grads))
    down_got.append(send_down(3, head_grads))
    other_out_sums = sum_cores(other_parts[0], after(other_out_got, head_grads), S)
    come = sum_first(other_out_sums, S)
    query_back, key_back, value_back = attention_backward(
        query_low, key_low, value_low, head_grads, lse, seg_row, seg_col
    )
    query_back, far_sums[2], down_got[3], come = tie(query_back, far_sums[2], down_got[3], come)

    singles, other_total = sum_more(other_out_sums, come, S)
    come = sum_last(singles, S)
    far_sums.append(far_sum(3, query_back))
    attended_rel = relative(after(attended_blocks, singles), s).reshape(2, L // 2, C)
    output_term = t_matmul(attended_rel[0], branch_even) + t_matmul(attended_rel[1], branch_odd)
    output_term = by_index(output_term.astype(BF16).reshape(F, part, D), f, F)
    output_got = swap(output_term[: F // 2], "fsdp", F, 1)
    value_rel = relative(value_back.reshape(S, T, C), s).reshape(2, L // 2, C)

    def weight_term(even, odd):
        term = (t_matmul(normed_even, even) + t_matmul(normed_odd, odd)).astype(BF16)
        return by_index(term.reshape(S, F, part, -1).transpose(1, 0, 2, 3), f, F)

    means, gain_term = rope_means(
        query_back, key_back, query_pre, key_pre, squares, head_gain, cosine, sine
    )
    means = sum_all(means, "seq", S)
    value_term = weight_term(value_rel[0], value_rel[1])
    means, come, far_sums[3], output_got, value_term = tie(
        means, come, far_sums[3], output_got, value_term
    )
    other_outs = add_all(other_total, come).astype(BF16)
    outs_back = [far_swap(other_outs[:half_rows])]
    value_got = swap(value_term[: F // 2], "fsdp", F, 1)
    pre_rel = rope_back(
        (query_back, key_back, value_back),
        query_pre,
        key_pre,
        squares,
        means,
        head_gain,
        cosine,
        sine,
        me,
        T,
    ).reshape(2, L // 2, 3 * C)
    normed_got = swap(matmul_t(pre_rel[1], w_qkv).astype(BF16), "seq", S, 1)
    normed_kept = matmul_t(pre_rel[0], w_qkv).astype(BF16)
    normed_got, normed_kept, value_got, outs_back[0] = tie(
        normed_got, normed_kept, value_got, outs_back[0]
    )

    normed_sums = sum_cores(normed_kept, normed_got, S)
    come = sum_first(normed_sums, S)
    value_sum = sum_rest(sum_even(value_term, value_got, F), F)
    turned_term = weight_term(
        after(pre_rel[0][:, : 2 * C], normed_got), after(pre_rel[1][:, : 2 * C], normed_got)
    )
    late_grads, late_logits = after(second_grads, normed_got), after(logit_grads, normed_got)
    router_term = jnp.dot(second_low.astype(F32).T, late_logits, precision=HIGHEST)
    moe_gain_term = jnp.sum(late_grads * residual_n, axis=0)
    gain_terms = jnp.concatenate(
        [router_term.reshape(S * F, part * E), moe_gain_term.reshape(S * F, part)], 1
    )
    gain_terms = in_relative(gain_terms, S, F, s, f).reshape(S, F, -1)
    head_terms = gain_term.reshape(2, F, part).transpose(1, 0, 2).reshape(F, 2 * part)
    head_terms = in_relative(head_terms, 1, F, 0, f)
    gain_terms = jnp.concatenate([gain_terms.transpose(1, 0, 2).reshape(F, -1), head_terms], 1)
    come, turned_term, value_sum, gain_terms = tie(come, turned_term, value_sum, gain_terms)
    turned_got = swap(turned_term[: F // 2], "fsdp", F, 1)
    singles, normed_total = sum_more(normed_sums, come, S)
    come = sum_last(singles, S)
    gain_got = swap(gain_terms[F // 2 :], "fsdp", F, half_f)
    for r in near_odd:
        in_products(r ^ 1, turned_term)
    come, turned_got, gain_got, in_terms = tie(come, turned_got, gain_got, in_terms)
    gain_terms = gain_terms[: F // 2] + gain_got
    normed_grads = add_all(normed_total, come)
    turned_sum = sum_rest(sum_even(turned_term, turned_got, F), F)
    middle = in_part // 2

    def send_near(first, dep):
        return {
            r: swap(after(in_terms[r][:, first : first + middle], dep), "fsdp", F, 1)
            for r in near_odd
        }

    near_got = [send_near(0, turned_got)]
    own_out_sums = sum_cores(own_parts[0], after(own_out_got, turned_got), S)
    come = sum_first(own_out_sums, S)
    gain_terms = halve(after(gain_terms, turned_got), "fsdp", F, half_f // 2)
    turned_sum, come, near_got[0], gain_terms = tie(turned_sum, come, near_got[0], gain_terms)
    near_got.append(send_near(middle, turned_sum))
    outs_back.append(far_swap(other_outs[half_rows:], turned_sum))
    count = S * part * (E + 1)
    head_terms = gain_terms[0, count:]
    gain_terms = halve(gain_terms[0, :count].reshape(S, -1), "seq", S, S // 2)[0]
    singles, own_total = sum_more(own_out_sums, come, S)
    own_outs = add_all(own_total, sum_last(singles, S))
    outs_back = jnp.concatenate(outs_back, 0).astype(F32)
    mixed = (residual + own_outs + outs_back).astype(BF16)[None]

    qkv_term = jnp.concatenate([turned_sum, value_sum], -1).astype(BF16)
    qkv_term = lax.all_to_all(qkv_term, "seq", split_axis=0, concat_axis=0, tiled=True)
    qkv_term = [
        qkv_term[:, :, j * C : (j + 1) * C].transpose(1, 0, 2).reshape(part, D).astype(F32)
        for j in range(3)
    ]
    grad_output = sum_rest(sum_even(output_term, output_got, F), F)

    near_got = {r: jnp.concatenate([got[r] for got in near_got], 1) for r in near_odd}
    own_term = sum_near(
        {r ^ 1: in_terms[r ^ 1].astype(F32) + near_got[r].astype(F32) for r in near_odd}
    )
    far_term = jnp.concatenate(far_sums, 1).astype(F32)
    first_half = half_at == 0
    lower = jnp.where(first_half, own_term, far_term)
    upper = jnp.where(first_half, far_term, own_term)
    grad_gate, grad_up = (
        jnp.concatenate([lower[..., at], upper[..., at]], axis=-1)
        for at in (slice(0, hidden_half), slice(hidden_half, 2 * hidden_half))
    )
    down_got = after(down_got, turned_sum)
    down_got = {r: jnp.concatenate([got[r] for got in down_got], 1) for r in down_sent}
    grad_down = sum_near(
        {r ^ 1: down_terms[r ^ 1].astype(F32) + down_got[r].astype(F32) for r in down_sent}
    )

    attn_factor = rms_factor(inputs)
    inputs_n = inputs * attn_factor
    attn_pulled = normed_grads * gain_attn
    grad_tokens = residual_grads + attn_factor * (
        attn_pulled - inputs_n * jnp.mean(attn_pulled * inputs_n, axis=-1, keepdims=True)
    )
    grad_attn_gain = sum(
        jnp.sum(term * weight.astype(F32), axis=1)
        for term, weight in zip(qkv_term, (w_query, w_key, w_value))
    ) / attn_gain.astype(F32)
    return (
        mixed,
        grad_tokens[None],
        qkv_term[0],
        qkv_term[1],
        qkv_term[2],
        grad_output,
        gain_terms[: part * E].reshape(part, E),
        grad_attn_gain,
        gain_terms[part * E :],
        head_terms[:part],
        head_terms[part:],
        grad_gate,
        grad_up,
        grad_down,
    )


def solution(mesh):
    tokens_spec = P("fsdp", "seq", None)
    rows_spec = P(("seq", "fsdp"), None)
    gain_spec = P(("seq", "fsdp"))
    expert_spec = P("seq", "fsdp", None)
    in_specs = (
        (tokens_spec, P("fsdp", None), tokens_spec, tokens_spec)
        + (rows_spec,) * 5
        + (gain_spec,) * 4
        + (expert_spec,) * 3
    )
    out_specs = (tokens_spec,) * 2 + (rows_spec,) * 5 + (gain_spec,) * 4 + (expert_spec,) * 3
    return jax.shard_map(
        partial(per_device, mesh.shape["seq"], mesh.shape["fsdp"]),
        mesh=mesh,
        in_specs=in_specs,
        out_specs=out_specs,
        check_vma=False,
    )
```

```python
from functools import partial

import jax
import jax.numpy as jnp
from jax import lax
from jax.experimental import pallas as pl
from jax.experimental.pallas import tpu as pltpu
from jax.sharding import PartitionSpec as P

D = 2048
H = 16
DH = 128
E = 16
WINDOW = 1024
CAP = 144

EPSILON = 1e-06
ROPE_BASE = 50000.0
HIGHEST = lax.Precision.HIGHEST
BF16 = jnp.bfloat16
F32 = jnp.float32
MIB = 1024 * 1024


def matmul(left, right):
    return jnp.dot(left, right, preferred_element_type=F32)


def matmul_t(left, right):
    return lax.dot_general(left, right, (((1,), (1,)), ((), ())), preferred_element_type=F32)


def t_matmul(left, right):
    return lax.dot_general(left, right, (((0,), (0,)), ((), ())), preferred_element_type=F32)


def rms_factor(values):
    return lax.rsqrt(jnp.mean(values * values, axis=-1, keepdims=True) + EPSILON)


def swap(values, axis, size, mask):
    return lax.ppermute(values, axis, [(i, i ^ mask) for i in range(size)])


def high_bit(number):
    return 1 << (number.bit_length() - 1)


def low_bit(number):
    return number & -number


def after(values, *others):
    return lax.optimization_barrier((values, others))[0]


def tie(*values):
    return lax.optimization_barrier(values)


def gather_first(values, size):
    return {r: swap(values, "seq", size, r) for r in range(2, size, 2) if r == low_bit(r)}


def gather_more(values, first, size):
    rows = values.shape[0] // 2
    pieces = dict(first)
    for r in range(2, size, 2):
        if r not in pieces:
            up, down = high_bit(r), low_bit(r)
            upper, lower = pieces[r ^ up], pieces[r ^ down]
            upper = upper[0] if isinstance(upper, tuple) else upper[:rows]
            lower = lower[1] if isinstance(lower, tuple) else lower[rows:]
            pieces[r] = (swap(upper, "seq", size, up), swap(lower, "seq", size, down))
    return {r: piece for r, piece in pieces.items() if r not in first}


def gather_end(values, first, more, size):
    blocks = [values]
    for r in range(2, size, 2):
        blocks.extend([first[r]] if r in first else more[r])
    even = jnp.concatenate(blocks, 0)
    return even, swap(even, "seq", size, 1)


def relative(blocks, me):
    size = blocks.shape[0]
    order = list(range(0, size, 2)) + list(range(1, size, 2))
    return jnp.concatenate([lax.dynamic_slice_in_dim(blocks, me ^ r, 1, 0) for r in order], 0)


def absolute(blocks, me):
    size = blocks.shape[0]
    places = [((me ^ j) // 2) + ((me ^ j) % 2) * (size // 2) for j in range(size)]
    return jnp.concatenate([lax.dynamic_slice_in_dim(blocks, at, 1, 0) for at in places], 0)


def sum_cores(even, got, size):
    rows = even.shape[0] // (size // 2)
    half = rows // 2

    def part(r, first):
        at = slice(r // 2 * rows + first, r // 2 * rows + first + half)
        return even[at].astype(F32) + got[at].astype(F32)

    return {r: [part(r, 0), part(r, half)] for r in range(0, size, 2)}


def sum_first(sums, size, held=None):
    sums = {r: list(value) for r, value in sums.items()}
    come = {}
    for r in range(size - 2, 0, -2):
        if r != low_bit(r):
            up, down = high_bit(r), low_bit(r)
            for (goal, k, _), piece in come.items():
                if goal == r:
                    sums[r][k] += piece.astype(F32)
            upper, lower, held = tie(sums[r][0].astype(BF16), sums[r][1].astype(BF16), held)
            come[r ^ up, 0, r] = swap(upper, "seq", size, up)
            come[r ^ down, 1, r] = swap(lower, "seq", size, down)
    return come if held is None else (come, held)


def sum_more(sums, come, size):
    sums = {r: list(value) for r, value in sums.items() if r == 0 or r == low_bit(r)}
    for (goal, k, _), piece in come.items():
        if goal in sums:
            sums[goal][k] += piece.astype(F32)
    singles = {
        r: jnp.concatenate([v.astype(BF16) for v in value], 0) for r, value in sums.items() if r
    }
    return tie(singles)[0], jnp.concatenate(sums[0], 0)


def sum_last(singles, size):
    return {r: swap(value, "seq", size, r) for r, value in singles.items()}


def add_all(total, pieces):
    for piece in pieces.values():
        total += piece.astype(F32)
    return total


def quarters(values, axis):
    step = values.shape[axis] // 4
    return [lax.slice_in_dim(values, k * step, (k + 1) * step, axis=axis) for k in range(4)]


def sum_all(values, axis, size):
    mask = 1
    while mask < size:
        values = values + swap(values, axis, size, mask)
        mask *= 2
    return values


def fsdp_pieces(values, size):
    pieces = {0: values}
    for r in range(1, size):
        low = low_bit(r)
        pieces[r] = swap(pieces[r ^ low], "fsdp", size, low)
    return pieces


def place_fsdp(pieces, me, axis):
    size = len(pieces)
    shape = pieces[0].shape
    whole = jnp.zeros(shape[:axis] + (size,) + shape[axis:], pieces[0].dtype)
    for r, piece in pieces.items():
        whole = lax.dynamic_update_slice_in_dim(whole, jnp.expand_dims(piece, axis), me ^ r, axis)
    return whole


def near_pieces(values, size):
    pieces = {0: values}
    for r in range(1, size // 2):
        up = high_bit(r)
        pieces[r] = swap(pieces[r ^ up], "fsdp", size, up)
    return pieces


def double(values, axis, size):
    mask = 1
    while mask < size:
        values = jnp.concatenate([values, swap(values, axis, size, mask)], 0)
        mask *= 2
    return values


def halve(values, axis, size, mask):
    while mask:
        half = values.shape[0] // 2
        values = values[:half] + swap(values[half:], axis, size, mask)
        mask //= 2
    return values


def relative_pick(seq_size, fsdp_size, s, f):
    index = jnp.arange(seq_size * fsdp_size, dtype=jnp.int32)
    source = ((index // fsdp_size) ^ s) * fsdp_size + ((index % fsdp_size) ^ f)
    return source[:, None] == index[None, :]


def in_order(values, seq_size, fsdp_size, s, f):
    pick = relative_pick(seq_size, fsdp_size, s, f).astype(values.dtype)
    return matmul(pick, values).astype(values.dtype)


def in_relative(values, seq_size, fsdp_size, s, f):
    pick = relative_pick(seq_size, fsdp_size, s, f).astype(F32)
    return jnp.dot(pick, values, precision=HIGHEST)


def by_index(partial_sum, me, size):
    order = [r for r in range(size) if r & 1] + [r for r in range(size) if not r & 1]
    return jnp.concatenate([lax.dynamic_slice_in_dim(partial_sum, me ^ r, 1, 0) for r in order], 0)


def sum_even(stacked, got, size):
    return (stacked[size // 2 :].astype(F32) + got.astype(F32)).astype(BF16)


def sum_rest(stacked, size):
    mask = 2
    values = stacked.astype(F32)
    while mask < size:
        count = values.shape[0] // 2
        pairs = values.reshape((count, 2) + values.shape[1:])
        got = swap(pairs[:, 1].astype(BF16), "fsdp", size, mask)
        values = pairs[:, 0] + got.astype(F32)
        mask *= 2
    return values[0]


def allowed_keys(seg_row, seg_col, first_query, first_key, rows, span, half_window):
    query_at = first_query + lax.broadcasted_iota(jnp.int32, (span, rows), 1)
    key_at = first_key + lax.broadcasted_iota(jnp.int32, (span, rows), 0)
    return (jnp.abs(query_at - key_at) <= half_window) & (seg_col == seg_row)


def first_key_of(block, rows, span, length):
    start = jnp.clip(block * rows - (span - rows) // 2, 0, length - span)
    return pl.multiple_of(start, rows)


def forward_kernel(span, q_ref, k_ref, v_ref, seg_row_ref, seg_col_ref, o_ref, lse_ref):
    block = pl.program_id(1)
    rows, length = q_ref.shape[0], k_ref.shape[0]
    first_key = first_key_of(block, rows, span, length)
    keys = k_ref[pl.ds(first_key, span), :]
    values = v_ref[pl.ds(first_key, span), :]
    scores = matmul_t(keys, q_ref[...]) * DH ** (-0.5)
    allowed = allowed_keys(
        seg_row_ref[...],
        seg_col_ref[pl.ds(first_key, span), :],
        block * rows,
        first_key,
        rows,
        span,
        WINDOW // 2,
    )
    scores = jnp.where(allowed, scores, -1e30)
    peak = jnp.max(scores, axis=0, keepdims=True)
    expos = jnp.exp(scores - peak)
    totals = jnp.sum(expos, axis=0, keepdims=True)
    probs = (expos * (1.0 / totals)).astype(BF16)
    o_ref[...] = t_matmul(values, probs).T.astype(BF16)
    lse_ref[...] = (peak + jnp.log(totals))[None]


def backward_kernel(
    span,
    q_ref,
    k_ref,
    v_ref,
    do_ref,
    lse_ref,
    seg_row_ref,
    seg_col_ref,
    dq_ref,
    dk_ref,
    dv_ref,
    dk_sum,
    dv_sum,
):
    block = pl.program_id(1)
    rows, length = q_ref.shape[0], k_ref.shape[0]

    @pl.when(block == 0)
    def _():
        dk_sum[...] = jnp.zeros_like(dk_sum)
        dv_sum[...] = jnp.zeros_like(dv_sum)

    first_key = first_key_of(block, rows, span, length)
    at = pl.ds(first_key, span)
    keys = k_ref[at, :]
    values = v_ref[at, :]
    queries = q_ref[...]
    grads = do_ref[...]
    scores = matmul_t(keys, queries) * DH ** (-0.5)
    allowed = allowed_keys(
        seg_row_ref[...],
        seg_col_ref[at, :],
        block * rows,
        first_key,
        rows,
        span,
        WINDOW // 2,
    )
    probs = jnp.where(allowed, jnp.exp(scores - lse_ref[0]), 0.0)
    dv_sum[at, :] += matmul(probs.astype(BF16), grads)
    prob_grads = matmul_t(values, grads)
    center = jnp.sum(probs * prob_grads, axis=0, keepdims=True)
    score_grads = (probs * (prob_grads - center)).astype(BF16)
    dk_sum[at, :] += matmul(score_grads, queries)
    dq_ref[...] = (t_matmul(keys, score_grads) * DH ** (-0.5)).T.astype(BF16)

    @pl.when(block == length // rows - 1)
    def _():
        dk_ref[...] = (dk_sum[...] * DH ** (-0.5)).astype(BF16)
        dv_ref[...] = dv_sum[...].astype(BF16)


def attention_sizes(length):
    rows = 256
    return rows, min(length, rows + WINDOW)


def attention_forward(queries, keys, values, seg_row, seg_col):
    length, columns = queries.shape
    heads = columns // DH
    rows, span = attention_sizes(length)
    block = pl.BlockSpec((rows, DH), lambda h, i: (i, h))
    whole = pl.BlockSpec((length, DH), lambda h, i: (0, h))
    return pl.pallas_call(
        partial(forward_kernel, span),
        grid=(heads, length // rows),
        in_specs=[
            block,
            whole,
            whole,
            pl.BlockSpec((1, rows), lambda h, i: (0, i)),
            pl.BlockSpec((length, 1), lambda h, i: (0, 0)),
        ],
        out_specs=[block, pl.BlockSpec((1, 1, rows), lambda h, i: (h, 0, i))],
        out_shape=[
            jax.ShapeDtypeStruct((length, columns), BF16),
            jax.ShapeDtypeStruct((heads, 1, length), F32),
        ],
        compiler_params=pltpu.CompilerParams(vmem_limit_bytes=48 * MIB),
        cost_estimate=pl.CostEstimate(
            flops=4 * heads * length * span * DH,
            bytes_accessed=8 * length * columns,
            transcendentals=heads * length * span,
        ),
        name="attend",
    )(queries, keys, values, seg_row, seg_col)


def attention_backward(queries, keys, values, grads, lse, seg_row, seg_col):
    length, columns = queries.shape
    heads = columns // DH
    rows, span = attention_sizes(length)
    block = pl.BlockSpec((rows, DH), lambda h, i: (i, h))
    whole = pl.BlockSpec((length, DH), lambda h, i: (0, h))
    shape = jax.ShapeDtypeStruct((length, columns), BF16)
    return pl.pallas_call(
        partial(backward_kernel, span),
        grid=(heads, length // rows),
        in_specs=[
            block,
            whole,
            whole,
            block,
            pl.BlockSpec((1, 1, rows), lambda h, i: (h, 0, i)),
            pl.BlockSpec((1, rows), lambda h, i: (0, i)),
            pl.BlockSpec((length, 1), lambda h, i: (0, 0)),
        ],
        out_specs=[block, whole, whole],
        out_shape=[shape, shape, shape],
        scratch_shapes=[pltpu.VMEM((length, DH), F32), pltpu.VMEM((length, DH), F32)],
        compiler_params=pltpu.CompilerParams(vmem_limit_bytes=48 * MIB),
        cost_estimate=pl.CostEstimate(
            flops=10 * heads * length * span * DH,
            bytes_accessed=14 * length * columns,
            transcendentals=heads * length * span,
        ),
        name="attend_back",
    )(queries, keys, values, grads, lse, seg_row, seg_col)


def qkv_kernel(
    me_ref,
    even_ref,
    odd_ref,
    weight_ref,
    gain_ref,
    normed_even_ref,
    normed_odd_ref,
    q_ref,
    k_ref,
    v_ref,
    square_ref,
):
    turned = me_ref[0] % 2
    rows = even_ref.shape[0]
    columns = q_ref.shape[1]
    for k, (token_ref, normed_ref) in enumerate(
        ((even_ref, normed_even_ref), (odd_ref, normed_odd_ref))
    ):
        at = pl.ds(pl.multiple_of((turned ^ k) * rows, rows), rows)
        wide = token_ref[...].astype(F32)
        normed = (wide * rms_factor(wide) * gain_ref[...]).astype(BF16)
        normed_ref[...] = normed
        pre = matmul(normed, weight_ref[...])
        q_ref[at, :] = pre[:, :columns]
        k_ref[at, :] = pre[:, columns : 2 * columns]
        v_ref[at, :] = pre[:, 2 * columns :].astype(BF16)
        for j in range(2):
            squares = 0.0
            for c in range(j * columns, (j + 1) * columns, DH):
                squares += pre[:, c : c + DH] * pre[:, c : c + DH]
            square_ref[j : j + 1, at] = jnp.sum(squares.T, axis=0, keepdims=True)


def project(even, odd, weight, gain, me, rows):
    pairs = even.shape[0] // rows
    length = 2 * even.shape[0]
    depth, columns = weight.shape[0], weight.shape[1] // 3
    token = pl.BlockSpec((rows, depth), lambda i, me: (i, 0))

    def placed(shape):
        return pl.BlockSpec(shape, lambda i, me: (i ^ (me[0] // 2), 0))

    head = jax.ShapeDtypeStruct((length, columns), F32)
    return pl.pallas_call(
        qkv_kernel,
        grid_spec=pltpu.PrefetchScalarGridSpec(
            num_scalar_prefetch=1,
            grid=(pairs,),
            in_specs=[
                token,
                token,
                pl.BlockSpec(weight.shape, lambda i, me: (0, 0)),
                pl.BlockSpec((1, depth), lambda i, me: (0, 0)),
            ],
            out_specs=[
                token,
                token,
                placed((2 * rows, columns)),
                placed((2 * rows, columns)),
                placed((2 * rows, columns)),
                pl.BlockSpec((2, 2 * rows), lambda i, me: (0, i ^ (me[0] // 2))),
            ],
        ),
        out_shape=[
            jax.ShapeDtypeStruct((length // 2, depth), BF16),
            jax.ShapeDtypeStruct((length // 2, depth), BF16),
            head,
            head,
            jax.ShapeDtypeStruct((length, columns), BF16),
            jax.ShapeDtypeStruct((2, length), F32),
        ],
        compiler_params=pltpu.CompilerParams(vmem_limit_bytes=48 * MIB),
        cost_estimate=pl.CostEstimate(
            flops=6 * length * depth * columns,
            bytes_accessed=length * (4 * depth + 10 * columns) + 6 * depth * columns,
            transcendentals=length,
        ),
        name="project",
    )(me, even, odd, weight, gain)


def split_kernel(q_ref, k_ref, v_ref, out_ref):
    columns = q_ref.shape[1]
    for j, ref in enumerate((q_ref, k_ref, v_ref)):
        out_ref[0, :, j * columns : (j + 1) * columns] = ref[...]


def split_heads(w_query, w_key, w_value, parts):
    rows, columns = w_query.shape[0], w_query.shape[1] // parts
    block = pl.BlockSpec((rows, columns), lambda i: (0, i))
    return pl.pallas_call(
        split_kernel,
        grid=(parts,),
        in_specs=[block] * 3,
        out_specs=pl.BlockSpec((1, rows, 3 * columns), lambda i: (i, 0, 0)),
        out_shape=jax.ShapeDtypeStruct((parts, rows, 3 * columns), BF16),
        name="split_heads",
    )(w_query, w_key, w_value)


def spread(row, columns):
    return jnp.broadcast_to(row, (columns, row.shape[1])).T


def factor_of(square_row):
    return lax.rsqrt(square_row / D + EPSILON)


def turn(values, cosine, sine):
    return values * cosine + pltpu.roll(values, DH // 2, 1) * sine


def rope_kernel(q_ref, k_ref, square_ref, gain_ref, cos_ref, sin_ref, q_out, k_out):
    cosine, sine = cos_ref[...], sin_ref[...]
    for j, (pre_ref, out_ref) in enumerate(((q_ref, q_out), (k_ref, k_out))):
        factor = spread(factor_of(square_ref[j : j + 1, :]), DH)
        for c in range(0, pre_ref.shape[1], DH):
            at = slice(c, c + DH)
            normed = pre_ref[:, at] * factor * gain_ref[j : j + 1, at]
            out_ref[:, at] = turn(normed, cosine, sine).astype(BF16)


def rope(query_pre, key_pre, squares, gains, cosine, sine):
    length, columns = query_pre.shape
    rows = min(512, length)
    block = pl.BlockSpec((rows, columns), lambda i: (i, 0))
    table = pl.BlockSpec((rows, DH), lambda i: (i, 0))
    return pl.pallas_call(
        rope_kernel,
        grid=(length // rows,),
        in_specs=[
            block,
            block,
            pl.BlockSpec((2, rows), lambda i: (0, i)),
            pl.BlockSpec((2, columns), lambda i: (0, 0)),
            table,
            table,
        ],
        out_specs=[block, block],
        out_shape=[jax.ShapeDtypeStruct((length, columns), BF16)] * 2,
        compiler_params=pltpu.CompilerParams(vmem_limit_bytes=32 * MIB),
        name="rope",
    )(query_pre, key_pre, squares, gains, cosine, sine)


def pulled_of(grad_ref, pre_ref, factor, gain_ref, cosine, sine, j, at):
    turned = turn(grad_ref[:, at].astype(F32), cosine, -sine)
    return turned, turned * gain_ref[j : j + 1, at], pre_ref[:, at] * factor


def rope_mean_kernel(
    dq_ref, dk_ref, q_ref, k_ref, square_ref, gain_ref, cos_ref, sin_ref, mean_ref, term_ref
):
    @pl.when(pl.program_id(0) == 0)
    def _():
        term_ref[...] = jnp.zeros_like(term_ref)

    cosine, sine = cos_ref[...], sin_ref[...]
    for j, (grad_ref, pre_ref) in enumerate(((dq_ref, q_ref), (dk_ref, k_ref))):
        factor = spread(factor_of(square_ref[j : j + 1, :]), DH)
        total = 0.0
        for c in range(0, pre_ref.shape[1], DH):
            at = slice(c, c + DH)
            turned, pulled, normed = pulled_of(
                grad_ref, pre_ref, factor, gain_ref, cosine, sine, j, at
            )
            term_ref[j : j + 1, at] += jnp.sum(turned * normed, axis=0, keepdims=True)
            total += pulled * normed
        mean_ref[j : j + 1, :] = jnp.sum(total.T, axis=0, keepdims=True)


def rope_means(query_back, key_back, query_pre, key_pre, squares, gains, cosine, sine):
    length, columns = query_pre.shape
    rows = min(512, length)
    block = pl.BlockSpec((rows, columns), lambda i: (i, 0))
    table = pl.BlockSpec((rows, DH), lambda i: (i, 0))
    row = pl.BlockSpec((2, rows), lambda i: (0, i))
    fixed = pl.BlockSpec((2, columns), lambda i: (0, 0))
    return pl.pallas_call(
        rope_mean_kernel,
        grid=(length // rows,),
        in_specs=[block, block, block, block, row, fixed, table, table],
        out_specs=[row, fixed],
        out_shape=[
            jax.ShapeDtypeStruct((2, length), F32),
            jax.ShapeDtypeStruct((2, columns), F32),
        ],
        compiler_params=pltpu.CompilerParams(vmem_limit_bytes=32 * MIB),
        name="rope_means",
    )(query_back, key_back, query_pre, key_pre, squares, gains, cosine, sine)


def rope_back_kernel(
    me_ref,
    dq_ref,
    dk_ref,
    dv_ref,
    q_ref,
    k_ref,
    square_ref,
    mean_ref,
    gain_ref,
    cos_ref,
    sin_ref,
    out_ref,
):
    cosine, sine = cos_ref[...], sin_ref[...]
    columns = q_ref.shape[1]
    for j, (grad_ref, pre_ref) in enumerate(((dq_ref, q_ref), (dk_ref, k_ref))):
        factor = spread(factor_of(square_ref[j : j + 1, :]), DH)
        mean = spread(mean_ref[j : j + 1, :] / D, DH)
        for c in range(0, columns, DH):
            at = slice(c, c + DH)
            _, pulled, normed = pulled_of(grad_ref, pre_ref, factor, gain_ref, cosine, sine, j, at)
            out_ref[:, j * columns + c : j * columns + c + DH] = (
                factor * (pulled - normed * mean)
            ).astype(BF16)
    out_ref[:, 2 * columns :] = dv_ref[...]


def rope_back(grads, query_pre, key_pre, squares, means, gains, cosine, sine, me, rows):
    length, columns = query_pre.shape
    half = length // rows // 2

    def source(p, me):
        return me[0] ^ (p % half * 2 + p // half)

    block = pl.BlockSpec((rows, columns), lambda p, me: (source(p, me), 0))
    table = pl.BlockSpec((rows, DH), lambda p, me: (source(p, me), 0))
    row = pl.BlockSpec((2, rows), lambda p, me: (0, source(p, me)))
    return pl.pallas_call(
        rope_back_kernel,
        grid_spec=pltpu.PrefetchScalarGridSpec(
            num_scalar_prefetch=1,
            grid=(2 * half,),
            in_specs=[block] * 5
            + [row, row, pl.BlockSpec((2, columns), lambda p, me: (0, 0)), table, table],
            out_specs=pl.BlockSpec((rows, 3 * columns), lambda p, me: (p, 0)),
        ),
        out_shape=jax.ShapeDtypeStruct((length, 3 * columns), BF16),
        compiler_params=pltpu.CompilerParams(vmem_limit_bytes=32 * MIB),
        name="rope_back",
    )(me, *grads, query_pre, key_pre, squares, means, gains, cosine, sine)


def expert_kernel(
    in_places, down_places, first_ref, xa_ref, xb_ref, ua_ref, ub_ref, ra_ref, rb_ref, router_ref, *refs
):
    weight_refs = refs[: len(in_places) + len(down_places)]
    (ya_ref, yb_ref, za_ref, zb_ref, ga_ref, gb_ref, xc_ref, uc_ref, dg_ref, hid_ref) = refs[-13:-3]
    wi_ref, wd_ref, sems = refs[-3:]
    experts, _, hidden = hid_ref.shape
    rows = xa_ref.shape[0]

    @pl.when(pl.program_id(0) == 0)
    def _():
        copies = []
        for n, (ref, (r, first, part)) in enumerate(zip(weight_refs, in_places + down_places)):
            goal = wi_ref if n < len(in_places) else wd_ref
            place = lax.rem(first_ref[1] ^ r, goal.shape[1] // part)
            at = pl.ds(pl.multiple_of(place * part + first, ref.shape[1]), ref.shape[1])
            copies.append(pltpu.make_async_copy(ref, goal.at[:, at, :], sems.at[n]))
        for copy in copies:
            copy.start()
        for copy in copies:
            copy.wait()

    slot = lax.broadcasted_iota(jnp.int32, (CAP, rows), 0)
    blocks = (
        (xa_ref, ua_ref, ra_ref, ya_ref, za_ref, ga_ref),
        (xb_ref, ub_ref, rb_ref, yb_ref, zb_ref, gb_ref),
    )
    picks = []
    for k, (x_ref, u_ref, rank_ref, _, _, _) in enumerate(blocks):
        hits = jnp.concatenate([slot == rank_ref[0, e : e + 1, :] for e in range(experts)], 0)
        pick = hits.astype(F32).astype(BF16)
        picks.append(pick)
        x_rows = matmul(pick, x_ref[...]).astype(BF16)
        u_rows = matmul(pick, u_ref[...]).astype(BF16)
        for e in range(experts):
            xc_ref[e, k * CAP : (k + 1) * CAP, :] = x_rows[e * CAP : (e + 1) * CAP]
            uc_ref[e, k * CAP : (k + 1) * CAP, :] = u_rows[e * CAP : (e + 1) * CAP]
    outs, backs, gate_grads = [], [], []
    for e in range(experts):
        x_rows, u_rows = xc_ref[e], uc_ref[e]
        logits = matmul(x_rows, router_ref[...])
        lane = lax.broadcasted_iota(jnp.int32, logits.shape, 1)
        logits = jnp.where(lane < E, logits, -1e30)
        expos = jnp.exp(logits - jnp.max(logits, axis=-1, keepdims=True))
        own = jnp.sum(jnp.where(lane == first_ref[0] + e, expos, 0.0), axis=-1, keepdims=True)
        gate = own / jnp.sum(expos, axis=-1, keepdims=True)
        gated = matmul(x_rows, wi_ref[e, :, :hidden])
        upward = matmul(x_rows, wi_ref[e, :, hidden:])
        pulled = matmul_t(u_rows, wd_ref[e])
        sig = jax.nn.sigmoid(gated)
        silu = gated * sig
        acts = silu * upward
        gate_grads.append(jnp.sum(acts * pulled, axis=-1, keepdims=True))
        hidden_gate = (acts * gate).astype(BF16)
        hidden_grads = pulled * gate
        hid_ref[e] = hidden_gate
        dg_ref[e, :, :hidden] = (hidden_grads * upward * sig * (1.0 + gated * (1.0 - sig))).astype(BF16)
        dg_ref[e, :, hidden:] = (hidden_grads * silu).astype(BF16)
        outs.append(matmul(hidden_gate, wd_ref[e]).astype(BF16))
        backs.append(matmul_t(dg_ref[e], wi_ref[e]).astype(BF16))
    for k, (_, _, rank_ref, y_ref, z_ref, g_ref) in enumerate(blocks):
        at = slice(k * CAP, (k + 1) * CAP)
        y_ref[...] = t_matmul(picks[k], jnp.concatenate([v[at] for v in outs], 0)).astype(BF16)
        z_ref[...] = t_matmul(picks[k], jnp.concatenate([v[at] for v in backs], 0)).astype(BF16)
        for e in range(experts):
            hit = slot == rank_ref[0, e : e + 1, :]
            g_ref[0, e : e + 1, :] = jnp.sum(
                jnp.where(hit, gate_grads[e][at], 0.0), axis=0, keepdims=True
            )


def run_experts(x, u, ranks, in_pieces, down_pieces, router, places, which, compact, parts):
    experts, _, hidden = in_pieces[0][2].shape
    hidden = hidden // 2
    depth = x[0].shape[1]
    in_places = [(r, at, parts[0]) for r, at, _ in in_pieces]
    down_places = [(r, at, parts[1]) for r, at, _ in down_pieces]
    pieces = [array for _, _, array in in_pieces + down_pieces]
    rows = ranks[0].shape[2]
    steps = x[0].shape[0] // rows
    token = pl.BlockSpec((rows, depth), lambda i: (i, 0))
    rank = pl.BlockSpec((1, experts, rows), lambda i: (i, 0, 0))
    anywhere = pl.BlockSpec(memory_space=pl.ANY)

    def slots(columns):
        return pl.BlockSpec((experts, 2 * CAP, columns), lambda i: (0, i + which * steps, 0))

    shape = jax.ShapeDtypeStruct
    tokens = shape(x[0].shape, BF16)
    gates = shape((steps, experts, rows), F32)
    count = 4 * steps * CAP
    wide = shape((experts, count, depth), BF16)
    inputs = [places, *x, *u, *ranks, router, *pieces]
    return pl.pallas_call(
        partial(expert_kernel, in_places, down_places),
        grid=(steps,),
        in_specs=[pl.BlockSpec(memory_space=pltpu.SMEM)]
        + [token] * 4
        + [rank] * 2
        + [pl.BlockSpec(router.shape, lambda i: (0, 0), pipeline_mode=pl.Buffered(1))]
        + [anywhere] * (len(pieces) + len(compact)),
        out_specs=[token] * 4 + [rank] * 2 + [slots(depth)] * 2 + [slots(2 * hidden), slots(hidden)],
        out_shape=[tokens] * 4
        + [gates] * 2
        + [wide] * 2
        + [shape((experts, count, 2 * hidden), BF16), shape((experts, count, hidden), BF16)],
        scratch_shapes=[
            pltpu.VMEM((experts, depth, 2 * hidden), BF16),
            pltpu.VMEM((experts, hidden, depth), BF16),
            pltpu.SemaphoreType.DMA((len(pieces),)),
        ],
        input_output_aliases={len(inputs) + i: 6 + i for i in range(len(compact))},
        compiler_params=pltpu.CompilerParams(vmem_limit_bytes=60 * MIB),
        cost_estimate=pl.CostEstimate(
            flops=4 * steps * CAP * experts * depth * (7 * hidden + 2 * rows),
            bytes_accessed=60 * MIB,
            transcendentals=2 * steps * CAP * experts * hidden,
        ),
        name="experts",
    )(*inputs, *compact)


def product_kernel(me_ref, left_ref, right_ref, out_ref):
    out_ref[0] = t_matmul(left_ref[0], right_ref[0]).astype(BF16)


def products(left, right, part, r, count, me, name):
    experts, rows, _ = left.shape
    columns = right.shape[2]
    wide = min(columns, 1024)
    return pl.pallas_call(
        product_kernel,
        grid_spec=pltpu.PrefetchScalarGridSpec(
            num_scalar_prefetch=1,
            grid=(experts, columns // wide),
            in_specs=[
                pl.BlockSpec((1, rows, part), lambda e, j, me: (e, 0, lax.rem(me[0] ^ r, count))),
                pl.BlockSpec((1, rows, wide), lambda e, j, me: (e, 0, j)),
            ],
            out_specs=pl.BlockSpec((1, part, wide), lambda e, j, me: (e, 0, j)),
        ),
        out_shape=jax.ShapeDtypeStruct((experts, part, columns), BF16),
        compiler_params=pltpu.CompilerParams(vmem_limit_bytes=56 * MIB),
        cost_estimate=pl.CostEstimate(
            flops=2 * experts * rows * part * columns,
            bytes_accessed=2 * experts * rows * (part + columns),
            transcendentals=0,
        ),
        name=name,
    )(me, left, right)


def per_device(
    S,
    F,
    tokens,
    segments,
    routes,
    cotangent,
    w_query,
    w_key,
    w_value,
    w_output,
    router,
    attn_gain,
    moe_gain,
    query_gain,
    key_gain,
    w_gate,
    w_up,
    w_down,
):
    s = lax.axis_index("seq")
    f = lax.axis_index("fsdp")
    T = tokens.shape[1]
    L = S * T
    heads = H // S
    C = heads * DH
    experts = E // S
    part = w_query.shape[0]
    half_f = F // 2
    hidden_half = w_gate.shape[2] // 2

    me = s.reshape(1).astype(jnp.int32)
    f_at = f.reshape(1).astype(jnp.int32)
    half_at = f // half_f
    tokens_low = tokens[0]
    upstream_low = cotangent[0]
    inputs = tokens_low.astype(F32)
    half_rows = T // 2
    in_part, down_part = w_gate.shape[1], w_down.shape[1]
    quarter = in_part // 4

    def hidden_part(which, first, count):
        return jnp.concatenate(
            [
                lax.dynamic_slice(
                    weight, (0, first, which * hidden_half), (experts, count, hidden_half)
                )
                for weight in (w_gate, w_up)
            ],
            2,
        )

    def far_swap(values, *dep):
        return swap(after(values, dep), "fsdp", F, half_f)

    def near_swap(values, *dep):
        return near_pieces(after(values, dep), F)

    named = routes[0].T[None] == jnp.arange(E, dtype=jnp.int32)[:, None, None]
    chosen = jnp.any(named, axis=1)
    index = jnp.arange(T, dtype=jnp.int32)
    before = (index[:, None] <= index[None, :]).astype(BF16)
    ranks = jnp.where(chosen, matmul(chosen.astype(BF16), before) - 1.0, -1.0)
    small = jnp.concatenate(
        [
            router.reshape(-1),
            attn_gain,
            moe_gain,
            query_gain,
            key_gain,
            ranks.astype(BF16).reshape(-1),
        ]
    )[None]
    crossed = split_heads(w_query, w_key, w_value, S)
    small = double(after(small, crossed), "fsdp", F)
    crossed = lax.all_to_all(crossed, "seq", split_axis=0, concat_axis=0, tiled=True)
    near_own = [near_swap(hidden_part(half_at, 0, 2 * quarter), small)]
    out_dep = small
    small = double(small, "seq", S)
    out_far = far_swap(w_output, out_dep)
    crossed, near_own[0], small, out_far = tie(crossed, near_own[0], small, out_far)

    held = after((w_gate, w_up, w_down, upstream_low), crossed)

    def held_part(which, first, count):
        return jnp.concatenate(
            [
                lax.dynamic_slice(
                    weight, (0, first, which * hidden_half), (experts, count, hidden_half)
                )
                for weight in held[:2]
            ],
            2,
        )

    own_quarters = {n: held_part(half_at, n * quarter, quarter) for n in (2, 3)}
    far_quarters = [held_part(1 - half_at, n * quarter, quarter) for n in range(4)]
    down_rows = quarters(held[2], 1)
    down_rows = [down_rows[0], jnp.concatenate(down_rows[1:3], 1), down_rows[3]]
    upstream_halves = [held[3][:half_rows], held[3][half_rows:]]
    small = in_order(small, S, F, s, f).reshape(S, F, -1)
    prepared = (own_quarters, far_quarters, down_rows, upstream_halves, small)
    token_first = gather_first(after(tokens_low, crossed), S)
    qkv_pieces = {0: crossed}
    for r in range(1, F):
        low = low_bit(r)
        qkv_pieces[r] = swap(qkv_pieces[r ^ low], "fsdp", F, low)
        if r == half_f:
            qkv_pieces, token_first, prepared = tie(qkv_pieces, token_first, prepared)
            own_quarters, far_quarters, down_rows, upstream_halves, small = prepared
            partner_up = [far_swap(upstream_halves[0])]
    token_more = gather_more(tokens_low, token_first, S)
    qkv_pieces, partner_up[0], token_more = tie(qkv_pieces, partner_up[0], token_more)
    tokens_even, tokens_odd = gather_end(tokens_low, token_first, token_more, S)
    w_qkv = place_fsdp(qkv_pieces, f, 1).reshape(D, 3 * C)

    full_router = small[:, :, : part * E].reshape(D, E)
    gains = [
        small[:, :, part * (E + i) : part * (E + i + 1)].reshape(D).astype(F32) for i in range(4)
    ]
    gain_attn, gain_moe = gains[0], gains[1]
    head_gain = lax.dynamic_slice(jnp.stack(gains[2:], 0), (0, s * C), (2, C))
    rank_part = small[:, :, part * (E + 4) :].reshape(S, F, E, T)

    def ranks_of(index):
        ranks = lax.dynamic_slice(rank_part, (0, index, s * experts, 0), (S, 1, experts, T))
        ranks = relative(ranks[:, 0], s).astype(jnp.int32)
        return ranks[: S // 2], ranks[S // 2 :]

    places = jnp.arange(L, dtype=jnp.int32).astype(F32)
    freqs = ROPE_BASE ** (-(jnp.arange(DH // 2, dtype=F32) * 2.0 / DH))
    angles = places[:, None] * freqs[None, :]
    cosine, sine = jnp.cos(angles), jnp.sin(angles)
    cosine = jnp.concatenate([cosine, cosine], 1)
    sine = jnp.concatenate([-sine, sine], 1)

    def far_part(n, *dep):
        return far_swap(far_quarters[n], *dep)

    partner_up.append(far_swap(upstream_halves[1], w_qkv))
    out_pieces = {0: after(w_output, w_qkv), half_f: after(out_far, w_qkv)}
    for r in range(1, F):
        if r != half_f:
            low = low_bit(r)
            out_pieces[r] = swap(out_pieces[r ^ low], "fsdp", F, low)
    own_up_first = gather_first(after(upstream_low, w_qkv), S)
    normed_even, normed_odd, query_pre, key_pre, value_low, squares = project(
        tokens_even, tokens_odd, w_qkv, gain_attn[None], me, T
    )
    squares, partner_up[1], out_pieces, own_up_first = tie(
        squares, partner_up[1], out_pieces, own_up_first
    )
    partner_up = jnp.concatenate(partner_up, 0)
    own_output = place_fsdp(out_pieces, f, 0).reshape(C, D)

    out_first = gather_first(own_output, S)
    far = [far_part(0, squares)]
    near_own.append(near_swap(own_quarters[2], squares))
    squares = sum_all(squares, "seq", S)
    query_low, key_low = rope(query_pre, key_pre, squares, head_gain, cosine, sine)
    query_low, out_first, far[0], near_own[1] = tie(query_low, out_first, far[0], near_own[1])

    seg_row = segments
    seg_col = segments.reshape(L, 1)
    out_more = gather_more(own_output, out_first, S)
    far.append(far_part(1, query_low))
    near_own.append(near_swap(own_quarters[3], query_low))
    down = [near_swap(down_rows[0], query_low)]
    attended, lse = attention_forward(query_low, key_low, value_low, seg_row, seg_col)
    attended, out_more, far[1], down[0], near_own[2] = tie(
        attended, out_more, far[1], down[0], near_own[2]
    )
    attended_blocks = attended.reshape(S, T, C)
    come = lax.all_to_all(attended_blocks, "seq", split_axis=0, concat_axis=0, tiled=True)
    out_even, out_odd = gather_end(own_output, out_first, out_more, S)
    far.append(far_part(2, attended))
    near_far = [near_swap(far[0], attended)]
    own_up_more = gather_more(after(upstream_low, attended), own_up_first, S)
    come, far[2], near_far[0], own_up_more = tie(come, far[2], near_far[0], own_up_more)
    own_u = gather_end(upstream_low, own_up_first, own_up_more, S)
    far.append(far_part(3, come))
    near_far.append(near_swap(far[1], come))
    partner_up_first = gather_first(after(partner_up, come), S)
    come = relative(come, s).transpose(1, 0, 2).reshape(T, D)
    residual = inputs + matmul(come[:, : D // 2], out_even) + matmul(come[:, D // 2 :], out_odd)
    moe_factor = rms_factor(residual)
    residual_n = residual * moe_factor
    second_low = (residual_n * gain_moe).astype(BF16)
    second_low, far[3], near_far[1], partner_up_first, own_u = tie(
        second_low, far[3], near_far[1], partner_up_first, own_u
    )

    own_first = gather_first(second_low, S)
    partner_low = [far_swap(second_low[:half_rows])]
    near_far.append(near_swap(far[2], second_low))
    own_ranks, other_ranks = ranks_of(f), ranks_of(f ^ half_f)
    own_first, partner_low[0], near_far[2], own_ranks, other_ranks = tie(
        own_first, partner_low[0], near_far[2], own_ranks, other_ranks
    )
    own_more = gather_more(second_low, own_first, S)
    partner_low.append(far_swap(second_low[half_rows:], own_first))
    near_far.append(near_swap(far[3], own_first))
    partner_up_more = gather_more(after(partner_up, own_first), partner_up_first, S)
    own_more, partner_low[1], near_far[3], partner_up_more = tie(
        own_more, partner_low[1], near_far[3], partner_up_more
    )
    partner_low = jnp.concatenate(partner_low, 0)
    own_x = gather_end(second_low, own_first, own_more, S)
    partner_first = gather_first(after(partner_low, own_more), S)
    down.append(near_swap(down_rows[1], own_more))
    partner_first, down[1], own_x = tie(partner_first, down[1], own_x)
    other_u = gather_end(after(partner_up, partner_first), partner_up_first, partner_up_more, S)
    partner_more = gather_more(partner_low, partner_first, S)
    down.append(near_swap(down_rows[2], partner_first))
    partner_more, down[2], other_u = tie(partner_more, down[2], other_u)
    other_x = gather_end(partner_low, partner_first, partner_more, S)
    in_pieces = []
    for r in range(F):
        for n, rows in enumerate(near_own if r < half_f else near_far):
            first = (0, 2, 3)[n] if r < half_f else n
            in_pieces.append((r, first * quarter, rows[r % half_f]))
    down_pieces = [
        (r, (0, 1, 3)[n] * (down_part // 4), down[n][r]) for r in range(half_f) for n in range(3)
    ]
    wide_router = jnp.pad(full_router, ((0, 0), (0, 128 - E)))
    expert_places = jnp.stack([s * experts, f]).astype(jnp.int32)
    parts = (in_part, down_part)
    own_parts = run_experts(
        own_x, own_u, own_ranks, in_pieces, down_pieces, wide_router, expert_places, 0, (), parts
    )
    own_parts, other_x = tie(own_parts, other_x)
    own_got = swap(own_parts[3], "seq", S, 1)
    own_out_got = swap(own_parts[1], "seq", S, 1)
    other_parts = run_experts(
        other_x,
        other_u,
        other_ranks,
        in_pieces,
        down_pieces,
        wide_router,
        expert_places,
        1,
        own_parts[6:],
        parts,
    )
    other_parts, own_got, own_out_got = tie(other_parts, own_got, own_out_got)
    logits = matmul(second_low, full_router)
    router_probs = jax.nn.softmax(logits, axis=-1)

    x_rows, u_rows, in_grads, hidden_gate = other_parts[6:]
    in_terms, down_terms = {}, {}

    def in_products(r, *dep):
        in_terms[r] = products(
            x_rows, after(in_grads, dep), in_part, r, F, f_at, "in_products"
        )

    odd = [r for r in range(F) if r & 1]
    far_odd = [r for r in odd if r & half_f]
    near_odd = [r for r in odd if not r & half_f]

    def to_home(even, odd):
        return absolute(jnp.concatenate([even, odd], 0).transpose(0, 2, 1), s)

    gate_grads = jnp.stack(
        [to_home(own_parts[4], own_parts[5]), to_home(other_parts[4], other_parts[5])], 1
    ).reshape(S, -1)
    other_got = swap(other_parts[3], "seq", S, 1)
    for r in far_odd:
        in_products(r)
    gate_grads = lax.all_to_all(gate_grads, "seq", split_axis=0, concat_axis=0, tiled=True)
    other_got, in_terms, gate_grads = tie(other_got, in_terms, gate_grads)
    sent = {r: quarters(in_terms[r], 1) for r in far_odd}

    def send_in(n, *dep):
        return {r: swap(after(sent[r][n], dep), "fsdp", F, 1) for r in sent}

    other_sums = sum_cores(other_parts[2], other_got, S)
    come = sum_first(other_sums, S)
    far_got = [send_in(0, other_got)]
    other_out_got = swap(after(other_parts[1], other_got), "seq", S, 1)
    come, far_got[0], other_out_got = tie(come, far_got[0], other_out_got)
    gate_grads = gate_grads.reshape(S, 2, T * experts)
    partner_grads = far_swap(gate_grads[:, 1], come)
    singles, other_total = sum_more(other_sums, come, S)
    come = sum_last(singles, S)
    middle_sent = {r: jnp.concatenate(sent[r][1:3], 1) for r in sent}
    middle_got = {
        r: swap(after(middle_sent[r], far_got[0]), "fsdp", F, 1) for r in middle_sent
    }

    def down_products(r, dep):
        down_terms[r] = products(
            after(hidden_gate, dep), u_rows, down_part, r, half_f, f_at, "down_products"
        )

    for r in range(1, half_f, 2):
        down_products(r, singles)
    come, middle_got, partner_grads, down_terms = tie(
        come, middle_got, partner_grads, down_terms
    )
    for n in range(2):
        far_got.append({r: got[:, n * quarter : (n + 1) * quarter] for r, got in middle_got.items()})
    other_rows = add_all(other_total, come).astype(BF16)
    gate_grads = gate_grads[:, 0] + partner_grads
    gate_grads = gate_grads.reshape(S, T, experts).transpose(1, 0, 2).reshape(T, E)
    back = [far_swap(other_rows[:half_rows])]
    own_sums = sum_cores(own_parts[2], after(own_got, other_rows), S)
    come = sum_first(own_sums, S)
    far_got.append(send_in(3, other_rows))
    for r in far_odd:
        in_products(r ^ 1, other_rows)
    come, back[0], far_got[3], in_terms = tie(come, back[0], far_got[3], in_terms)
    back.append(far_swap(other_rows[half_rows:], come))
    singles, own_total = sum_more(own_sums, come, S)
    come = sum_last(singles, S)
    down_sent = {r: quarters(down_terms[r], 1) for r in range(1, half_f, 2)}

    def send_down(n, *dep):
        return {r: swap(after(down_sent[r][n], dep), "fsdp", F, 1) for r in down_sent}

    down_got = [send_down(0, singles)]
    for r in near_odd:
        in_products(r, singles)
    come, back[1], down_got[0], in_terms = tie(come, back[1], down_got[0], in_terms)
    row_grads = add_all(own_total, come) + jnp.concatenate(back, 0).astype(F32)

    upstream = upstream_low.astype(F32)
    logit_grads = router_probs * (
        gate_grads - jnp.sum(router_probs * gate_grads, axis=-1, keepdims=True)
    )
    router_wide = full_router.astype(F32)
    second_grads = row_grads + jnp.dot(logit_grads, router_wide.T, precision=HIGHEST)
    pulled = second_grads * gain_moe
    residual_grads = upstream + moe_factor * (
        pulled - residual_n * jnp.mean(pulled * residual_n, axis=-1, keepdims=True)
    )
    branch_low = residual_grads.astype(BF16)

    def sum_near(terms):
        mask = 2
        while mask < half_f:
            terms = {
                r: terms[r] + swap(terms[r | mask].astype(BF16), "fsdp", F, mask).astype(F32)
                for r in terms
                if not r & mask
            }
            mask *= 2
        (total,) = terms.values()
        return total

    def far_sum(n, *dep):
        terms = {
            r ^ 1: quarters(in_terms[r ^ 1], 1)[n].astype(F32) + far_got[n][r].astype(F32)
            for r in far_odd
        }
        return far_swap(sum_near(terms).astype(BF16), *dep)

    branch_first = gather_first(branch_low, S)
    far_sums = [far_sum(0, branch_low)]
    down_got.append(send_down(1, branch_low))
    for r in range(0, half_f, 2):
        down_products(r, branch_low)
    branch_first, far_sums[0], down_got[1], down_terms = tie(
        branch_first, far_sums[0], down_got[1], down_terms
    )
    branch_more = gather_more(branch_low, branch_first, S)
    far_sums.append(far_sum(1, branch_first))
    down_got.append(send_down(2, branch_first))
    branch_even, branch_odd = gather_end(branch_low, branch_first, branch_more, S)

    head_grads = jnp.concatenate(
        [matmul_t(branch_even, own_output), matmul_t(branch_odd, own_output)], 0
    ).astype(BF16)
    head_grads = absolute(head_grads.reshape(S, T, C), s).reshape(L, C)
    head_grads, far_sums[1], down_got[2] = tie(head_grads, far_sums[1], down_got[2])
    far_sums.append(far_sum(2, head_grads))
    down_got.append(send_down(3, head_grads))
    other_out_sums = sum_cores(other_parts[0], after(other_out_got, head_grads), S)
    come, head_grads = sum_first(other_out_sums, S, head_grads)
    query_back, key_back, value_back = attention_backward(
        query_low, key_low, value_low, head_grads, lse, seg_row, seg_col
    )
    query_back, key_back, value_back, far_sums[2], down_got[3], come = tie(
        query_back, key_back, value_back, far_sums[2], down_got[3], come
    )

    singles, other_total = sum_more(other_out_sums, come, S)
    come = sum_last(singles, S)
    far_sums.append(far_sum(3, query_back))
    attended_rel = relative(after(attended_blocks, singles), s).reshape(2, L // 2, C)
    output_term = t_matmul(attended_rel[0], branch_even) + t_matmul(attended_rel[1], branch_odd)
    output_term = by_index(output_term.astype(BF16).reshape(F, part, D), f, F)
    output_got = swap(output_term[: F // 2], "fsdp", F, 1)
    value_rel = relative(value_back.reshape(S, T, C), s).reshape(2, L // 2, C)

    def weight_term(even, odd):
        term = (t_matmul(normed_even, even) + t_matmul(normed_odd, odd)).astype(BF16)
        return by_index(term.reshape(S, F, part, -1).transpose(1, 0, 2, 3), f, F)

    means, gain_term = rope_means(
        query_back, key_back, query_pre, key_pre, squares, head_gain, cosine, sine
    )
    means = sum_all(means, "seq", S)
    value_term = weight_term(value_rel[0], value_rel[1])
    means, come, far_sums[3], output_got, value_term = tie(
        means, come, far_sums[3], output_got, value_term
    )
    other_outs = add_all(other_total, come).astype(BF16)
    outs_back = [far_swap(other_outs[:half_rows])]
    value_got = swap(value_term[: F // 2], "fsdp", F, 1)
    pre_rel = rope_back(
        (query_back, key_back, value_back),
        query_pre,
        key_pre,
        squares,
        means,
        head_gain,
        cosine,
        sine,
        me,
        T,
    ).reshape(2, L // 2, 3 * C)
    normed_got = swap(matmul_t(pre_rel[1], w_qkv).astype(BF16), "seq", S, 1)
    normed_kept = matmul_t(pre_rel[0], w_qkv).astype(BF16)
    normed_got, normed_kept, value_got, outs_back[0] = tie(
        normed_got, normed_kept, value_got, outs_back[0]
    )

    normed_sums = sum_cores(normed_kept, normed_got, S)
    come = sum_first(normed_sums, S)
    value_sum = sum_rest(sum_even(value_term, value_got, F), F)
    turned_term = weight_term(
        after(pre_rel[0][:, : 2 * C], normed_got), after(pre_rel[1][:, : 2 * C], normed_got)
    )
    late_grads, late_logits = after(second_grads, normed_got), after(logit_grads, normed_got)
    router_term = jnp.dot(second_low.astype(F32).T, late_logits, precision=HIGHEST)
    moe_gain_term = jnp.sum(late_grads * residual_n, axis=0)
    gain_terms = jnp.concatenate(
        [router_term.reshape(S * F, part * E), moe_gain_term.reshape(S * F, part)], 1
    )
    gain_terms = in_relative(gain_terms, S, F, s, f).reshape(S, F, -1)
    head_terms = gain_term.reshape(2, F, part).transpose(1, 0, 2).reshape(F, 2 * part)
    head_terms = in_relative(head_terms, 1, F, 0, f)
    gain_terms = jnp.concatenate([gain_terms.transpose(1, 0, 2).reshape(F, -1), head_terms], 1)
    own_out_sums = sum_cores(own_parts[0], after(own_out_got, normed_got), S)
    own_come = sum_first(own_out_sums, S)
    come, turned_term, value_sum, gain_terms, own_come = tie(
        come, turned_term, value_sum, gain_terms, own_come
    )
    turned_got = swap(turned_term[: F // 2], "fsdp", F, 1)
    singles, normed_total = sum_more(normed_sums, come, S)
    come = sum_last(singles, S)
    gain_got = swap(gain_terms[F // 2 :], "fsdp", F, half_f)
    for r in near_odd:
        in_products(r ^ 1, turned_term)
    come, turned_got, gain_got, in_terms = tie(come, turned_got, gain_got, in_terms)
    gain_terms = gain_terms[: F // 2] + gain_got
    normed_grads = add_all(normed_total, come)
    turned_sum = sum_rest(sum_even(turned_term, turned_got, F), F)
    middle = in_part // 2

    def send_near(first, dep):
        return {
            r: swap(after(in_terms[r][:, first : first + middle], dep), "fsdp", F, 1)
            for r in near_odd
        }

    near_got = [send_near(0, turned_got)]
    gain_terms = halve(after(gain_terms, turned_got), "fsdp", F, half_f // 2)
    singles, own_total = sum_more(after(own_out_sums, turned_got), own_come, S)
    own_come = sum_last(singles, S)
    turned_sum, own_come, near_got[0], gain_terms = tie(
        turned_sum, own_come, near_got[0], gain_terms
    )
    near_got.append(send_near(middle, turned_sum))
    outs_back.append(far_swap(other_outs[half_rows:], turned_sum))
    count = S * part * (E + 1)
    head_terms = gain_terms[0, count:]
    gain_terms = halve(gain_terms[0, :count].reshape(S, -1), "seq", S, S // 2)[0]
    own_outs = add_all(own_total, own_come)
    outs_back = jnp.concatenate(outs_back, 0).astype(F32)
    mixed = (residual + own_outs + outs_back).astype(BF16)[None]

    qkv_term = jnp.concatenate([turned_sum, value_sum], -1).astype(BF16)
    qkv_term = lax.all_to_all(qkv_term, "seq", split_axis=0, concat_axis=0, tiled=True)
    qkv_term = [
        qkv_term[:, :, j * C : (j + 1) * C].transpose(1, 0, 2).reshape(part, D).astype(F32)
        for j in range(3)
    ]
    grad_output = sum_rest(sum_even(output_term, output_got, F), F)

    near_got = {r: jnp.concatenate([got[r] for got in near_got], 1) for r in near_odd}
    own_term = sum_near(
        {r ^ 1: in_terms[r ^ 1].astype(F32) + near_got[r].astype(F32) for r in near_odd}
    )
    far_term = jnp.concatenate(far_sums, 1).astype(F32)
    first_half = half_at == 0
    lower = jnp.where(first_half, own_term, far_term)
    upper = jnp.where(first_half, far_term, own_term)
    grad_gate, grad_up = (
        jnp.concatenate([lower[..., at], upper[..., at]], axis=-1)
        for at in (slice(0, hidden_half), slice(hidden_half, 2 * hidden_half))
    )
    down_got = after(down_got, turned_sum)
    down_got = {r: jnp.concatenate([got[r] for got in down_got], 1) for r in down_sent}
    grad_down = sum_near(
        {r ^ 1: down_terms[r ^ 1].astype(F32) + down_got[r].astype(F32) for r in down_sent}
    )

    attn_factor = rms_factor(inputs)
    inputs_n = inputs * attn_factor
    attn_pulled = normed_grads * gain_attn
    grad_tokens = residual_grads + attn_factor * (
        attn_pulled - inputs_n * jnp.mean(attn_pulled * inputs_n, axis=-1, keepdims=True)
    )
    grad_attn_gain = sum(
        jnp.sum(term * weight.astype(F32), axis=1)
        for term, weight in zip(qkv_term, (w_query, w_key, w_value))
    ) / attn_gain.astype(F32)
    return (
        mixed,
        grad_tokens[None],
        qkv_term[0],
        qkv_term[1],
        qkv_term[2],
        grad_output,
        gain_terms[: part * E].reshape(part, E),
        grad_attn_gain,
        gain_terms[part * E :],
        head_terms[:part],
        head_terms[part:],
        grad_gate,
        grad_up,
        grad_down,
    )


def solution(mesh):
    tokens_spec = P("fsdp", "seq", None)
    rows_spec = P(("seq", "fsdp"), None)
    gain_spec = P(("seq", "fsdp"))
    expert_spec = P("seq", "fsdp", None)
    in_specs = (
        (tokens_spec, P("fsdp", None), tokens_spec, tokens_spec)
        + (rows_spec,) * 5
        + (gain_spec,) * 4
        + (expert_spec,) * 3
    )
    out_specs = (tokens_spec,) * 2 + (rows_spec,) * 5 + (gain_spec,) * 4 + (expert_spec,) * 3
    return jax.shard_map(
        partial(per_device, mesh.shape["seq"], mesh.shape["fsdp"]),
        mesh=mesh,
        in_specs=in_specs,
        out_specs=out_specs,
        check_vma=False,
    )
```

```python
from functools import partial

import jax
import jax.numpy as jnp
from jax import lax
from jax.experimental import pallas as pl
from jax.experimental.pallas import tpu as pltpu
from jax.sharding import PartitionSpec as P

D = 2048
H = 16
DH = 128
E = 16
WINDOW = 1024
CAP = 144

EPSILON = 1e-06
ROPE_BASE = 50000.0
HIGHEST = lax.Precision.HIGHEST
BF16 = jnp.bfloat16
F32 = jnp.float32
MIB = 1024 * 1024


def matmul(left, right):
    return jnp.dot(left, right, preferred_element_type=F32)


def matmul_t(left, right):
    return lax.dot_general(left, right, (((1,), (1,)), ((), ())), preferred_element_type=F32)


def t_matmul(left, right):
    return lax.dot_general(left, right, (((0,), (0,)), ((), ())), preferred_element_type=F32)


def rms_factor(values):
    return lax.rsqrt(jnp.mean(values * values, axis=-1, keepdims=True) + EPSILON)


def swap(values, axis, size, mask):
    return lax.ppermute(values, axis, [(i, i ^ mask) for i in range(size)])


def high_bit(number):
    return 1 << (number.bit_length() - 1)


def low_bit(number):
    return number & -number


def after(values, *others):
    return lax.optimization_barrier((values, others))[0]


def tie(*values):
    return lax.optimization_barrier(values)


def gather_first(values, size):
    return {r: swap(values, "seq", size, r) for r in range(2, size, 2) if r == low_bit(r)}


def gather_more(values, first, size):
    rows = values.shape[0] // 2
    pieces = dict(first)
    for r in range(2, size, 2):
        if r not in pieces:
            up, down = high_bit(r), low_bit(r)
            upper, lower = pieces[r ^ up], pieces[r ^ down]
            upper = upper[0] if isinstance(upper, tuple) else upper[:rows]
            lower = lower[1] if isinstance(lower, tuple) else lower[rows:]
            pieces[r] = (swap(upper, "seq", size, up), swap(lower, "seq", size, down))
    return {r: piece for r, piece in pieces.items() if r not in first}


def gather_end(values, first, more, size):
    blocks = [values]
    for r in range(2, size, 2):
        blocks.extend([first[r]] if r in first else more[r])
    even = jnp.concatenate(blocks, 0)
    return even, swap(even, "seq", size, 1)


def relative(blocks, me):
    size = blocks.shape[0]
    order = list(range(0, size, 2)) + list(range(1, size, 2))
    return jnp.concatenate([lax.dynamic_slice_in_dim(blocks, me ^ r, 1, 0) for r in order], 0)


def absolute(blocks, me):
    size = blocks.shape[0]
    places = [((me ^ j) // 2) + ((me ^ j) % 2) * (size // 2) for j in range(size)]
    return jnp.concatenate([lax.dynamic_slice_in_dim(blocks, at, 1, 0) for at in places], 0)


def sum_cores(even, got, size):
    rows = even.shape[0] // (size // 2)
    half = rows // 2

    def part(r, first):
        at = slice(r // 2 * rows + first, r // 2 * rows + first + half)
        return even[at].astype(F32) + got[at].astype(F32)

    return {r: [part(r, 0), part(r, half)] for r in range(0, size, 2)}


def sum_first(sums, size, held=None):
    sums = {r: list(value) for r, value in sums.items()}
    come = {}
    for r in range(size - 2, 0, -2):
        if r != low_bit(r):
            up, down = high_bit(r), low_bit(r)
            for (goal, k, _), piece in come.items():
                if goal == r:
                    sums[r][k] += piece.astype(F32)
            upper, lower, held = tie(sums[r][0].astype(BF16), sums[r][1].astype(BF16), held)
            come[r ^ up, 0, r] = swap(upper, "seq", size, up)
            come[r ^ down, 1, r] = swap(lower, "seq", size, down)
    return come if held is None else (come, held)


def sum_more(sums, come, size):
    sums = {r: list(value) for r, value in sums.items() if r == 0 or r == low_bit(r)}
    for (goal, k, _), piece in come.items():
        if goal in sums:
            sums[goal][k] += piece.astype(F32)
    singles = {
        r: jnp.concatenate([v.astype(BF16) for v in value], 0) for r, value in sums.items() if r
    }
    return tie(singles)[0], jnp.concatenate(sums[0], 0)


def sum_last(singles, size):
    return {r: swap(value, "seq", size, r) for r, value in singles.items()}


def add_all(total, pieces):
    for piece in pieces.values():
        total += piece.astype(F32)
    return total


def quarters(values, axis):
    step = values.shape[axis] // 4
    return [lax.slice_in_dim(values, k * step, (k + 1) * step, axis=axis) for k in range(4)]


def sum_all(values, axis, size):
    mask = 1
    while mask < size:
        values = values + swap(values, axis, size, mask)
        mask *= 2
    return values


def fsdp_pieces(values, size):
    pieces = {0: values}
    for r in range(1, size):
        low = low_bit(r)
        pieces[r] = swap(pieces[r ^ low], "fsdp", size, low)
    return pieces


def place_fsdp(pieces, me, axis):
    size = len(pieces)
    shape = pieces[0].shape
    whole = jnp.zeros(shape[:axis] + (size,) + shape[axis:], pieces[0].dtype)
    for r, piece in pieces.items():
        whole = lax.dynamic_update_slice_in_dim(whole, jnp.expand_dims(piece, axis), me ^ r, axis)
    return whole


def near_pieces(values, size):
    pieces = {0: values}
    for r in range(1, size // 2):
        up = high_bit(r)
        pieces[r] = swap(pieces[r ^ up], "fsdp", size, up)
    return pieces


def double(values, axis, size):
    mask = 1
    while mask < size:
        values = jnp.concatenate([values, swap(values, axis, size, mask)], 0)
        mask *= 2
    return values


def halve(values, axis, size, mask):
    while mask:
        half = values.shape[0] // 2
        values = values[:half] + swap(values[half:], axis, size, mask)
        mask //= 2
    return values


def relative_pick(seq_size, fsdp_size, s, f):
    index = jnp.arange(seq_size * fsdp_size, dtype=jnp.int32)
    source = ((index // fsdp_size) ^ s) * fsdp_size + ((index % fsdp_size) ^ f)
    return source[:, None] == index[None, :]


def in_order(values, seq_size, fsdp_size, s, f):
    pick = relative_pick(seq_size, fsdp_size, s, f).astype(values.dtype)
    return matmul(pick, values).astype(values.dtype)


def in_relative(values, seq_size, fsdp_size, s, f):
    pick = relative_pick(seq_size, fsdp_size, s, f).astype(F32)
    return jnp.dot(pick, values, precision=HIGHEST)


def by_index(partial_sum, me, size):
    order = [r for r in range(size) if r & 1] + [r for r in range(size) if not r & 1]
    return jnp.concatenate([lax.dynamic_slice_in_dim(partial_sum, me ^ r, 1, 0) for r in order], 0)


def sum_even(stacked, got, size):
    return (stacked[size // 2 :].astype(F32) + got.astype(F32)).astype(BF16)


def sum_rest(stacked, size):
    mask = 2
    values = stacked.astype(F32)
    while mask < size:
        count = values.shape[0] // 2
        pairs = values.reshape((count, 2) + values.shape[1:])
        got = swap(pairs[:, 1].astype(BF16), "fsdp", size, mask)
        values = pairs[:, 0] + got.astype(F32)
        mask *= 2
    return values[0]


def allowed_keys(seg_row, seg_col, first_query, first_key, rows, span, half_window):
    query_at = first_query + lax.broadcasted_iota(jnp.int32, (span, rows), 1)
    key_at = first_key + lax.broadcasted_iota(jnp.int32, (span, rows), 0)
    return (jnp.abs(query_at - key_at) <= half_window) & (seg_col == seg_row)


def first_key_of(block, rows, span, length):
    start = jnp.clip(block * rows - (span - rows) // 2, 0, length - span)
    return pl.multiple_of(start, rows)


def forward_kernel(span, q_ref, k_ref, v_ref, seg_row_ref, seg_col_ref, o_ref, lse_ref):
    block = pl.program_id(1)
    rows, length = q_ref.shape[0], k_ref.shape[0]
    first_key = first_key_of(block, rows, span, length)
    keys = k_ref[pl.ds(first_key, span), :]
    values = v_ref[pl.ds(first_key, span), :]
    scores = matmul_t(keys, q_ref[...]) * DH ** (-0.5)
    allowed = allowed_keys(
        seg_row_ref[...],
        seg_col_ref[pl.ds(first_key, span), :],
        block * rows,
        first_key,
        rows,
        span,
        WINDOW // 2,
    )
    scores = jnp.where(allowed, scores, -1e30)
    peak = jnp.max(scores, axis=0, keepdims=True)
    expos = jnp.exp(scores - peak)
    totals = jnp.sum(expos, axis=0, keepdims=True)
    probs = (expos * (1.0 / totals)).astype(BF16)
    o_ref[...] = t_matmul(values, probs).T.astype(BF16)
    lse_ref[...] = (peak + jnp.log(totals))[None]


def backward_kernel(
    span,
    q_ref,
    k_ref,
    v_ref,
    do_ref,
    lse_ref,
    seg_row_ref,
    seg_col_ref,
    dq_ref,
    dk_ref,
    dv_ref,
    dk_sum,
    dv_sum,
):
    block = pl.program_id(1)
    rows, length = q_ref.shape[0], k_ref.shape[0]

    @pl.when(block == 0)
    def _():
        dk_sum[...] = jnp.zeros_like(dk_sum)
        dv_sum[...] = jnp.zeros_like(dv_sum)

    first_key = first_key_of(block, rows, span, length)
    at = pl.ds(first_key, span)
    keys = k_ref[at, :]
    values = v_ref[at, :]
    queries = q_ref[...]
    grads = do_ref[...]
    scores = matmul_t(keys, queries) * DH ** (-0.5)
    allowed = allowed_keys(
        seg_row_ref[...],
        seg_col_ref[at, :],
        block * rows,
        first_key,
        rows,
        span,
        WINDOW // 2,
    )
    probs = jnp.where(allowed, jnp.exp(scores - lse_ref[0]), 0.0)
    dv_sum[at, :] += matmul(probs.astype(BF16), grads)
    prob_grads = matmul_t(values, grads)
    center = jnp.sum(probs * prob_grads, axis=0, keepdims=True)
    score_grads = (probs * (prob_grads - center)).astype(BF16)
    dk_sum[at, :] += matmul(score_grads, queries)
    dq_ref[...] = (t_matmul(keys, score_grads) * DH ** (-0.5)).T.astype(BF16)

    @pl.when(block == length // rows - 1)
    def _():
        dk_ref[...] = (dk_sum[...] * DH ** (-0.5)).astype(BF16)
        dv_ref[...] = dv_sum[...].astype(BF16)


def attention_sizes(length):
    rows = 256
    return rows, min(length, rows + WINDOW)


def attention_forward(queries, keys, values, seg_row, seg_col):
    length, columns = queries.shape
    heads = columns // DH
    rows, span = attention_sizes(length)
    block = pl.BlockSpec((rows, DH), lambda h, i: (i, h))
    whole = pl.BlockSpec((length, DH), lambda h, i: (0, h))
    return pl.pallas_call(
        partial(forward_kernel, span),
        grid=(heads, length // rows),
        in_specs=[
            block,
            whole,
            whole,
            pl.BlockSpec((1, rows), lambda h, i: (0, i)),
            pl.BlockSpec((length, 1), lambda h, i: (0, 0)),
        ],
        out_specs=[block, pl.BlockSpec((1, 1, rows), lambda h, i: (h, 0, i))],
        out_shape=[
            jax.ShapeDtypeStruct((length, columns), BF16),
            jax.ShapeDtypeStruct((heads, 1, length), F32),
        ],
        compiler_params=pltpu.CompilerParams(vmem_limit_bytes=48 * MIB),
        cost_estimate=pl.CostEstimate(
            flops=4 * heads * length * span * DH,
            bytes_accessed=8 * length * columns,
            transcendentals=heads * length * span,
        ),
        name="attend",
    )(queries, keys, values, seg_row, seg_col)


def attention_backward(queries, keys, values, grads, lse, seg_row, seg_col):
    length, columns = queries.shape
    heads = columns // DH
    rows, span = attention_sizes(length)
    block = pl.BlockSpec((rows, DH), lambda h, i: (i, h))
    whole = pl.BlockSpec((length, DH), lambda h, i: (0, h))
    shape = jax.ShapeDtypeStruct((length, columns), BF16)
    return pl.pallas_call(
        partial(backward_kernel, span),
        grid=(heads, length // rows),
        in_specs=[
            block,
            whole,
            whole,
            block,
            pl.BlockSpec((1, 1, rows), lambda h, i: (h, 0, i)),
            pl.BlockSpec((1, rows), lambda h, i: (0, i)),
            pl.BlockSpec((length, 1), lambda h, i: (0, 0)),
        ],
        out_specs=[block, whole, whole],
        out_shape=[shape, shape, shape],
        scratch_shapes=[pltpu.VMEM((length, DH), F32), pltpu.VMEM((length, DH), F32)],
        compiler_params=pltpu.CompilerParams(vmem_limit_bytes=48 * MIB),
        cost_estimate=pl.CostEstimate(
            flops=10 * heads * length * span * DH,
            bytes_accessed=14 * length * columns,
            transcendentals=heads * length * span,
        ),
        name="attend_back",
    )(queries, keys, values, grads, lse, seg_row, seg_col)


def qkv_kernel(
    me_ref,
    even_ref,
    odd_ref,
    weight_ref,
    gain_ref,
    normed_even_ref,
    normed_odd_ref,
    q_ref,
    k_ref,
    v_ref,
    square_ref,
):
    turned = me_ref[0] % 2
    rows = even_ref.shape[0]
    columns = q_ref.shape[1]
    for k, (token_ref, normed_ref) in enumerate(
        ((even_ref, normed_even_ref), (odd_ref, normed_odd_ref))
    ):
        at = pl.ds(pl.multiple_of((turned ^ k) * rows, rows), rows)
        wide = token_ref[...].astype(F32)
        normed = (wide * rms_factor(wide) * gain_ref[...]).astype(BF16)
        normed_ref[...] = normed
        pre = matmul(normed, weight_ref[...])
        q_ref[at, :] = pre[:, :columns]
        k_ref[at, :] = pre[:, columns : 2 * columns]
        v_ref[at, :] = pre[:, 2 * columns :].astype(BF16)
        for j in range(2):
            squares = 0.0
            for c in range(j * columns, (j + 1) * columns, DH):
                squares += pre[:, c : c + DH] * pre[:, c : c + DH]
            square_ref[j : j + 1, at] = jnp.sum(squares.T, axis=0, keepdims=True)


def project(even, odd, weight, gain, me, rows):
    pairs = even.shape[0] // rows
    length = 2 * even.shape[0]
    depth, columns = weight.shape[0], weight.shape[1] // 3
    token = pl.BlockSpec((rows, depth), lambda i, me: (i, 0))

    def placed(shape):
        return pl.BlockSpec(shape, lambda i, me: (i ^ (me[0] // 2), 0))

    head = jax.ShapeDtypeStruct((length, columns), F32)
    return pl.pallas_call(
        qkv_kernel,
        grid_spec=pltpu.PrefetchScalarGridSpec(
            num_scalar_prefetch=1,
            grid=(pairs,),
            in_specs=[
                token,
                token,
                pl.BlockSpec(weight.shape, lambda i, me: (0, 0)),
                pl.BlockSpec((1, depth), lambda i, me: (0, 0)),
            ],
            out_specs=[
                token,
                token,
                placed((2 * rows, columns)),
                placed((2 * rows, columns)),
                placed((2 * rows, columns)),
                pl.BlockSpec((2, 2 * rows), lambda i, me: (0, i ^ (me[0] // 2))),
            ],
        ),
        out_shape=[
            jax.ShapeDtypeStruct((length // 2, depth), BF16),
            jax.ShapeDtypeStruct((length // 2, depth), BF16),
            head,
            head,
            jax.ShapeDtypeStruct((length, columns), BF16),
            jax.ShapeDtypeStruct((2, length), F32),
        ],
        compiler_params=pltpu.CompilerParams(vmem_limit_bytes=48 * MIB),
        cost_estimate=pl.CostEstimate(
            flops=6 * length * depth * columns,
            bytes_accessed=length * (4 * depth + 10 * columns) + 6 * depth * columns,
            transcendentals=length,
        ),
        name="project",
    )(me, even, odd, weight, gain)


def split_kernel(q_ref, k_ref, v_ref, out_ref):
    columns = q_ref.shape[1]
    for j, ref in enumerate((q_ref, k_ref, v_ref)):
        out_ref[0, :, j * columns : (j + 1) * columns] = ref[...]


def split_heads(w_query, w_key, w_value, parts):
    rows, columns = w_query.shape[0], w_query.shape[1] // parts
    block = pl.BlockSpec((rows, columns), lambda i: (0, i))
    return pl.pallas_call(
        split_kernel,
        grid=(parts,),
        in_specs=[block] * 3,
        out_specs=pl.BlockSpec((1, rows, 3 * columns), lambda i: (i, 0, 0)),
        out_shape=jax.ShapeDtypeStruct((parts, rows, 3 * columns), BF16),
        name="split_heads",
    )(w_query, w_key, w_value)


def spread(row, columns):
    return jnp.broadcast_to(row, (columns, row.shape[1])).T


def factor_of(square_row):
    return lax.rsqrt(square_row / D + EPSILON)


def turn(values, cosine, sine):
    return values * cosine + pltpu.roll(values, DH // 2, 1) * sine


def rope_kernel(q_ref, k_ref, square_ref, gain_ref, cos_ref, sin_ref, q_out, k_out):
    cosine, sine = cos_ref[...], sin_ref[...]
    for j, (pre_ref, out_ref) in enumerate(((q_ref, q_out), (k_ref, k_out))):
        factor = spread(factor_of(square_ref[j : j + 1, :]), DH)
        for c in range(0, pre_ref.shape[1], DH):
            at = slice(c, c + DH)
            normed = pre_ref[:, at] * factor * gain_ref[j : j + 1, at]
            out_ref[:, at] = turn(normed, cosine, sine).astype(BF16)


def rope(query_pre, key_pre, squares, gains, cosine, sine):
    length, columns = query_pre.shape
    rows = min(512, length)
    block = pl.BlockSpec((rows, columns), lambda i: (i, 0))
    table = pl.BlockSpec((rows, DH), lambda i: (i, 0))
    return pl.pallas_call(
        rope_kernel,
        grid=(length // rows,),
        in_specs=[
            block,
            block,
            pl.BlockSpec((2, rows), lambda i: (0, i)),
            pl.BlockSpec((2, columns), lambda i: (0, 0)),
            table,
            table,
        ],
        out_specs=[block, block],
        out_shape=[jax.ShapeDtypeStruct((length, columns), BF16)] * 2,
        compiler_params=pltpu.CompilerParams(vmem_limit_bytes=32 * MIB),
        name="rope",
    )(query_pre, key_pre, squares, gains, cosine, sine)


def pulled_of(grad_ref, pre_ref, factor, gain_ref, cosine, sine, j, at):
    turned = turn(grad_ref[:, at].astype(F32), cosine, -sine)
    return turned, turned * gain_ref[j : j + 1, at], pre_ref[:, at] * factor


def rope_mean_kernel(
    dq_ref, dk_ref, q_ref, k_ref, square_ref, gain_ref, cos_ref, sin_ref, mean_ref, term_ref
):
    @pl.when(pl.program_id(0) == 0)
    def _():
        term_ref[...] = jnp.zeros_like(term_ref)

    cosine, sine = cos_ref[...], sin_ref[...]
    for j, (grad_ref, pre_ref) in enumerate(((dq_ref, q_ref), (dk_ref, k_ref))):
        factor = spread(factor_of(square_ref[j : j + 1, :]), DH)
        total = 0.0
        for c in range(0, pre_ref.shape[1], DH):
            at = slice(c, c + DH)
            turned, pulled, normed = pulled_of(
                grad_ref, pre_ref, factor, gain_ref, cosine, sine, j, at
            )
            term_ref[j : j + 1, at] += jnp.sum(turned * normed, axis=0, keepdims=True)
            total += pulled * normed
        mean_ref[j : j + 1, :] = jnp.sum(total.T, axis=0, keepdims=True)


def rope_means(query_back, key_back, query_pre, key_pre, squares, gains, cosine, sine):
    length, columns = query_pre.shape
    rows = min(512, length)
    block = pl.BlockSpec((rows, columns), lambda i: (i, 0))
    table = pl.BlockSpec((rows, DH), lambda i: (i, 0))
    row = pl.BlockSpec((2, rows), lambda i: (0, i))
    fixed = pl.BlockSpec((2, columns), lambda i: (0, 0))
    return pl.pallas_call(
        rope_mean_kernel,
        grid=(length // rows,),
        in_specs=[block, block, block, block, row, fixed, table, table],
        out_specs=[row, fixed],
        out_shape=[
            jax.ShapeDtypeStruct((2, length), F32),
            jax.ShapeDtypeStruct((2, columns), F32),
        ],
        compiler_params=pltpu.CompilerParams(vmem_limit_bytes=32 * MIB),
        name="rope_means",
    )(query_back, key_back, query_pre, key_pre, squares, gains, cosine, sine)


def rope_back_kernel(
    me_ref,
    dq_ref,
    dk_ref,
    dv_ref,
    q_ref,
    k_ref,
    square_ref,
    mean_ref,
    gain_ref,
    cos_ref,
    sin_ref,
    out_ref,
):
    cosine, sine = cos_ref[...], sin_ref[...]
    columns = q_ref.shape[1]
    for j, (grad_ref, pre_ref) in enumerate(((dq_ref, q_ref), (dk_ref, k_ref))):
        factor = spread(factor_of(square_ref[j : j + 1, :]), DH)
        mean = spread(mean_ref[j : j + 1, :] / D, DH)
        for c in range(0, columns, DH):
            at = slice(c, c + DH)
            _, pulled, normed = pulled_of(grad_ref, pre_ref, factor, gain_ref, cosine, sine, j, at)
            out_ref[:, j * columns + c : j * columns + c + DH] = (
                factor * (pulled - normed * mean)
            ).astype(BF16)
    out_ref[:, 2 * columns :] = dv_ref[...]


def rope_back(grads, query_pre, key_pre, squares, means, gains, cosine, sine, me, rows):
    length, columns = query_pre.shape
    half = length // rows // 2

    def source(p, me):
        return me[0] ^ (p % half * 2 + p // half)

    block = pl.BlockSpec((rows, columns), lambda p, me: (source(p, me), 0))
    table = pl.BlockSpec((rows, DH), lambda p, me: (source(p, me), 0))
    row = pl.BlockSpec((2, rows), lambda p, me: (0, source(p, me)))
    return pl.pallas_call(
        rope_back_kernel,
        grid_spec=pltpu.PrefetchScalarGridSpec(
            num_scalar_prefetch=1,
            grid=(2 * half,),
            in_specs=[block] * 5
            + [row, row, pl.BlockSpec((2, columns), lambda p, me: (0, 0)), table, table],
            out_specs=pl.BlockSpec((rows, 3 * columns), lambda p, me: (p, 0)),
        ),
        out_shape=jax.ShapeDtypeStruct((length, 3 * columns), BF16),
        compiler_params=pltpu.CompilerParams(vmem_limit_bytes=32 * MIB),
        name="rope_back",
    )(me, *grads, query_pre, key_pre, squares, means, gains, cosine, sine)


def expert_kernel(
    in_places, down_places, first_ref, xa_ref, xb_ref, ua_ref, ub_ref, ra_ref, rb_ref, router_ref, *refs
):
    weight_refs = refs[: len(in_places) + len(down_places)]
    (ya_ref, yb_ref, za_ref, zb_ref, ga_ref, gb_ref, xc_ref, uc_ref, dg_ref, hid_ref) = refs[-13:-3]
    wi_ref, wd_ref, sems = refs[-3:]
    experts, _, hidden = hid_ref.shape
    rows = xa_ref.shape[0]

    @pl.when(pl.program_id(0) == 0)
    def _():
        copies = []
        for n, (ref, (r, first, part)) in enumerate(zip(weight_refs, in_places + down_places)):
            goal = wi_ref if n < len(in_places) else wd_ref
            place = lax.rem(first_ref[1] ^ r, goal.shape[1] // part)
            at = pl.ds(pl.multiple_of(place * part + first, ref.shape[1]), ref.shape[1])
            copies.append(pltpu.make_async_copy(ref, goal.at[:, at, :], sems.at[n]))
        for copy in copies:
            copy.start()
        for copy in copies:
            copy.wait()

    slot = lax.broadcasted_iota(jnp.int32, (CAP, rows), 0)
    blocks = (
        (xa_ref, ua_ref, ra_ref, ya_ref, za_ref, ga_ref),
        (xb_ref, ub_ref, rb_ref, yb_ref, zb_ref, gb_ref),
    )
    picks = []
    for k, (x_ref, u_ref, rank_ref, _, _, _) in enumerate(blocks):
        hits = jnp.concatenate([slot == rank_ref[0, e : e + 1, :] for e in range(experts)], 0)
        pick = hits.astype(F32).astype(BF16)
        picks.append(pick)
        x_rows = matmul(pick, x_ref[...]).astype(BF16)
        u_rows = matmul(pick, u_ref[...]).astype(BF16)
        for e in range(experts):
            xc_ref[e, k * CAP : (k + 1) * CAP, :] = x_rows[e * CAP : (e + 1) * CAP]
            uc_ref[e, k * CAP : (k + 1) * CAP, :] = u_rows[e * CAP : (e + 1) * CAP]
    outs, backs, gate_grads = [], [], []
    for e in range(experts):
        x_rows, u_rows = xc_ref[e], uc_ref[e]
        logits = matmul(x_rows, router_ref[...])
        lane = lax.broadcasted_iota(jnp.int32, logits.shape, 1)
        logits = jnp.where(lane < E, logits, -1e30)
        expos = jnp.exp(logits - jnp.max(logits, axis=-1, keepdims=True))
        own = jnp.sum(jnp.where(lane == first_ref[0] + e, expos, 0.0), axis=-1, keepdims=True)
        gate = own / jnp.sum(expos, axis=-1, keepdims=True)
        gated = matmul(x_rows, wi_ref[e, :, :hidden])
        upward = matmul(x_rows, wi_ref[e, :, hidden:])
        pulled = matmul_t(u_rows, wd_ref[e])
        sig = jax.nn.sigmoid(gated)
        silu = gated * sig
        acts = silu * upward
        gate_grads.append(jnp.sum(acts * pulled, axis=-1, keepdims=True))
        hidden_gate = (acts * gate).astype(BF16)
        hidden_grads = pulled * gate
        hid_ref[e] = hidden_gate
        dg_ref[e, :, :hidden] = (hidden_grads * upward * sig * (1.0 + gated * (1.0 - sig))).astype(BF16)
        dg_ref[e, :, hidden:] = (hidden_grads * silu).astype(BF16)
        outs.append(matmul(hidden_gate, wd_ref[e]).astype(BF16))
        backs.append(matmul_t(dg_ref[e], wi_ref[e]).astype(BF16))
    for k, (_, _, rank_ref, y_ref, z_ref, g_ref) in enumerate(blocks):
        at = slice(k * CAP, (k + 1) * CAP)
        y_ref[...] = t_matmul(picks[k], jnp.concatenate([v[at] for v in outs], 0)).astype(BF16)
        z_ref[...] = t_matmul(picks[k], jnp.concatenate([v[at] for v in backs], 0)).astype(BF16)
        for e in range(experts):
            hit = slot == rank_ref[0, e : e + 1, :]
            g_ref[0, e : e + 1, :] = jnp.sum(
                jnp.where(hit, gate_grads[e][at], 0.0), axis=0, keepdims=True
            )


def run_experts(x, u, ranks, in_pieces, down_pieces, router, places, which, filled, parts, at, steps):
    experts, _, hidden = in_pieces[0][2].shape
    hidden = hidden // 2
    depth = x[0].shape[1]
    in_places = [(r, row, parts[0]) for r, row, _ in in_pieces]
    down_places = [(r, row, parts[1]) for r, row, _ in down_pieces]
    pieces = [array for _, _, array in in_pieces + down_pieces]
    rows = ranks[0].shape[2]
    pairs = x[0].shape[0] // rows
    token = pl.BlockSpec((rows, depth), lambda i: (i + at, 0))
    rank = pl.BlockSpec((1, experts, rows), lambda i: (i + at, 0, 0))
    anywhere = pl.BlockSpec(memory_space=pl.ANY)

    def slots(columns):
        return pl.BlockSpec((experts, 2 * CAP, columns), lambda i: (0, i + at + which * pairs, 0))

    shape = jax.ShapeDtypeStruct
    tokens = shape(x[0].shape, BF16)
    gates = shape((pairs, experts, rows), F32)
    count = 4 * pairs * CAP
    wide = shape((experts, count, depth), BF16)
    inputs = [places, *x, *u, *ranks, router, *pieces]
    return pl.pallas_call(
        partial(expert_kernel, in_places, down_places),
        grid=(steps,),
        in_specs=[pl.BlockSpec(memory_space=pltpu.SMEM)]
        + [token] * 4
        + [rank] * 2
        + [pl.BlockSpec(router.shape, lambda i: (0, 0), pipeline_mode=pl.Buffered(1))]
        + [anywhere] * (len(pieces) + len(filled)),
        out_specs=[token] * 4 + [rank] * 2 + [slots(depth)] * 2 + [slots(2 * hidden), slots(hidden)],
        out_shape=[tokens] * 4
        + [gates] * 2
        + [wide] * 2
        + [shape((experts, count, 2 * hidden), BF16), shape((experts, count, hidden), BF16)],
        scratch_shapes=[
            pltpu.VMEM((experts, depth, 2 * hidden), BF16),
            pltpu.VMEM((experts, hidden, depth), BF16),
            pltpu.SemaphoreType.DMA((len(pieces),)),
        ],
        input_output_aliases={len(inputs) + i: k for i, k in enumerate(filled)},
        compiler_params=pltpu.CompilerParams(vmem_limit_bytes=60 * MIB),
        cost_estimate=pl.CostEstimate(
            flops=4 * steps * CAP * experts * depth * (7 * hidden + 2 * rows),
            bytes_accessed=60 * MIB,
            transcendentals=2 * steps * CAP * experts * hidden,
        ),
        name="experts",
    )(*inputs, *filled.values())


def product_kernel(me_ref, left_ref, right_ref, out_ref):
    out_ref[0] = t_matmul(left_ref[0], right_ref[0]).astype(BF16)


def products(left, right, part, r, count, me, name):
    experts, rows, _ = left.shape
    columns = right.shape[2]
    wide = min(columns, 1024)
    return pl.pallas_call(
        product_kernel,
        grid_spec=pltpu.PrefetchScalarGridSpec(
            num_scalar_prefetch=1,
            grid=(experts, columns // wide),
            in_specs=[
                pl.BlockSpec((1, rows, part), lambda e, j, me: (e, 0, lax.rem(me[0] ^ r, count))),
                pl.BlockSpec((1, rows, wide), lambda e, j, me: (e, 0, j)),
            ],
            out_specs=pl.BlockSpec((1, part, wide), lambda e, j, me: (e, 0, j)),
        ),
        out_shape=jax.ShapeDtypeStruct((experts, part, columns), BF16),
        compiler_params=pltpu.CompilerParams(vmem_limit_bytes=56 * MIB),
        cost_estimate=pl.CostEstimate(
            flops=2 * experts * rows * part * columns,
            bytes_accessed=2 * experts * rows * (part + columns),
            transcendentals=0,
        ),
        name=name,
    )(me, left, right)


def per_device(
    S,
    F,
    tokens,
    segments,
    routes,
    cotangent,
    w_query,
    w_key,
    w_value,
    w_output,
    router,
    attn_gain,
    moe_gain,
    query_gain,
    key_gain,
    w_gate,
    w_up,
    w_down,
):
    s = lax.axis_index("seq")
    f = lax.axis_index("fsdp")
    T = tokens.shape[1]
    L = S * T
    heads = H // S
    C = heads * DH
    experts = E // S
    part = w_query.shape[0]
    half_f = F // 2
    hidden_half = w_gate.shape[2] // 2

    me = s.reshape(1).astype(jnp.int32)
    f_at = f.reshape(1).astype(jnp.int32)
    half_at = f // half_f
    tokens_low = tokens[0]
    upstream_low = cotangent[0]
    inputs = tokens_low.astype(F32)
    half_rows = T // 2
    in_part, down_part = w_gate.shape[1], w_down.shape[1]
    quarter = in_part // 4

    def hidden_part(which, first, count):
        return jnp.concatenate(
            [
                lax.dynamic_slice(
                    weight, (0, first, which * hidden_half), (experts, count, hidden_half)
                )
                for weight in (w_gate, w_up)
            ],
            2,
        )

    def far_swap(values, *dep):
        return swap(after(values, dep), "fsdp", F, half_f)

    def near_swap(values, *dep):
        return near_pieces(after(values, dep), F)

    named = routes[0].T[None] == jnp.arange(E, dtype=jnp.int32)[:, None, None]
    chosen = jnp.any(named, axis=1)
    index = jnp.arange(T, dtype=jnp.int32)
    before = (index[:, None] <= index[None, :]).astype(BF16)
    ranks = jnp.where(chosen, matmul(chosen.astype(BF16), before) - 1.0, -1.0)
    small = jnp.concatenate(
        [
            router.reshape(-1),
            attn_gain,
            moe_gain,
            query_gain,
            key_gain,
            ranks.astype(BF16).reshape(-1),
        ]
    )[None]
    crossed = split_heads(w_query, w_key, w_value, S)
    small = double(after(small, crossed), "fsdp", F)
    crossed = lax.all_to_all(crossed, "seq", split_axis=0, concat_axis=0, tiled=True)
    near_own = [near_swap(hidden_part(half_at, 0, 2 * quarter), small)]
    out_dep = small
    small = double(small, "seq", S)
    out_far = far_swap(w_output, out_dep)
    crossed, near_own[0], small, out_far = tie(crossed, near_own[0], small, out_far)

    held = after((w_gate, w_up, w_down, upstream_low), crossed)

    def held_part(which, first, count):
        return jnp.concatenate(
            [
                lax.dynamic_slice(
                    weight, (0, first, which * hidden_half), (experts, count, hidden_half)
                )
                for weight in held[:2]
            ],
            2,
        )

    own_quarters = {n: held_part(half_at, n * quarter, quarter) for n in (2, 3)}
    far_quarters = [held_part(1 - half_at, n * quarter, quarter) for n in range(4)]
    down_rows = quarters(held[2], 1)
    upstream_halves = [held[3][:half_rows], held[3][half_rows:]]
    small = in_order(small, S, F, s, f).reshape(S, F, -1)
    prepared = (own_quarters, far_quarters, down_rows, upstream_halves, small)
    token_first = gather_first(after(tokens_low, crossed), S)
    qkv_pieces = {0: crossed}
    for r in range(1, F):
        low = low_bit(r)
        qkv_pieces[r] = swap(qkv_pieces[r ^ low], "fsdp", F, low)
        if r == half_f:
            qkv_pieces, token_first, prepared = tie(qkv_pieces, token_first, prepared)
            own_quarters, far_quarters, down_rows, upstream_halves, small = prepared
            partner_up = [far_swap(upstream_halves[0])]
    token_more = gather_more(tokens_low, token_first, S)
    qkv_pieces, partner_up[0], token_more = tie(qkv_pieces, partner_up[0], token_more)
    tokens_even, tokens_odd = gather_end(tokens_low, token_first, token_more, S)
    w_qkv = place_fsdp(qkv_pieces, f, 1).reshape(D, 3 * C)

    full_router = small[:, :, : part * E].reshape(D, E)
    gains = [
        small[:, :, part * (E + i) : part * (E + i + 1)].reshape(D).astype(F32) for i in range(4)
    ]
    gain_attn, gain_moe = gains[0], gains[1]
    head_gain = lax.dynamic_slice(jnp.stack(gains[2:], 0), (0, s * C), (2, C))
    rank_part = small[:, :, part * (E + 4) :].reshape(S, F, E, T)

    def ranks_of(index):
        ranks = lax.dynamic_slice(rank_part, (0, index, s * experts, 0), (S, 1, experts, T))
        ranks = relative(ranks[:, 0], s).astype(jnp.int32)
        return ranks[: S // 2], ranks[S // 2 :]

    places = jnp.arange(L, dtype=jnp.int32).astype(F32)
    freqs = ROPE_BASE ** (-(jnp.arange(DH // 2, dtype=F32) * 2.0 / DH))
    angles = places[:, None] * freqs[None, :]
    cosine, sine = jnp.cos(angles), jnp.sin(angles)
    cosine = jnp.concatenate([cosine, cosine], 1)
    sine = jnp.concatenate([-sine, sine], 1)

    def far_part(n, *dep):
        return far_swap(far_quarters[n], *dep)

    partner_up.append(far_swap(upstream_halves[1], w_qkv))
    out_pieces = {0: after(w_output, w_qkv), half_f: after(out_far, w_qkv)}
    for r in range(1, F):
        if r != half_f:
            low = low_bit(r)
            out_pieces[r] = swap(out_pieces[r ^ low], "fsdp", F, low)
    own_up_first = gather_first(after(upstream_low, w_qkv), S)
    normed_even, normed_odd, query_pre, key_pre, value_low, squares = project(
        tokens_even, tokens_odd, w_qkv, gain_attn[None], me, T
    )
    squares, partner_up[1], out_pieces, own_up_first = tie(
        squares, partner_up[1], out_pieces, own_up_first
    )
    partner_up = jnp.concatenate(partner_up, 0)
    own_output = place_fsdp(out_pieces, f, 0).reshape(C, D)

    out_first = gather_first(own_output, S)
    far = [far_part(0, squares)]
    near_own.append(near_swap(own_quarters[2], squares))
    squares = sum_all(squares, "seq", S)
    query_low, key_low = rope(query_pre, key_pre, squares, head_gain, cosine, sine)
    query_low, out_first, far[0], near_own[1] = tie(query_low, out_first, far[0], near_own[1])

    seg_row = segments
    seg_col = segments.reshape(L, 1)
    out_more = gather_more(own_output, out_first, S)
    far.append(far_part(1, query_low))
    near_own.append(near_swap(own_quarters[3], query_low))
    attended, lse = attention_forward(query_low, key_low, value_low, seg_row, seg_col)
    attended, out_more, far[1], near_own[2] = tie(attended, out_more, far[1], near_own[2])
    attended_blocks = attended.reshape(S, T, C)
    come = lax.all_to_all(attended_blocks, "seq", split_axis=0, concat_axis=0, tiled=True)
    out_even, out_odd = gather_end(own_output, out_first, out_more, S)
    far.append(far_part(2, attended))
    near_far = [near_swap(far[0], attended)]
    own_up_more = gather_more(after(upstream_low, attended), own_up_first, S)
    come, far[2], near_far[0], own_up_more = tie(come, far[2], near_far[0], own_up_more)
    own_u = gather_end(upstream_low, own_up_first, own_up_more, S)
    near_far.append(near_swap(far[1], come))
    down = [near_swap(down_rows[0], come)]
    partner_up_first = gather_first(after(partner_up, come), S)
    come = relative(come, s).transpose(1, 0, 2).reshape(T, D)
    residual = inputs + matmul(come[:, : D // 2], out_even) + matmul(come[:, D // 2 :], out_odd)
    moe_factor = rms_factor(residual)
    residual_n = residual * moe_factor
    second_low = (residual_n * gain_moe).astype(BF16)
    second_low, down[0], near_far[1], partner_up_first, own_u = tie(
        second_low, down[0], near_far[1], partner_up_first, own_u
    )

    own_first = gather_first(second_low, S)
    partner_low = [far_swap(second_low[:half_rows])]
    near_far.append(near_swap(far[2], second_low))
    own_ranks, other_ranks = ranks_of(f), ranks_of(f ^ half_f)
    own_first, partner_low[0], near_far[2], own_ranks, other_ranks = tie(
        own_first, partner_low[0], near_far[2], own_ranks, other_ranks
    )
    own_more = gather_more(second_low, own_first, S)
    partner_low.append(far_swap(second_low[half_rows:], own_first))
    down.append(near_swap(down_rows[1], own_first))
    partner_up_more = gather_more(after(partner_up, own_first), partner_up_first, S)
    own_more, partner_low[1], down[1], partner_up_more = tie(
        own_more, partner_low[1], down[1], partner_up_more
    )
    partner_low = jnp.concatenate(partner_low, 0)
    own_x = gather_end(second_low, own_first, own_more, S)
    partner_first = gather_first(after(partner_low, own_more), S)
    down.append(near_swap(down_rows[2], own_more))
    far.append(far_part(3, own_more))
    partner_first, down[2], own_x, far[3] = tie(partner_first, down[2], own_x, far[3])
    other_u = gather_end(after(partner_up, partner_first), partner_up_first, partner_up_more, S)
    partner_more = gather_more(partner_low, partner_first, S)
    down.append(near_swap(down_rows[3], partner_first))
    near_far.append(near_swap(far[3], partner_first))
    partner_more, down[3], other_u, near_far[3] = tie(partner_more, down[3], other_u, near_far[3])
    other_x = gather_end(partner_low, partner_first, partner_more, S)
    in_pieces = []
    for r in range(F):
        for n, rows in enumerate(near_own if r < half_f else near_far):
            first = (0, 2, 3)[n] if r < half_f else n
            in_pieces.append((r, first * quarter, rows[r % half_f]))
    down_pieces = [
        (r, n * (down_part // 4), down[n][r]) for r in range(half_f) for n in range(4)
    ]
    wide_router = jnp.pad(full_router, ((0, 0), (0, 128 - E)))
    expert_places = jnp.stack([s * experts, f]).astype(jnp.int32)
    parts = (in_part, down_part)
    pairs = S // 2
    short = max(1, pairs // 4)

    def call(x, u, ranks, which, filled, at, steps):
        filled = {k: filled[k] for k in sorted(filled)}
        return run_experts(
            x,
            u,
            ranks,
            in_pieces,
            down_pieces,
            wide_router,
            expert_places,
            which,
            filled,
            parts,
            at,
            steps,
        )

    own_parts = call(own_x, own_u, own_ranks, 0, {}, 0, short)
    own_parts, other_x = tie(own_parts, other_x)
    compact = {k: own_parts[k] for k in range(6, 10)}
    other_parts = call(other_x, other_u, other_ranks, 1, compact, 0, pairs)
    other_got = swap(other_parts[3], "seq", S, 1)
    filled = {k: (own_parts if k < 6 else other_parts)[k] for k in range(10)}
    own_parts = call(own_x, own_u, own_ranks, 0, filled, short, short)
    own_parts, other_got = tie(own_parts, other_got)
    other_sums = sum_cores(other_parts[2], other_got, S)
    come, own_x = sum_first(other_sums, S, own_x)
    other_out_got = swap(after(other_parts[1], other_got), "seq", S, 1)
    own_parts = call(
        own_x, own_u, own_ranks, 0, dict(enumerate(own_parts)), 2 * short, pairs - 2 * short
    )
    own_parts, come, other_out_got = tie(own_parts, come, other_out_got)
    logits = matmul(second_low, full_router)
    router_probs = jax.nn.softmax(logits, axis=-1)

    x_rows, u_rows, in_grads, hidden_gate = own_parts[6:]
    in_terms, down_terms = {}, {}

    def in_products(r, *dep):
        in_terms[r] = products(
            x_rows, after(in_grads, dep), in_part, r, F, f_at, "in_products"
        )

    odd = [r for r in range(F) if r & 1]
    far_odd = [r for r in odd if r & half_f]
    near_odd = [r for r in odd if not r & half_f]

    def to_home(even, odd):
        return absolute(jnp.concatenate([even, odd], 0).transpose(0, 2, 1), s)

    gate_grads = jnp.stack(
        [to_home(own_parts[4], own_parts[5]), to_home(other_parts[4], other_parts[5])], 1
    ).reshape(S, -1)
    singles, other_total = sum_more(other_sums, come, S)
    come = sum_last(singles, S)
    own_got = swap(own_parts[3], "seq", S, 1)
    for r in far_odd:
        in_products(r)
    gate_grads = lax.all_to_all(gate_grads, "seq", split_axis=0, concat_axis=0, tiled=True)
    come, own_got, in_terms, gate_grads = tie(come, own_got, in_terms, gate_grads)
    sent = {r: quarters(in_terms[r], 1) for r in far_odd}

    def send_in(n, *dep):
        return {r: swap(after(sent[r][n], dep), "fsdp", F, 1) for r in sent}

    def down_products(r, dep):
        down_terms[r] = products(
            after(hidden_gate, dep), u_rows, down_part, r, half_f, f_at, "down_products"
        )

    gate_grads = gate_grads.reshape(S, 2, T * experts)
    other_rows = add_all(other_total, come).astype(BF16)
    own_sums = sum_cores(own_parts[2], after(own_got, other_rows), S)
    come, other_rows = sum_first(own_sums, S, other_rows)
    back = [far_swap(other_rows[:half_rows])]
    far_got = [send_in(0, other_rows)]
    own_out_got = swap(after(own_parts[1], own_got), "seq", S, 1)
    for r in far_odd:
        in_products(r ^ 1, other_rows)
    for r in range(1, half_f, 2):
        down_products(r, other_rows)
    come, back[0], far_got[0], in_terms, down_terms, own_out_got = tie(
        come, back[0], far_got[0], in_terms, down_terms, own_out_got
    )
    partner_grads = far_swap(gate_grads[:, 1], come)
    back.append(far_swap(other_rows[half_rows:], come))
    singles, own_total = sum_more(own_sums, come, S)
    come = sum_last(singles, S)
    far_got.append(send_in(1, singles))
    down_sent = {
        r: [down_terms[r][:, : down_part // 2], down_terms[r][:, down_part // 2 :]]
        for r in range(1, half_f, 2)
    }

    def send_down(n, *dep):
        return {r: swap(after(down_sent[r][n], dep), "fsdp", F, 1) for r in down_sent}

    for r in near_odd:
        in_products(r, singles)
    come, back[1], far_got[1], in_terms, partner_grads = tie(
        come, back[1], far_got[1], in_terms, partner_grads
    )
    gate_grads = gate_grads[:, 0] + partner_grads
    gate_grads = gate_grads.reshape(S, T, experts).transpose(1, 0, 2).reshape(T, E)
    row_grads = add_all(own_total, come) + jnp.concatenate(back, 0).astype(F32)

    upstream = upstream_low.astype(F32)
    logit_grads = router_probs * (
        gate_grads - jnp.sum(router_probs * gate_grads, axis=-1, keepdims=True)
    )
    router_wide = full_router.astype(F32)
    second_grads = row_grads + jnp.dot(logit_grads, router_wide.T, precision=HIGHEST)
    pulled = second_grads * gain_moe
    residual_grads = upstream + moe_factor * (
        pulled - residual_n * jnp.mean(pulled * residual_n, axis=-1, keepdims=True)
    )
    branch_low = residual_grads.astype(BF16)

    def sum_near(terms):
        mask = 2
        while mask < half_f:
            terms = {
                r: terms[r] + swap(terms[r | mask].astype(BF16), "fsdp", F, mask).astype(F32)
                for r in terms
                if not r & mask
            }
            mask *= 2
        (total,) = terms.values()
        return total

    def far_sum(n, *dep):
        terms = {
            r ^ 1: quarters(in_terms[r ^ 1], 1)[n].astype(F32) + far_got[n][r].astype(F32)
            for r in far_odd
        }
        return far_swap(sum_near(terms).astype(BF16), *dep)

    branch_first = gather_first(branch_low, S)
    far_sums = [far_sum(0, branch_low)]
    far_got.append(send_in(2, branch_low))
    for r in range(0, half_f, 2):
        down_products(r, branch_low)
    branch_first, far_sums[0], far_got[2], down_terms = tie(
        branch_first, far_sums[0], far_got[2], down_terms
    )
    branch_more = gather_more(branch_low, branch_first, S)
    far_sums.append(far_sum(1, branch_first))
    far_got.append(send_in(3, branch_first))
    branch_even, branch_odd = gather_end(branch_low, branch_first, branch_more, S)

    head_grads = jnp.concatenate(
        [matmul_t(branch_even, own_output), matmul_t(branch_odd, own_output)], 0
    ).astype(BF16)
    head_grads = absolute(head_grads.reshape(S, T, C), s).reshape(L, C)
    head_grads, far_sums[1], far_got[3] = tie(head_grads, far_sums[1], far_got[3])
    far_sums.append(far_sum(2, head_grads))
    down_got = [send_down(0, head_grads)]
    other_out_sums = sum_cores(other_parts[0], after(other_out_got, head_grads), S)
    come, head_grads = sum_first(other_out_sums, S, head_grads)
    query_back, key_back, value_back = attention_backward(
        query_low, key_low, value_low, head_grads, lse, seg_row, seg_col
    )
    query_back, key_back, value_back, far_sums[2], down_got[0], come = tie(
        query_back, key_back, value_back, far_sums[2], down_got[0], come
    )

    singles, other_total = sum_more(other_out_sums, come, S)
    come = sum_last(singles, S)
    far_sums.append(far_sum(3, query_back))
    attended_rel = relative(after(attended_blocks, singles), s).reshape(2, L // 2, C)
    output_term = t_matmul(attended_rel[0], branch_even) + t_matmul(attended_rel[1], branch_odd)
    output_term = by_index(output_term.astype(BF16).reshape(F, part, D), f, F)
    output_got = swap(output_term[: F // 2], "fsdp", F, 1)
    value_rel = relative(value_back.reshape(S, T, C), s).reshape(2, L // 2, C)

    def weight_term(even, odd):
        term = (t_matmul(normed_even, even) + t_matmul(normed_odd, odd)).astype(BF16)
        return by_index(term.reshape(S, F, part, -1).transpose(1, 0, 2, 3), f, F)

    means, gain_term = rope_means(
        query_back, key_back, query_pre, key_pre, squares, head_gain, cosine, sine
    )
    means = sum_all(means, "seq", S)
    value_term = weight_term(value_rel[0], value_rel[1])
    means, come, far_sums[3], output_got, value_term = tie(
        means, come, far_sums[3], output_got, value_term
    )
    other_outs = add_all(other_total, come).astype(BF16)
    outs_back = [far_swap(other_outs[:half_rows])]
    value_got = swap(value_term[: F // 2], "fsdp", F, 1)
    down_got.append(send_down(1, means))
    pre_rel = rope_back(
        (query_back, key_back, value_back),
        query_pre,
        key_pre,
        squares,
        means,
        head_gain,
        cosine,
        sine,
        me,
        T,
    ).reshape(2, L // 2, 3 * C)
    normed_got = swap(matmul_t(pre_rel[1], w_qkv).astype(BF16), "seq", S, 1)
    normed_kept = matmul_t(pre_rel[0], w_qkv).astype(BF16)
    normed_got, normed_kept, value_got, outs_back[0], down_got[1] = tie(
        normed_got, normed_kept, value_got, outs_back[0], down_got[1]
    )

    normed_sums = sum_cores(normed_kept, normed_got, S)
    come = sum_first(normed_sums, S)
    value_sum = sum_rest(sum_even(value_term, value_got, F), F)
    turned_term = weight_term(
        after(pre_rel[0][:, : 2 * C], normed_got), after(pre_rel[1][:, : 2 * C], normed_got)
    )
    late_grads, late_logits = after(second_grads, normed_got), after(logit_grads, normed_got)
    router_term = jnp.dot(second_low.astype(F32).T, late_logits, precision=HIGHEST)
    moe_gain_term = jnp.sum(late_grads * residual_n, axis=0)
    gain_terms = jnp.concatenate(
        [router_term.reshape(S * F, part * E), moe_gain_term.reshape(S * F, part)], 1
    )
    gain_terms = in_relative(gain_terms, S, F, s, f).reshape(S, F, -1)
    head_terms = gain_term.reshape(2, F, part).transpose(1, 0, 2).reshape(F, 2 * part)
    head_terms = in_relative(head_terms, 1, F, 0, f)
    gain_terms = jnp.concatenate([gain_terms.transpose(1, 0, 2).reshape(F, -1), head_terms], 1)
    own_out_sums = sum_cores(own_parts[0], after(own_out_got, normed_got), S)
    own_come = sum_first(own_out_sums, S)
    come, turned_term, value_sum, gain_terms, own_come = tie(
        come, turned_term, value_sum, gain_terms, own_come
    )
    turned_got = swap(turned_term[: F // 2], "fsdp", F, 1)
    singles, normed_total = sum_more(normed_sums, come, S)
    come = sum_last(singles, S)
    gain_got = swap(gain_terms[F // 2 :], "fsdp", F, half_f)
    for r in near_odd:
        in_products(r ^ 1, turned_term)
    outs_back.append(far_swap(other_outs[half_rows:], turned_term))
    come, turned_got, gain_got, in_terms, outs_back[1] = tie(
        come, turned_got, gain_got, in_terms, outs_back[1]
    )
    gain_terms = gain_terms[: F // 2] + gain_got
    normed_grads = add_all(normed_total, come)
    turned_sum = sum_rest(sum_even(turned_term, turned_got, F), F)
    middle = in_part // 2

    def send_near(first, dep):
        return {
            r: swap(after(in_terms[r][:, first : first + middle], dep), "fsdp", F, 1)
            for r in near_odd
        }

    near_got = [send_near(0, turned_got)]
    gain_terms = halve(after(gain_terms, turned_got), "fsdp", F, half_f // 2)
    singles, own_total = sum_more(after(own_out_sums, turned_got), own_come, S)
    own_come = sum_last(singles, S)
    turned_sum, own_come, near_got[0], gain_terms = tie(
        turned_sum, own_come, near_got[0], gain_terms
    )
    near_got.append(send_near(middle, turned_sum))
    count = S * part * (E + 1)
    head_terms = gain_terms[0, count:]
    gain_terms = halve(gain_terms[0, :count].reshape(S, -1), "seq", S, S // 2)[0]
    own_outs = add_all(own_total, own_come)
    outs_back = jnp.concatenate(outs_back, 0).astype(F32)
    mixed = (residual + own_outs + outs_back).astype(BF16)[None]

    qkv_term = jnp.concatenate([turned_sum, value_sum], -1).astype(BF16)
    qkv_term = lax.all_to_all(qkv_term, "seq", split_axis=0, concat_axis=0, tiled=True)
    qkv_term = [
        qkv_term[:, :, j * C : (j + 1) * C].transpose(1, 0, 2).reshape(part, D).astype(F32)
        for j in range(3)
    ]
    grad_output = sum_rest(sum_even(output_term, output_got, F), F)

    near_got = {r: jnp.concatenate([got[r] for got in near_got], 1) for r in near_odd}
    own_term = sum_near(
        {r ^ 1: in_terms[r ^ 1].astype(F32) + near_got[r].astype(F32) for r in near_odd}
    )
    far_term = jnp.concatenate(far_sums, 1).astype(F32)
    first_half = half_at == 0
    lower = jnp.where(first_half, own_term, far_term)
    upper = jnp.where(first_half, far_term, own_term)
    grad_gate, grad_up = (
        jnp.concatenate([lower[..., at], upper[..., at]], axis=-1)
        for at in (slice(0, hidden_half), slice(hidden_half, 2 * hidden_half))
    )
    down_got = after(down_got, turned_sum)
    down_got = {r: jnp.concatenate([got[r] for got in down_got], 1) for r in down_sent}
    grad_down = sum_near(
        {r ^ 1: down_terms[r ^ 1].astype(F32) + down_got[r].astype(F32) for r in down_sent}
    )

    attn_factor = rms_factor(inputs)
    inputs_n = inputs * attn_factor
    attn_pulled = normed_grads * gain_attn
    grad_tokens = residual_grads + attn_factor * (
        attn_pulled - inputs_n * jnp.mean(attn_pulled * inputs_n, axis=-1, keepdims=True)
    )
    grad_attn_gain = sum(
        jnp.sum(term * weight.astype(F32), axis=1)
        for term, weight in zip(qkv_term, (w_query, w_key, w_value))
    ) / attn_gain.astype(F32)
    return (
        mixed,
        grad_tokens[None],
        qkv_term[0],
        qkv_term[1],
        qkv_term[2],
        grad_output,
        gain_terms[: part * E].reshape(part, E),
        grad_attn_gain,
        gain_terms[part * E :],
        head_terms[:part],
        head_terms[part:],
        grad_gate,
        grad_up,
        grad_down,
    )


def solution(mesh):
    tokens_spec = P("fsdp", "seq", None)
    rows_spec = P(("seq", "fsdp"), None)
    gain_spec = P(("seq", "fsdp"))
    expert_spec = P("seq", "fsdp", None)
    in_specs = (
        (tokens_spec, P("fsdp", None), tokens_spec, tokens_spec)
        + (rows_spec,) * 5
        + (gain_spec,) * 4
        + (expert_spec,) * 3
    )
    out_specs = (tokens_spec,) * 2 + (rows_spec,) * 5 + (gain_spec,) * 4 + (expert_spec,) * 3
    return jax.shard_map(
        partial(per_device, mesh.shape["seq"], mesh.shape["fsdp"]),
        mesh=mesh,
        in_specs=in_specs,
        out_specs=out_specs,
        check_vma=False,
    )
```

```python
from functools import partial

import jax
import jax.numpy as jnp
from jax import lax
from jax.experimental import pallas as pl
from jax.experimental.pallas import tpu as pltpu
from jax.sharding import PartitionSpec as P

D = 2048
H = 16
DH = 128
E = 16
WINDOW = 1024
CAP = 144

EPSILON = 1e-06
ROPE_BASE = 50000.0
HIGHEST = lax.Precision.HIGHEST
BF16 = jnp.bfloat16
F32 = jnp.float32
MIB = 1024 * 1024


def matmul(left, right):
    return jnp.dot(left, right, preferred_element_type=F32)


def matmul_t(left, right):
    return lax.dot_general(left, right, (((1,), (1,)), ((), ())), preferred_element_type=F32)


def t_matmul(left, right):
    return lax.dot_general(left, right, (((0,), (0,)), ((), ())), preferred_element_type=F32)


def rms_factor(values):
    return lax.rsqrt(jnp.mean(values * values, axis=-1, keepdims=True) + EPSILON)


def swap(values, axis, size, mask):
    return lax.ppermute(values, axis, [(i, i ^ mask) for i in range(size)])


def high_bit(number):
    return 1 << (number.bit_length() - 1)


def low_bit(number):
    return number & -number


def after(values, *others):
    return lax.optimization_barrier((values, others))[0]


def tie(*values):
    return lax.optimization_barrier(values)


def gather_first(values, size):
    return {r: swap(values, "seq", size, r) for r in range(2, size, 2) if r == low_bit(r)}


def gather_more(values, first, size):
    rows = values.shape[0] // 2
    pieces = dict(first)
    for r in range(2, size, 2):
        if r not in pieces:
            up, down = high_bit(r), low_bit(r)
            upper, lower = pieces[r ^ up], pieces[r ^ down]
            upper = upper[0] if isinstance(upper, tuple) else upper[:rows]
            lower = lower[1] if isinstance(lower, tuple) else lower[rows:]
            pieces[r] = (swap(upper, "seq", size, up), swap(lower, "seq", size, down))
    return {r: piece for r, piece in pieces.items() if r not in first}


def gather_end(values, first, more, size):
    blocks = [values]
    for r in range(2, size, 2):
        blocks.extend([first[r]] if r in first else more[r])
    even = jnp.concatenate(blocks, 0)
    return even, swap(even, "seq", size, 1)


def relative(blocks, me):
    size = blocks.shape[0]
    order = list(range(0, size, 2)) + list(range(1, size, 2))
    return jnp.concatenate([lax.dynamic_slice_in_dim(blocks, me ^ r, 1, 0) for r in order], 0)


def absolute(blocks, me):
    size = blocks.shape[0]
    places = [((me ^ j) // 2) + ((me ^ j) % 2) * (size // 2) for j in range(size)]
    return jnp.concatenate([lax.dynamic_slice_in_dim(blocks, at, 1, 0) for at in places], 0)


def sum_cores(even, got, size):
    rows = even.shape[0] // (size // 2)
    half = rows // 2

    def part(r, first):
        at = slice(r // 2 * rows + first, r // 2 * rows + first + half)
        return even[at].astype(F32) + got[at].astype(F32)

    return {r: [part(r, 0), part(r, half)] for r in range(0, size, 2)}


def sum_first(sums, size, held=None):
    sums = {r: list(value) for r, value in sums.items()}
    come = {}
    for r in range(size - 2, 0, -2):
        if r != low_bit(r):
            up, down = high_bit(r), low_bit(r)
            for (goal, k, _), piece in come.items():
                if goal == r:
                    sums[r][k] += piece.astype(F32)
            upper, lower, held = tie(sums[r][0].astype(BF16), sums[r][1].astype(BF16), held)
            come[r ^ up, 0, r] = swap(upper, "seq", size, up)
            come[r ^ down, 1, r] = swap(lower, "seq", size, down)
    return come if held is None else (come, held)


def sum_more(sums, come, size):
    sums = {r: list(value) for r, value in sums.items() if r == 0 or r == low_bit(r)}
    for (goal, k, _), piece in come.items():
        if goal in sums:
            sums[goal][k] += piece.astype(F32)
    singles = {
        r: jnp.concatenate([v.astype(BF16) for v in value], 0) for r, value in sums.items() if r
    }
    return tie(singles)[0], jnp.concatenate(sums[0], 0)


def sum_last(singles, size):
    return {r: swap(value, "seq", size, r) for r, value in singles.items()}


def add_all(total, pieces):
    for piece in pieces.values():
        total += piece.astype(F32)
    return total


def quarters(values, axis):
    step = values.shape[axis] // 4
    return [lax.slice_in_dim(values, k * step, (k + 1) * step, axis=axis) for k in range(4)]


def sum_all(values, axis, size):
    mask = 1
    while mask < size:
        values = values + swap(values, axis, size, mask)
        mask *= 2
    return values


def fsdp_pieces(values, size):
    pieces = {0: values}
    for r in range(1, size):
        low = low_bit(r)
        pieces[r] = swap(pieces[r ^ low], "fsdp", size, low)
    return pieces


def place_fsdp(pieces, me, axis):
    size = len(pieces)
    shape = pieces[0].shape
    whole = jnp.zeros(shape[:axis] + (size,) + shape[axis:], pieces[0].dtype)
    for r, piece in pieces.items():
        whole = lax.dynamic_update_slice_in_dim(whole, jnp.expand_dims(piece, axis), me ^ r, axis)
    return whole


def near_pieces(values, size):
    pieces = {0: values}
    for r in range(1, size // 2):
        up = high_bit(r)
        pieces[r] = swap(pieces[r ^ up], "fsdp", size, up)
    return pieces


def double(values, axis, size):
    mask = 1
    while mask < size:
        values = jnp.concatenate([values, swap(values, axis, size, mask)], 0)
        mask *= 2
    return values


def halve(values, axis, size, mask):
    while mask:
        half = values.shape[0] // 2
        values = values[:half] + swap(values[half:], axis, size, mask)
        mask //= 2
    return values


def relative_pick(seq_size, fsdp_size, s, f):
    index = jnp.arange(seq_size * fsdp_size, dtype=jnp.int32)
    source = ((index // fsdp_size) ^ s) * fsdp_size + ((index % fsdp_size) ^ f)
    return source[:, None] == index[None, :]


def in_order(values, seq_size, fsdp_size, s, f):
    pick = relative_pick(seq_size, fsdp_size, s, f).astype(values.dtype)
    return matmul(pick, values).astype(values.dtype)


def in_relative(values, seq_size, fsdp_size, s, f):
    pick = relative_pick(seq_size, fsdp_size, s, f).astype(F32)
    return jnp.dot(pick, values, precision=HIGHEST)


def by_index(partial_sum, me, size):
    order = [r for r in range(size) if r & 1] + [r for r in range(size) if not r & 1]
    return jnp.concatenate([lax.dynamic_slice_in_dim(partial_sum, me ^ r, 1, 0) for r in order], 0)


def sum_even(stacked, got, size):
    return (stacked[size // 2 :].astype(F32) + got.astype(F32)).astype(BF16)


def sum_rest(stacked, size):
    mask = 2
    values = stacked.astype(F32)
    while mask < size:
        count = values.shape[0] // 2
        pairs = values.reshape((count, 2) + values.shape[1:])
        got = swap(pairs[:, 1].astype(BF16), "fsdp", size, mask)
        values = pairs[:, 0] + got.astype(F32)
        mask *= 2
    return values[0]


def allowed_keys(seg_row, seg_col, first_query, first_key, rows, span, half_window):
    query_at = first_query + lax.broadcasted_iota(jnp.int32, (span, rows), 1)
    key_at = first_key + lax.broadcasted_iota(jnp.int32, (span, rows), 0)
    return (jnp.abs(query_at - key_at) <= half_window) & (seg_col == seg_row)


def first_key_of(block, rows, span, length):
    start = jnp.clip(block * rows - (span - rows) // 2, 0, length - span)
    return pl.multiple_of(start, rows)


def forward_kernel(span, q_ref, k_ref, v_ref, seg_row_ref, seg_col_ref, o_ref, lse_ref):
    block = pl.program_id(1)
    rows, length = q_ref.shape[0], k_ref.shape[0]
    first_key = first_key_of(block, rows, span, length)
    keys = k_ref[pl.ds(first_key, span), :]
    values = v_ref[pl.ds(first_key, span), :]
    scores = matmul_t(keys, q_ref[...]) * DH ** (-0.5)
    allowed = allowed_keys(
        seg_row_ref[...],
        seg_col_ref[pl.ds(first_key, span), :],
        block * rows,
        first_key,
        rows,
        span,
        WINDOW // 2,
    )
    scores = jnp.where(allowed, scores, -1e30)
    peak = jnp.max(scores, axis=0, keepdims=True)
    expos = jnp.exp(scores - peak)
    totals = jnp.sum(expos, axis=0, keepdims=True)
    probs = (expos * (1.0 / totals)).astype(BF16)
    o_ref[...] = t_matmul(values, probs).T.astype(BF16)
    lse_ref[...] = (peak + jnp.log(totals))[None]


def backward_kernel(
    span,
    q_ref,
    k_ref,
    v_ref,
    do_ref,
    lse_ref,
    seg_row_ref,
    seg_col_ref,
    dq_ref,
    dk_ref,
    dv_ref,
    dk_sum,
    dv_sum,
):
    block = pl.program_id(1)
    rows, length = q_ref.shape[0], k_ref.shape[0]

    @pl.when(block == 0)
    def _():
        dk_sum[...] = jnp.zeros_like(dk_sum)
        dv_sum[...] = jnp.zeros_like(dv_sum)

    first_key = first_key_of(block, rows, span, length)
    at = pl.ds(first_key, span)
    keys = k_ref[at, :]
    values = v_ref[at, :]
    queries = q_ref[...]
    grads = do_ref[...]
    scores = matmul_t(keys, queries) * DH ** (-0.5)
    allowed = allowed_keys(
        seg_row_ref[...],
        seg_col_ref[at, :],
        block * rows,
        first_key,
        rows,
        span,
        WINDOW // 2,
    )
    probs = jnp.where(allowed, jnp.exp(scores - lse_ref[0]), 0.0)
    dv_sum[at, :] += matmul(probs.astype(BF16), grads)
    prob_grads = matmul_t(values, grads)
    center = jnp.sum(probs * prob_grads, axis=0, keepdims=True)
    score_grads = (probs * (prob_grads - center)).astype(BF16)
    dk_sum[at, :] += matmul(score_grads, queries)
    dq_ref[...] = (t_matmul(keys, score_grads) * DH ** (-0.5)).T.astype(BF16)

    @pl.when(block == length // rows - 1)
    def _():
        dk_ref[...] = (dk_sum[...] * DH ** (-0.5)).astype(BF16)
        dv_ref[...] = dv_sum[...].astype(BF16)


def attention_sizes(length):
    rows = 256
    return rows, min(length, rows + WINDOW)


def attention_forward(queries, keys, values, seg_row, seg_col):
    length, columns = queries.shape
    heads = columns // DH
    rows, span = attention_sizes(length)
    block = pl.BlockSpec((rows, DH), lambda h, i: (i, h))
    whole = pl.BlockSpec((length, DH), lambda h, i: (0, h))
    return pl.pallas_call(
        partial(forward_kernel, span),
        grid=(heads, length // rows),
        in_specs=[
            block,
            whole,
            whole,
            pl.BlockSpec((1, rows), lambda h, i: (0, i)),
            pl.BlockSpec((length, 1), lambda h, i: (0, 0)),
        ],
        out_specs=[block, pl.BlockSpec((1, 1, rows), lambda h, i: (h, 0, i))],
        out_shape=[
            jax.ShapeDtypeStruct((length, columns), BF16),
            jax.ShapeDtypeStruct((heads, 1, length), F32),
        ],
        compiler_params=pltpu.CompilerParams(vmem_limit_bytes=48 * MIB),
        cost_estimate=pl.CostEstimate(
            flops=4 * heads * length * span * DH,
            bytes_accessed=8 * length * columns,
            transcendentals=heads * length * span,
        ),
        name="attend",
    )(queries, keys, values, seg_row, seg_col)


def attention_backward(queries, keys, values, grads, lse, seg_row, seg_col):
    length, columns = queries.shape
    heads = columns // DH
    rows, span = attention_sizes(length)
    block = pl.BlockSpec((rows, DH), lambda h, i: (i, h))
    whole = pl.BlockSpec((length, DH), lambda h, i: (0, h))
    shape = jax.ShapeDtypeStruct((length, columns), BF16)
    return pl.pallas_call(
        partial(backward_kernel, span),
        grid=(heads, length // rows),
        in_specs=[
            block,
            whole,
            whole,
            block,
            pl.BlockSpec((1, 1, rows), lambda h, i: (h, 0, i)),
            pl.BlockSpec((1, rows), lambda h, i: (0, i)),
            pl.BlockSpec((length, 1), lambda h, i: (0, 0)),
        ],
        out_specs=[block, whole, whole],
        out_shape=[shape, shape, shape],
        scratch_shapes=[pltpu.VMEM((length, DH), F32), pltpu.VMEM((length, DH), F32)],
        compiler_params=pltpu.CompilerParams(vmem_limit_bytes=48 * MIB),
        cost_estimate=pl.CostEstimate(
            flops=10 * heads * length * span * DH,
            bytes_accessed=14 * length * columns,
            transcendentals=heads * length * span,
        ),
        name="attend_back",
    )(queries, keys, values, grads, lse, seg_row, seg_col)


def qkv_kernel(
    me_ref,
    even_ref,
    odd_ref,
    weight_ref,
    gain_ref,
    normed_even_ref,
    normed_odd_ref,
    q_ref,
    k_ref,
    v_ref,
    square_ref,
):
    turned = me_ref[0] % 2
    rows = even_ref.shape[0]
    columns = q_ref.shape[1]
    for k, (token_ref, normed_ref) in enumerate(
        ((even_ref, normed_even_ref), (odd_ref, normed_odd_ref))
    ):
        at = pl.ds(pl.multiple_of((turned ^ k) * rows, rows), rows)
        wide = token_ref[...].astype(F32)
        normed = (wide * rms_factor(wide) * gain_ref[...]).astype(BF16)
        normed_ref[...] = normed
        pre = matmul(normed, weight_ref[...])
        q_ref[at, :] = pre[:, :columns]
        k_ref[at, :] = pre[:, columns : 2 * columns]
        v_ref[at, :] = pre[:, 2 * columns :].astype(BF16)
        for j in range(2):
            squares = 0.0
            for c in range(j * columns, (j + 1) * columns, DH):
                squares += pre[:, c : c + DH] * pre[:, c : c + DH]
            square_ref[j : j + 1, at] = jnp.sum(squares.T, axis=0, keepdims=True)


def project(even, odd, weight, gain, me, rows):
    pairs = even.shape[0] // rows
    length = 2 * even.shape[0]
    depth, columns = weight.shape[0], weight.shape[1] // 3
    token = pl.BlockSpec((rows, depth), lambda i, me: (i, 0))

    def placed(shape):
        return pl.BlockSpec(shape, lambda i, me: (i ^ (me[0] // 2), 0))

    head = jax.ShapeDtypeStruct((length, columns), F32)
    return pl.pallas_call(
        qkv_kernel,
        grid_spec=pltpu.PrefetchScalarGridSpec(
            num_scalar_prefetch=1,
            grid=(pairs,),
            in_specs=[
                token,
                token,
                pl.BlockSpec(weight.shape, lambda i, me: (0, 0)),
                pl.BlockSpec((1, depth), lambda i, me: (0, 0)),
            ],
            out_specs=[
                token,
                token,
                placed((2 * rows, columns)),
                placed((2 * rows, columns)),
                placed((2 * rows, columns)),
                pl.BlockSpec((2, 2 * rows), lambda i, me: (0, i ^ (me[0] // 2))),
            ],
        ),
        out_shape=[
            jax.ShapeDtypeStruct((length // 2, depth), BF16),
            jax.ShapeDtypeStruct((length // 2, depth), BF16),
            head,
            head,
            jax.ShapeDtypeStruct((length, columns), BF16),
            jax.ShapeDtypeStruct((2, length), F32),
        ],
        compiler_params=pltpu.CompilerParams(vmem_limit_bytes=48 * MIB),
        cost_estimate=pl.CostEstimate(
            flops=6 * length * depth * columns,
            bytes_accessed=length * (4 * depth + 10 * columns) + 6 * depth * columns,
            transcendentals=length,
        ),
        name="project",
    )(me, even, odd, weight, gain)


def split_kernel(q_ref, k_ref, v_ref, out_ref):
    columns = q_ref.shape[1]
    for j, ref in enumerate((q_ref, k_ref, v_ref)):
        out_ref[0, :, j * columns : (j + 1) * columns] = ref[...]


def split_heads(w_query, w_key, w_value, parts):
    rows, columns = w_query.shape[0], w_query.shape[1] // parts
    block = pl.BlockSpec((rows, columns), lambda i: (0, i))
    return pl.pallas_call(
        split_kernel,
        grid=(parts,),
        in_specs=[block] * 3,
        out_specs=pl.BlockSpec((1, rows, 3 * columns), lambda i: (i, 0, 0)),
        out_shape=jax.ShapeDtypeStruct((parts, rows, 3 * columns), BF16),
        name="split_heads",
    )(w_query, w_key, w_value)


def spread(row, columns):
    return jnp.broadcast_to(row, (columns, row.shape[1])).T


def factor_of(square_row):
    return lax.rsqrt(square_row / D + EPSILON)


def turn(values, cosine, sine):
    return values * cosine + pltpu.roll(values, DH // 2, 1) * sine


def rope_kernel(q_ref, k_ref, square_ref, gain_ref, cos_ref, sin_ref, q_out, k_out):
    cosine, sine = cos_ref[...], sin_ref[...]
    for j, (pre_ref, out_ref) in enumerate(((q_ref, q_out), (k_ref, k_out))):
        factor = spread(factor_of(square_ref[j : j + 1, :]), DH)
        for c in range(0, pre_ref.shape[1], DH):
            at = slice(c, c + DH)
            normed = pre_ref[:, at] * factor * gain_ref[j : j + 1, at]
            out_ref[:, at] = turn(normed, cosine, sine).astype(BF16)


def rope(query_pre, key_pre, squares, gains, cosine, sine):
    length, columns = query_pre.shape
    rows = min(512, length)
    block = pl.BlockSpec((rows, columns), lambda i: (i, 0))
    table = pl.BlockSpec((rows, DH), lambda i: (i, 0))
    return pl.pallas_call(
        rope_kernel,
        grid=(length // rows,),
        in_specs=[
            block,
            block,
            pl.BlockSpec((2, rows), lambda i: (0, i)),
            pl.BlockSpec((2, columns), lambda i: (0, 0)),
            table,
            table,
        ],
        out_specs=[block, block],
        out_shape=[jax.ShapeDtypeStruct((length, columns), BF16)] * 2,
        compiler_params=pltpu.CompilerParams(vmem_limit_bytes=32 * MIB),
        name="rope",
    )(query_pre, key_pre, squares, gains, cosine, sine)


def pulled_of(grad_ref, pre_ref, factor, gain_ref, cosine, sine, j, at):
    turned = turn(grad_ref[:, at].astype(F32), cosine, -sine)
    return turned, turned * gain_ref[j : j + 1, at], pre_ref[:, at] * factor


def rope_mean_kernel(
    dq_ref, dk_ref, q_ref, k_ref, square_ref, gain_ref, cos_ref, sin_ref, mean_ref, term_ref
):
    @pl.when(pl.program_id(0) == 0)
    def _():
        term_ref[...] = jnp.zeros_like(term_ref)

    cosine, sine = cos_ref[...], sin_ref[...]
    for j, (grad_ref, pre_ref) in enumerate(((dq_ref, q_ref), (dk_ref, k_ref))):
        factor = spread(factor_of(square_ref[j : j + 1, :]), DH)
        total = 0.0
        for c in range(0, pre_ref.shape[1], DH):
            at = slice(c, c + DH)
            turned, pulled, normed = pulled_of(
                grad_ref, pre_ref, factor, gain_ref, cosine, sine, j, at
            )
            term_ref[j : j + 1, at] += jnp.sum(turned * normed, axis=0, keepdims=True)
            total += pulled * normed
        mean_ref[j : j + 1, :] = jnp.sum(total.T, axis=0, keepdims=True)


def rope_means(query_back, key_back, query_pre, key_pre, squares, gains, cosine, sine):
    length, columns = query_pre.shape
    rows = min(512, length)
    block = pl.BlockSpec((rows, columns), lambda i: (i, 0))
    table = pl.BlockSpec((rows, DH), lambda i: (i, 0))
    row = pl.BlockSpec((2, rows), lambda i: (0, i))
    fixed = pl.BlockSpec((2, columns), lambda i: (0, 0))
    return pl.pallas_call(
        rope_mean_kernel,
        grid=(length // rows,),
        in_specs=[block, block, block, block, row, fixed, table, table],
        out_specs=[row, fixed],
        out_shape=[
            jax.ShapeDtypeStruct((2, length), F32),
            jax.ShapeDtypeStruct((2, columns), F32),
        ],
        compiler_params=pltpu.CompilerParams(vmem_limit_bytes=32 * MIB),
        name="rope_means",
    )(query_back, key_back, query_pre, key_pre, squares, gains, cosine, sine)


def rope_back_kernel(
    me_ref,
    dq_ref,
    dk_ref,
    dv_ref,
    q_ref,
    k_ref,
    square_ref,
    mean_ref,
    gain_ref,
    cos_ref,
    sin_ref,
    out_ref,
):
    cosine, sine = cos_ref[...], sin_ref[...]
    columns = q_ref.shape[1]
    for j, (grad_ref, pre_ref) in enumerate(((dq_ref, q_ref), (dk_ref, k_ref))):
        factor = spread(factor_of(square_ref[j : j + 1, :]), DH)
        mean = spread(mean_ref[j : j + 1, :] / D, DH)
        for c in range(0, columns, DH):
            at = slice(c, c + DH)
            _, pulled, normed = pulled_of(grad_ref, pre_ref, factor, gain_ref, cosine, sine, j, at)
            out_ref[:, j * columns + c : j * columns + c + DH] = (
                factor * (pulled - normed * mean)
            ).astype(BF16)
    out_ref[:, 2 * columns :] = dv_ref[...]


def rope_back(grads, query_pre, key_pre, squares, means, gains, cosine, sine, me, rows):
    length, columns = query_pre.shape
    half = length // rows // 2

    def source(p, me):
        return me[0] ^ (p % half * 2 + p // half)

    block = pl.BlockSpec((rows, columns), lambda p, me: (source(p, me), 0))
    table = pl.BlockSpec((rows, DH), lambda p, me: (source(p, me), 0))
    row = pl.BlockSpec((2, rows), lambda p, me: (0, source(p, me)))
    return pl.pallas_call(
        rope_back_kernel,
        grid_spec=pltpu.PrefetchScalarGridSpec(
            num_scalar_prefetch=1,
            grid=(2 * half,),
            in_specs=[block] * 5
            + [row, row, pl.BlockSpec((2, columns), lambda p, me: (0, 0)), table, table],
            out_specs=pl.BlockSpec((rows, 3 * columns), lambda p, me: (p, 0)),
        ),
        out_shape=jax.ShapeDtypeStruct((length, 3 * columns), BF16),
        compiler_params=pltpu.CompilerParams(vmem_limit_bytes=32 * MIB),
        name="rope_back",
    )(me, *grads, query_pre, key_pre, squares, means, gains, cosine, sine)


def expert_kernel(
    in_places, down_places, first_ref, xa_ref, xb_ref, ua_ref, ub_ref, ra_ref, rb_ref, router_ref, *refs
):
    weight_refs = refs[: len(in_places) + len(down_places)]
    (ya_ref, yb_ref, za_ref, zb_ref, ga_ref, gb_ref, xc_ref, uc_ref, dg_ref, hid_ref) = refs[-13:-3]
    wi_ref, wd_ref, sems = refs[-3:]
    experts, _, hidden = hid_ref.shape
    rows = xa_ref.shape[0]

    @pl.when(pl.program_id(0) == 0)
    def _():
        copies = []
        for n, (ref, (r, first, part)) in enumerate(zip(weight_refs, in_places + down_places)):
            goal = wi_ref if n < len(in_places) else wd_ref
            place = lax.rem(first_ref[1] ^ r, goal.shape[1] // part)
            at = pl.ds(pl.multiple_of(place * part + first, ref.shape[1]), ref.shape[1])
            copies.append(pltpu.make_async_copy(ref, goal.at[:, at, :], sems.at[n]))
        for copy in copies:
            copy.start()
        for copy in copies:
            copy.wait()

    slot = lax.broadcasted_iota(jnp.int32, (CAP, rows), 0)
    blocks = (
        (xa_ref, ua_ref, ra_ref, ya_ref, za_ref, ga_ref),
        (xb_ref, ub_ref, rb_ref, yb_ref, zb_ref, gb_ref),
    )
    picks = []
    for k, (x_ref, u_ref, rank_ref, _, _, _) in enumerate(blocks):
        hits = jnp.concatenate([slot == rank_ref[0, e : e + 1, :] for e in range(experts)], 0)
        pick = hits.astype(F32).astype(BF16)
        picks.append(pick)
        x_rows = matmul(pick, x_ref[...]).astype(BF16)
        u_rows = matmul(pick, u_ref[...]).astype(BF16)
        for e in range(experts):
            xc_ref[e, k * CAP : (k + 1) * CAP, :] = x_rows[e * CAP : (e + 1) * CAP]
            uc_ref[e, k * CAP : (k + 1) * CAP, :] = u_rows[e * CAP : (e + 1) * CAP]
    outs, backs, gate_grads = [], [], []
    for e in range(experts):
        x_rows, u_rows = xc_ref[e], uc_ref[e]
        logits = matmul(x_rows, router_ref[...])
        lane = lax.broadcasted_iota(jnp.int32, logits.shape, 1)
        logits = jnp.where(lane < E, logits, -1e30)
        expos = jnp.exp(logits - jnp.max(logits, axis=-1, keepdims=True))
        own = jnp.sum(jnp.where(lane == first_ref[0] + e, expos, 0.0), axis=-1, keepdims=True)
        gate = own / jnp.sum(expos, axis=-1, keepdims=True)
        gated = matmul(x_rows, wi_ref[e, :, :hidden])
        upward = matmul(x_rows, wi_ref[e, :, hidden:])
        pulled = matmul_t(u_rows, wd_ref[e])
        sig = jax.nn.sigmoid(gated)
        silu = gated * sig
        acts = silu * upward
        gate_grads.append(jnp.sum(acts * pulled, axis=-1, keepdims=True))
        hidden_gate = (acts * gate).astype(BF16)
        hidden_grads = pulled * gate
        hid_ref[e] = hidden_gate
        dg_ref[e, :, :hidden] = (hidden_grads * upward * sig * (1.0 + gated * (1.0 - sig))).astype(BF16)
        dg_ref[e, :, hidden:] = (hidden_grads * silu).astype(BF16)
        outs.append(matmul(hidden_gate, wd_ref[e]).astype(BF16))
        backs.append(matmul_t(dg_ref[e], wi_ref[e]).astype(BF16))
    for k, (_, _, rank_ref, y_ref, z_ref, g_ref) in enumerate(blocks):
        at = slice(k * CAP, (k + 1) * CAP)
        y_ref[...] = t_matmul(picks[k], jnp.concatenate([v[at] for v in outs], 0)).astype(BF16)
        z_ref[...] = t_matmul(picks[k], jnp.concatenate([v[at] for v in backs], 0)).astype(BF16)
        for e in range(experts):
            hit = slot == rank_ref[0, e : e + 1, :]
            g_ref[0, e : e + 1, :] = jnp.sum(
                jnp.where(hit, gate_grads[e][at], 0.0), axis=0, keepdims=True
            )


def run_experts(x, u, ranks, in_pieces, down_pieces, router, places, which, compact, parts):
    experts, _, hidden = in_pieces[0][2].shape
    hidden = hidden // 2
    depth = x[0].shape[1]
    in_places = [(r, at, parts[0]) for r, at, _ in in_pieces]
    down_places = [(r, at, parts[1]) for r, at, _ in down_pieces]
    pieces = [array for _, _, array in in_pieces + down_pieces]
    rows = ranks[0].shape[2]
    steps = x[0].shape[0] // rows
    token = pl.BlockSpec((rows, depth), lambda i: (i, 0))
    rank = pl.BlockSpec((1, experts, rows), lambda i: (i, 0, 0))
    anywhere = pl.BlockSpec(memory_space=pl.ANY)

    def slots(columns):
        return pl.BlockSpec((experts, 2 * CAP, columns), lambda i: (0, i + which * steps, 0))

    shape = jax.ShapeDtypeStruct
    tokens = shape(x[0].shape, BF16)
    gates = shape((steps, experts, rows), F32)
    count = 4 * steps * CAP
    wide = shape((experts, count, depth), BF16)
    inputs = [places, *x, *u, *ranks, router, *pieces]
    return pl.pallas_call(
        partial(expert_kernel, in_places, down_places),
        grid=(steps,),
        in_specs=[pl.BlockSpec(memory_space=pltpu.SMEM)]
        + [token] * 4
        + [rank] * 2
        + [pl.BlockSpec(router.shape, lambda i: (0, 0), pipeline_mode=pl.Buffered(1))]
        + [anywhere] * (len(pieces) + len(compact)),
        out_specs=[token] * 4 + [rank] * 2 + [slots(depth)] * 2 + [slots(2 * hidden), slots(hidden)],
        out_shape=[tokens] * 4
        + [gates] * 2
        + [wide] * 2
        + [shape((experts, count, 2 * hidden), BF16), shape((experts, count, hidden), BF16)],
        scratch_shapes=[
            pltpu.VMEM((experts, depth, 2 * hidden), BF16),
            pltpu.VMEM((experts, hidden, depth), BF16),
            pltpu.SemaphoreType.DMA((len(pieces),)),
        ],
        input_output_aliases={len(inputs) + i: 6 + i for i in range(len(compact))},
        compiler_params=pltpu.CompilerParams(vmem_limit_bytes=60 * MIB),
        cost_estimate=pl.CostEstimate(
            flops=4 * steps * CAP * experts * depth * (7 * hidden + 2 * rows),
            bytes_accessed=60 * MIB,
            transcendentals=2 * steps * CAP * experts * hidden,
        ),
        name="experts",
    )(*inputs, *compact)


def product_kernel(me_ref, left_ref, right_ref, out_ref):
    out_ref[0] = t_matmul(left_ref[0], right_ref[0]).astype(BF16)


def products(left, right, part, r, count, me, name):
    experts, rows, _ = left.shape
    columns = right.shape[2]
    wide = min(columns, 1024)
    return pl.pallas_call(
        product_kernel,
        grid_spec=pltpu.PrefetchScalarGridSpec(
            num_scalar_prefetch=1,
            grid=(experts, columns // wide),
            in_specs=[
                pl.BlockSpec((1, rows, part), lambda e, j, me: (e, 0, lax.rem(me[0] ^ r, count))),
                pl.BlockSpec((1, rows, wide), lambda e, j, me: (e, 0, j)),
            ],
            out_specs=pl.BlockSpec((1, part, wide), lambda e, j, me: (e, 0, j)),
        ),
        out_shape=jax.ShapeDtypeStruct((experts, part, columns), BF16),
        compiler_params=pltpu.CompilerParams(vmem_limit_bytes=56 * MIB),
        cost_estimate=pl.CostEstimate(
            flops=2 * experts * rows * part * columns,
            bytes_accessed=2 * experts * rows * (part + columns),
            transcendentals=0,
        ),
        name=name,
    )(me, left, right)


def per_device(
    S,
    F,
    tokens,
    segments,
    routes,
    cotangent,
    w_query,
    w_key,
    w_value,
    w_output,
    router,
    attn_gain,
    moe_gain,
    query_gain,
    key_gain,
    w_gate,
    w_up,
    w_down,
):
    s = lax.axis_index("seq")
    f = lax.axis_index("fsdp")
    T = tokens.shape[1]
    L = S * T
    heads = H // S
    C = heads * DH
    experts = E // S
    part = w_query.shape[0]
    half_f = F // 2
    hidden_half = w_gate.shape[2] // 2

    me = s.reshape(1).astype(jnp.int32)
    f_at = f.reshape(1).astype(jnp.int32)
    half_at = f // half_f
    tokens_low = tokens[0]
    upstream_low = cotangent[0]
    inputs = tokens_low.astype(F32)
    half_rows = T // 2
    in_part, down_part = w_gate.shape[1], w_down.shape[1]
    quarter = in_part // 4

    def hidden_part(which, first, count):
        return jnp.concatenate(
            [
                lax.dynamic_slice(
                    weight, (0, first, which * hidden_half), (experts, count, hidden_half)
                )
                for weight in (w_gate, w_up)
            ],
            2,
        )

    def far_swap(values, *dep):
        return swap(after(values, dep), "fsdp", F, half_f)

    def near_swap(values, *dep):
        return near_pieces(after(values, dep), F)

    named = routes[0].T[None] == jnp.arange(E, dtype=jnp.int32)[:, None, None]
    chosen = jnp.any(named, axis=1)
    index = jnp.arange(T, dtype=jnp.int32)
    before = (index[:, None] <= index[None, :]).astype(BF16)
    ranks = jnp.where(chosen, matmul(chosen.astype(BF16), before) - 1.0, -1.0)
    small = jnp.concatenate(
        [
            router.reshape(-1),
            attn_gain,
            moe_gain,
            query_gain,
            key_gain,
            ranks.astype(BF16).reshape(-1),
        ]
    )[None]
    crossed = split_heads(w_query, w_key, w_value, S)
    small = double(after(small, crossed), "fsdp", F)
    crossed = lax.all_to_all(crossed, "seq", split_axis=0, concat_axis=0, tiled=True)
    near_own = [near_swap(hidden_part(half_at, 0, 2 * quarter), small)]
    out_dep = small
    small = double(small, "seq", S)
    out_far = far_swap(w_output, out_dep)
    crossed, near_own[0], small, out_far = tie(crossed, near_own[0], small, out_far)

    held = after((w_gate, w_up, w_down, upstream_low), crossed)

    def held_part(which, first, count):
        return jnp.concatenate(
            [
                lax.dynamic_slice(
                    weight, (0, first, which * hidden_half), (experts, count, hidden_half)
                )
                for weight in held[:2]
            ],
            2,
        )

    own_quarters = {n: held_part(half_at, n * quarter, quarter) for n in (2, 3)}
    far_quarters = [held_part(1 - half_at, n * quarter, quarter) for n in range(4)]
    down_rows = quarters(held[2], 1)
    upstream_halves = [held[3][:half_rows], held[3][half_rows:]]
    small = in_order(small, S, F, s, f).reshape(S, F, -1)
    prepared = (own_quarters, far_quarters, down_rows, upstream_halves, small)
    token_first = gather_first(after(tokens_low, crossed), S)
    qkv_pieces = {0: crossed}
    for r in range(1, F):
        low = low_bit(r)
        qkv_pieces[r] = swap(qkv_pieces[r ^ low], "fsdp", F, low)
        if r == half_f:
            qkv_pieces, token_first, prepared = tie(qkv_pieces, token_first, prepared)
            own_quarters, far_quarters, down_rows, upstream_halves, small = prepared
            partner_up = [far_swap(upstream_halves[0])]
    token_more = gather_more(tokens_low, token_first, S)
    qkv_pieces, partner_up[0], token_more = tie(qkv_pieces, partner_up[0], token_more)
    tokens_even, tokens_odd = gather_end(tokens_low, token_first, token_more, S)
    w_qkv = place_fsdp(qkv_pieces, f, 1).reshape(D, 3 * C)

    full_router = small[:, :, : part * E].reshape(D, E)
    gains = [
        small[:, :, part * (E + i) : part * (E + i + 1)].reshape(D).astype(F32) for i in range(4)
    ]
    gain_attn, gain_moe = gains[0], gains[1]
    head_gain = lax.dynamic_slice(jnp.stack(gains[2:], 0), (0, s * C), (2, C))
    rank_part = small[:, :, part * (E + 4) :].reshape(S, F, E, T)

    def ranks_of(index):
        ranks = lax.dynamic_slice(rank_part, (0, index, s * experts, 0), (S, 1, experts, T))
        ranks = relative(ranks[:, 0], s).astype(jnp.int32)
        return ranks[: S // 2], ranks[S // 2 :]

    places = jnp.arange(L, dtype=jnp.int32).astype(F32)
    freqs = ROPE_BASE ** (-(jnp.arange(DH // 2, dtype=F32) * 2.0 / DH))
    angles = places[:, None] * freqs[None, :]
    cosine, sine = jnp.cos(angles), jnp.sin(angles)
    cosine = jnp.concatenate([cosine, cosine], 1)
    sine = jnp.concatenate([-sine, sine], 1)

    def far_part(n, *dep):
        return far_swap(far_quarters[n], *dep)

    partner_up.append(far_swap(upstream_halves[1], w_qkv))
    out_pieces = {0: after(w_output, w_qkv), half_f: after(out_far, w_qkv)}
    for r in range(1, F):
        if r != half_f:
            low = low_bit(r)
            out_pieces[r] = swap(out_pieces[r ^ low], "fsdp", F, low)
    own_up_first = gather_first(after(upstream_low, w_qkv), S)
    normed_even, normed_odd, query_pre, key_pre, value_low, squares = project(
        tokens_even, tokens_odd, w_qkv, gain_attn[None], me, T
    )
    squares, partner_up[1], out_pieces, own_up_first = tie(
        squares, partner_up[1], out_pieces, own_up_first
    )
    partner_up = jnp.concatenate(partner_up, 0)
    own_output = place_fsdp(out_pieces, f, 0).reshape(C, D)

    out_first = gather_first(own_output, S)
    far = [far_part(0, squares)]
    near_own.append(near_swap(own_quarters[2], squares))
    squares = sum_all(squares, "seq", S)
    query_low, key_low = rope(query_pre, key_pre, squares, head_gain, cosine, sine)
    query_low, out_first, far[0], near_own[1] = tie(query_low, out_first, far[0], near_own[1])

    seg_row = segments
    seg_col = segments.reshape(L, 1)
    out_more = gather_more(own_output, out_first, S)
    far.append(far_part(1, query_low))
    near_own.append(near_swap(own_quarters[3], query_low))
    attended, lse = attention_forward(query_low, key_low, value_low, seg_row, seg_col)
    attended, out_more, far[1], near_own[2] = tie(attended, out_more, far[1], near_own[2])
    attended_blocks = attended.reshape(S, T, C)
    come = lax.all_to_all(attended_blocks, "seq", split_axis=0, concat_axis=0, tiled=True)
    out_even, out_odd = gather_end(own_output, out_first, out_more, S)
    far.append(far_part(2, attended))
    near_far = [near_swap(far[0], attended)]
    own_up_more = gather_more(after(upstream_low, attended), own_up_first, S)
    come, far[2], near_far[0], own_up_more = tie(come, far[2], near_far[0], own_up_more)
    own_u = gather_end(upstream_low, own_up_first, own_up_more, S)
    near_far.append(near_swap(far[1], come))
    down = [near_swap(down_rows[0], come)]
    partner_up_first = gather_first(after(partner_up, come), S)
    come = relative(come, s).transpose(1, 0, 2).reshape(T, D)
    residual = inputs + matmul(come[:, : D // 2], out_even) + matmul(come[:, D // 2 :], out_odd)
    moe_factor = rms_factor(residual)
    residual_n = residual * moe_factor
    second_low = (residual_n * gain_moe).astype(BF16)
    second_low, down[0], near_far[1], partner_up_first, own_u = tie(
        second_low, down[0], near_far[1], partner_up_first, own_u
    )

    own_first = gather_first(second_low, S)
    partner_low = [far_swap(second_low[:half_rows])]
    near_far.append(near_swap(far[2], second_low))
    own_ranks, other_ranks = ranks_of(f), ranks_of(f ^ half_f)
    own_first, partner_low[0], near_far[2], own_ranks, other_ranks = tie(
        own_first, partner_low[0], near_far[2], own_ranks, other_ranks
    )
    own_more = gather_more(second_low, own_first, S)
    partner_low.append(far_swap(second_low[half_rows:], own_first))
    down.append(near_swap(down_rows[1], own_first))
    partner_up_more = gather_more(after(partner_up, own_first), partner_up_first, S)
    own_more, partner_low[1], down[1], partner_up_more = tie(
        own_more, partner_low[1], down[1], partner_up_more
    )
    partner_low = jnp.concatenate(partner_low, 0)
    own_x = gather_end(second_low, own_first, own_more, S)
    partner_first = gather_first(after(partner_low, own_more), S)
    down.append(near_swap(down_rows[2], own_more))
    far.append(far_part(3, own_more))
    partner_first, down[2], own_x, far[3] = tie(partner_first, down[2], own_x, far[3])
    other_u = gather_end(after(partner_up, partner_first), partner_up_first, partner_up_more, S)
    partner_more = gather_more(partner_low, partner_first, S)
    down.append(near_swap(down_rows[3], partner_first))
    near_far.append(near_swap(far[3], partner_first))
    partner_more, down[3], other_u, near_far[3] = tie(partner_more, down[3], other_u, near_far[3])
    other_x = gather_end(partner_low, partner_first, partner_more, S)
    in_pieces = []
    for r in range(F):
        for n, rows in enumerate(near_own if r < half_f else near_far):
            first = (0, 2, 3)[n] if r < half_f else n
            in_pieces.append((r, first * quarter, rows[r % half_f]))
    down_pieces = [
        (r, n * (down_part // 4), down[n][r]) for r in range(half_f) for n in range(4)
    ]
    wide_router = jnp.pad(full_router, ((0, 0), (0, 128 - E)))
    expert_places = jnp.stack([s * experts, f]).astype(jnp.int32)
    parts = (in_part, down_part)
    own_parts = run_experts(
        own_x, own_u, own_ranks, in_pieces, down_pieces, wide_router, expert_places, 0, (), parts
    )
    own_parts, other_x = tie(own_parts, other_x)
    own_got = swap(own_parts[3], "seq", S, 1)
    own_out_got = swap(own_parts[1], "seq", S, 1)
    other_parts = run_experts(
        other_x,
        other_u,
        other_ranks,
        in_pieces,
        down_pieces,
        wide_router,
        expert_places,
        1,
        own_parts[6:],
        parts,
    )
    other_parts, own_got, own_out_got = tie(other_parts, own_got, own_out_got)
    logits = matmul(second_low, full_router)
    router_probs = jax.nn.softmax(logits, axis=-1)

    x_rows, u_rows, in_grads, hidden_gate = other_parts[6:]
    in_terms, down_terms = {}, {}

    def in_products(r, *dep):
        in_terms[r] = products(
            x_rows, after(in_grads, dep), in_part, r, F, f_at, "in_products"
        )

    odd = [r for r in range(F) if r & 1]
    far_odd = [r for r in odd if r & half_f]
    near_odd = [r for r in odd if not r & half_f]

    def to_home(even, odd):
        return absolute(jnp.concatenate([even, odd], 0).transpose(0, 2, 1), s)

    gate_grads = jnp.stack(
        [to_home(own_parts[4], own_parts[5]), to_home(other_parts[4], other_parts[5])], 1
    ).reshape(S, -1)
    other_got = swap(other_parts[3], "seq", S, 1)
    for r in far_odd:
        in_products(r)
    gate_grads = lax.all_to_all(gate_grads, "seq", split_axis=0, concat_axis=0, tiled=True)
    other_got, in_terms, gate_grads = tie(other_got, in_terms, gate_grads)
    sent = {r: quarters(in_terms[r], 1) for r in far_odd}

    def send_in(n, *dep):
        return {r: swap(after(sent[r][n], dep), "fsdp", F, 1) for r in sent}

    other_sums = sum_cores(other_parts[2], other_got, S)
    come = sum_first(other_sums, S)
    far_got = [send_in(0, other_got)]
    other_out_got = swap(after(other_parts[1], other_got), "seq", S, 1)
    gate_grads = gate_grads.reshape(S, 2, T * experts)
    partner_grads = far_swap(gate_grads[:, 1])
    come, far_got[0], other_out_got, partner_grads = tie(
        come, far_got[0], other_out_got, partner_grads
    )
    singles, other_total = sum_more(other_sums, come, S)
    come = sum_last(singles, S)
    middle_sent = {r: jnp.concatenate(sent[r][1:3], 1) for r in sent}
    middle_got = {
        r: swap(after(middle_sent[r], far_got[0]), "fsdp", F, 1) for r in middle_sent
    }

    def down_products(r, dep):
        down_terms[r] = products(
            after(hidden_gate, dep), u_rows, down_part, r, half_f, f_at, "down_products"
        )

    for r in range(1, half_f, 2):
        down_products(r, singles)
    come, middle_got, down_terms = tie(come, middle_got, down_terms)
    for n in range(2):
        far_got.append({r: got[:, n * quarter : (n + 1) * quarter] for r, got in middle_got.items()})
    other_rows = add_all(other_total, come).astype(BF16)
    gate_grads = gate_grads[:, 0] + partner_grads
    gate_grads = gate_grads.reshape(S, T, experts).transpose(1, 0, 2).reshape(T, E)
    back = [far_swap(other_rows[:half_rows])]
    own_sums = sum_cores(own_parts[2], after(own_got, other_rows), S)
    come = sum_first(own_sums, S)
    far_got.append(send_in(3, other_rows))
    for r in far_odd:
        in_products(r ^ 1, other_rows)
    come, back[0], far_got[3], in_terms = tie(come, back[0], far_got[3], in_terms)
    back.append(far_swap(other_rows[half_rows:], come))
    singles, own_total = sum_more(own_sums, come, S)
    come = sum_last(singles, S)
    down_sent = {r: quarters(down_terms[r], 1) for r in range(1, half_f, 2)}

    def send_down(n, *dep):
        return {r: swap(after(down_sent[r][n], dep), "fsdp", F, 1) for r in down_sent}

    down_got = [send_down(0, singles)]
    for r in near_odd:
        in_products(r, singles)
    come, back[1], down_got[0], in_terms = tie(come, back[1], down_got[0], in_terms)
    row_grads = add_all(own_total, come) + jnp.concatenate(back, 0).astype(F32)

    upstream = upstream_low.astype(F32)
    logit_grads = router_probs * (
        gate_grads - jnp.sum(router_probs * gate_grads, axis=-1, keepdims=True)
    )
    router_wide = full_router.astype(F32)
    second_grads = row_grads + jnp.dot(logit_grads, router_wide.T, precision=HIGHEST)
    pulled = second_grads * gain_moe
    residual_grads = upstream + moe_factor * (
        pulled - residual_n * jnp.mean(pulled * residual_n, axis=-1, keepdims=True)
    )
    branch_low = residual_grads.astype(BF16)

    def sum_near(terms):
        mask = 2
        while mask < half_f:
            terms = {
                r: terms[r] + swap(terms[r | mask].astype(BF16), "fsdp", F, mask).astype(F32)
                for r in terms
                if not r & mask
            }
            mask *= 2
        (total,) = terms.values()
        return total

    def far_sum(n, *dep):
        terms = {
            r ^ 1: quarters(in_terms[r ^ 1], 1)[n].astype(F32) + far_got[n][r].astype(F32)
            for r in far_odd
        }
        return far_swap(sum_near(terms).astype(BF16), *dep)

    branch_first = gather_first(branch_low, S)
    far_sums = [far_sum(0, branch_low)]
    down_got.append(send_down(1, branch_low))
    for r in range(0, half_f, 2):
        down_products(r, branch_low)
    branch_first, far_sums[0], down_got[1], down_terms = tie(
        branch_first, far_sums[0], down_got[1], down_terms
    )
    branch_more = gather_more(branch_low, branch_first, S)
    far_sums.append(far_sum(1, branch_first))
    down_got.append(send_down(2, branch_first))
    branch_even, branch_odd = gather_end(branch_low, branch_first, branch_more, S)

    head_grads = jnp.concatenate(
        [matmul_t(branch_even, own_output), matmul_t(branch_odd, own_output)], 0
    ).astype(BF16)
    head_grads = absolute(head_grads.reshape(S, T, C), s).reshape(L, C)
    head_grads, far_sums[1], down_got[2] = tie(head_grads, far_sums[1], down_got[2])
    far_sums.append(far_sum(2, head_grads))
    down_got.append(send_down(3, head_grads))
    other_out_sums = sum_cores(other_parts[0], after(other_out_got, head_grads), S)
    come, head_grads = sum_first(other_out_sums, S, head_grads)
    query_back, key_back, value_back = attention_backward(
        query_low, key_low, value_low, head_grads, lse, seg_row, seg_col
    )
    query_back, key_back, value_back, far_sums[2], down_got[3], come = tie(
        query_back, key_back, value_back, far_sums[2], down_got[3], come
    )

    singles, other_total = sum_more(other_out_sums, come, S)
    come = sum_last(singles, S)
    far_sums.append(far_sum(3, query_back))
    attended_rel = relative(after(attended_blocks, singles), s).reshape(2, L // 2, C)
    output_term = t_matmul(attended_rel[0], branch_even) + t_matmul(attended_rel[1], branch_odd)
    output_term = by_index(output_term.astype(BF16).reshape(F, part, D), f, F)
    output_got = swap(output_term[: F // 2], "fsdp", F, 1)
    value_rel = relative(value_back.reshape(S, T, C), s).reshape(2, L // 2, C)

    def weight_term(even, odd):
        term = (t_matmul(normed_even, even) + t_matmul(normed_odd, odd)).astype(BF16)
        return by_index(term.reshape(S, F, part, -1).transpose(1, 0, 2, 3), f, F)

    means, gain_term = rope_means(
        query_back, key_back, query_pre, key_pre, squares, head_gain, cosine, sine
    )
    means = sum_all(means, "seq", S)
    value_term = weight_term(value_rel[0], value_rel[1])
    means, come, far_sums[3], output_got, value_term = tie(
        means, come, far_sums[3], output_got, value_term
    )
    other_outs = add_all(other_total, come).astype(BF16)
    outs_back = [far_swap(other_outs[:half_rows])]
    value_got = swap(value_term[: F // 2], "fsdp", F, 1)
    pre_rel = rope_back(
        (query_back, key_back, value_back),
        query_pre,
        key_pre,
        squares,
        means,
        head_gain,
        cosine,
        sine,
        me,
        T,
    ).reshape(2, L // 2, 3 * C)
    normed_got = swap(matmul_t(pre_rel[1], w_qkv).astype(BF16), "seq", S, 1)
    normed_kept = matmul_t(pre_rel[0], w_qkv).astype(BF16)
    normed_got, normed_kept, value_got, outs_back[0] = tie(
        normed_got, normed_kept, value_got, outs_back[0]
    )

    normed_sums = sum_cores(normed_kept, normed_got, S)
    come = sum_first(normed_sums, S)
    value_sum = sum_rest(sum_even(value_term, value_got, F), F)
    turned_term = weight_term(
        after(pre_rel[0][:, : 2 * C], normed_got), after(pre_rel[1][:, : 2 * C], normed_got)
    )
    late_grads, late_logits = after(second_grads, normed_got), after(logit_grads, normed_got)
    router_term = jnp.dot(second_low.astype(F32).T, late_logits, precision=HIGHEST)
    moe_gain_term = jnp.sum(late_grads * residual_n, axis=0)
    gain_terms = jnp.concatenate(
        [router_term.reshape(S * F, part * E), moe_gain_term.reshape(S * F, part)], 1
    )
    gain_terms = in_relative(gain_terms, S, F, s, f).reshape(S, F, -1)
    head_terms = gain_term.reshape(2, F, part).transpose(1, 0, 2).reshape(F, 2 * part)
    head_terms = in_relative(head_terms, 1, F, 0, f)
    gain_terms = jnp.concatenate([gain_terms.transpose(1, 0, 2).reshape(F, -1), head_terms], 1)
    own_out_sums = sum_cores(own_parts[0], after(own_out_got, normed_got), S)
    own_come = sum_first(own_out_sums, S)
    come, turned_term, value_sum, gain_terms, own_come = tie(
        come, turned_term, value_sum, gain_terms, own_come
    )
    turned_got = swap(turned_term[: F // 2], "fsdp", F, 1)
    singles, normed_total = sum_more(normed_sums, come, S)
    come = sum_last(singles, S)
    gain_got = swap(gain_terms[F // 2 :], "fsdp", F, half_f)
    for r in near_odd:
        in_products(r ^ 1, turned_term)
    come, turned_got, gain_got, in_terms = tie(come, turned_got, gain_got, in_terms)
    gain_terms = gain_terms[: F // 2] + gain_got
    normed_grads = add_all(normed_total, come)
    turned_sum = sum_rest(sum_even(turned_term, turned_got, F), F)
    middle = in_part // 2

    def send_near(first, dep):
        return {
            r: swap(after(in_terms[r][:, first : first + middle], dep), "fsdp", F, 1)
            for r in near_odd
        }

    near_got = [send_near(0, turned_got)]
    gain_terms = halve(after(gain_terms, turned_got), "fsdp", F, half_f // 2)
    singles, own_total = sum_more(after(own_out_sums, turned_got), own_come, S)
    own_come = sum_last(singles, S)
    turned_sum, own_come, near_got[0], gain_terms = tie(
        turned_sum, own_come, near_got[0], gain_terms
    )
    near_got.append(send_near(middle, turned_sum))
    outs_back.append(far_swap(other_outs[half_rows:], turned_sum))
    count = S * part * (E + 1)
    head_terms = gain_terms[0, count:]
    gain_terms = halve(gain_terms[0, :count].reshape(S, -1), "seq", S, S // 2)[0]
    own_outs = add_all(own_total, own_come)
    qkv_term = jnp.concatenate([turned_sum, value_sum], -1).astype(BF16)
    qkv_term = lax.all_to_all(qkv_term, "seq", split_axis=0, concat_axis=0, tiled=True)
    qkv_term, outs_back[1], near_got[1], gain_terms = tie(
        qkv_term, outs_back[1], near_got[1], gain_terms
    )
    outs_back = jnp.concatenate(outs_back, 0).astype(F32)
    mixed = (residual + own_outs + outs_back).astype(BF16)[None]
    qkv_term = [
        qkv_term[:, :, j * C : (j + 1) * C].transpose(1, 0, 2).reshape(part, D).astype(F32)
        for j in range(3)
    ]
    grad_output = sum_rest(sum_even(output_term, output_got, F), F)

    near_got = {r: jnp.concatenate([got[r] for got in near_got], 1) for r in near_odd}
    own_term = sum_near(
        {r ^ 1: in_terms[r ^ 1].astype(F32) + near_got[r].astype(F32) for r in near_odd}
    )
    far_term = jnp.concatenate(far_sums, 1).astype(F32)
    first_half = half_at == 0
    lower = jnp.where(first_half, own_term, far_term)
    upper = jnp.where(first_half, far_term, own_term)
    grad_gate, grad_up = (
        jnp.concatenate([lower[..., at], upper[..., at]], axis=-1)
        for at in (slice(0, hidden_half), slice(hidden_half, 2 * hidden_half))
    )
    down_got = after(down_got, turned_sum)
    down_got = {r: jnp.concatenate([got[r] for got in down_got], 1) for r in down_sent}
    grad_down = sum_near(
        {r ^ 1: down_terms[r ^ 1].astype(F32) + down_got[r].astype(F32) for r in down_sent}
    )

    attn_factor = rms_factor(inputs)
    inputs_n = inputs * attn_factor
    attn_pulled = normed_grads * gain_attn
    grad_tokens = residual_grads + attn_factor * (
        attn_pulled - inputs_n * jnp.mean(attn_pulled * inputs_n, axis=-1, keepdims=True)
    )
    grad_attn_gain = sum(
        jnp.sum(term * weight.astype(F32), axis=1)
        for term, weight in zip(qkv_term, (w_query, w_key, w_value))
    ) / attn_gain.astype(F32)
    return (
        mixed,
        grad_tokens[None],
        qkv_term[0],
        qkv_term[1],
        qkv_term[2],
        grad_output,
        gain_terms[: part * E].reshape(part, E),
        grad_attn_gain,
        gain_terms[part * E :],
        head_terms[:part],
        head_terms[part:],
        grad_gate,
        grad_up,
        grad_down,
    )


def solution(mesh):
    tokens_spec = P("fsdp", "seq", None)
    rows_spec = P(("seq", "fsdp"), None)
    gain_spec = P(("seq", "fsdp"))
    expert_spec = P("seq", "fsdp", None)
    in_specs = (
        (tokens_spec, P("fsdp", None), tokens_spec, tokens_spec)
        + (rows_spec,) * 5
        + (gain_spec,) * 4
        + (expert_spec,) * 3
    )
    out_specs = (tokens_spec,) * 2 + (rows_spec,) * 5 + (gain_spec,) * 4 + (expert_spec,) * 3
    return jax.shard_map(
        partial(per_device, mesh.shape["seq"], mesh.shape["fsdp"]),
        mesh=mesh,
        in_specs=in_specs,
        out_specs=out_specs,
        check_vma=False,
    )
```

```python
from functools import partial

import jax
import jax.numpy as jnp
from jax import lax
from jax.experimental import pallas as pl
from jax.experimental.pallas import tpu as pltpu
from jax.sharding import PartitionSpec as P

D = 2048
H = 16
DH = 128
E = 16
WINDOW = 1024
CAP = 144

EPSILON = 1e-06
ROPE_BASE = 50000.0
HIGHEST = lax.Precision.HIGHEST
BF16 = jnp.bfloat16
F32 = jnp.float32
MIB = 1024 * 1024


def matmul(left, right):
    return jnp.dot(left, right, preferred_element_type=F32)


def matmul_t(left, right):
    return lax.dot_general(left, right, (((1,), (1,)), ((), ())), preferred_element_type=F32)


def t_matmul(left, right):
    return lax.dot_general(left, right, (((0,), (0,)), ((), ())), preferred_element_type=F32)


def rms_factor(values):
    return lax.rsqrt(jnp.mean(values * values, axis=-1, keepdims=True) + EPSILON)


def swap(values, axis, size, mask):
    return lax.ppermute(values, axis, [(i, i ^ mask) for i in range(size)])


def high_bit(number):
    return 1 << (number.bit_length() - 1)


def low_bit(number):
    return number & -number


def after(values, *others):
    return lax.optimization_barrier((values, others))[0]


def tie(*values):
    return lax.optimization_barrier(values)


def gather_first(values, size):
    return {r: swap(values, "seq", size, r) for r in range(2, size, 2) if r == low_bit(r)}


def gather_more(values, first, size):
    rows = values.shape[0] // 2
    pieces = dict(first)
    for r in range(2, size, 2):
        if r not in pieces:
            up, down = high_bit(r), low_bit(r)
            upper, lower = pieces[r ^ up], pieces[r ^ down]
            upper = upper[0] if isinstance(upper, tuple) else upper[:rows]
            lower = lower[1] if isinstance(lower, tuple) else lower[rows:]
            pieces[r] = (swap(upper, "seq", size, up), swap(lower, "seq", size, down))
    return {r: piece for r, piece in pieces.items() if r not in first}


def gather_end(values, first, more, size):
    blocks = [values]
    for r in range(2, size, 2):
        blocks.extend([first[r]] if r in first else more[r])
    even = jnp.concatenate(blocks, 0)
    return even, swap(even, "seq", size, 1)


def relative(blocks, me):
    size = blocks.shape[0]
    order = list(range(0, size, 2)) + list(range(1, size, 2))
    return jnp.concatenate([lax.dynamic_slice_in_dim(blocks, me ^ r, 1, 0) for r in order], 0)


def absolute(blocks, me):
    size = blocks.shape[0]
    places = [((me ^ j) // 2) + ((me ^ j) % 2) * (size // 2) for j in range(size)]
    return jnp.concatenate([lax.dynamic_slice_in_dim(blocks, at, 1, 0) for at in places], 0)


def sum_cores(even, got, size):
    rows = even.shape[0] // (size // 2)
    half = rows // 2

    def part(r, first):
        at = slice(r // 2 * rows + first, r // 2 * rows + first + half)
        return even[at].astype(F32) + got[at].astype(F32)

    return {r: [part(r, 0), part(r, half)] for r in range(0, size, 2)}


def sum_first(sums, size, held=None):
    sums = {r: list(value) for r, value in sums.items()}
    come = {}
    for r in range(size - 2, 0, -2):
        if r != low_bit(r):
            up, down = high_bit(r), low_bit(r)
            for (goal, k, _), piece in come.items():
                if goal == r:
                    sums[r][k] += piece.astype(F32)
            upper, lower, held = tie(sums[r][0].astype(BF16), sums[r][1].astype(BF16), held)
            come[r ^ up, 0, r] = swap(upper, "seq", size, up)
            come[r ^ down, 1, r] = swap(lower, "seq", size, down)
    return come if held is None else (come, held)


def sum_more(sums, come, size):
    sums = {r: list(value) for r, value in sums.items() if r == 0 or r == low_bit(r)}
    for (goal, k, _), piece in come.items():
        if goal in sums:
            sums[goal][k] += piece.astype(F32)
    singles = {
        r: jnp.concatenate([v.astype(BF16) for v in value], 0) for r, value in sums.items() if r
    }
    return tie(singles)[0], jnp.concatenate(sums[0], 0)


def sum_last(singles, size):
    return {r: swap(value, "seq", size, r) for r, value in singles.items()}


def add_all(total, pieces):
    for piece in pieces.values():
        total += piece.astype(F32)
    return total


def quarters(values, axis):
    step = values.shape[axis] // 4
    return [lax.slice_in_dim(values, k * step, (k + 1) * step, axis=axis) for k in range(4)]


def sum_all(values, axis, size):
    mask = 1
    while mask < size:
        values = values + swap(values, axis, size, mask)
        mask *= 2
    return values


def fsdp_pieces(values, size):
    pieces = {0: values}
    for r in range(1, size):
        low = low_bit(r)
        pieces[r] = swap(pieces[r ^ low], "fsdp", size, low)
    return pieces


def place_fsdp(pieces, me, axis):
    size = len(pieces)
    shape = pieces[0].shape
    whole = jnp.zeros(shape[:axis] + (size,) + shape[axis:], pieces[0].dtype)
    for r, piece in pieces.items():
        whole = lax.dynamic_update_slice_in_dim(whole, jnp.expand_dims(piece, axis), me ^ r, axis)
    return whole


def near_pieces(values, size):
    pieces = {0: values}
    for r in range(1, size // 2):
        up = high_bit(r)
        pieces[r] = swap(pieces[r ^ up], "fsdp", size, up)
    return pieces


def double(values, axis, size):
    mask = 1
    while mask < size:
        values = jnp.concatenate([values, swap(values, axis, size, mask)], 0)
        mask *= 2
    return values


def halve(values, axis, size, mask):
    while mask:
        half = values.shape[0] // 2
        values = values[:half] + swap(values[half:], axis, size, mask)
        mask //= 2
    return values


def relative_pick(seq_size, fsdp_size, s, f):
    index = jnp.arange(seq_size * fsdp_size, dtype=jnp.int32)
    source = ((index // fsdp_size) ^ s) * fsdp_size + ((index % fsdp_size) ^ f)
    return source[:, None] == index[None, :]


def in_order(values, seq_size, fsdp_size, s, f):
    pick = relative_pick(seq_size, fsdp_size, s, f).astype(values.dtype)
    return matmul(pick, values).astype(values.dtype)


def in_relative(values, seq_size, fsdp_size, s, f):
    pick = relative_pick(seq_size, fsdp_size, s, f).astype(F32)
    return jnp.dot(pick, values, precision=HIGHEST)


def by_index(partial_sum, me, size):
    order = [r for r in range(size) if r & 1] + [r for r in range(size) if not r & 1]
    return jnp.concatenate([lax.dynamic_slice_in_dim(partial_sum, me ^ r, 1, 0) for r in order], 0)


def sum_even(stacked, got, size):
    return (stacked[size // 2 :].astype(F32) + got.astype(F32)).astype(BF16)


def sum_rest(stacked, size):
    mask = 2
    values = stacked.astype(F32)
    while mask < size:
        count = values.shape[0] // 2
        pairs = values.reshape((count, 2) + values.shape[1:])
        got = swap(pairs[:, 1].astype(BF16), "fsdp", size, mask)
        values = pairs[:, 0] + got.astype(F32)
        mask *= 2
    return values[0]


def allowed_keys(seg_row, seg_col, first_query, first_key, rows, span, half_window):
    query_at = first_query + lax.broadcasted_iota(jnp.int32, (span, rows), 1)
    key_at = first_key + lax.broadcasted_iota(jnp.int32, (span, rows), 0)
    return (jnp.abs(query_at - key_at) <= half_window) & (seg_col == seg_row)


def first_key_of(block, rows, span, length):
    start = jnp.clip(block * rows - (span - rows) // 2, 0, length - span)
    return pl.multiple_of(start, rows)


def forward_kernel(span, q_ref, k_ref, v_ref, seg_row_ref, seg_col_ref, o_ref, lse_ref):
    block = pl.program_id(1)
    rows, length = q_ref.shape[0], k_ref.shape[0]
    first_key = first_key_of(block, rows, span, length)
    keys = k_ref[pl.ds(first_key, span), :]
    values = v_ref[pl.ds(first_key, span), :]
    scores = matmul_t(keys, q_ref[...]) * DH ** (-0.5)
    allowed = allowed_keys(
        seg_row_ref[...],
        seg_col_ref[pl.ds(first_key, span), :],
        block * rows,
        first_key,
        rows,
        span,
        WINDOW // 2,
    )
    scores = jnp.where(allowed, scores, -1e30)
    peak = jnp.max(scores, axis=0, keepdims=True)
    expos = jnp.exp(scores - peak)
    totals = jnp.sum(expos, axis=0, keepdims=True)
    probs = (expos * (1.0 / totals)).astype(BF16)
    o_ref[...] = t_matmul(values, probs).T.astype(BF16)
    lse_ref[...] = (peak + jnp.log(totals))[None]


def backward_kernel(
    span,
    q_ref,
    k_ref,
    v_ref,
    do_ref,
    lse_ref,
    seg_row_ref,
    seg_col_ref,
    dq_ref,
    dk_ref,
    dv_ref,
    dk_sum,
    dv_sum,
):
    block = pl.program_id(1)
    rows, length = q_ref.shape[0], k_ref.shape[0]

    @pl.when(block == 0)
    def _():
        dk_sum[...] = jnp.zeros_like(dk_sum)
        dv_sum[...] = jnp.zeros_like(dv_sum)

    first_key = first_key_of(block, rows, span, length)
    at = pl.ds(first_key, span)
    keys = k_ref[at, :]
    values = v_ref[at, :]
    queries = q_ref[...]
    grads = do_ref[...]
    scores = matmul_t(keys, queries) * DH ** (-0.5)
    allowed = allowed_keys(
        seg_row_ref[...],
        seg_col_ref[at, :],
        block * rows,
        first_key,
        rows,
        span,
        WINDOW // 2,
    )
    probs = jnp.where(allowed, jnp.exp(scores - lse_ref[0]), 0.0)
    dv_sum[at, :] += matmul(probs.astype(BF16), grads)
    prob_grads = matmul_t(values, grads)
    center = jnp.sum(probs * prob_grads, axis=0, keepdims=True)
    score_grads = (probs * (prob_grads - center)).astype(BF16)
    dk_sum[at, :] += matmul(score_grads, queries)
    dq_ref[...] = (t_matmul(keys, score_grads) * DH ** (-0.5)).T.astype(BF16)

    @pl.when(block == length // rows - 1)
    def _():
        dk_ref[...] = (dk_sum[...] * DH ** (-0.5)).astype(BF16)
        dv_ref[...] = dv_sum[...].astype(BF16)


def attention_sizes(length):
    rows = 256
    return rows, min(length, rows + WINDOW)


def attention_forward(queries, keys, values, seg_row, seg_col):
    length, columns = queries.shape
    heads = columns // DH
    rows, span = attention_sizes(length)
    block = pl.BlockSpec((rows, DH), lambda h, i: (i, h))
    whole = pl.BlockSpec((length, DH), lambda h, i: (0, h))
    return pl.pallas_call(
        partial(forward_kernel, span),
        grid=(heads, length // rows),
        in_specs=[
            block,
            whole,
            whole,
            pl.BlockSpec((1, rows), lambda h, i: (0, i)),
            pl.BlockSpec((length, 1), lambda h, i: (0, 0)),
        ],
        out_specs=[block, pl.BlockSpec((1, 1, rows), lambda h, i: (h, 0, i))],
        out_shape=[
            jax.ShapeDtypeStruct((length, columns), BF16),
            jax.ShapeDtypeStruct((heads, 1, length), F32),
        ],
        compiler_params=pltpu.CompilerParams(vmem_limit_bytes=48 * MIB),
        cost_estimate=pl.CostEstimate(
            flops=4 * heads * length * span * DH,
            bytes_accessed=8 * length * columns,
            transcendentals=heads * length * span,
        ),
        name="attend",
    )(queries, keys, values, seg_row, seg_col)


def attention_backward(queries, keys, values, grads, lse, seg_row, seg_col):
    length, columns = queries.shape
    heads = columns // DH
    rows, span = attention_sizes(length)
    block = pl.BlockSpec((rows, DH), lambda h, i: (i, h))
    whole = pl.BlockSpec((length, DH), lambda h, i: (0, h))
    shape = jax.ShapeDtypeStruct((length, columns), BF16)
    return pl.pallas_call(
        partial(backward_kernel, span),
        grid=(heads, length // rows),
        in_specs=[
            block,
            whole,
            whole,
            block,
            pl.BlockSpec((1, 1, rows), lambda h, i: (h, 0, i)),
            pl.BlockSpec((1, rows), lambda h, i: (0, i)),
            pl.BlockSpec((length, 1), lambda h, i: (0, 0)),
        ],
        out_specs=[block, whole, whole],
        out_shape=[shape, shape, shape],
        scratch_shapes=[pltpu.VMEM((length, DH), F32), pltpu.VMEM((length, DH), F32)],
        compiler_params=pltpu.CompilerParams(vmem_limit_bytes=48 * MIB),
        cost_estimate=pl.CostEstimate(
            flops=10 * heads * length * span * DH,
            bytes_accessed=14 * length * columns,
            transcendentals=heads * length * span,
        ),
        name="attend_back",
    )(queries, keys, values, grads, lse, seg_row, seg_col)


def qkv_kernel(
    me_ref,
    even_ref,
    odd_ref,
    weight_ref,
    gain_ref,
    normed_even_ref,
    normed_odd_ref,
    q_ref,
    k_ref,
    v_ref,
    square_ref,
):
    turned = me_ref[0] % 2
    rows = even_ref.shape[0]
    columns = q_ref.shape[1]
    for k, (token_ref, normed_ref) in enumerate(
        ((even_ref, normed_even_ref), (odd_ref, normed_odd_ref))
    ):
        at = pl.ds(pl.multiple_of((turned ^ k) * rows, rows), rows)
        wide = token_ref[...].astype(F32)
        normed = (wide * rms_factor(wide) * gain_ref[...]).astype(BF16)
        normed_ref[...] = normed
        pre = matmul(normed, weight_ref[...])
        q_ref[at, :] = pre[:, :columns]
        k_ref[at, :] = pre[:, columns : 2 * columns]
        v_ref[at, :] = pre[:, 2 * columns :].astype(BF16)
        for j in range(2):
            squares = 0.0
            for c in range(j * columns, (j + 1) * columns, DH):
                squares += pre[:, c : c + DH] * pre[:, c : c + DH]
            square_ref[j : j + 1, at] = jnp.sum(squares.T, axis=0, keepdims=True)


def project(even, odd, weight, gain, me, rows):
    pairs = even.shape[0] // rows
    length = 2 * even.shape[0]
    depth, columns = weight.shape[0], weight.shape[1] // 3
    token = pl.BlockSpec((rows, depth), lambda i, me: (i, 0))

    def placed(shape):
        return pl.BlockSpec(shape, lambda i, me: (i ^ (me[0] // 2), 0))

    head = jax.ShapeDtypeStruct((length, columns), F32)
    return pl.pallas_call(
        qkv_kernel,
        grid_spec=pltpu.PrefetchScalarGridSpec(
            num_scalar_prefetch=1,
            grid=(pairs,),
            in_specs=[
                token,
                token,
                pl.BlockSpec(weight.shape, lambda i, me: (0, 0)),
                pl.BlockSpec((1, depth), lambda i, me: (0, 0)),
            ],
            out_specs=[
                token,
                token,
                placed((2 * rows, columns)),
                placed((2 * rows, columns)),
                placed((2 * rows, columns)),
                pl.BlockSpec((2, 2 * rows), lambda i, me: (0, i ^ (me[0] // 2))),
            ],
        ),
        out_shape=[
            jax.ShapeDtypeStruct((length // 2, depth), BF16),
            jax.ShapeDtypeStruct((length // 2, depth), BF16),
            head,
            head,
            jax.ShapeDtypeStruct((length, columns), BF16),
            jax.ShapeDtypeStruct((2, length), F32),
        ],
        compiler_params=pltpu.CompilerParams(vmem_limit_bytes=48 * MIB),
        cost_estimate=pl.CostEstimate(
            flops=6 * length * depth * columns,
            bytes_accessed=length * (4 * depth + 10 * columns) + 6 * depth * columns,
            transcendentals=length,
        ),
        name="project",
    )(me, even, odd, weight, gain)


def split_kernel(q_ref, k_ref, v_ref, out_ref):
    columns = q_ref.shape[1]
    for j, ref in enumerate((q_ref, k_ref, v_ref)):
        out_ref[0, :, j * columns : (j + 1) * columns] = ref[...]


def split_heads(w_query, w_key, w_value, parts):
    rows, columns = w_query.shape[0], w_query.shape[1] // parts
    block = pl.BlockSpec((rows, columns), lambda i: (0, i))
    return pl.pallas_call(
        split_kernel,
        grid=(parts,),
        in_specs=[block] * 3,
        out_specs=pl.BlockSpec((1, rows, 3 * columns), lambda i: (i, 0, 0)),
        out_shape=jax.ShapeDtypeStruct((parts, rows, 3 * columns), BF16),
        name="split_heads",
    )(w_query, w_key, w_value)


def spread(row, columns):
    return jnp.broadcast_to(row, (columns, row.shape[1])).T


def factor_of(square_row):
    return lax.rsqrt(square_row / D + EPSILON)


def turn(values, cosine, sine):
    return values * cosine + pltpu.roll(values, DH // 2, 1) * sine


def rope_kernel(q_ref, k_ref, square_ref, gain_ref, cos_ref, sin_ref, q_out, k_out):
    cosine, sine = cos_ref[...], sin_ref[...]
    for j, (pre_ref, out_ref) in enumerate(((q_ref, q_out), (k_ref, k_out))):
        factor = spread(factor_of(square_ref[j : j + 1, :]), DH)
        for c in range(0, pre_ref.shape[1], DH):
            at = slice(c, c + DH)
            normed = pre_ref[:, at] * factor * gain_ref[j : j + 1, at]
            out_ref[:, at] = turn(normed, cosine, sine).astype(BF16)


def rope(query_pre, key_pre, squares, gains, cosine, sine):
    length, columns = query_pre.shape
    rows = min(512, length)
    block = pl.BlockSpec((rows, columns), lambda i: (i, 0))
    table = pl.BlockSpec((rows, DH), lambda i: (i, 0))
    return pl.pallas_call(
        rope_kernel,
        grid=(length // rows,),
        in_specs=[
            block,
            block,
            pl.BlockSpec((2, rows), lambda i: (0, i)),
            pl.BlockSpec((2, columns), lambda i: (0, 0)),
            table,
            table,
        ],
        out_specs=[block, block],
        out_shape=[jax.ShapeDtypeStruct((length, columns), BF16)] * 2,
        compiler_params=pltpu.CompilerParams(vmem_limit_bytes=32 * MIB),
        name="rope",
    )(query_pre, key_pre, squares, gains, cosine, sine)


def pulled_of(grad_ref, pre_ref, factor, gain_ref, cosine, sine, j, at):
    turned = turn(grad_ref[:, at].astype(F32), cosine, -sine)
    return turned, turned * gain_ref[j : j + 1, at], pre_ref[:, at] * factor


def rope_mean_kernel(
    dq_ref, dk_ref, q_ref, k_ref, square_ref, gain_ref, cos_ref, sin_ref, mean_ref, term_ref
):
    @pl.when(pl.program_id(0) == 0)
    def _():
        term_ref[...] = jnp.zeros_like(term_ref)

    cosine, sine = cos_ref[...], sin_ref[...]
    for j, (grad_ref, pre_ref) in enumerate(((dq_ref, q_ref), (dk_ref, k_ref))):
        factor = spread(factor_of(square_ref[j : j + 1, :]), DH)
        total = 0.0
        for c in range(0, pre_ref.shape[1], DH):
            at = slice(c, c + DH)
            turned, pulled, normed = pulled_of(
                grad_ref, pre_ref, factor, gain_ref, cosine, sine, j, at
            )
            term_ref[j : j + 1, at] += jnp.sum(turned * normed, axis=0, keepdims=True)
            total += pulled * normed
        mean_ref[j : j + 1, :] = jnp.sum(total.T, axis=0, keepdims=True)


def rope_means(query_back, key_back, query_pre, key_pre, squares, gains, cosine, sine):
    length, columns = query_pre.shape
    rows = min(512, length)
    block = pl.BlockSpec((rows, columns), lambda i: (i, 0))
    table = pl.BlockSpec((rows, DH), lambda i: (i, 0))
    row = pl.BlockSpec((2, rows), lambda i: (0, i))
    fixed = pl.BlockSpec((2, columns), lambda i: (0, 0))
    return pl.pallas_call(
        rope_mean_kernel,
        grid=(length // rows,),
        in_specs=[block, block, block, block, row, fixed, table, table],
        out_specs=[row, fixed],
        out_shape=[
            jax.ShapeDtypeStruct((2, length), F32),
            jax.ShapeDtypeStruct((2, columns), F32),
        ],
        compiler_params=pltpu.CompilerParams(vmem_limit_bytes=32 * MIB),
        name="rope_means",
    )(query_back, key_back, query_pre, key_pre, squares, gains, cosine, sine)


def rope_back_kernel(
    me_ref,
    dq_ref,
    dk_ref,
    dv_ref,
    q_ref,
    k_ref,
    square_ref,
    mean_ref,
    gain_ref,
    cos_ref,
    sin_ref,
    out_ref,
):
    cosine, sine = cos_ref[...], sin_ref[...]
    columns = q_ref.shape[1]
    for j, (grad_ref, pre_ref) in enumerate(((dq_ref, q_ref), (dk_ref, k_ref))):
        factor = spread(factor_of(square_ref[j : j + 1, :]), DH)
        mean = spread(mean_ref[j : j + 1, :] / D, DH)
        for c in range(0, columns, DH):
            at = slice(c, c + DH)
            _, pulled, normed = pulled_of(grad_ref, pre_ref, factor, gain_ref, cosine, sine, j, at)
            out_ref[:, j * columns + c : j * columns + c + DH] = (
                factor * (pulled - normed * mean)
            ).astype(BF16)
    out_ref[:, 2 * columns :] = dv_ref[...]


def rope_back(grads, query_pre, key_pre, squares, means, gains, cosine, sine, me, rows):
    length, columns = query_pre.shape
    half = length // rows // 2

    def source(p, me):
        return me[0] ^ (p % half * 2 + p // half)

    block = pl.BlockSpec((rows, columns), lambda p, me: (source(p, me), 0))
    table = pl.BlockSpec((rows, DH), lambda p, me: (source(p, me), 0))
    row = pl.BlockSpec((2, rows), lambda p, me: (0, source(p, me)))
    return pl.pallas_call(
        rope_back_kernel,
        grid_spec=pltpu.PrefetchScalarGridSpec(
            num_scalar_prefetch=1,
            grid=(2 * half,),
            in_specs=[block] * 5
            + [row, row, pl.BlockSpec((2, columns), lambda p, me: (0, 0)), table, table],
            out_specs=pl.BlockSpec((rows, 3 * columns), lambda p, me: (p, 0)),
        ),
        out_shape=jax.ShapeDtypeStruct((length, 3 * columns), BF16),
        compiler_params=pltpu.CompilerParams(vmem_limit_bytes=32 * MIB),
        name="rope_back",
    )(me, *grads, query_pre, key_pre, squares, means, gains, cosine, sine)


def output_kernel(
    me_ref, come_ref, even_ref, odd_ref, token_ref, gain_ref, residual_ref, second_ref, total_ref
):
    step, half = pl.program_id(0), pl.num_programs(0) // 2

    @pl.when(step == 0)
    def _():
        total_ref[...] = token_ref[...].astype(F32)

    @pl.when(step < half)
    def _():
        total_ref[...] += matmul(come_ref[0], even_ref[...])

    @pl.when(step >= half)
    def _():
        total_ref[...] += matmul(come_ref[0], odd_ref[...])

    @pl.when(step == 2 * half - 1)
    def _():
        total = total_ref[...]
        residual_ref[...] = total
        second_ref[...] = (total * rms_factor(total) * gain_ref[...]).astype(BF16)


def project_out(come, even, odd, tokens, gain, me):
    size, rows, columns = come.shape
    depth = even.shape[1]
    half = size // 2
    whole = pl.BlockSpec((rows, depth), lambda p, me: (0, 0))
    return pl.pallas_call(
        output_kernel,
        grid_spec=pltpu.PrefetchScalarGridSpec(
            num_scalar_prefetch=1,
            grid=(size,),
            in_specs=[
                pl.BlockSpec(
                    (1, rows, columns), lambda p, me: (me[0] ^ (p % half * 2 + p // half), 0, 0)
                ),
                pl.BlockSpec((columns, depth), lambda p, me: (jnp.minimum(p, half - 1), 0)),
                pl.BlockSpec((columns, depth), lambda p, me: (jnp.maximum(p - half, 0), 0)),
                whole,
                pl.BlockSpec((1, depth), lambda p, me: (0, 0)),
            ],
            out_specs=[whole, whole],
            scratch_shapes=[pltpu.VMEM((rows, depth), F32)],
        ),
        out_shape=[
            jax.ShapeDtypeStruct((rows, depth), F32),
            jax.ShapeDtypeStruct((rows, depth), BF16),
        ],
        compiler_params=pltpu.CompilerParams(vmem_limit_bytes=32 * MIB),
        name="project_out",
    )(me, come, even, odd, tokens, gain)


def expert_kernel(
    in_places, down_places, first_ref, xa_ref, xb_ref, ua_ref, ub_ref, ra_ref, rb_ref, router_ref, *refs
):
    weight_refs = refs[: len(in_places) + len(down_places)]
    (ya_ref, yb_ref, za_ref, zb_ref, ga_ref, gb_ref, xc_ref, uc_ref, dg_ref, hid_ref) = refs[-13:-3]
    wi_ref, wd_ref, sems = refs[-3:]
    experts, _, hidden = hid_ref.shape
    rows = xa_ref.shape[0]

    @pl.when(pl.program_id(0) == 0)
    def _():
        copies = []
        for n, (ref, (r, first, part)) in enumerate(zip(weight_refs, in_places + down_places)):
            goal = wi_ref if n < len(in_places) else wd_ref
            place = lax.rem(first_ref[1] ^ r, goal.shape[1] // part)
            at = pl.ds(pl.multiple_of(place * part + first, ref.shape[1]), ref.shape[1])
            copies.append(pltpu.make_async_copy(ref, goal.at[:, at, :], sems.at[n]))
        for copy in copies:
            copy.start()
        for copy in copies:
            copy.wait()

    slot = lax.broadcasted_iota(jnp.int32, (CAP, rows), 0)
    blocks = (
        (xa_ref, ua_ref, ra_ref, ya_ref, za_ref, ga_ref),
        (xb_ref, ub_ref, rb_ref, yb_ref, zb_ref, gb_ref),
    )
    picks = []
    for k, (x_ref, u_ref, rank_ref, _, _, _) in enumerate(blocks):
        hits = jnp.concatenate([slot == rank_ref[0, e : e + 1, :] for e in range(experts)], 0)
        pick = hits.astype(F32).astype(BF16)
        picks.append(pick)
        x_rows = matmul(pick, x_ref[...]).astype(BF16)
        u_rows = matmul(pick, u_ref[...]).astype(BF16)
        for e in range(experts):
            xc_ref[e, k * CAP : (k + 1) * CAP, :] = x_rows[e * CAP : (e + 1) * CAP]
            uc_ref[e, k * CAP : (k + 1) * CAP, :] = u_rows[e * CAP : (e + 1) * CAP]
    outs, backs, gate_grads = [], [], []
    for e in range(experts):
        x_rows, u_rows = xc_ref[e], uc_ref[e]
        logits = matmul(x_rows, router_ref[...])
        lane = lax.broadcasted_iota(jnp.int32, logits.shape, 1)
        logits = jnp.where(lane < E, logits, -1e30)
        expos = jnp.exp(logits - jnp.max(logits, axis=-1, keepdims=True))
        own = jnp.sum(jnp.where(lane == first_ref[0] + e, expos, 0.0), axis=-1, keepdims=True)
        gate = own / jnp.sum(expos, axis=-1, keepdims=True)
        gated = matmul(x_rows, wi_ref[e, :, :hidden])
        upward = matmul(x_rows, wi_ref[e, :, hidden:])
        pulled = matmul_t(u_rows, wd_ref[e])
        sig = jax.nn.sigmoid(gated)
        silu = gated * sig
        acts = silu * upward
        gate_grads.append(jnp.sum(acts * pulled, axis=-1, keepdims=True))
        hidden_gate = (acts * gate).astype(BF16)
        hidden_grads = pulled * gate
        hid_ref[e] = hidden_gate
        dg_ref[e, :, :hidden] = (hidden_grads * upward * sig * (1.0 + gated * (1.0 - sig))).astype(BF16)
        dg_ref[e, :, hidden:] = (hidden_grads * silu).astype(BF16)
        outs.append(matmul(hidden_gate, wd_ref[e]).astype(BF16))
        backs.append(matmul_t(dg_ref[e], wi_ref[e]).astype(BF16))
    for k, (_, _, rank_ref, y_ref, z_ref, g_ref) in enumerate(blocks):
        at = slice(k * CAP, (k + 1) * CAP)
        y_ref[...] = t_matmul(picks[k], jnp.concatenate([v[at] for v in outs], 0)).astype(BF16)
        z_ref[...] = t_matmul(picks[k], jnp.concatenate([v[at] for v in backs], 0)).astype(BF16)
        for e in range(experts):
            hit = slot == rank_ref[0, e : e + 1, :]
            g_ref[0, e : e + 1, :] = jnp.sum(
                jnp.where(hit, gate_grads[e][at], 0.0), axis=0, keepdims=True
            )


def run_experts(x, u, ranks, in_pieces, down_pieces, router, places, which, compact, parts):
    experts, _, hidden = in_pieces[0][2].shape
    hidden = hidden // 2
    depth = x[0].shape[1]
    in_places = [(r, at, parts[0]) for r, at, _ in in_pieces]
    down_places = [(r, at, parts[1]) for r, at, _ in down_pieces]
    pieces = [array for _, _, array in in_pieces + down_pieces]
    rows = ranks[0].shape[2]
    steps = x[0].shape[0] // rows
    token = pl.BlockSpec((rows, depth), lambda i: (i, 0))
    rank = pl.BlockSpec((1, experts, rows), lambda i: (i, 0, 0))
    anywhere = pl.BlockSpec(memory_space=pl.ANY)

    def slots(columns):
        return pl.BlockSpec((experts, 2 * CAP, columns), lambda i: (0, i + which * steps, 0))

    shape = jax.ShapeDtypeStruct
    tokens = shape(x[0].shape, BF16)
    gates = shape((steps, experts, rows), F32)
    count = 4 * steps * CAP
    wide = shape((experts, count, depth), BF16)
    inputs = [places, *x, *u, *ranks, router, *pieces]
    return pl.pallas_call(
        partial(expert_kernel, in_places, down_places),
        grid=(steps,),
        in_specs=[pl.BlockSpec(memory_space=pltpu.SMEM)]
        + [token] * 4
        + [rank] * 2
        + [pl.BlockSpec(router.shape, lambda i: (0, 0), pipeline_mode=pl.Buffered(1))]
        + [anywhere] * (len(pieces) + len(compact)),
        out_specs=[token] * 4 + [rank] * 2 + [slots(depth)] * 2 + [slots(2 * hidden), slots(hidden)],
        out_shape=[tokens] * 4
        + [gates] * 2
        + [wide] * 2
        + [shape((experts, count, 2 * hidden), BF16), shape((experts, count, hidden), BF16)],
        scratch_shapes=[
            pltpu.VMEM((experts, depth, 2 * hidden), BF16),
            pltpu.VMEM((experts, hidden, depth), BF16),
            pltpu.SemaphoreType.DMA((len(pieces),)),
        ],
        input_output_aliases={len(inputs) + i: 6 + i for i in range(len(compact))},
        compiler_params=pltpu.CompilerParams(vmem_limit_bytes=60 * MIB),
        cost_estimate=pl.CostEstimate(
            flops=4 * steps * CAP * experts * depth * (7 * hidden + 2 * rows),
            bytes_accessed=60 * MIB,
            transcendentals=2 * steps * CAP * experts * hidden,
        ),
        name="experts",
    )(*inputs, *compact)


def product_kernel(me_ref, left_ref, right_ref, out_ref):
    out_ref[0] = t_matmul(left_ref[0], right_ref[0]).astype(BF16)


def products(left, right, part, r, count, me, name):
    experts, rows, _ = left.shape
    columns = right.shape[2]
    wide = min(columns, 1024)
    return pl.pallas_call(
        product_kernel,
        grid_spec=pltpu.PrefetchScalarGridSpec(
            num_scalar_prefetch=1,
            grid=(experts, columns // wide),
            in_specs=[
                pl.BlockSpec((1, rows, part), lambda e, j, me: (e, 0, lax.rem(me[0] ^ r, count))),
                pl.BlockSpec((1, rows, wide), lambda e, j, me: (e, 0, j)),
            ],
            out_specs=pl.BlockSpec((1, part, wide), lambda e, j, me: (e, 0, j)),
        ),
        out_shape=jax.ShapeDtypeStruct((experts, part, columns), BF16),
        compiler_params=pltpu.CompilerParams(vmem_limit_bytes=56 * MIB),
        cost_estimate=pl.CostEstimate(
            flops=2 * experts * rows * part * columns,
            bytes_accessed=2 * experts * rows * (part + columns),
            transcendentals=0,
        ),
        name=name,
    )(me, left, right)


def per_device(
    S,
    F,
    tokens,
    segments,
    routes,
    cotangent,
    w_query,
    w_key,
    w_value,
    w_output,
    router,
    attn_gain,
    moe_gain,
    query_gain,
    key_gain,
    w_gate,
    w_up,
    w_down,
):
    s = lax.axis_index("seq")
    f = lax.axis_index("fsdp")
    T = tokens.shape[1]
    L = S * T
    heads = H // S
    C = heads * DH
    experts = E // S
    part = w_query.shape[0]
    half_f = F // 2
    hidden_half = w_gate.shape[2] // 2

    me = s.reshape(1).astype(jnp.int32)
    f_at = f.reshape(1).astype(jnp.int32)
    half_at = f // half_f
    tokens_low = tokens[0]
    upstream_low = cotangent[0]
    inputs = tokens_low.astype(F32)
    half_rows = T // 2
    in_part, down_part = w_gate.shape[1], w_down.shape[1]
    quarter = in_part // 4

    def hidden_part(which, first, count):
        return jnp.concatenate(
            [
                lax.dynamic_slice(
                    weight, (0, first, which * hidden_half), (experts, count, hidden_half)
                )
                for weight in (w_gate, w_up)
            ],
            2,
        )

    def far_swap(values, *dep):
        return swap(after(values, dep), "fsdp", F, half_f)

    def near_swap(values, *dep):
        return near_pieces(after(values, dep), F)

    named = routes[0].T[None] == jnp.arange(E, dtype=jnp.int32)[:, None, None]
    chosen = jnp.any(named, axis=1)
    index = jnp.arange(T, dtype=jnp.int32)
    before = (index[:, None] <= index[None, :]).astype(BF16)
    ranks = jnp.where(chosen, matmul(chosen.astype(BF16), before) - 1.0, -1.0)
    small = jnp.concatenate(
        [
            router.reshape(-1),
            attn_gain,
            moe_gain,
            query_gain,
            key_gain,
            ranks.astype(BF16).reshape(-1),
        ]
    )[None]
    crossed = split_heads(w_query, w_key, w_value, S)
    small = double(after(small, crossed), "fsdp", F)
    crossed = lax.all_to_all(crossed, "seq", split_axis=0, concat_axis=0, tiled=True)
    near_own = [near_swap(hidden_part(half_at, 0, 2 * quarter), small)]
    out_dep = small
    small = double(small, "seq", S)
    out_far = far_swap(w_output, out_dep)
    crossed, near_own[0], small, out_far = tie(crossed, near_own[0], small, out_far)

    held = after((w_gate, w_up, w_down, upstream_low), crossed)

    def held_part(which, first, count):
        return jnp.concatenate(
            [
                lax.dynamic_slice(
                    weight, (0, first, which * hidden_half), (experts, count, hidden_half)
                )
                for weight in held[:2]
            ],
            2,
        )

    own_quarters = {n: held_part(half_at, n * quarter, quarter) for n in (2, 3)}
    far_quarters = [held_part(1 - half_at, n * quarter, quarter) for n in range(4)]
    down_rows = quarters(held[2], 1)
    upstream_halves = [held[3][:half_rows], held[3][half_rows:]]
    small = in_order(small, S, F, s, f).reshape(S, F, -1)
    prepared = (own_quarters, far_quarters, down_rows, upstream_halves, small)
    token_first = gather_first(after(tokens_low, crossed), S)
    qkv_pieces = {0: crossed}
    for r in range(1, F):
        low = low_bit(r)
        qkv_pieces[r] = swap(qkv_pieces[r ^ low], "fsdp", F, low)
        if r == half_f:
            qkv_pieces, token_first, prepared = tie(qkv_pieces, token_first, prepared)
            own_quarters, far_quarters, down_rows, upstream_halves, small = prepared
            partner_up = [far_swap(upstream_halves[0])]
    token_more = gather_more(tokens_low, token_first, S)
    rank_part = small[:, :, part * (E + 4) :].reshape(S, F, E, T)

    def ranks_of(index):
        ranks = lax.dynamic_slice(rank_part, (0, index, s * experts, 0), (S, 1, experts, T))
        ranks = relative(ranks[:, 0], s).astype(jnp.int32)
        return ranks[: S // 2], ranks[S // 2 :]

    own_ranks, other_ranks = ranks_of(f), ranks_of(f ^ half_f)
    qkv_pieces, partner_up[0], token_more, own_ranks, other_ranks = tie(
        qkv_pieces, partner_up[0], token_more, own_ranks, other_ranks
    )
    tokens_even, tokens_odd = gather_end(tokens_low, token_first, token_more, S)
    w_qkv = place_fsdp(qkv_pieces, f, 1).reshape(D, 3 * C)

    full_router = small[:, :, : part * E].reshape(D, E)
    gains = [
        small[:, :, part * (E + i) : part * (E + i + 1)].reshape(D).astype(F32) for i in range(4)
    ]
    gain_attn, gain_moe = gains[0], gains[1]
    head_gain = lax.dynamic_slice(jnp.stack(gains[2:], 0), (0, s * C), (2, C))
    places = jnp.arange(L, dtype=jnp.int32).astype(F32)
    freqs = ROPE_BASE ** (-(jnp.arange(DH // 2, dtype=F32) * 2.0 / DH))
    angles = places[:, None] * freqs[None, :]
    cosine, sine = jnp.cos(angles), jnp.sin(angles)
    cosine = jnp.concatenate([cosine, cosine], 1)
    sine = jnp.concatenate([-sine, sine], 1)

    def far_part(n, *dep):
        return far_swap(far_quarters[n], *dep)

    partner_up.append(far_swap(upstream_halves[1], w_qkv))
    out_pieces = {0: after(w_output, w_qkv), half_f: after(out_far, w_qkv)}
    for r in range(1, F):
        if r != half_f:
            low = low_bit(r)
            out_pieces[r] = swap(out_pieces[r ^ low], "fsdp", F, low)
    own_up_first = gather_first(after(upstream_low, w_qkv), S)
    normed_even, normed_odd, query_pre, key_pre, value_low, squares = project(
        tokens_even, tokens_odd, w_qkv, gain_attn[None], me, T
    )
    squares, partner_up[1], out_pieces, own_up_first = tie(
        squares, partner_up[1], out_pieces, own_up_first
    )
    partner_up = jnp.concatenate(partner_up, 0)
    own_output = place_fsdp(out_pieces, f, 0).reshape(C, D)

    out_first = gather_first(own_output, S)
    far = [far_part(0, squares)]
    near_own.append(near_swap(own_quarters[2], squares))
    squares = sum_all(squares, "seq", S)
    query_low, key_low = rope(query_pre, key_pre, squares, head_gain, cosine, sine)
    query_low, out_first, far[0], near_own[1] = tie(query_low, out_first, far[0], near_own[1])

    seg_row = segments
    seg_col = segments.reshape(L, 1)
    out_more = gather_more(own_output, out_first, S)
    far.append(far_part(1, query_low))
    near_own.append(near_swap(own_quarters[3], query_low))
    attended, lse = attention_forward(query_low, key_low, value_low, seg_row, seg_col)
    attended, out_more, far[1], near_own[2] = tie(attended, out_more, far[1], near_own[2])
    attended_blocks = attended.reshape(S, T, C)
    come = lax.all_to_all(attended_blocks, "seq", split_axis=0, concat_axis=0, tiled=True)
    out_even, out_odd = gather_end(own_output, out_first, out_more, S)
    far.append(far_part(2, attended))
    near_far = [near_swap(far[0], attended)]
    own_up_more = gather_more(after(upstream_low, attended), own_up_first, S)
    come, far[2], near_far[0], own_up_more = tie(come, far[2], near_far[0], own_up_more)
    own_u = gather_end(upstream_low, own_up_first, own_up_more, S)
    near_far.append(near_swap(far[1], come))
    down = [near_swap(down_rows[0], come)]
    partner_up_first = gather_first(after(partner_up, come), S)
    residual, second_low = project_out(come, out_even, out_odd, tokens_low, gain_moe[None], me)
    second_low, down[0], near_far[1], partner_up_first, own_u = tie(
        second_low, down[0], near_far[1], partner_up_first, own_u
    )

    own_first = gather_first(second_low, S)
    partner_low = [far_swap(second_low[:half_rows])]
    near_far.append(near_swap(far[2], second_low))
    own_first, partner_low[0], near_far[2] = tie(own_first, partner_low[0], near_far[2])
    own_more = gather_more(second_low, own_first, S)
    partner_low.append(far_swap(second_low[half_rows:], own_first))
    down.append(near_swap(down_rows[1], own_first))
    partner_up_more = gather_more(after(partner_up, own_first), partner_up_first, S)
    own_more, partner_low[1], down[1], partner_up_more = tie(
        own_more, partner_low[1], down[1], partner_up_more
    )
    partner_low = jnp.concatenate(partner_low, 0)
    own_x = gather_end(second_low, own_first, own_more, S)
    partner_first = gather_first(after(partner_low, own_more), S)
    down.append(near_swap(down_rows[2], own_more))
    far.append(far_part(3, own_more))
    partner_first, down[2], own_x, far[3] = tie(partner_first, down[2], own_x, far[3])
    other_u = gather_end(after(partner_up, partner_first), partner_up_first, partner_up_more, S)
    partner_more = gather_more(partner_low, partner_first, S)
    down.append(near_swap(down_rows[3], partner_first))
    near_far.append(near_swap(far[3], partner_first))
    partner_more, down[3], other_u, near_far[3] = tie(partner_more, down[3], other_u, near_far[3])
    other_x = gather_end(partner_low, partner_first, partner_more, S)
    in_pieces = []
    for r in range(F):
        for n, rows in enumerate(near_own if r < half_f else near_far):
            first = (0, 2, 3)[n] if r < half_f else n
            in_pieces.append((r, first * quarter, rows[r % half_f]))
    down_pieces = [
        (r, n * (down_part // 4), down[n][r]) for r in range(half_f) for n in range(4)
    ]
    wide_router = jnp.pad(full_router, ((0, 0), (0, 128 - E)))
    expert_places = jnp.stack([s * experts, f]).astype(jnp.int32)
    parts = (in_part, down_part)
    own_parts = run_experts(
        own_x, own_u, own_ranks, in_pieces, down_pieces, wide_router, expert_places, 0, (), parts
    )
    own_parts, other_x = tie(own_parts, other_x)
    own_got = swap(own_parts[3], "seq", S, 1)
    own_out_got = swap(own_parts[1], "seq", S, 1)
    other_parts = run_experts(
        other_x,
        other_u,
        other_ranks,
        in_pieces,
        down_pieces,
        wide_router,
        expert_places,
        1,
        own_parts[6:],
        parts,
    )
    other_parts, own_got, own_out_got = tie(other_parts, own_got, own_out_got)
    moe_factor = rms_factor(residual)
    residual_n = residual * moe_factor
    logits = matmul(second_low, full_router)
    router_probs = jax.nn.softmax(logits, axis=-1)

    x_rows, u_rows, in_grads, hidden_gate = other_parts[6:]
    in_terms, down_terms = {}, {}

    def in_products(r, *dep):
        in_terms[r] = products(
            x_rows, after(in_grads, dep), in_part, r, F, f_at, "in_products"
        )

    odd = [r for r in range(F) if r & 1]
    far_odd = [r for r in odd if r & half_f]
    near_odd = [r for r in odd if not r & half_f]

    def to_home(even, odd):
        return absolute(jnp.concatenate([even, odd], 0).transpose(0, 2, 1), s)

    gate_grads = jnp.stack(
        [to_home(own_parts[4], own_parts[5]), to_home(other_parts[4], other_parts[5])], 1
    ).reshape(S, -1)
    other_got = swap(other_parts[3], "seq", S, 1)
    gate_grads = lax.all_to_all(gate_grads, "seq", split_axis=0, concat_axis=0, tiled=True)
    other_got, gate_grads = tie(other_got, gate_grads)
    for r in far_odd:
        in_products(r, other_got)

    def send_in(n, *dep):
        return {r: swap(after(sent[r][n], dep), "fsdp", F, 1) for r in sent}

    other_sums = sum_cores(other_parts[2], other_got, S)
    come = sum_first(other_sums, S)
    other_out_got = swap(after(other_parts[1], other_got), "seq", S, 1)
    gate_grads = gate_grads.reshape(S, 2, T * experts)
    partner_grads = far_swap(gate_grads[:, 1])
    come, in_terms, other_out_got, partner_grads = tie(
        come, in_terms, other_out_got, partner_grads
    )
    sent = {r: quarters(in_terms[r], 1) for r in far_odd}
    singles, other_total = sum_more(other_sums, come, S)
    come = sum_last(singles, S)
    start_got = {r: swap(in_terms[r][:, : 2 * quarter], "fsdp", F, 1) for r in far_odd}

    def down_products(r, dep):
        down_terms[r] = products(
            after(hidden_gate, dep), u_rows, down_part, r, half_f, f_at, "down_products"
        )

    for r in range(1, half_f, 2):
        down_products(r, singles)
    come, start_got, down_terms = tie(come, start_got, down_terms)
    far_got = [
        {r: got[:, n * quarter : (n + 1) * quarter] for r, got in start_got.items()}
        for n in range(2)
    ]
    other_rows = add_all(other_total, come).astype(BF16)
    gate_grads = gate_grads[:, 0] + partner_grads
    gate_grads = gate_grads.reshape(S, T, experts).transpose(1, 0, 2).reshape(T, E)
    back = [far_swap(other_rows[:half_rows])]
    own_sums = sum_cores(own_parts[2], after(own_got, other_rows), S)
    come = sum_first(own_sums, S)
    far_got.append(send_in(2, other_rows))
    for r in far_odd:
        in_products(r ^ 1, other_rows)
    come, back[0], far_got[2], in_terms = tie(come, back[0], far_got[2], in_terms)
    back.append(far_swap(other_rows[half_rows:], come))
    singles, own_total = sum_more(own_sums, come, S)
    come = sum_last(singles, S)
    down_sent = {r: quarters(down_terms[r], 1) for r in range(1, half_f, 2)}
    for r in down_sent:
        down_sent[r] = down_sent[r][:2] + [jnp.concatenate(down_sent[r][2:], 1)]

    def send_down(n, *dep):
        return {r: swap(after(down_sent[r][n], dep), "fsdp", F, 1) for r in down_sent}

    far_got.append(send_in(3, singles))
    for r in near_odd:
        in_products(r, singles)
    come, back[1], far_got[3], in_terms = tie(come, back[1], far_got[3], in_terms)
    row_grads = add_all(own_total, come) + jnp.concatenate(back, 0).astype(F32)

    upstream = upstream_low.astype(F32)
    logit_grads = router_probs * (
        gate_grads - jnp.sum(router_probs * gate_grads, axis=-1, keepdims=True)
    )
    router_wide = full_router.astype(F32)
    second_grads = row_grads + jnp.dot(logit_grads, router_wide.T, precision=HIGHEST)
    pulled = second_grads * gain_moe
    residual_grads = upstream + moe_factor * (
        pulled - residual_n * jnp.mean(pulled * residual_n, axis=-1, keepdims=True)
    )
    branch_low = residual_grads.astype(BF16)

    def sum_near(terms):
        mask = 2
        while mask < half_f:
            terms = {
                r: terms[r] + swap(terms[r | mask].astype(BF16), "fsdp", F, mask).astype(F32)
                for r in terms
                if not r & mask
            }
            mask *= 2
        (total,) = terms.values()
        return total

    def far_sum(n, *dep):
        terms = {
            r ^ 1: quarters(in_terms[r ^ 1], 1)[n].astype(F32) + far_got[n][r].astype(F32)
            for r in far_odd
        }
        return far_swap(sum_near(terms).astype(BF16), *dep)

    branch_first = gather_first(branch_low, S)
    far_sums = [far_sum(0, branch_low)]
    down_got = [send_down(0, branch_low)]
    for r in range(0, half_f, 2):
        down_products(r, branch_low)
    branch_first, far_sums[0], down_got[0], down_terms = tie(
        branch_first, far_sums[0], down_got[0], down_terms
    )
    branch_more = gather_more(branch_low, branch_first, S)
    far_sums.append(far_sum(1, branch_first))
    down_got.append(send_down(1, branch_first))
    branch_even, branch_odd = gather_end(branch_low, branch_first, branch_more, S)

    head_grads = jnp.concatenate(
        [matmul_t(branch_even, own_output), matmul_t(branch_odd, own_output)], 0
    ).astype(BF16)
    head_grads = absolute(head_grads.reshape(S, T, C), s).reshape(L, C)
    head_grads, far_sums[1], down_got[1] = tie(head_grads, far_sums[1], down_got[1])
    far_sums.append(far_sum(2, head_grads))
    down_got.append(send_down(2, head_grads))
    other_out_sums = sum_cores(other_parts[0], after(other_out_got, head_grads), S)
    come, head_grads = sum_first(other_out_sums, S, head_grads)
    query_back, key_back, value_back = attention_backward(
        query_low, key_low, value_low, head_grads, lse, seg_row, seg_col
    )
    query_back, key_back, value_back, far_sums[2], down_got[2], come = tie(
        query_back, key_back, value_back, far_sums[2], down_got[2], come
    )

    singles, other_total = sum_more(other_out_sums, come, S)
    come = sum_last(singles, S)
    far_sums.append(far_sum(3, query_back))
    attended_rel = relative(after(attended_blocks, singles), s).reshape(2, L // 2, C)
    output_term = t_matmul(attended_rel[0], branch_even) + t_matmul(attended_rel[1], branch_odd)
    output_term = by_index(output_term.astype(BF16).reshape(F, part, D), f, F)
    output_got = swap(output_term[: F // 2], "fsdp", F, 1)
    value_rel = relative(value_back.reshape(S, T, C), s).reshape(2, L // 2, C)

    def weight_term(even, odd):
        term = (t_matmul(normed_even, even) + t_matmul(normed_odd, odd)).astype(BF16)
        return by_index(term.reshape(S, F, part, -1).transpose(1, 0, 2, 3), f, F)

    means, gain_term = rope_means(
        query_back, key_back, query_pre, key_pre, squares, head_gain, cosine, sine
    )
    means = sum_all(means, "seq", S)
    value_term = weight_term(value_rel[0], value_rel[1])
    means, come, far_sums[3], output_got, value_term = tie(
        means, come, far_sums[3], output_got, value_term
    )
    other_outs = add_all(other_total, come).astype(BF16)
    value_got = swap(value_term[: F // 2], "fsdp", F, 1)
    pre_rel = rope_back(
        (query_back, key_back, value_back),
        query_pre,
        key_pre,
        squares,
        means,
        head_gain,
        cosine,
        sine,
        me,
        T,
    ).reshape(2, L // 2, 3 * C)
    normed_got = swap(matmul_t(pre_rel[1], w_qkv).astype(BF16), "seq", S, 1)
    normed_kept = matmul_t(pre_rel[0], w_qkv).astype(BF16)
    normed_got, normed_kept, value_got = tie(normed_got, normed_kept, value_got)

    normed_sums = sum_cores(normed_kept, normed_got, S)
    come = sum_first(normed_sums, S)
    value_sum = sum_rest(sum_even(value_term, value_got, F), F)
    turned_term = weight_term(
        after(pre_rel[0][:, : 2 * C], normed_got), after(pre_rel[1][:, : 2 * C], normed_got)
    )
    late_grads, late_logits = after(second_grads, normed_got), after(logit_grads, normed_got)
    router_term = jnp.dot(second_low.astype(F32).T, late_logits, precision=HIGHEST)
    moe_gain_term = jnp.sum(late_grads * residual_n, axis=0)
    gain_terms = jnp.concatenate(
        [router_term.reshape(S * F, part * E), moe_gain_term.reshape(S * F, part)], 1
    )
    gain_terms = in_relative(gain_terms, S, F, s, f).reshape(S, F, -1)
    head_terms = gain_term.reshape(2, F, part).transpose(1, 0, 2).reshape(F, 2 * part)
    head_terms = in_relative(head_terms, 1, F, 0, f)
    gain_terms = jnp.concatenate([gain_terms.transpose(1, 0, 2).reshape(F, -1), head_terms], 1)
    own_out_sums = sum_cores(own_parts[0], after(own_out_got, normed_got), S)
    own_come = sum_first(own_out_sums, S)
    come, turned_term, value_sum, gain_terms, own_come = tie(
        come, turned_term, value_sum, gain_terms, own_come
    )
    turned_got = swap(turned_term[: F // 2], "fsdp", F, 1)
    singles, normed_total = sum_more(normed_sums, come, S)
    come = sum_last(singles, S)
    gain_got = swap(gain_terms[F // 2 :], "fsdp", F, half_f)
    for r in near_odd:
        in_products(r ^ 1, turned_term)
    outs_back = [far_swap(other_outs[:half_rows], turned_term)]
    come, turned_got, gain_got, in_terms, outs_back[0] = tie(
        come, turned_got, gain_got, in_terms, outs_back[0]
    )
    gain_terms = gain_terms[: F // 2] + gain_got
    normed_grads = add_all(normed_total, come)
    turned_sum = sum_rest(sum_even(turned_term, turned_got, F), F)
    middle = in_part // 2

    def send_near(first, dep):
        return {
            r: swap(after(in_terms[r][:, first : first + middle], dep), "fsdp", F, 1)
            for r in near_odd
        }

    near_got = [send_near(0, turned_got)]
    gain_terms = halve(after(gain_terms, turned_got), "fsdp", F, half_f // 2)
    singles, own_total = sum_more(after(own_out_sums, turned_got), own_come, S)
    own_come = sum_last(singles, S)
    turned_sum, own_come, near_got[0], gain_terms = tie(
        turned_sum, own_come, near_got[0], gain_terms
    )
    near_got.append(send_near(middle, turned_sum))
    outs_back.append(far_swap(other_outs[half_rows:], turned_sum))
    count = S * part * (E + 1)
    head_terms = gain_terms[0, count:]
    gain_terms = halve(gain_terms[0, :count].reshape(S, -1), "seq", S, S // 2)[0]
    own_outs = add_all(own_total, own_come)
    qkv_term = jnp.concatenate([turned_sum, value_sum], -1).astype(BF16)
    qkv_term = lax.all_to_all(qkv_term, "seq", split_axis=0, concat_axis=0, tiled=True)
    qkv_term, outs_back[1], near_got[1], gain_terms = tie(
        qkv_term, outs_back[1], near_got[1], gain_terms
    )
    outs_back = jnp.concatenate(outs_back, 0).astype(F32)
    mixed = (residual + own_outs + outs_back).astype(BF16)[None]
    qkv_term = [
        qkv_term[:, :, j * C : (j + 1) * C].transpose(1, 0, 2).reshape(part, D).astype(F32)
        for j in range(3)
    ]
    grad_output = sum_rest(sum_even(output_term, output_got, F), F)

    near_got = {r: jnp.concatenate([got[r] for got in near_got], 1) for r in near_odd}
    own_term = sum_near(
        {r ^ 1: in_terms[r ^ 1].astype(F32) + near_got[r].astype(F32) for r in near_odd}
    )
    far_term = jnp.concatenate(far_sums, 1).astype(F32)
    first_half = half_at == 0
    lower = jnp.where(first_half, own_term, far_term)
    upper = jnp.where(first_half, far_term, own_term)
    grad_gate, grad_up = (
        jnp.concatenate([lower[..., at], upper[..., at]], axis=-1)
        for at in (slice(0, hidden_half), slice(hidden_half, 2 * hidden_half))
    )
    down_got = after(down_got, turned_sum)
    down_got = {r: jnp.concatenate([got[r] for got in down_got], 1) for r in down_sent}
    grad_down = sum_near(
        {r ^ 1: down_terms[r ^ 1].astype(F32) + down_got[r].astype(F32) for r in down_sent}
    )

    attn_factor = rms_factor(inputs)
    inputs_n = inputs * attn_factor
    attn_pulled = normed_grads * gain_attn
    grad_tokens = residual_grads + attn_factor * (
        attn_pulled - inputs_n * jnp.mean(attn_pulled * inputs_n, axis=-1, keepdims=True)
    )
    grad_attn_gain = sum(
        jnp.sum(term * weight.astype(F32), axis=1)
        for term, weight in zip(qkv_term, (w_query, w_key, w_value))
    ) / attn_gain.astype(F32)
    return (
        mixed,
        grad_tokens[None],
        qkv_term[0],
        qkv_term[1],
        qkv_term[2],
        grad_output,
        gain_terms[: part * E].reshape(part, E),
        grad_attn_gain,
        gain_terms[part * E :],
        head_terms[:part],
        head_terms[part:],
        grad_gate,
        grad_up,
        grad_down,
    )


def solution(mesh):
    tokens_spec = P("fsdp", "seq", None)
    rows_spec = P(("seq", "fsdp"), None)
    gain_spec = P(("seq", "fsdp"))
    expert_spec = P("seq", "fsdp", None)
    in_specs = (
        (tokens_spec, P("fsdp", None), tokens_spec, tokens_spec)
        + (rows_spec,) * 5
        + (gain_spec,) * 4
        + (expert_spec,) * 3
    )
    out_specs = (tokens_spec,) * 2 + (rows_spec,) * 5 + (gain_spec,) * 4 + (expert_spec,) * 3
    return jax.shard_map(
        partial(per_device, mesh.shape["seq"], mesh.shape["fsdp"]),
        mesh=mesh,
        in_specs=in_specs,
        out_specs=out_specs,
        check_vma=False,
    )
```

```python
from functools import partial

import jax
import jax.numpy as jnp
from jax import lax
from jax.experimental import pallas as pl
from jax.experimental.pallas import tpu as pltpu
from jax.sharding import PartitionSpec as P

D = 2048
H = 16
DH = 128
E = 16
WINDOW = 1024
CAP = 144

EPSILON = 1e-06
ROPE_BASE = 50000.0
HIGHEST = lax.Precision.HIGHEST
BF16 = jnp.bfloat16
F32 = jnp.float32
MIB = 1024 * 1024


def matmul(left, right):
    return jnp.dot(left, right, preferred_element_type=F32)


def matmul_t(left, right):
    return lax.dot_general(left, right, (((1,), (1,)), ((), ())), preferred_element_type=F32)


def t_matmul(left, right):
    return lax.dot_general(left, right, (((0,), (0,)), ((), ())), preferred_element_type=F32)


def rms_factor(values):
    return lax.rsqrt(jnp.mean(values * values, axis=-1, keepdims=True) + EPSILON)


def swap(values, axis, size, mask):
    return lax.ppermute(values, axis, [(i, i ^ mask) for i in range(size)])


def high_bit(number):
    return 1 << (number.bit_length() - 1)


def low_bit(number):
    return number & -number


def after(values, *others):
    return lax.optimization_barrier((values, others))[0]


def tie(*values):
    return lax.optimization_barrier(values)


def gather_first(values, size):
    return {r: swap(values, "seq", size, r) for r in range(2, size, 2) if r == low_bit(r)}


def gather_more(values, first, size):
    rows = values.shape[0] // 2
    pieces = dict(first)
    for r in range(2, size, 2):
        if r not in pieces:
            up, down = high_bit(r), low_bit(r)
            upper, lower = pieces[r ^ up], pieces[r ^ down]
            upper = upper[0] if isinstance(upper, tuple) else upper[:rows]
            lower = lower[1] if isinstance(lower, tuple) else lower[rows:]
            pieces[r] = (swap(upper, "seq", size, up), swap(lower, "seq", size, down))
    return {r: piece for r, piece in pieces.items() if r not in first}


def gather_end(values, first, more, size):
    blocks = [values]
    for r in range(2, size, 2):
        blocks.extend([first[r]] if r in first else more[r])
    even = jnp.concatenate(blocks, 0)
    return even, swap(even, "seq", size, 1)


def relative(blocks, me):
    size = blocks.shape[0]
    order = list(range(0, size, 2)) + list(range(1, size, 2))
    return jnp.concatenate([lax.dynamic_slice_in_dim(blocks, me ^ r, 1, 0) for r in order], 0)


def absolute(blocks, me):
    size = blocks.shape[0]
    places = [((me ^ j) // 2) + ((me ^ j) % 2) * (size // 2) for j in range(size)]
    return jnp.concatenate([lax.dynamic_slice_in_dim(blocks, at, 1, 0) for at in places], 0)


def sum_cores(even, got, size):
    rows = even.shape[0] // (size // 2)
    half = rows // 2

    def part(r, first):
        at = slice(r // 2 * rows + first, r // 2 * rows + first + half)
        return even[at].astype(F32) + got[at].astype(F32)

    return {r: [part(r, 0), part(r, half)] for r in range(0, size, 2)}


def sum_first(sums, size, held=None):
    sums = {r: list(value) for r, value in sums.items()}
    come = {}
    for r in range(size - 2, 0, -2):
        if r != low_bit(r):
            up, down = high_bit(r), low_bit(r)
            for (goal, k, _), piece in come.items():
                if goal == r:
                    sums[r][k] += piece.astype(F32)
            upper, lower, held = tie(sums[r][0].astype(BF16), sums[r][1].astype(BF16), held)
            come[r ^ up, 0, r] = swap(upper, "seq", size, up)
            come[r ^ down, 1, r] = swap(lower, "seq", size, down)
    return come if held is None else (come, held)


def sum_more(sums, come, size):
    sums = {r: list(value) for r, value in sums.items() if r == 0 or r == low_bit(r)}
    for (goal, k, _), piece in come.items():
        if goal in sums:
            sums[goal][k] += piece.astype(F32)
    singles = {
        r: jnp.concatenate([v.astype(BF16) for v in value], 0) for r, value in sums.items() if r
    }
    return tie(singles)[0], jnp.concatenate(sums[0], 0)


def sum_last(singles, size):
    return {r: swap(value, "seq", size, r) for r, value in singles.items()}


def add_all(total, pieces):
    for piece in pieces.values():
        total += piece.astype(F32)
    return total


def quarters(values, axis):
    step = values.shape[axis] // 4
    return [lax.slice_in_dim(values, k * step, (k + 1) * step, axis=axis) for k in range(4)]


def sum_all(values, axis, size):
    mask = 1
    while mask < size:
        values = values + swap(values, axis, size, mask)
        mask *= 2
    return values


def fsdp_pieces(values, size):
    pieces = {0: values}
    for r in range(1, size):
        low = low_bit(r)
        pieces[r] = swap(pieces[r ^ low], "fsdp", size, low)
    return pieces


def place_fsdp(pieces, me, axis):
    size = len(pieces)
    shape = pieces[0].shape
    whole = jnp.zeros(shape[:axis] + (size,) + shape[axis:], pieces[0].dtype)
    for r, piece in pieces.items():
        whole = lax.dynamic_update_slice_in_dim(whole, jnp.expand_dims(piece, axis), me ^ r, axis)
    return whole


def near_pieces(values, size):
    pieces = {0: values}
    for r in range(1, size // 2):
        up = high_bit(r)
        pieces[r] = swap(pieces[r ^ up], "fsdp", size, up)
    return pieces


def double(values, axis, size):
    mask = 1
    while mask < size:
        values = jnp.concatenate([values, swap(values, axis, size, mask)], 0)
        mask *= 2
    return values


def halve(values, axis, size, mask):
    while mask:
        half = values.shape[0] // 2
        values = values[:half] + swap(values[half:], axis, size, mask)
        mask //= 2
    return values


def relative_pick(seq_size, fsdp_size, s, f):
    index = jnp.arange(seq_size * fsdp_size, dtype=jnp.int32)
    source = ((index // fsdp_size) ^ s) * fsdp_size + ((index % fsdp_size) ^ f)
    return source[:, None] == index[None, :]


def in_order(values, seq_size, fsdp_size, s, f):
    pick = relative_pick(seq_size, fsdp_size, s, f).astype(values.dtype)
    return matmul(pick, values).astype(values.dtype)


def in_relative(values, seq_size, fsdp_size, s, f):
    pick = relative_pick(seq_size, fsdp_size, s, f).astype(F32)
    return jnp.dot(pick, values, precision=HIGHEST)


def by_index(partial_sum, me, size):
    order = [r for r in range(size) if r & 1] + [r for r in range(size) if not r & 1]
    return jnp.concatenate([lax.dynamic_slice_in_dim(partial_sum, me ^ r, 1, 0) for r in order], 0)


def sum_even(stacked, got, size):
    return (stacked[size // 2 :].astype(F32) + got.astype(F32)).astype(BF16)


def sum_rest(stacked, size):
    mask = 2
    values = stacked.astype(F32)
    while mask < size:
        count = values.shape[0] // 2
        pairs = values.reshape((count, 2) + values.shape[1:])
        got = swap(pairs[:, 1].astype(BF16), "fsdp", size, mask)
        values = pairs[:, 0] + got.astype(F32)
        mask *= 2
    return values[0]


def allowed_keys(seg_row, seg_col, first_query, first_key, rows, span, half_window):
    query_at = first_query + lax.broadcasted_iota(jnp.int32, (span, rows), 1)
    key_at = first_key + lax.broadcasted_iota(jnp.int32, (span, rows), 0)
    return (jnp.abs(query_at - key_at) <= half_window) & (seg_col == seg_row)


def first_key_of(block, rows, span, length):
    start = jnp.clip(block * rows - (span - rows) // 2, 0, length - span)
    return pl.multiple_of(start, rows)


def forward_kernel(span, q_ref, k_ref, v_ref, seg_row_ref, seg_col_ref, o_ref, lse_ref):
    block = pl.program_id(1)
    rows, length = q_ref.shape[0], k_ref.shape[0]
    first_key = first_key_of(block, rows, span, length)
    keys = k_ref[pl.ds(first_key, span), :]
    values = v_ref[pl.ds(first_key, span), :]
    scores = matmul_t(keys, q_ref[...]) * DH ** (-0.5)
    allowed = allowed_keys(
        seg_row_ref[...],
        seg_col_ref[pl.ds(first_key, span), :],
        block * rows,
        first_key,
        rows,
        span,
        WINDOW // 2,
    )
    scores = jnp.where(allowed, scores, -1e30)
    peak = jnp.max(scores, axis=0, keepdims=True)
    expos = jnp.exp(scores - peak)
    totals = jnp.sum(expos, axis=0, keepdims=True)
    probs = (expos * (1.0 / totals)).astype(BF16)
    o_ref[...] = t_matmul(values, probs).T.astype(BF16)
    lse_ref[...] = (peak + jnp.log(totals))[None]


def backward_kernel(
    span,
    q_ref,
    k_ref,
    v_ref,
    do_ref,
    lse_ref,
    seg_row_ref,
    seg_col_ref,
    dq_ref,
    dk_ref,
    dv_ref,
    dk_sum,
    dv_sum,
):
    block = pl.program_id(1)
    rows, length = q_ref.shape[0], k_ref.shape[0]

    @pl.when(block == 0)
    def _():
        dk_sum[...] = jnp.zeros_like(dk_sum)
        dv_sum[...] = jnp.zeros_like(dv_sum)

    first_key = first_key_of(block, rows, span, length)
    at = pl.ds(first_key, span)
    keys = k_ref[at, :]
    values = v_ref[at, :]
    queries = q_ref[...]
    grads = do_ref[...]
    scores = matmul_t(keys, queries) * DH ** (-0.5)
    allowed = allowed_keys(
        seg_row_ref[...],
        seg_col_ref[at, :],
        block * rows,
        first_key,
        rows,
        span,
        WINDOW // 2,
    )
    probs = jnp.where(allowed, jnp.exp(scores - lse_ref[0]), 0.0)
    dv_sum[at, :] += matmul(probs.astype(BF16), grads)
    prob_grads = matmul_t(values, grads)
    center = jnp.sum(probs * prob_grads, axis=0, keepdims=True)
    score_grads = (probs * (prob_grads - center)).astype(BF16)
    dk_sum[at, :] += matmul(score_grads, queries)
    dq_ref[...] = (t_matmul(keys, score_grads) * DH ** (-0.5)).T.astype(BF16)

    @pl.when(block == length // rows - 1)
    def _():
        dk_ref[...] = (dk_sum[...] * DH ** (-0.5)).astype(BF16)
        dv_ref[...] = dv_sum[...].astype(BF16)


def attention_sizes(length):
    rows = 256
    return rows, min(length, rows + WINDOW)


def attention_forward(queries, keys, values, seg_row, seg_col):
    length, columns = queries.shape
    heads = columns // DH
    rows, span = attention_sizes(length)
    block = pl.BlockSpec((rows, DH), lambda h, i: (i, h))
    whole = pl.BlockSpec((length, DH), lambda h, i: (0, h))
    return pl.pallas_call(
        partial(forward_kernel, span),
        grid=(heads, length // rows),
        in_specs=[
            block,
            whole,
            whole,
            pl.BlockSpec((1, rows), lambda h, i: (0, i)),
            pl.BlockSpec((length, 1), lambda h, i: (0, 0)),
        ],
        out_specs=[block, pl.BlockSpec((1, 1, rows), lambda h, i: (h, 0, i))],
        out_shape=[
            jax.ShapeDtypeStruct((length, columns), BF16),
            jax.ShapeDtypeStruct((heads, 1, length), F32),
        ],
        compiler_params=pltpu.CompilerParams(vmem_limit_bytes=48 * MIB),
        cost_estimate=pl.CostEstimate(
            flops=4 * heads * length * span * DH,
            bytes_accessed=8 * length * columns,
            transcendentals=heads * length * span,
        ),
        name="attend",
    )(queries, keys, values, seg_row, seg_col)


def attention_backward(queries, keys, values, grads, lse, seg_row, seg_col):
    length, columns = queries.shape
    heads = columns // DH
    rows, span = attention_sizes(length)
    block = pl.BlockSpec((rows, DH), lambda h, i: (i, h))
    whole = pl.BlockSpec((length, DH), lambda h, i: (0, h))
    shape = jax.ShapeDtypeStruct((length, columns), BF16)
    return pl.pallas_call(
        partial(backward_kernel, span),
        grid=(heads, length // rows),
        in_specs=[
            block,
            whole,
            whole,
            block,
            pl.BlockSpec((1, 1, rows), lambda h, i: (h, 0, i)),
            pl.BlockSpec((1, rows), lambda h, i: (0, i)),
            pl.BlockSpec((length, 1), lambda h, i: (0, 0)),
        ],
        out_specs=[block, whole, whole],
        out_shape=[shape, shape, shape],
        scratch_shapes=[pltpu.VMEM((length, DH), F32), pltpu.VMEM((length, DH), F32)],
        compiler_params=pltpu.CompilerParams(vmem_limit_bytes=48 * MIB),
        cost_estimate=pl.CostEstimate(
            flops=10 * heads * length * span * DH,
            bytes_accessed=14 * length * columns,
            transcendentals=heads * length * span,
        ),
        name="attend_back",
    )(queries, keys, values, grads, lse, seg_row, seg_col)


def qkv_kernel(
    me_ref,
    even_ref,
    odd_ref,
    weight_ref,
    gain_ref,
    normed_even_ref,
    normed_odd_ref,
    q_ref,
    k_ref,
    v_ref,
    square_ref,
):
    turned = me_ref[0] % 2
    rows = even_ref.shape[0]
    columns = q_ref.shape[1]
    for k, (token_ref, normed_ref) in enumerate(
        ((even_ref, normed_even_ref), (odd_ref, normed_odd_ref))
    ):
        at = pl.ds(pl.multiple_of((turned ^ k) * rows, rows), rows)
        wide = token_ref[...].astype(F32)
        normed = (wide * rms_factor(wide) * gain_ref[...]).astype(BF16)
        normed_ref[...] = normed
        pre = matmul(normed, weight_ref[...])
        q_ref[at, :] = pre[:, :columns]
        k_ref[at, :] = pre[:, columns : 2 * columns]
        v_ref[at, :] = pre[:, 2 * columns :].astype(BF16)
        for j in range(2):
            squares = 0.0
            for c in range(j * columns, (j + 1) * columns, DH):
                squares += pre[:, c : c + DH] * pre[:, c : c + DH]
            square_ref[j : j + 1, at] = jnp.sum(squares.T, axis=0, keepdims=True)


def project(even, odd, weight, gain, me, rows):
    pairs = even.shape[0] // rows
    length = 2 * even.shape[0]
    depth, columns = weight.shape[0], weight.shape[1] // 3
    token = pl.BlockSpec((rows, depth), lambda i, me: (i, 0))

    def placed(shape):
        return pl.BlockSpec(shape, lambda i, me: (i ^ (me[0] // 2), 0))

    head = jax.ShapeDtypeStruct((length, columns), F32)
    return pl.pallas_call(
        qkv_kernel,
        grid_spec=pltpu.PrefetchScalarGridSpec(
            num_scalar_prefetch=1,
            grid=(pairs,),
            in_specs=[
                token,
                token,
                pl.BlockSpec(weight.shape, lambda i, me: (0, 0)),
                pl.BlockSpec((1, depth), lambda i, me: (0, 0)),
            ],
            out_specs=[
                token,
                token,
                placed((2 * rows, columns)),
                placed((2 * rows, columns)),
                placed((2 * rows, columns)),
                pl.BlockSpec((2, 2 * rows), lambda i, me: (0, i ^ (me[0] // 2))),
            ],
        ),
        out_shape=[
            jax.ShapeDtypeStruct((length // 2, depth), BF16),
            jax.ShapeDtypeStruct((length // 2, depth), BF16),
            head,
            head,
            jax.ShapeDtypeStruct((length, columns), BF16),
            jax.ShapeDtypeStruct((2, length), F32),
        ],
        compiler_params=pltpu.CompilerParams(vmem_limit_bytes=48 * MIB),
        cost_estimate=pl.CostEstimate(
            flops=6 * length * depth * columns,
            bytes_accessed=length * (4 * depth + 10 * columns) + 6 * depth * columns,
            transcendentals=length,
        ),
        name="project",
    )(me, even, odd, weight, gain)


def split_kernel(q_ref, k_ref, v_ref, out_ref):
    columns = q_ref.shape[1]
    for j, ref in enumerate((q_ref, k_ref, v_ref)):
        out_ref[0, :, j * columns : (j + 1) * columns] = ref[...]


def split_heads(w_query, w_key, w_value, parts):
    rows, columns = w_query.shape[0], w_query.shape[1] // parts
    block = pl.BlockSpec((rows, columns), lambda i: (0, i))
    return pl.pallas_call(
        split_kernel,
        grid=(parts,),
        in_specs=[block] * 3,
        out_specs=pl.BlockSpec((1, rows, 3 * columns), lambda i: (i, 0, 0)),
        out_shape=jax.ShapeDtypeStruct((parts, rows, 3 * columns), BF16),
        name="split_heads",
    )(w_query, w_key, w_value)


def spread(row, columns):
    return jnp.broadcast_to(row, (columns, row.shape[1])).T


def factor_of(square_row):
    return lax.rsqrt(square_row / D + EPSILON)


def turn(values, cosine, sine):
    return values * cosine + pltpu.roll(values, DH // 2, 1) * sine


def rope_kernel(q_ref, k_ref, square_ref, gain_ref, cos_ref, sin_ref, q_out, k_out):
    cosine, sine = cos_ref[...], sin_ref[...]
    for j, (pre_ref, out_ref) in enumerate(((q_ref, q_out), (k_ref, k_out))):
        factor = spread(factor_of(square_ref[j : j + 1, :]), DH)
        for c in range(0, pre_ref.shape[1], DH):
            at = slice(c, c + DH)
            normed = pre_ref[:, at] * factor * gain_ref[j : j + 1, at]
            out_ref[:, at] = turn(normed, cosine, sine).astype(BF16)


def rope(query_pre, key_pre, squares, gains, cosine, sine):
    length, columns = query_pre.shape
    rows = min(512, length)
    block = pl.BlockSpec((rows, columns), lambda i: (i, 0))
    table = pl.BlockSpec((rows, DH), lambda i: (i, 0))
    return pl.pallas_call(
        rope_kernel,
        grid=(length // rows,),
        in_specs=[
            block,
            block,
            pl.BlockSpec((2, rows), lambda i: (0, i)),
            pl.BlockSpec((2, columns), lambda i: (0, 0)),
            table,
            table,
        ],
        out_specs=[block, block],
        out_shape=[jax.ShapeDtypeStruct((length, columns), BF16)] * 2,
        compiler_params=pltpu.CompilerParams(vmem_limit_bytes=32 * MIB),
        name="rope",
    )(query_pre, key_pre, squares, gains, cosine, sine)


def pulled_of(grad_ref, pre_ref, factor, gain_ref, cosine, sine, j, at):
    turned = turn(grad_ref[:, at].astype(F32), cosine, -sine)
    return turned, turned * gain_ref[j : j + 1, at], pre_ref[:, at] * factor


def rope_mean_kernel(
    dq_ref, dk_ref, q_ref, k_ref, square_ref, gain_ref, cos_ref, sin_ref, mean_ref, term_ref
):
    @pl.when(pl.program_id(0) == 0)
    def _():
        term_ref[...] = jnp.zeros_like(term_ref)

    cosine, sine = cos_ref[...], sin_ref[...]
    for j, (grad_ref, pre_ref) in enumerate(((dq_ref, q_ref), (dk_ref, k_ref))):
        factor = spread(factor_of(square_ref[j : j + 1, :]), DH)
        total = 0.0
        for c in range(0, pre_ref.shape[1], DH):
            at = slice(c, c + DH)
            turned, pulled, normed = pulled_of(
                grad_ref, pre_ref, factor, gain_ref, cosine, sine, j, at
            )
            term_ref[j : j + 1, at] += jnp.sum(turned * normed, axis=0, keepdims=True)
            total += pulled * normed
        mean_ref[j : j + 1, :] = jnp.sum(total.T, axis=0, keepdims=True)


def rope_means(query_back, key_back, query_pre, key_pre, squares, gains, cosine, sine):
    length, columns = query_pre.shape
    rows = min(512, length)
    block = pl.BlockSpec((rows, columns), lambda i: (i, 0))
    table = pl.BlockSpec((rows, DH), lambda i: (i, 0))
    row = pl.BlockSpec((2, rows), lambda i: (0, i))
    fixed = pl.BlockSpec((2, columns), lambda i: (0, 0))
    return pl.pallas_call(
        rope_mean_kernel,
        grid=(length // rows,),
        in_specs=[block, block, block, block, row, fixed, table, table],
        out_specs=[row, fixed],
        out_shape=[
            jax.ShapeDtypeStruct((2, length), F32),
            jax.ShapeDtypeStruct((2, columns), F32),
        ],
        compiler_params=pltpu.CompilerParams(vmem_limit_bytes=32 * MIB),
        name="rope_means",
    )(query_back, key_back, query_pre, key_pre, squares, gains, cosine, sine)


def rope_back_kernel(
    me_ref,
    dq_ref,
    dk_ref,
    dv_ref,
    q_ref,
    k_ref,
    square_ref,
    mean_ref,
    gain_ref,
    cos_ref,
    sin_ref,
    out_ref,
):
    cosine, sine = cos_ref[...], sin_ref[...]
    columns = q_ref.shape[1]
    for j, (grad_ref, pre_ref) in enumerate(((dq_ref, q_ref), (dk_ref, k_ref))):
        factor = spread(factor_of(square_ref[j : j + 1, :]), DH)
        mean = spread(mean_ref[j : j + 1, :] / D, DH)
        for c in range(0, columns, DH):
            at = slice(c, c + DH)
            _, pulled, normed = pulled_of(grad_ref, pre_ref, factor, gain_ref, cosine, sine, j, at)
            out_ref[:, j * columns + c : j * columns + c + DH] = (
                factor * (pulled - normed * mean)
            ).astype(BF16)
    out_ref[:, 2 * columns :] = dv_ref[...]


def rope_back(grads, query_pre, key_pre, squares, means, gains, cosine, sine, me, rows):
    length, columns = query_pre.shape
    half = length // rows // 2

    def source(p, me):
        return me[0] ^ (p % half * 2 + p // half)

    block = pl.BlockSpec((rows, columns), lambda p, me: (source(p, me), 0))
    table = pl.BlockSpec((rows, DH), lambda p, me: (source(p, me), 0))
    row = pl.BlockSpec((2, rows), lambda p, me: (0, source(p, me)))
    return pl.pallas_call(
        rope_back_kernel,
        grid_spec=pltpu.PrefetchScalarGridSpec(
            num_scalar_prefetch=1,
            grid=(2 * half,),
            in_specs=[block] * 5
            + [row, row, pl.BlockSpec((2, columns), lambda p, me: (0, 0)), table, table],
            out_specs=pl.BlockSpec((rows, 3 * columns), lambda p, me: (p, 0)),
        ),
        out_shape=jax.ShapeDtypeStruct((length, 3 * columns), BF16),
        compiler_params=pltpu.CompilerParams(vmem_limit_bytes=32 * MIB),
        name="rope_back",
    )(me, *grads, query_pre, key_pre, squares, means, gains, cosine, sine)


def output_kernel(
    me_ref, come_ref, even_ref, odd_ref, token_ref, gain_ref, residual_ref, second_ref, total_ref
):
    step, half = pl.program_id(0), pl.num_programs(0) // 2

    @pl.when(step == 0)
    def _():
        total_ref[...] = token_ref[...].astype(F32)

    @pl.when(step < half)
    def _():
        total_ref[...] += matmul(come_ref[0], even_ref[...])

    @pl.when(step >= half)
    def _():
        total_ref[...] += matmul(come_ref[0], odd_ref[...])

    @pl.when(step == 2 * half - 1)
    def _():
        total = total_ref[...]
        residual_ref[...] = total
        second_ref[...] = (total * rms_factor(total) * gain_ref[...]).astype(BF16)


def project_out(come, even, odd, tokens, gain, me):
    size, rows, columns = come.shape
    depth = even.shape[1]
    half = size // 2
    whole = pl.BlockSpec((rows, depth), lambda p, me: (0, 0))
    return pl.pallas_call(
        output_kernel,
        grid_spec=pltpu.PrefetchScalarGridSpec(
            num_scalar_prefetch=1,
            grid=(size,),
            in_specs=[
                pl.BlockSpec(
                    (1, rows, columns), lambda p, me: (me[0] ^ (p % half * 2 + p // half), 0, 0)
                ),
                pl.BlockSpec((columns, depth), lambda p, me: (jnp.minimum(p, half - 1), 0)),
                pl.BlockSpec((columns, depth), lambda p, me: (jnp.maximum(p - half, 0), 0)),
                whole,
                pl.BlockSpec((1, depth), lambda p, me: (0, 0)),
            ],
            out_specs=[whole, whole],
            scratch_shapes=[pltpu.VMEM((rows, depth), F32)],
        ),
        out_shape=[
            jax.ShapeDtypeStruct((rows, depth), F32),
            jax.ShapeDtypeStruct((rows, depth), BF16),
        ],
        compiler_params=pltpu.CompilerParams(vmem_limit_bytes=32 * MIB),
        name="project_out",
    )(me, come, even, odd, tokens, gain)


def expert_kernel(
    in_places, down_places, first_ref, xa_ref, xb_ref, ua_ref, ub_ref, ra_ref, rb_ref, router_ref, *refs
):
    weight_refs = refs[: len(in_places) + len(down_places)]
    (ya_ref, yb_ref, za_ref, zb_ref, ga_ref, gb_ref, xc_ref, uc_ref, dg_ref, hid_ref) = refs[-13:-3]
    wi_ref, wd_ref, sems = refs[-3:]
    experts, _, hidden = hid_ref.shape
    rows = xa_ref.shape[0]

    @pl.when(pl.program_id(0) == 0)
    def _():
        copies = []
        for n, (ref, (r, first, part)) in enumerate(zip(weight_refs, in_places + down_places)):
            goal = wi_ref if n < len(in_places) else wd_ref
            place = lax.rem(first_ref[1] ^ r, goal.shape[1] // part)
            at = pl.ds(pl.multiple_of(place * part + first, ref.shape[1]), ref.shape[1])
            copies.append(pltpu.make_async_copy(ref, goal.at[:, at, :], sems.at[n]))
        for copy in copies:
            copy.start()
        for copy in copies:
            copy.wait()

    slot = lax.broadcasted_iota(jnp.int32, (CAP, rows), 0)
    blocks = (
        (xa_ref, ua_ref, ra_ref, ya_ref, za_ref, ga_ref),
        (xb_ref, ub_ref, rb_ref, yb_ref, zb_ref, gb_ref),
    )
    picks = []
    for k, (x_ref, u_ref, rank_ref, _, _, _) in enumerate(blocks):
        hits = jnp.concatenate([slot == rank_ref[0, e : e + 1, :] for e in range(experts)], 0)
        pick = hits.astype(F32).astype(BF16)
        picks.append(pick)
        x_rows = matmul(pick, x_ref[...]).astype(BF16)
        u_rows = matmul(pick, u_ref[...]).astype(BF16)
        for e in range(experts):
            xc_ref[e, k * CAP : (k + 1) * CAP, :] = x_rows[e * CAP : (e + 1) * CAP]
            uc_ref[e, k * CAP : (k + 1) * CAP, :] = u_rows[e * CAP : (e + 1) * CAP]
    outs, backs, gate_grads = [], [], []
    for e in range(experts):
        x_rows, u_rows = xc_ref[e], uc_ref[e]
        logits = matmul(x_rows, router_ref[...])
        lane = lax.broadcasted_iota(jnp.int32, logits.shape, 1)
        logits = jnp.where(lane < E, logits, -1e30)
        expos = jnp.exp(logits - jnp.max(logits, axis=-1, keepdims=True))
        own = jnp.sum(jnp.where(lane == first_ref[0] + e, expos, 0.0), axis=-1, keepdims=True)
        gate = own / jnp.sum(expos, axis=-1, keepdims=True)
        gated = matmul(x_rows, wi_ref[e, :, :hidden])
        upward = matmul(x_rows, wi_ref[e, :, hidden:])
        pulled = matmul_t(u_rows, wd_ref[e])
        sig = jax.nn.sigmoid(gated)
        silu = gated * sig
        acts = silu * upward
        gate_grads.append(jnp.sum(acts * pulled, axis=-1, keepdims=True))
        hidden_gate = (acts * gate).astype(BF16)
        hidden_grads = pulled * gate
        hid_ref[e] = hidden_gate
        dg_ref[e, :, :hidden] = (hidden_grads * upward * sig * (1.0 + gated * (1.0 - sig))).astype(BF16)
        dg_ref[e, :, hidden:] = (hidden_grads * silu).astype(BF16)
        outs.append(matmul(hidden_gate, wd_ref[e]).astype(BF16))
        backs.append(matmul_t(dg_ref[e], wi_ref[e]).astype(BF16))
    for k, (_, _, rank_ref, y_ref, z_ref, g_ref) in enumerate(blocks):
        at = slice(k * CAP, (k + 1) * CAP)
        y_ref[...] = t_matmul(picks[k], jnp.concatenate([v[at] for v in outs], 0)).astype(BF16)
        z_ref[...] = t_matmul(picks[k], jnp.concatenate([v[at] for v in backs], 0)).astype(BF16)
        for e in range(experts):
            hit = slot == rank_ref[0, e : e + 1, :]
            g_ref[0, e : e + 1, :] = jnp.sum(
                jnp.where(hit, gate_grads[e][at], 0.0), axis=0, keepdims=True
            )


def run_experts(x, u, ranks, in_pieces, down_pieces, router, places, which, compact, parts):
    experts, _, hidden = in_pieces[0][2].shape
    hidden = hidden // 2
    depth = x[0].shape[1]
    in_places = [(r, at, parts[0]) for r, at, _ in in_pieces]
    down_places = [(r, at, parts[1]) for r, at, _ in down_pieces]
    pieces = [array for _, _, array in in_pieces + down_pieces]
    rows = ranks[0].shape[2]
    steps = x[0].shape[0] // rows
    token = pl.BlockSpec((rows, depth), lambda i: (i, 0))
    rank = pl.BlockSpec((1, experts, rows), lambda i: (i, 0, 0))
    anywhere = pl.BlockSpec(memory_space=pl.ANY)

    def slots(columns):
        return pl.BlockSpec((experts, 2 * CAP, columns), lambda i: (0, i + which * steps, 0))

    shape = jax.ShapeDtypeStruct
    tokens = shape(x[0].shape, BF16)
    gates = shape((steps, experts, rows), F32)
    count = 4 * steps * CAP
    wide = shape((experts, count, depth), BF16)
    inputs = [places, *x, *u, *ranks, router, *pieces]
    return pl.pallas_call(
        partial(expert_kernel, in_places, down_places),
        grid=(steps,),
        in_specs=[pl.BlockSpec(memory_space=pltpu.SMEM)]
        + [token] * 4
        + [rank] * 2
        + [pl.BlockSpec(router.shape, lambda i: (0, 0), pipeline_mode=pl.Buffered(1))]
        + [anywhere] * (len(pieces) + len(compact)),
        out_specs=[token] * 4 + [rank] * 2 + [slots(depth)] * 2 + [slots(2 * hidden), slots(hidden)],
        out_shape=[tokens] * 4
        + [gates] * 2
        + [wide] * 2
        + [shape((experts, count, 2 * hidden), BF16), shape((experts, count, hidden), BF16)],
        scratch_shapes=[
            pltpu.VMEM((experts, depth, 2 * hidden), BF16),
            pltpu.VMEM((experts, hidden, depth), BF16),
            pltpu.SemaphoreType.DMA((len(pieces),)),
        ],
        input_output_aliases={len(inputs) + i: 6 + i for i in range(len(compact))},
        compiler_params=pltpu.CompilerParams(vmem_limit_bytes=60 * MIB),
        cost_estimate=pl.CostEstimate(
            flops=4 * steps * CAP * experts * depth * (7 * hidden + 2 * rows),
            bytes_accessed=60 * MIB,
            transcendentals=2 * steps * CAP * experts * hidden,
        ),
        name="experts",
    )(*inputs, *compact)


def product_kernel(me_ref, left_ref, right_ref, out_ref):
    out_ref[0] = t_matmul(left_ref[0], right_ref[0]).astype(BF16)


def products(left, right, part, r, count, me, name):
    experts, rows, _ = left.shape
    columns = right.shape[2]
    wide = min(columns, 1024)
    return pl.pallas_call(
        product_kernel,
        grid_spec=pltpu.PrefetchScalarGridSpec(
            num_scalar_prefetch=1,
            grid=(experts, columns // wide),
            in_specs=[
                pl.BlockSpec((1, rows, part), lambda e, j, me: (e, 0, lax.rem(me[0] ^ r, count))),
                pl.BlockSpec((1, rows, wide), lambda e, j, me: (e, 0, j)),
            ],
            out_specs=pl.BlockSpec((1, part, wide), lambda e, j, me: (e, 0, j)),
        ),
        out_shape=jax.ShapeDtypeStruct((experts, part, columns), BF16),
        compiler_params=pltpu.CompilerParams(vmem_limit_bytes=56 * MIB),
        cost_estimate=pl.CostEstimate(
            flops=2 * experts * rows * part * columns,
            bytes_accessed=2 * experts * rows * (part + columns),
            transcendentals=0,
        ),
        name=name,
    )(me, left, right)


def per_device(
    S,
    F,
    tokens,
    segments,
    routes,
    cotangent,
    w_query,
    w_key,
    w_value,
    w_output,
    router,
    attn_gain,
    moe_gain,
    query_gain,
    key_gain,
    w_gate,
    w_up,
    w_down,
):
    s = lax.axis_index("seq")
    f = lax.axis_index("fsdp")
    T = tokens.shape[1]
    L = S * T
    heads = H // S
    C = heads * DH
    experts = E // S
    part = w_query.shape[0]
    half_f = F // 2
    hidden_half = w_gate.shape[2] // 2

    me = s.reshape(1).astype(jnp.int32)
    f_at = f.reshape(1).astype(jnp.int32)
    half_at = f // half_f
    tokens_low = tokens[0]
    upstream_low = cotangent[0]
    inputs = tokens_low.astype(F32)
    half_rows = T // 2
    in_part, down_part = w_gate.shape[1], w_down.shape[1]
    quarter = in_part // 4

    def hidden_part(which, first, count):
        return jnp.concatenate(
            [
                lax.dynamic_slice(
                    weight, (0, first, which * hidden_half), (experts, count, hidden_half)
                )
                for weight in (w_gate, w_up)
            ],
            2,
        )

    def far_swap(values, *dep):
        return swap(after(values, dep), "fsdp", F, half_f)

    def near_swap(values, *dep):
        return near_pieces(after(values, dep), F)

    named = routes[0].T[None] == jnp.arange(E, dtype=jnp.int32)[:, None, None]
    chosen = jnp.any(named, axis=1)
    index = jnp.arange(T, dtype=jnp.int32)
    before = (index[:, None] <= index[None, :]).astype(BF16)
    ranks = jnp.where(chosen, matmul(chosen.astype(BF16), before) - 1.0, -1.0)
    small = jnp.concatenate(
        [
            router.reshape(-1),
            attn_gain,
            moe_gain,
            query_gain,
            key_gain,
            ranks.astype(BF16).reshape(-1),
        ]
    )[None]
    crossed = split_heads(w_query, w_key, w_value, S)
    small = double(after(small, crossed), "fsdp", F)
    crossed = lax.all_to_all(crossed, "seq", split_axis=0, concat_axis=0, tiled=True)
    near_own = [near_swap(hidden_part(half_at, 0, 2 * quarter), small)]
    out_dep = small
    small = double(small, "seq", S)
    out_far = far_swap(w_output, out_dep)
    crossed, near_own[0], small, out_far = tie(crossed, near_own[0], small, out_far)

    held = after((w_gate, w_up, w_down, upstream_low), crossed)

    def held_part(which, first, count):
        return jnp.concatenate(
            [
                lax.dynamic_slice(
                    weight, (0, first, which * hidden_half), (experts, count, hidden_half)
                )
                for weight in held[:2]
            ],
            2,
        )

    own_quarters = {n: held_part(half_at, n * quarter, quarter) for n in (2, 3)}
    far_quarters = [held_part(1 - half_at, n * quarter, quarter) for n in range(4)]
    down_rows = quarters(held[2], 1)
    upstream_halves = [held[3][:half_rows], held[3][half_rows:]]
    small = in_order(small, S, F, s, f).reshape(S, F, -1)
    prepared = (own_quarters, far_quarters, down_rows, upstream_halves, small)
    token_first = gather_first(after(tokens_low, crossed), S)
    qkv_pieces = {0: crossed}
    for r in range(1, F):
        low = low_bit(r)
        qkv_pieces[r] = swap(qkv_pieces[r ^ low], "fsdp", F, low)
        if r == half_f:
            qkv_pieces, token_first, prepared = tie(qkv_pieces, token_first, prepared)
            own_quarters, far_quarters, down_rows, upstream_halves, small = prepared
            partner_up = [far_swap(upstream_halves[0])]
    token_more = gather_more(tokens_low, token_first, S)
    qkv_pieces, partner_up[0], token_more = tie(qkv_pieces, partner_up[0], token_more)
    tokens_even, tokens_odd = gather_end(tokens_low, token_first, token_more, S)
    w_qkv = place_fsdp(qkv_pieces, f, 1).reshape(D, 3 * C)

    full_router = small[:, :, : part * E].reshape(D, E)
    gains = [
        small[:, :, part * (E + i) : part * (E + i + 1)].reshape(D).astype(F32) for i in range(4)
    ]
    gain_attn, gain_moe = gains[0], gains[1]
    head_gain = lax.dynamic_slice(jnp.stack(gains[2:], 0), (0, s * C), (2, C))
    places = jnp.arange(L, dtype=jnp.int32).astype(F32)
    freqs = ROPE_BASE ** (-(jnp.arange(DH // 2, dtype=F32) * 2.0 / DH))
    angles = places[:, None] * freqs[None, :]
    cosine, sine = jnp.cos(angles), jnp.sin(angles)
    cosine = jnp.concatenate([cosine, cosine], 1)
    sine = jnp.concatenate([-sine, sine], 1)

    def far_part(n, *dep):
        return far_swap(far_quarters[n], *dep)

    partner_up.append(far_swap(upstream_halves[1], w_qkv))
    out_pieces = {0: after(w_output, w_qkv), half_f: after(out_far, w_qkv)}
    for r in range(1, F):
        if r != half_f:
            low = low_bit(r)
            out_pieces[r] = swap(out_pieces[r ^ low], "fsdp", F, low)
    own_up_first = gather_first(after(upstream_low, w_qkv), S)
    normed_even, normed_odd, query_pre, key_pre, value_low, squares = project(
        tokens_even, tokens_odd, w_qkv, gain_attn[None], me, T
    )
    squares, partner_up[1], out_pieces, own_up_first = tie(
        squares, partner_up[1], out_pieces, own_up_first
    )
    partner_up = jnp.concatenate(partner_up, 0)
    own_output = place_fsdp(out_pieces, f, 0).reshape(C, D)

    out_first = gather_first(own_output, S)
    far = [far_part(0, squares)]
    near_own.append(near_swap(own_quarters[2], squares))
    squares = sum_all(squares, "seq", S)
    query_low, key_low = rope(query_pre, key_pre, squares, head_gain, cosine, sine)
    query_low, out_first, far[0], near_own[1] = tie(query_low, out_first, far[0], near_own[1])

    seg_row = segments
    seg_col = segments.reshape(L, 1)
    out_more = gather_more(own_output, out_first, S)
    far.append(far_part(1, query_low))
    near_own.append(near_swap(own_quarters[3], query_low))
    down = [near_swap(down_rows[0], query_low)]
    attended, lse = attention_forward(query_low, key_low, value_low, seg_row, seg_col)
    attended, out_more, far[1], near_own[2], down[0] = tie(
        attended, out_more, far[1], near_own[2], down[0]
    )
    attended_blocks = attended.reshape(S, T, C)
    come = lax.all_to_all(attended_blocks, "seq", split_axis=0, concat_axis=0, tiled=True)
    out_even, out_odd = gather_end(own_output, out_first, out_more, S)
    far.append(far_part(2, attended))
    near_far = [near_swap(far[0], attended)]
    own_up_more = gather_more(after(upstream_low, attended), own_up_first, S)
    come, far[2], near_far[0], own_up_more = tie(come, far[2], near_far[0], own_up_more)
    own_u = gather_end(upstream_low, own_up_first, own_up_more, S)
    near_far.append(near_swap(far[1], come))
    partner_up_first = gather_first(after(partner_up, come), S)
    residual, second_low = project_out(come, out_even, out_odd, tokens_low, gain_moe[None], me)
    second_low, near_far[1], partner_up_first, own_u = tie(
        second_low, near_far[1], partner_up_first, own_u
    )

    own_first = gather_first(second_low, S)
    partner_low = [far_swap(second_low[:half_rows])]
    near_far.append(near_swap(far[2], second_low))
    rank_part = after(small, second_low)[:, :, part * (E + 4) :].reshape(S, F, E, T)

    def ranks_of(index):
        ranks = lax.dynamic_slice(rank_part, (0, index, s * experts, 0), (S, 1, experts, T))
        ranks = relative(ranks[:, 0], s).astype(jnp.int32)
        return ranks[: S // 2], ranks[S // 2 :]

    own_ranks, other_ranks = ranks_of(f), ranks_of(f ^ half_f)
    own_first, partner_low[0], near_far[2], own_ranks, other_ranks = tie(
        own_first, partner_low[0], near_far[2], own_ranks, other_ranks
    )
    own_more = gather_more(second_low, own_first, S)
    partner_low.append(far_swap(second_low[half_rows:], own_first))
    down.append(near_swap(down_rows[1], own_first))
    partner_up_more = gather_more(after(partner_up, own_first), partner_up_first, S)
    own_more, partner_low[1], down[1], partner_up_more = tie(
        own_more, partner_low[1], down[1], partner_up_more
    )
    partner_low = jnp.concatenate(partner_low, 0)
    own_x = gather_end(second_low, own_first, own_more, S)
    partner_first = gather_first(after(partner_low, own_more), S)
    down.append(near_swap(down_rows[2], own_more))
    far.append(far_part(3, own_more))
    partner_first, down[2], own_x, far[3] = tie(partner_first, down[2], own_x, far[3])
    other_u = gather_end(after(partner_up, partner_first), partner_up_first, partner_up_more, S)
    partner_more = gather_more(partner_low, partner_first, S)
    down.append(near_swap(down_rows[3], partner_first))
    near_far.append(near_swap(far[3], partner_first))
    partner_more, down[3], other_u, near_far[3] = tie(partner_more, down[3], other_u, near_far[3])
    other_x = gather_end(partner_low, partner_first, partner_more, S)
    in_pieces = []
    for r in range(F):
        for n, rows in enumerate(near_own if r < half_f else near_far):
            first = (0, 2, 3)[n] if r < half_f else n
            in_pieces.append((r, first * quarter, rows[r % half_f]))
    down_pieces = [
        (r, n * (down_part // 4), down[n][r]) for r in range(half_f) for n in range(4)
    ]
    wide_router = jnp.pad(full_router, ((0, 0), (0, 128 - E)))
    expert_places = jnp.stack([s * experts, f]).astype(jnp.int32)
    parts = (in_part, down_part)
    own_parts = run_experts(
        own_x, own_u, own_ranks, in_pieces, down_pieces, wide_router, expert_places, 0, (), parts
    )
    own_parts, other_x = tie(own_parts, other_x)
    own_got = swap(own_parts[3], "seq", S, 1)
    own_out_got = swap(own_parts[1], "seq", S, 1)
    other_parts = run_experts(
        other_x,
        other_u,
        other_ranks,
        in_pieces,
        down_pieces,
        wide_router,
        expert_places,
        1,
        own_parts[6:],
        parts,
    )
    other_parts, own_got, own_out_got = tie(other_parts, own_got, own_out_got)
    moe_factor = rms_factor(residual)
    residual_n = residual * moe_factor
    logits = matmul(second_low, full_router)
    router_probs = jax.nn.softmax(logits, axis=-1)

    x_rows, u_rows, in_grads, hidden_gate = other_parts[6:]
    in_terms, down_terms = {}, {}

    def in_products(r, *dep):
        in_terms[r] = products(
            x_rows, after(in_grads, dep), in_part, r, F, f_at, "in_products"
        )

    odd = [r for r in range(F) if r & 1]
    far_odd = [r for r in odd if r & half_f]
    near_odd = [r for r in odd if not r & half_f]

    def to_home(even, odd):
        return absolute(jnp.concatenate([even, odd], 0).transpose(0, 2, 1), s)

    gate_grads = jnp.stack(
        [to_home(own_parts[4], own_parts[5]), to_home(other_parts[4], other_parts[5])], 1
    ).reshape(S, -1)
    other_got = swap(other_parts[3], "seq", S, 1)
    gate_grads = lax.all_to_all(gate_grads, "seq", split_axis=0, concat_axis=0, tiled=True)
    other_got, gate_grads = tie(other_got, gate_grads)
    for r in far_odd:
        in_products(r, other_got)

    def send_in(n, *dep):
        return {r: swap(after(sent[r][n], dep), "fsdp", F, 1) for r in sent}

    other_sums = sum_cores(other_parts[2], other_got, S)
    come = sum_first(other_sums, S)
    other_out_got = swap(after(other_parts[1], other_got), "seq", S, 1)
    gate_grads = gate_grads.reshape(S, 2, T * experts)
    partner_grads = far_swap(gate_grads[:, 1])
    come, in_terms, other_out_got, partner_grads = tie(
        come, in_terms, other_out_got, partner_grads
    )
    sent = {r: quarters(in_terms[r], 1) for r in far_odd}
    singles, other_total = sum_more(other_sums, come, S)
    come = sum_last(singles, S)
    start_got = {r: swap(in_terms[r][:, : 2 * quarter], "fsdp", F, 1) for r in far_odd}

    def down_products(r, dep):
        down_terms[r] = products(
            after(hidden_gate, dep), u_rows, down_part, r, half_f, f_at, "down_products"
        )

    for r in range(1, half_f, 2):
        down_products(r, singles)
    come, start_got, down_terms = tie(come, start_got, down_terms)
    far_got = [
        {r: got[:, n * quarter : (n + 1) * quarter] for r, got in start_got.items()}
        for n in range(2)
    ]
    other_rows = add_all(other_total, come).astype(BF16)
    gate_grads = gate_grads[:, 0] + partner_grads
    gate_grads = gate_grads.reshape(S, T, experts).transpose(1, 0, 2).reshape(T, E)
    back = [far_swap(other_rows[:half_rows])]
    own_sums = sum_cores(own_parts[2], after(own_got, other_rows), S)
    come = sum_first(own_sums, S)
    far_got.append(send_in(2, other_rows))
    for r in far_odd:
        in_products(r ^ 1, other_rows)
    come, back[0], far_got[2], in_terms = tie(come, back[0], far_got[2], in_terms)
    back.append(far_swap(other_rows[half_rows:], come))
    singles, own_total = sum_more(own_sums, come, S)
    come = sum_last(singles, S)
    down_sent = {r: quarters(down_terms[r], 1) for r in range(1, half_f, 2)}
    for r in down_sent:
        down_sent[r] = down_sent[r][:2] + [jnp.concatenate(down_sent[r][2:], 1)]

    def send_down(n, *dep):
        return {r: swap(after(down_sent[r][n], dep), "fsdp", F, 1) for r in down_sent}

    far_got.append(send_in(3, singles))
    for r in near_odd:
        in_products(r, singles)
    come, back[1], far_got[3], in_terms = tie(come, back[1], far_got[3], in_terms)
    row_grads = add_all(own_total, come) + jnp.concatenate(back, 0).astype(F32)

    upstream = upstream_low.astype(F32)
    logit_grads = router_probs * (
        gate_grads - jnp.sum(router_probs * gate_grads, axis=-1, keepdims=True)
    )
    router_wide = full_router.astype(F32)
    second_grads = row_grads + jnp.dot(logit_grads, router_wide.T, precision=HIGHEST)
    pulled = second_grads * gain_moe
    residual_grads = upstream + moe_factor * (
        pulled - residual_n * jnp.mean(pulled * residual_n, axis=-1, keepdims=True)
    )
    branch_low = residual_grads.astype(BF16)

    def sum_near(terms):
        mask = 2
        while mask < half_f:
            terms = {
                r: terms[r] + swap(terms[r | mask].astype(BF16), "fsdp", F, mask).astype(F32)
                for r in terms
                if not r & mask
            }
            mask *= 2
        (total,) = terms.values()
        return total

    def far_sum(n, *dep):
        terms = {
            r ^ 1: quarters(in_terms[r ^ 1], 1)[n].astype(F32) + far_got[n][r].astype(F32)
            for r in far_odd
        }
        return far_swap(sum_near(terms).astype(BF16), *dep)

    branch_first = gather_first(branch_low, S)
    far_sums = [far_sum(0, branch_low)]
    down_got = [send_down(0, branch_low)]
    for r in range(0, half_f, 2):
        down_products(r, branch_low)
    branch_first, far_sums[0], down_got[0], down_terms = tie(
        branch_first, far_sums[0], down_got[0], down_terms
    )
    branch_more = gather_more(branch_low, branch_first, S)
    far_sums.append(far_sum(1, branch_first))
    down_got.append(send_down(1, branch_first))
    branch_even, branch_odd = gather_end(branch_low, branch_first, branch_more, S)

    head_grads = jnp.concatenate(
        [matmul_t(branch_even, own_output), matmul_t(branch_odd, own_output)], 0
    ).astype(BF16)
    head_grads = absolute(head_grads.reshape(S, T, C), s).reshape(L, C)
    head_grads, far_sums[1], down_got[1] = tie(head_grads, far_sums[1], down_got[1])
    far_sums.append(far_sum(2, head_grads))
    down_got.append(send_down(2, head_grads))
    other_out_sums = sum_cores(other_parts[0], after(other_out_got, head_grads), S)
    come, head_grads = sum_first(other_out_sums, S, head_grads)
    query_back, key_back, value_back = attention_backward(
        query_low, key_low, value_low, head_grads, lse, seg_row, seg_col
    )
    query_back, key_back, value_back, far_sums[2], down_got[2], come = tie(
        query_back, key_back, value_back, far_sums[2], down_got[2], come
    )

    singles, other_total = sum_more(other_out_sums, come, S)
    come = sum_last(singles, S)
    far_sums.append(far_sum(3, query_back))
    attended_rel = relative(after(attended_blocks, singles), s).reshape(2, L // 2, C)
    output_term = t_matmul(attended_rel[0], branch_even) + t_matmul(attended_rel[1], branch_odd)
    output_term = by_index(output_term.astype(BF16).reshape(F, part, D), f, F)
    output_got = swap(output_term[: F // 2], "fsdp", F, 1)
    value_rel = relative(value_back.reshape(S, T, C), s).reshape(2, L // 2, C)

    def weight_term(even, odd):
        term = (t_matmul(normed_even, even) + t_matmul(normed_odd, odd)).astype(BF16)
        return by_index(term.reshape(S, F, part, -1).transpose(1, 0, 2, 3), f, F)

    means, gain_term = rope_means(
        query_back, key_back, query_pre, key_pre, squares, head_gain, cosine, sine
    )
    means = sum_all(means, "seq", S)
    value_term = weight_term(value_rel[0], value_rel[1])
    means, come, far_sums[3], output_got, value_term = tie(
        means, come, far_sums[3], output_got, value_term
    )
    other_outs = add_all(other_total, come).astype(BF16)
    outs_back = [far_swap(other_outs[:half_rows])]
    value_got = swap(value_term[: F // 2], "fsdp", F, 1)
    pre_rel = rope_back(
        (query_back, key_back, value_back),
        query_pre,
        key_pre,
        squares,
        means,
        head_gain,
        cosine,
        sine,
        me,
        T,
    ).reshape(2, L // 2, 3 * C)
    normed_got = swap(matmul_t(pre_rel[1], w_qkv).astype(BF16), "seq", S, 1)
    normed_kept = matmul_t(pre_rel[0], w_qkv).astype(BF16)
    normed_got, normed_kept, value_got, outs_back[0] = tie(
        normed_got, normed_kept, value_got, outs_back[0]
    )

    normed_sums = sum_cores(normed_kept, normed_got, S)
    come = sum_first(normed_sums, S)
    value_sum = sum_rest(sum_even(value_term, value_got, F), F)
    turned_term = weight_term(
        after(pre_rel[0][:, : 2 * C], normed_got), after(pre_rel[1][:, : 2 * C], normed_got)
    )
    late_grads, late_logits = after(second_grads, normed_got), after(logit_grads, normed_got)
    router_term = jnp.dot(second_low.astype(F32).T, late_logits, precision=HIGHEST)
    moe_gain_term = jnp.sum(late_grads * residual_n, axis=0)
    gain_terms = jnp.concatenate(
        [router_term.reshape(S * F, part * E), moe_gain_term.reshape(S * F, part)], 1
    )
    gain_terms = in_relative(gain_terms, S, F, s, f).reshape(S, F, -1)
    head_terms = gain_term.reshape(2, F, part).transpose(1, 0, 2).reshape(F, 2 * part)
    head_terms = in_relative(head_terms, 1, F, 0, f)
    gain_terms = jnp.concatenate([gain_terms.transpose(1, 0, 2).reshape(F, -1), head_terms], 1)
    own_out_sums = sum_cores(own_parts[0], after(own_out_got, normed_got), S)
    own_come = sum_first(own_out_sums, S)
    come, turned_term, value_sum, gain_terms, own_come = tie(
        come, turned_term, value_sum, gain_terms, own_come
    )
    turned_got = swap(turned_term[: F // 2], "fsdp", F, 1)
    singles, normed_total = sum_more(normed_sums, come, S)
    come = sum_last(singles, S)
    gain_got = swap(gain_terms[F // 2 :], "fsdp", F, half_f)
    for r in near_odd:
        in_products(r ^ 1, turned_term)
    come, turned_got, gain_got, in_terms = tie(come, turned_got, gain_got, in_terms)
    gain_terms = gain_terms[: F // 2] + gain_got
    normed_grads = add_all(normed_total, come)
    turned_sum = sum_rest(sum_even(turned_term, turned_got, F), F)
    middle = in_part // 2

    def send_near(first, dep):
        return {
            r: swap(after(in_terms[r][:, first : first + middle], dep), "fsdp", F, 1)
            for r in near_odd
        }

    near_got = [send_near(0, turned_got)]
    gain_terms = halve(after(gain_terms, turned_got), "fsdp", F, half_f // 2)
    singles, own_total = sum_more(after(own_out_sums, turned_got), own_come, S)
    own_come = sum_last(singles, S)
    turned_sum, own_come, near_got[0], gain_terms = tie(
        turned_sum, own_come, near_got[0], gain_terms
    )
    near_got.append(send_near(middle, turned_sum))
    outs_back.append(far_swap(other_outs[half_rows:], turned_sum))
    count = S * part * (E + 1)
    head_terms = gain_terms[0, count:]
    gain_terms = halve(gain_terms[0, :count].reshape(S, -1), "seq", S, S // 2)[0]
    own_outs = add_all(own_total, own_come)
    qkv_term = jnp.concatenate([turned_sum, value_sum], -1).astype(BF16)
    qkv_term = lax.all_to_all(qkv_term, "seq", split_axis=0, concat_axis=0, tiled=True)
    qkv_term, outs_back[1], near_got[1], gain_terms = tie(
        qkv_term, outs_back[1], near_got[1], gain_terms
    )
    outs_back = jnp.concatenate(outs_back, 0).astype(F32)
    mixed = (residual + own_outs + outs_back).astype(BF16)[None]
    qkv_term = [
        qkv_term[:, :, j * C : (j + 1) * C].transpose(1, 0, 2).reshape(part, D).astype(F32)
        for j in range(3)
    ]
    grad_output = sum_rest(sum_even(output_term, output_got, F), F)

    near_got = {r: jnp.concatenate([got[r] for got in near_got], 1) for r in near_odd}
    own_term = sum_near(
        {r ^ 1: in_terms[r ^ 1].astype(F32) + near_got[r].astype(F32) for r in near_odd}
    )
    far_term = jnp.concatenate(far_sums, 1).astype(F32)
    first_half = half_at == 0
    lower = jnp.where(first_half, own_term, far_term)
    upper = jnp.where(first_half, far_term, own_term)
    grad_gate, grad_up = (
        jnp.concatenate([lower[..., at], upper[..., at]], axis=-1)
        for at in (slice(0, hidden_half), slice(hidden_half, 2 * hidden_half))
    )
    down_got = after(down_got, turned_sum)
    down_got = {r: jnp.concatenate([got[r] for got in down_got], 1) for r in down_sent}
    grad_down = sum_near(
        {r ^ 1: down_terms[r ^ 1].astype(F32) + down_got[r].astype(F32) for r in down_sent}
    )

    attn_factor = rms_factor(inputs)
    inputs_n = inputs * attn_factor
    attn_pulled = normed_grads * gain_attn
    grad_tokens = residual_grads + attn_factor * (
        attn_pulled - inputs_n * jnp.mean(attn_pulled * inputs_n, axis=-1, keepdims=True)
    )
    grad_attn_gain = sum(
        jnp.sum(term * weight.astype(F32), axis=1)
        for term, weight in zip(qkv_term, (w_query, w_key, w_value))
    ) / attn_gain.astype(F32)
    return (
        mixed,
        grad_tokens[None],
        qkv_term[0],
        qkv_term[1],
        qkv_term[2],
        grad_output,
        gain_terms[: part * E].reshape(part, E),
        grad_attn_gain,
        gain_terms[part * E :],
        head_terms[:part],
        head_terms[part:],
        grad_gate,
        grad_up,
        grad_down,
    )


def solution(mesh):
    tokens_spec = P("fsdp", "seq", None)
    rows_spec = P(("seq", "fsdp"), None)
    gain_spec = P(("seq", "fsdp"))
    expert_spec = P("seq", "fsdp", None)
    in_specs = (
        (tokens_spec, P("fsdp", None), tokens_spec, tokens_spec)
        + (rows_spec,) * 5
        + (gain_spec,) * 4
        + (expert_spec,) * 3
    )
    out_specs = (tokens_spec,) * 2 + (rows_spec,) * 5 + (gain_spec,) * 4 + (expert_spec,) * 3
    return jax.shard_map(
        partial(per_device, mesh.shape["seq"], mesh.shape["fsdp"]),
        mesh=mesh,
        in_specs=in_specs,
        out_specs=out_specs,
        check_vma=False,
    )
```

```python
from functools import partial

import jax
import jax.numpy as jnp
from jax import lax
from jax.experimental import pallas as pl
from jax.experimental.pallas import tpu as pltpu
from jax.sharding import PartitionSpec as P

D = 2048
H = 16
DH = 128
E = 16
WINDOW = 1024
CAP = 144

EPSILON = 1e-06
ROPE_BASE = 50000.0
HIGHEST = lax.Precision.HIGHEST
BF16 = jnp.bfloat16
F32 = jnp.float32
MIB = 1024 * 1024


def matmul(left, right):
    return jnp.dot(left, right, preferred_element_type=F32)


def matmul_t(left, right):
    return lax.dot_general(left, right, (((1,), (1,)), ((), ())), preferred_element_type=F32)


def t_matmul(left, right):
    return lax.dot_general(left, right, (((0,), (0,)), ((), ())), preferred_element_type=F32)


def rms_factor(values):
    return lax.rsqrt(jnp.mean(values * values, axis=-1, keepdims=True) + EPSILON)


def swap(values, axis, size, mask):
    return lax.ppermute(values, axis, [(i, i ^ mask) for i in range(size)])


def high_bit(number):
    return 1 << (number.bit_length() - 1)


def low_bit(number):
    return number & -number


def after(values, *others):
    return lax.optimization_barrier((values, others))[0]


def tie(*values):
    return lax.optimization_barrier(values)


def gather_first(values, size):
    return {r: swap(values, "seq", size, r) for r in range(2, size, 2) if r == low_bit(r)}


def gather_more(values, first, size):
    rows = values.shape[0] // 2
    pieces = dict(first)
    for r in range(2, size, 2):
        if r not in pieces:
            up, down = high_bit(r), low_bit(r)
            upper, lower = pieces[r ^ up], pieces[r ^ down]
            upper = upper[0] if isinstance(upper, tuple) else upper[:rows]
            lower = lower[1] if isinstance(lower, tuple) else lower[rows:]
            pieces[r] = (swap(upper, "seq", size, up), swap(lower, "seq", size, down))
    return {r: piece for r, piece in pieces.items() if r not in first}


def gather_end(values, first, more, size):
    blocks = [values]
    for r in range(2, size, 2):
        blocks.extend([first[r]] if r in first else more[r])
    even = jnp.concatenate(blocks, 0)
    return even, swap(even, "seq", size, 1)


def relative(blocks, me):
    size = blocks.shape[0]
    order = list(range(0, size, 2)) + list(range(1, size, 2))
    return jnp.concatenate([lax.dynamic_slice_in_dim(blocks, me ^ r, 1, 0) for r in order], 0)


def absolute(blocks, me):
    size = blocks.shape[0]
    places = [((me ^ j) // 2) + ((me ^ j) % 2) * (size // 2) for j in range(size)]
    return jnp.concatenate([lax.dynamic_slice_in_dim(blocks, at, 1, 0) for at in places], 0)


def sum_cores(even, got, size):
    rows = even.shape[0] // (size // 2)
    half = rows // 2

    def part(r, first):
        at = slice(r // 2 * rows + first, r // 2 * rows + first + half)
        return even[at].astype(F32) + got[at].astype(F32)

    return {r: [part(r, 0), part(r, half)] for r in range(0, size, 2)}


def sum_first(sums, size, held=None):
    sums = {r: list(value) for r, value in sums.items()}
    come = {}
    for r in range(size - 2, 0, -2):
        if r != low_bit(r):
            up, down = high_bit(r), low_bit(r)
            for (goal, k, _), piece in come.items():
                if goal == r:
                    sums[r][k] += piece.astype(F32)
            upper, lower, held = tie(sums[r][0].astype(BF16), sums[r][1].astype(BF16), held)
            come[r ^ up, 0, r] = swap(upper, "seq", size, up)
            come[r ^ down, 1, r] = swap(lower, "seq", size, down)
    return come if held is None else (come, held)


def sum_more(sums, come, size):
    sums = {r: list(value) for r, value in sums.items() if r == 0 or r == low_bit(r)}
    for (goal, k, _), piece in come.items():
        if goal in sums:
            sums[goal][k] += piece.astype(F32)
    singles = {
        r: jnp.concatenate([v.astype(BF16) for v in value], 0) for r, value in sums.items() if r
    }
    return tie(singles)[0], jnp.concatenate(sums[0], 0)


def sum_last(singles, size):
    return {r: swap(value, "seq", size, r) for r, value in singles.items()}


def add_all(total, pieces):
    for piece in pieces.values():
        total += piece.astype(F32)
    return total


def quarters(values, axis):
    step = values.shape[axis] // 4
    return [lax.slice_in_dim(values, k * step, (k + 1) * step, axis=axis) for k in range(4)]


def sum_all(values, axis, size):
    mask = 1
    while mask < size:
        values = values + swap(values, axis, size, mask)
        mask *= 2
    return values


def fsdp_pieces(values, size):
    pieces = {0: values}
    for r in range(1, size):
        low = low_bit(r)
        pieces[r] = swap(pieces[r ^ low], "fsdp", size, low)
    return pieces


def place_fsdp(pieces, me, axis):
    size = len(pieces)
    shape = pieces[0].shape
    whole = jnp.zeros(shape[:axis] + (size,) + shape[axis:], pieces[0].dtype)
    for r, piece in pieces.items():
        whole = lax.dynamic_update_slice_in_dim(whole, jnp.expand_dims(piece, axis), me ^ r, axis)
    return whole


def near_pieces(values, size):
    pieces = {0: values}
    for r in range(1, size // 2):
        up = high_bit(r)
        pieces[r] = swap(pieces[r ^ up], "fsdp", size, up)
    return pieces


def double(values, axis, size):
    mask = 1
    while mask < size:
        values = jnp.concatenate([values, swap(values, axis, size, mask)], 0)
        mask *= 2
    return values


def halve(values, axis, size, mask):
    while mask:
        half = values.shape[0] // 2
        values = values[:half] + swap(values[half:], axis, size, mask)
        mask //= 2
    return values


def relative_pick(seq_size, fsdp_size, s, f):
    index = jnp.arange(seq_size * fsdp_size, dtype=jnp.int32)
    source = ((index // fsdp_size) ^ s) * fsdp_size + ((index % fsdp_size) ^ f)
    return source[:, None] == index[None, :]


def in_order(values, seq_size, fsdp_size, s, f):
    pick = relative_pick(seq_size, fsdp_size, s, f).astype(values.dtype)
    return matmul(pick, values).astype(values.dtype)


def in_relative(values, seq_size, fsdp_size, s, f):
    pick = relative_pick(seq_size, fsdp_size, s, f).astype(F32)
    return jnp.dot(pick, values, precision=HIGHEST)


def by_index(partial_sum, me, size):
    order = [r for r in range(size) if r & 1] + [r for r in range(size) if not r & 1]
    return jnp.concatenate([lax.dynamic_slice_in_dim(partial_sum, me ^ r, 1, 0) for r in order], 0)


def sum_even(stacked, got, size):
    return (stacked[size // 2 :].astype(F32) + got.astype(F32)).astype(BF16)


def sum_rest(stacked, size):
    mask = 2
    values = stacked.astype(F32)
    while mask < size:
        count = values.shape[0] // 2
        pairs = values.reshape((count, 2) + values.shape[1:])
        got = swap(pairs[:, 1].astype(BF16), "fsdp", size, mask)
        values = pairs[:, 0] + got.astype(F32)
        mask *= 2
    return values[0]


def allowed_keys(seg_row, seg_col, first_query, first_key, rows, span, half_window):
    query_at = first_query + lax.broadcasted_iota(jnp.int32, (span, rows), 1)
    key_at = first_key + lax.broadcasted_iota(jnp.int32, (span, rows), 0)
    return (jnp.abs(query_at - key_at) <= half_window) & (seg_col == seg_row)


def first_key_of(block, rows, span, length):
    start = jnp.clip(block * rows - (span - rows) // 2, 0, length - span)
    return pl.multiple_of(start, rows)


def forward_kernel(span, q_ref, k_ref, v_ref, seg_row_ref, seg_col_ref, o_ref, lse_ref):
    block = pl.program_id(1)
    rows, length = q_ref.shape[0], k_ref.shape[0]
    first_key = first_key_of(block, rows, span, length)
    keys = k_ref[pl.ds(first_key, span), :]
    values = v_ref[pl.ds(first_key, span), :]
    scores = matmul_t(keys, q_ref[...]) * DH ** (-0.5)
    allowed = allowed_keys(
        seg_row_ref[...],
        seg_col_ref[pl.ds(first_key, span), :],
        block * rows,
        first_key,
        rows,
        span,
        WINDOW // 2,
    )
    scores = jnp.where(allowed, scores, -1e30)
    peak = jnp.max(scores, axis=0, keepdims=True)
    expos = jnp.exp(scores - peak)
    totals = jnp.sum(expos, axis=0, keepdims=True)
    probs = (expos * (1.0 / totals)).astype(BF16)
    o_ref[...] = t_matmul(values, probs).T.astype(BF16)
    lse_ref[...] = (peak + jnp.log(totals))[None]


def backward_kernel(
    span,
    q_ref,
    k_ref,
    v_ref,
    do_ref,
    lse_ref,
    seg_row_ref,
    seg_col_ref,
    dq_ref,
    dk_ref,
    dv_ref,
    dk_sum,
    dv_sum,
):
    block = pl.program_id(1)
    rows, length = q_ref.shape[0], k_ref.shape[0]

    @pl.when(block == 0)
    def _():
        dk_sum[...] = jnp.zeros_like(dk_sum)
        dv_sum[...] = jnp.zeros_like(dv_sum)

    first_key = first_key_of(block, rows, span, length)
    at = pl.ds(first_key, span)
    keys = k_ref[at, :]
    values = v_ref[at, :]
    queries = q_ref[...]
    grads = do_ref[...]
    scores = matmul_t(keys, queries) * DH ** (-0.5)
    allowed = allowed_keys(
        seg_row_ref[...],
        seg_col_ref[at, :],
        block * rows,
        first_key,
        rows,
        span,
        WINDOW // 2,
    )
    probs = jnp.where(allowed, jnp.exp(scores - lse_ref[0]), 0.0)
    dv_sum[at, :] += matmul(probs.astype(BF16), grads)
    prob_grads = matmul_t(values, grads)
    center = jnp.sum(probs * prob_grads, axis=0, keepdims=True)
    score_grads = (probs * (prob_grads - center)).astype(BF16)
    dk_sum[at, :] += matmul(score_grads, queries)
    dq_ref[...] = (t_matmul(keys, score_grads) * DH ** (-0.5)).T.astype(BF16)

    @pl.when(block == length // rows - 1)
    def _():
        dk_ref[...] = (dk_sum[...] * DH ** (-0.5)).astype(BF16)
        dv_ref[...] = dv_sum[...].astype(BF16)


def attention_sizes(length):
    rows = 256
    return rows, min(length, rows + WINDOW)


def attention_forward(queries, keys, values, seg_row, seg_col):
    length, columns = queries.shape
    heads = columns // DH
    rows, span = attention_sizes(length)
    block = pl.BlockSpec((rows, DH), lambda h, i: (i, h))
    whole = pl.BlockSpec((length, DH), lambda h, i: (0, h))
    return pl.pallas_call(
        partial(forward_kernel, span),
        grid=(heads, length // rows),
        in_specs=[
            block,
            whole,
            whole,
            pl.BlockSpec((1, rows), lambda h, i: (0, i)),
            pl.BlockSpec((length, 1), lambda h, i: (0, 0)),
        ],
        out_specs=[block, pl.BlockSpec((1, 1, rows), lambda h, i: (h, 0, i))],
        out_shape=[
            jax.ShapeDtypeStruct((length, columns), BF16),
            jax.ShapeDtypeStruct((heads, 1, length), F32),
        ],
        compiler_params=pltpu.CompilerParams(vmem_limit_bytes=48 * MIB),
        cost_estimate=pl.CostEstimate(
            flops=4 * heads * length * span * DH,
            bytes_accessed=8 * length * columns,
            transcendentals=heads * length * span,
        ),
        name="attend",
    )(queries, keys, values, seg_row, seg_col)


def attention_backward(queries, keys, values, grads, lse, seg_row, seg_col):
    length, columns = queries.shape
    heads = columns // DH
    rows, span = attention_sizes(length)
    block = pl.BlockSpec((rows, DH), lambda h, i: (i, h))
    whole = pl.BlockSpec((length, DH), lambda h, i: (0, h))
    shape = jax.ShapeDtypeStruct((length, columns), BF16)
    return pl.pallas_call(
        partial(backward_kernel, span),
        grid=(heads, length // rows),
        in_specs=[
            block,
            whole,
            whole,
            block,
            pl.BlockSpec((1, 1, rows), lambda h, i: (h, 0, i)),
            pl.BlockSpec((1, rows), lambda h, i: (0, i)),
            pl.BlockSpec((length, 1), lambda h, i: (0, 0)),
        ],
        out_specs=[block, whole, whole],
        out_shape=[shape, shape, shape],
        scratch_shapes=[pltpu.VMEM((length, DH), F32), pltpu.VMEM((length, DH), F32)],
        compiler_params=pltpu.CompilerParams(vmem_limit_bytes=48 * MIB),
        cost_estimate=pl.CostEstimate(
            flops=10 * heads * length * span * DH,
            bytes_accessed=14 * length * columns,
            transcendentals=heads * length * span,
        ),
        name="attend_back",
    )(queries, keys, values, grads, lse, seg_row, seg_col)


def qkv_kernel(
    me_ref,
    even_ref,
    odd_ref,
    weight_ref,
    gain_ref,
    normed_even_ref,
    normed_odd_ref,
    q_ref,
    k_ref,
    v_ref,
    square_ref,
):
    turned = me_ref[0] % 2
    rows = even_ref.shape[0]
    columns = q_ref.shape[1]
    for k, (token_ref, normed_ref) in enumerate(
        ((even_ref, normed_even_ref), (odd_ref, normed_odd_ref))
    ):
        at = pl.ds(pl.multiple_of((turned ^ k) * rows, rows), rows)
        wide = token_ref[...].astype(F32)
        normed = (wide * rms_factor(wide) * gain_ref[...]).astype(BF16)
        normed_ref[...] = normed
        pre = matmul(normed, weight_ref[...])
        q_ref[at, :] = pre[:, :columns]
        k_ref[at, :] = pre[:, columns : 2 * columns]
        v_ref[at, :] = pre[:, 2 * columns :].astype(BF16)
        for j in range(2):
            squares = 0.0
            for c in range(j * columns, (j + 1) * columns, DH):
                squares += pre[:, c : c + DH] * pre[:, c : c + DH]
            square_ref[j : j + 1, at] = jnp.sum(squares.T, axis=0, keepdims=True)


def project(even, odd, weight, gain, me, rows):
    pairs = even.shape[0] // rows
    length = 2 * even.shape[0]
    depth, columns = weight.shape[0], weight.shape[1] // 3
    token = pl.BlockSpec((rows, depth), lambda i, me: (i, 0))

    def placed(shape):
        return pl.BlockSpec(shape, lambda i, me: (i ^ (me[0] // 2), 0))

    head = jax.ShapeDtypeStruct((length, columns), F32)
    return pl.pallas_call(
        qkv_kernel,
        grid_spec=pltpu.PrefetchScalarGridSpec(
            num_scalar_prefetch=1,
            grid=(pairs,),
            in_specs=[
                token,
                token,
                pl.BlockSpec(weight.shape, lambda i, me: (0, 0)),
                pl.BlockSpec((1, depth), lambda i, me: (0, 0)),
            ],
            out_specs=[
                token,
                token,
                placed((2 * rows, columns)),
                placed((2 * rows, columns)),
                placed((2 * rows, columns)),
                pl.BlockSpec((2, 2 * rows), lambda i, me: (0, i ^ (me[0] // 2))),
            ],
        ),
        out_shape=[
            jax.ShapeDtypeStruct((length // 2, depth), BF16),
            jax.ShapeDtypeStruct((length // 2, depth), BF16),
            head,
            head,
            jax.ShapeDtypeStruct((length, columns), BF16),
            jax.ShapeDtypeStruct((2, length), F32),
        ],
        compiler_params=pltpu.CompilerParams(vmem_limit_bytes=48 * MIB),
        cost_estimate=pl.CostEstimate(
            flops=6 * length * depth * columns,
            bytes_accessed=length * (4 * depth + 10 * columns) + 6 * depth * columns,
            transcendentals=length,
        ),
        name="project",
    )(me, even, odd, weight, gain)


def split_kernel(q_ref, k_ref, v_ref, out_ref):
    columns = q_ref.shape[1]
    for j, ref in enumerate((q_ref, k_ref, v_ref)):
        out_ref[0, :, j * columns : (j + 1) * columns] = ref[...]


def split_heads(w_query, w_key, w_value, parts):
    rows, columns = w_query.shape[0], w_query.shape[1] // parts
    block = pl.BlockSpec((rows, columns), lambda i: (0, i))
    return pl.pallas_call(
        split_kernel,
        grid=(parts,),
        in_specs=[block] * 3,
        out_specs=pl.BlockSpec((1, rows, 3 * columns), lambda i: (i, 0, 0)),
        out_shape=jax.ShapeDtypeStruct((parts, rows, 3 * columns), BF16),
        name="split_heads",
    )(w_query, w_key, w_value)


def spread(row, columns):
    return jnp.broadcast_to(row, (columns, row.shape[1])).T


def factor_of(square_row):
    return lax.rsqrt(square_row / D + EPSILON)


def turn(values, cosine, sine):
    return values * cosine + pltpu.roll(values, DH // 2, 1) * sine


def rope_kernel(q_ref, k_ref, square_ref, gain_ref, cos_ref, sin_ref, q_out, k_out):
    cosine, sine = cos_ref[...], sin_ref[...]
    for j, (pre_ref, out_ref) in enumerate(((q_ref, q_out), (k_ref, k_out))):
        factor = spread(factor_of(square_ref[j : j + 1, :]), DH)
        for c in range(0, pre_ref.shape[1], DH):
            at = slice(c, c + DH)
            normed = pre_ref[:, at] * factor * gain_ref[j : j + 1, at]
            out_ref[:, at] = turn(normed, cosine, sine).astype(BF16)


def rope(query_pre, key_pre, squares, gains, cosine, sine):
    length, columns = query_pre.shape
    rows = min(512, length)
    block = pl.BlockSpec((rows, columns), lambda i: (i, 0))
    table = pl.BlockSpec((rows, DH), lambda i: (i, 0))
    return pl.pallas_call(
        rope_kernel,
        grid=(length // rows,),
        in_specs=[
            block,
            block,
            pl.BlockSpec((2, rows), lambda i: (0, i)),
            pl.BlockSpec((2, columns), lambda i: (0, 0)),
            table,
            table,
        ],
        out_specs=[block, block],
        out_shape=[jax.ShapeDtypeStruct((length, columns), BF16)] * 2,
        compiler_params=pltpu.CompilerParams(vmem_limit_bytes=32 * MIB),
        name="rope",
    )(query_pre, key_pre, squares, gains, cosine, sine)


def pulled_of(grad_ref, pre_ref, factor, gain_ref, cosine, sine, j, at):
    turned = turn(grad_ref[:, at].astype(F32), cosine, -sine)
    return turned, turned * gain_ref[j : j + 1, at], pre_ref[:, at] * factor


def rope_mean_kernel(
    dq_ref, dk_ref, q_ref, k_ref, square_ref, gain_ref, cos_ref, sin_ref, mean_ref, term_ref
):
    @pl.when(pl.program_id(0) == 0)
    def _():
        term_ref[...] = jnp.zeros_like(term_ref)

    cosine, sine = cos_ref[...], sin_ref[...]
    for j, (grad_ref, pre_ref) in enumerate(((dq_ref, q_ref), (dk_ref, k_ref))):
        factor = spread(factor_of(square_ref[j : j + 1, :]), DH)
        total = 0.0
        for c in range(0, pre_ref.shape[1], DH):
            at = slice(c, c + DH)
            turned, pulled, normed = pulled_of(
                grad_ref, pre_ref, factor, gain_ref, cosine, sine, j, at
            )
            term_ref[j : j + 1, at] += jnp.sum(turned * normed, axis=0, keepdims=True)
            total += pulled * normed
        mean_ref[j : j + 1, :] = jnp.sum(total.T, axis=0, keepdims=True)


def rope_means(query_back, key_back, query_pre, key_pre, squares, gains, cosine, sine):
    length, columns = query_pre.shape
    rows = min(512, length)
    block = pl.BlockSpec((rows, columns), lambda i: (i, 0))
    table = pl.BlockSpec((rows, DH), lambda i: (i, 0))
    row = pl.BlockSpec((2, rows), lambda i: (0, i))
    fixed = pl.BlockSpec((2, columns), lambda i: (0, 0))
    return pl.pallas_call(
        rope_mean_kernel,
        grid=(length // rows,),
        in_specs=[block, block, block, block, row, fixed, table, table],
        out_specs=[row, fixed],
        out_shape=[
            jax.ShapeDtypeStruct((2, length), F32),
            jax.ShapeDtypeStruct((2, columns), F32),
        ],
        compiler_params=pltpu.CompilerParams(vmem_limit_bytes=32 * MIB),
        name="rope_means",
    )(query_back, key_back, query_pre, key_pre, squares, gains, cosine, sine)


def rope_back_kernel(
    me_ref,
    dq_ref,
    dk_ref,
    dv_ref,
    q_ref,
    k_ref,
    square_ref,
    mean_ref,
    gain_ref,
    cos_ref,
    sin_ref,
    out_ref,
):
    cosine, sine = cos_ref[...], sin_ref[...]
    columns = q_ref.shape[1]
    for j, (grad_ref, pre_ref) in enumerate(((dq_ref, q_ref), (dk_ref, k_ref))):
        factor = spread(factor_of(square_ref[j : j + 1, :]), DH)
        mean = spread(mean_ref[j : j + 1, :] / D, DH)
        for c in range(0, columns, DH):
            at = slice(c, c + DH)
            _, pulled, normed = pulled_of(grad_ref, pre_ref, factor, gain_ref, cosine, sine, j, at)
            out_ref[:, j * columns + c : j * columns + c + DH] = (
                factor * (pulled - normed * mean)
            ).astype(BF16)
    out_ref[:, 2 * columns :] = dv_ref[...]


def rope_back(grads, query_pre, key_pre, squares, means, gains, cosine, sine, me, rows):
    length, columns = query_pre.shape
    half = length // rows // 2

    def source(p, me):
        return me[0] ^ (p % half * 2 + p // half)

    block = pl.BlockSpec((rows, columns), lambda p, me: (source(p, me), 0))
    table = pl.BlockSpec((rows, DH), lambda p, me: (source(p, me), 0))
    row = pl.BlockSpec((2, rows), lambda p, me: (0, source(p, me)))
    return pl.pallas_call(
        rope_back_kernel,
        grid_spec=pltpu.PrefetchScalarGridSpec(
            num_scalar_prefetch=1,
            grid=(2 * half,),
            in_specs=[block] * 5
            + [row, row, pl.BlockSpec((2, columns), lambda p, me: (0, 0)), table, table],
            out_specs=pl.BlockSpec((rows, 3 * columns), lambda p, me: (p, 0)),
        ),
        out_shape=jax.ShapeDtypeStruct((length, 3 * columns), BF16),
        compiler_params=pltpu.CompilerParams(vmem_limit_bytes=32 * MIB),
        name="rope_back",
    )(me, *grads, query_pre, key_pre, squares, means, gains, cosine, sine)


def expert_kernel(
    in_places, down_places, first_ref, xa_ref, xb_ref, ua_ref, ub_ref, ra_ref, rb_ref, router_ref, *refs
):
    weight_refs = refs[: len(in_places) + len(down_places)]
    (ya_ref, yb_ref, za_ref, zb_ref, ga_ref, gb_ref, xc_ref, uc_ref, dg_ref, hid_ref) = refs[-13:-3]
    wi_ref, wd_ref, sems = refs[-3:]
    experts, _, hidden = hid_ref.shape
    rows = xa_ref.shape[0]

    @pl.when(pl.program_id(0) == 0)
    def _():
        copies = []
        for n, (ref, (r, first, part)) in enumerate(zip(weight_refs, in_places + down_places)):
            goal = wi_ref if n < len(in_places) else wd_ref
            place = lax.rem(first_ref[1] ^ r, goal.shape[1] // part)
            at = pl.ds(pl.multiple_of(place * part + first, ref.shape[1]), ref.shape[1])
            copies.append(pltpu.make_async_copy(ref, goal.at[:, at, :], sems.at[n]))
        for copy in copies:
            copy.start()
        for copy in copies:
            copy.wait()

    slot = lax.broadcasted_iota(jnp.int32, (CAP, rows), 0)
    blocks = (
        (xa_ref, ua_ref, ra_ref, ya_ref, za_ref, ga_ref),
        (xb_ref, ub_ref, rb_ref, yb_ref, zb_ref, gb_ref),
    )
    picks = []
    for k, (x_ref, u_ref, rank_ref, _, _, _) in enumerate(blocks):
        hits = jnp.concatenate([slot == rank_ref[0, e : e + 1, :] for e in range(experts)], 0)
        pick = hits.astype(F32).astype(BF16)
        picks.append(pick)
        x_rows = matmul(pick, x_ref[...]).astype(BF16)
        u_rows = matmul(pick, u_ref[...]).astype(BF16)
        for e in range(experts):
            xc_ref[e, k * CAP : (k + 1) * CAP, :] = x_rows[e * CAP : (e + 1) * CAP]
            uc_ref[e, k * CAP : (k + 1) * CAP, :] = u_rows[e * CAP : (e + 1) * CAP]
    outs, backs, gate_grads = [], [], []
    for e in range(experts):
        x_rows, u_rows = xc_ref[e], uc_ref[e]
        logits = matmul(x_rows, router_ref[...])
        lane = lax.broadcasted_iota(jnp.int32, logits.shape, 1)
        logits = jnp.where(lane < E, logits, -1e30)
        expos = jnp.exp(logits - jnp.max(logits, axis=-1, keepdims=True))
        own = jnp.sum(jnp.where(lane == first_ref[0] + e, expos, 0.0), axis=-1, keepdims=True)
        gate = own / jnp.sum(expos, axis=-1, keepdims=True)
        gated = matmul(x_rows, wi_ref[e, :, :hidden])
        upward = matmul(x_rows, wi_ref[e, :, hidden:])
        pulled = matmul_t(u_rows, wd_ref[e])
        sig = jax.nn.sigmoid(gated)
        silu = gated * sig
        acts = silu * upward
        gate_grads.append(jnp.sum(acts * pulled, axis=-1, keepdims=True))
        hidden_gate = (acts * gate).astype(BF16)
        hidden_grads = pulled * gate
        hid_ref[e] = hidden_gate
        dg_ref[e, :, :hidden] = (hidden_grads * upward * sig * (1.0 + gated * (1.0 - sig))).astype(BF16)
        dg_ref[e, :, hidden:] = (hidden_grads * silu).astype(BF16)
        outs.append(matmul(hidden_gate, wd_ref[e]).astype(BF16))
        backs.append(matmul_t(dg_ref[e], wi_ref[e]).astype(BF16))
    for k, (_, _, rank_ref, y_ref, z_ref, g_ref) in enumerate(blocks):
        at = slice(k * CAP, (k + 1) * CAP)
        y_ref[...] = t_matmul(picks[k], jnp.concatenate([v[at] for v in outs], 0)).astype(BF16)
        z_ref[...] = t_matmul(picks[k], jnp.concatenate([v[at] for v in backs], 0)).astype(BF16)
        for e in range(experts):
            hit = slot == rank_ref[0, e : e + 1, :]
            g_ref[0, e : e + 1, :] = jnp.sum(
                jnp.where(hit, gate_grads[e][at], 0.0), axis=0, keepdims=True
            )


def run_experts(x, u, ranks, in_pieces, down_pieces, router, places, which, compact, parts):
    experts, _, hidden = in_pieces[0][2].shape
    hidden = hidden // 2
    depth = x[0].shape[1]
    in_places = [(r, at, parts[0]) for r, at, _ in in_pieces]
    down_places = [(r, at, parts[1]) for r, at, _ in down_pieces]
    pieces = [array for _, _, array in in_pieces + down_pieces]
    rows = ranks[0].shape[2]
    steps = x[0].shape[0] // rows
    token = pl.BlockSpec((rows, depth), lambda i: (i, 0))
    rank = pl.BlockSpec((1, experts, rows), lambda i: (i, 0, 0))
    anywhere = pl.BlockSpec(memory_space=pl.ANY)

    def slots(columns):
        return pl.BlockSpec((experts, 2 * CAP, columns), lambda i: (0, i + which * steps, 0))

    shape = jax.ShapeDtypeStruct
    tokens = shape(x[0].shape, BF16)
    gates = shape((steps, experts, rows), F32)
    count = 4 * steps * CAP
    wide = shape((experts, count, depth), BF16)
    inputs = [places, *x, *u, *ranks, router, *pieces]
    return pl.pallas_call(
        partial(expert_kernel, in_places, down_places),
        grid=(steps,),
        in_specs=[pl.BlockSpec(memory_space=pltpu.SMEM)]
        + [token] * 4
        + [rank] * 2
        + [pl.BlockSpec(router.shape, lambda i: (0, 0), pipeline_mode=pl.Buffered(1))]
        + [anywhere] * (len(pieces) + len(compact)),
        out_specs=[token] * 4 + [rank] * 2 + [slots(depth)] * 2 + [slots(2 * hidden), slots(hidden)],
        out_shape=[tokens] * 4
        + [gates] * 2
        + [wide] * 2
        + [shape((experts, count, 2 * hidden), BF16), shape((experts, count, hidden), BF16)],
        scratch_shapes=[
            pltpu.VMEM((experts, depth, 2 * hidden), BF16),
            pltpu.VMEM((experts, hidden, depth), BF16),
            pltpu.SemaphoreType.DMA((len(pieces),)),
        ],
        input_output_aliases={len(inputs) + i: 6 + i for i in range(len(compact))},
        compiler_params=pltpu.CompilerParams(vmem_limit_bytes=60 * MIB),
        cost_estimate=pl.CostEstimate(
            flops=4 * steps * CAP * experts * depth * (7 * hidden + 2 * rows),
            bytes_accessed=60 * MIB,
            transcendentals=2 * steps * CAP * experts * hidden,
        ),
        name="experts",
    )(*inputs, *compact)


def product_kernel(me_ref, left_ref, right_ref, out_ref):
    out_ref[0] = t_matmul(left_ref[0], right_ref[0]).astype(BF16)


def products(left, right, part, r, count, me, name):
    experts, rows, _ = left.shape
    columns = right.shape[2]
    wide = min(columns, 1024)
    return pl.pallas_call(
        product_kernel,
        grid_spec=pltpu.PrefetchScalarGridSpec(
            num_scalar_prefetch=1,
            grid=(experts, columns // wide),
            in_specs=[
                pl.BlockSpec((1, rows, part), lambda e, j, me: (e, 0, lax.rem(me[0] ^ r, count))),
                pl.BlockSpec((1, rows, wide), lambda e, j, me: (e, 0, j)),
            ],
            out_specs=pl.BlockSpec((1, part, wide), lambda e, j, me: (e, 0, j)),
        ),
        out_shape=jax.ShapeDtypeStruct((experts, part, columns), BF16),
        compiler_params=pltpu.CompilerParams(vmem_limit_bytes=56 * MIB),
        cost_estimate=pl.CostEstimate(
            flops=2 * experts * rows * part * columns,
            bytes_accessed=2 * experts * rows * (part + columns),
            transcendentals=0,
        ),
        name=name,
    )(me, left, right)


def per_device(
    S,
    F,
    tokens,
    segments,
    routes,
    cotangent,
    w_query,
    w_key,
    w_value,
    w_output,
    router,
    attn_gain,
    moe_gain,
    query_gain,
    key_gain,
    w_gate,
    w_up,
    w_down,
):
    s = lax.axis_index("seq")
    f = lax.axis_index("fsdp")
    T = tokens.shape[1]
    L = S * T
    heads = H // S
    C = heads * DH
    experts = E // S
    part = w_query.shape[0]
    half_f = F // 2
    hidden_half = w_gate.shape[2] // 2

    me = s.reshape(1).astype(jnp.int32)
    f_at = f.reshape(1).astype(jnp.int32)
    half_at = f // half_f
    tokens_low = tokens[0]
    upstream_low = cotangent[0]
    inputs = tokens_low.astype(F32)
    half_rows = T // 2
    in_part, down_part = w_gate.shape[1], w_down.shape[1]
    quarter = in_part // 4

    def hidden_part(which, first, count):
        return jnp.concatenate(
            [
                lax.dynamic_slice(
                    weight, (0, first, which * hidden_half), (experts, count, hidden_half)
                )
                for weight in (w_gate, w_up)
            ],
            2,
        )

    def far_swap(values, *dep):
        return swap(after(values, dep), "fsdp", F, half_f)

    def near_swap(values, *dep):
        return near_pieces(after(values, dep), F)

    named = routes[0].T[None] == jnp.arange(E, dtype=jnp.int32)[:, None, None]
    chosen = jnp.any(named, axis=1)
    index = jnp.arange(T, dtype=jnp.int32)
    before = (index[:, None] <= index[None, :]).astype(BF16)
    ranks = jnp.where(chosen, matmul(chosen.astype(BF16), before) - 1.0, -1.0)
    small = jnp.concatenate(
        [
            router.reshape(-1),
            attn_gain,
            moe_gain,
            query_gain,
            key_gain,
            ranks.astype(BF16).reshape(-1),
        ]
    )[None]
    crossed = split_heads(w_query, w_key, w_value, S)
    small = double(after(small, crossed), "fsdp", F)
    crossed = lax.all_to_all(crossed, "seq", split_axis=0, concat_axis=0, tiled=True)
    near_own = [near_swap(hidden_part(half_at, 0, 2 * quarter), small)]
    out_dep = small
    small = double(small, "seq", S)
    out_far = far_swap(w_output, out_dep)
    crossed, near_own[0], small, out_far = tie(crossed, near_own[0], small, out_far)

    held = after((w_gate, w_up, w_down, upstream_low), crossed)

    def held_part(which, first, count):
        return jnp.concatenate(
            [
                lax.dynamic_slice(
                    weight, (0, first, which * hidden_half), (experts, count, hidden_half)
                )
                for weight in held[:2]
            ],
            2,
        )

    own_quarters = {n: held_part(half_at, n * quarter, quarter) for n in (2, 3)}
    far_quarters = [held_part(1 - half_at, n * quarter, quarter) for n in range(4)]
    down_rows = quarters(held[2], 1)
    upstream_halves = [held[3][:half_rows], held[3][half_rows:]]
    small = in_order(small, S, F, s, f).reshape(S, F, -1)
    prepared = (own_quarters, far_quarters, down_rows, upstream_halves, small)
    token_first = gather_first(after(tokens_low, crossed), S)
    qkv_pieces = {0: crossed}
    for r in range(1, F):
        low = low_bit(r)
        qkv_pieces[r] = swap(qkv_pieces[r ^ low], "fsdp", F, low)
        if r == half_f:
            qkv_pieces, token_first, prepared = tie(qkv_pieces, token_first, prepared)
            own_quarters, far_quarters, down_rows, upstream_halves, small = prepared
            partner_up = [far_swap(upstream_halves[0])]
    token_more = gather_more(tokens_low, token_first, S)
    qkv_pieces, partner_up[0], token_more = tie(qkv_pieces, partner_up[0], token_more)
    tokens_even, tokens_odd = gather_end(tokens_low, token_first, token_more, S)
    w_qkv = place_fsdp(qkv_pieces, f, 1).reshape(D, 3 * C)

    full_router = small[:, :, : part * E].reshape(D, E)
    gains = [
        small[:, :, part * (E + i) : part * (E + i + 1)].reshape(D).astype(F32) for i in range(4)
    ]
    gain_attn, gain_moe = gains[0], gains[1]
    head_gain = lax.dynamic_slice(jnp.stack(gains[2:], 0), (0, s * C), (2, C))
    places = jnp.arange(L, dtype=jnp.int32).astype(F32)
    freqs = ROPE_BASE ** (-(jnp.arange(DH // 2, dtype=F32) * 2.0 / DH))
    angles = places[:, None] * freqs[None, :]
    cosine, sine = jnp.cos(angles), jnp.sin(angles)
    cosine = jnp.concatenate([cosine, cosine], 1)
    sine = jnp.concatenate([-sine, sine], 1)

    def far_part(n, *dep):
        return far_swap(far_quarters[n], *dep)

    partner_up.append(far_swap(upstream_halves[1], w_qkv))
    out_pieces = {0: after(w_output, w_qkv), half_f: after(out_far, w_qkv)}
    for r in range(1, F):
        if r != half_f:
            low = low_bit(r)
            out_pieces[r] = swap(out_pieces[r ^ low], "fsdp", F, low)
    own_up_first = gather_first(after(upstream_low, w_qkv), S)
    normed_even, normed_odd, query_pre, key_pre, value_low, squares = project(
        tokens_even, tokens_odd, w_qkv, gain_attn[None], me, T
    )
    squares, partner_up[1], out_pieces, own_up_first = tie(
        squares, partner_up[1], out_pieces, own_up_first
    )
    partner_up = jnp.concatenate(partner_up, 0)
    own_output = place_fsdp(out_pieces, f, 0).reshape(C, D)

    out_first = gather_first(own_output, S)
    far = [far_part(0, squares)]
    near_own.append(near_swap(own_quarters[2], squares))
    squares = sum_all(squares, "seq", S)
    query_low, key_low = rope(query_pre, key_pre, squares, head_gain, cosine, sine)
    query_low, out_first, far[0], near_own[1] = tie(query_low, out_first, far[0], near_own[1])

    seg_row = segments
    seg_col = segments.reshape(L, 1)
    out_more = gather_more(own_output, out_first, S)
    far.append(far_part(1, query_low))
    near_own.append(near_swap(own_quarters[3], query_low))
    attended, lse = attention_forward(query_low, key_low, value_low, seg_row, seg_col)
    attended, out_more, far[1], near_own[2] = tie(attended, out_more, far[1], near_own[2])
    attended_blocks = attended.reshape(S, T, C)
    come = lax.all_to_all(attended_blocks, "seq", split_axis=0, concat_axis=0, tiled=True)
    out_even, out_odd = gather_end(own_output, out_first, out_more, S)
    far.append(far_part(2, attended))
    near_far = [near_swap(far[0], attended)]
    own_up_more = gather_more(after(upstream_low, attended), own_up_first, S)
    come, far[2], near_far[0], own_up_more = tie(come, far[2], near_far[0], own_up_more)
    own_u = gather_end(upstream_low, own_up_first, own_up_more, S)
    near_far.append(near_swap(far[1], come))
    down = [near_swap(down_rows[0], come)]
    partner_up_first = gather_first(after(partner_up, come), S)
    come = relative(come, s).transpose(1, 0, 2).reshape(T, D)
    residual = inputs + matmul(come[:, : D // 2], out_even) + matmul(come[:, D // 2 :], out_odd)
    moe_factor = rms_factor(residual)
    residual_n = residual * moe_factor
    second_low = (residual_n * gain_moe).astype(BF16)
    second_low, down[0], near_far[1], partner_up_first, own_u = tie(
        second_low, down[0], near_far[1], partner_up_first, own_u
    )

    own_first = gather_first(second_low, S)
    partner_low = [far_swap(second_low[:half_rows])]
    near_far.append(near_swap(far[2], second_low))
    rank_part = after(small, second_low)[:, :, part * (E + 4) :].reshape(S, F, E, T)

    def ranks_of(index):
        ranks = lax.dynamic_slice(rank_part, (0, index, s * experts, 0), (S, 1, experts, T))
        ranks = relative(ranks[:, 0], s).astype(jnp.int32)
        return ranks[: S // 2], ranks[S // 2 :]

    own_ranks, other_ranks = ranks_of(f), ranks_of(f ^ half_f)
    own_first, partner_low[0], near_far[2], own_ranks, other_ranks = tie(
        own_first, partner_low[0], near_far[2], own_ranks, other_ranks
    )
    own_more = gather_more(second_low, own_first, S)
    partner_low.append(far_swap(second_low[half_rows:], own_first))
    down.append(near_swap(down_rows[1], own_first))
    partner_up_more = gather_more(after(partner_up, own_first), partner_up_first, S)
    own_more, partner_low[1], down[1], partner_up_more = tie(
        own_more, partner_low[1], down[1], partner_up_more
    )
    partner_low = jnp.concatenate(partner_low, 0)
    own_x = gather_end(second_low, own_first, own_more, S)
    partner_first = gather_first(after(partner_low, own_more), S)
    down.append(near_swap(down_rows[2], own_more))
    far.append(far_part(3, own_more))
    partner_first, down[2], own_x, far[3] = tie(partner_first, down[2], own_x, far[3])
    other_u = gather_end(after(partner_up, partner_first), partner_up_first, partner_up_more, S)
    partner_more = gather_more(partner_low, partner_first, S)
    down.append(near_swap(down_rows[3], partner_first))
    near_far.append(near_swap(far[3], partner_first))
    partner_more, down[3], other_u, near_far[3] = tie(partner_more, down[3], other_u, near_far[3])
    other_x = gather_end(partner_low, partner_first, partner_more, S)
    in_pieces = []
    for r in range(F):
        for n, rows in enumerate(near_own if r < half_f else near_far):
            first = (0, 2, 3)[n] if r < half_f else n
            in_pieces.append((r, first * quarter, rows[r % half_f]))
    down_pieces = [
        (r, n * (down_part // 4), down[n][r]) for r in range(half_f) for n in range(4)
    ]
    wide_router = jnp.pad(full_router, ((0, 0), (0, 128 - E)))
    expert_places = jnp.stack([s * experts, f]).astype(jnp.int32)
    parts = (in_part, down_part)
    own_parts = run_experts(
        own_x, own_u, own_ranks, in_pieces, down_pieces, wide_router, expert_places, 0, (), parts
    )
    own_parts, other_x = tie(own_parts, other_x)
    own_got = swap(own_parts[3], "seq", S, 1)
    own_out_got = swap(own_parts[1], "seq", S, 1)
    other_parts = run_experts(
        other_x,
        other_u,
        other_ranks,
        in_pieces,
        down_pieces,
        wide_router,
        expert_places,
        1,
        own_parts[6:],
        parts,
    )
    other_parts, own_got, own_out_got = tie(other_parts, own_got, own_out_got)
    logits = matmul(second_low, full_router)
    router_probs = jax.nn.softmax(logits, axis=-1)

    x_rows, u_rows, in_grads, hidden_gate = other_parts[6:]
    in_terms, down_terms = {}, {}

    def in_products(r, *dep):
        in_terms[r] = products(
            x_rows, after(in_grads, dep), in_part, r, F, f_at, "in_products"
        )

    odd = [r for r in range(F) if r & 1]
    far_odd = [r for r in odd if r & half_f]
    near_odd = [r for r in odd if not r & half_f]

    def to_home(even, odd):
        return absolute(jnp.concatenate([even, odd], 0).transpose(0, 2, 1), s)

    gate_grads = jnp.stack(
        [to_home(own_parts[4], own_parts[5]), to_home(other_parts[4], other_parts[5])], 1
    ).reshape(S, -1)
    other_got = swap(other_parts[3], "seq", S, 1)
    gate_grads = lax.all_to_all(gate_grads, "seq", split_axis=0, concat_axis=0, tiled=True)
    other_got, gate_grads = tie(other_got, gate_grads)
    for r in far_odd:
        in_products(r, other_got)

    def send_in(n, *dep):
        return {r: swap(after(sent[r][n], dep), "fsdp", F, 1) for r in sent}

    other_sums = sum_cores(other_parts[2], other_got, S)
    come = sum_first(other_sums, S)
    other_out_got = swap(after(other_parts[1], other_got), "seq", S, 1)
    gate_grads = gate_grads.reshape(S, 2, T * experts)
    partner_grads = far_swap(gate_grads[:, 1])
    come, in_terms, other_out_got, partner_grads = tie(
        come, in_terms, other_out_got, partner_grads
    )
    sent = {r: quarters(in_terms[r], 1) for r in far_odd}
    singles, other_total = sum_more(other_sums, come, S)
    come = sum_last(singles, S)
    start_got = {r: swap(in_terms[r][:, : 2 * quarter], "fsdp", F, 1) for r in far_odd}

    def down_products(r, dep):
        down_terms[r] = products(
            after(hidden_gate, dep), u_rows, down_part, r, half_f, f_at, "down_products"
        )

    for r in range(1, half_f, 2):
        down_products(r, singles)
    come, start_got, down_terms = tie(come, start_got, down_terms)
    far_got = [
        {r: got[:, n * quarter : (n + 1) * quarter] for r, got in start_got.items()}
        for n in range(2)
    ]
    other_rows = add_all(other_total, come).astype(BF16)
    gate_grads = gate_grads[:, 0] + partner_grads
    gate_grads = gate_grads.reshape(S, T, experts).transpose(1, 0, 2).reshape(T, E)
    back = [far_swap(other_rows[:half_rows])]
    own_sums = sum_cores(own_parts[2], after(own_got, other_rows), S)
    come = sum_first(own_sums, S)
    far_got.append(send_in(2, other_rows))
    for r in far_odd:
        in_products(r ^ 1, other_rows)
    come, back[0], far_got[2], in_terms = tie(come, back[0], far_got[2], in_terms)
    back.append(far_swap(other_rows[half_rows:], come))
    singles, own_total = sum_more(own_sums, come, S)
    come = sum_last(singles, S)
    down_sent = {r: quarters(down_terms[r], 1) for r in range(1, half_f, 2)}
    for r in down_sent:
        down_sent[r] = down_sent[r][:2] + [jnp.concatenate(down_sent[r][2:], 1)]

    def send_down(n, *dep):
        return {r: swap(after(down_sent[r][n], dep), "fsdp", F, 1) for r in down_sent}

    far_got.append(send_in(3, singles))
    for r in near_odd:
        in_products(r, singles)
    come, back[1], far_got[3], in_terms = tie(come, back[1], far_got[3], in_terms)
    row_grads = add_all(own_total, come) + jnp.concatenate(back, 0).astype(F32)

    upstream = upstream_low.astype(F32)
    logit_grads = router_probs * (
        gate_grads - jnp.sum(router_probs * gate_grads, axis=-1, keepdims=True)
    )
    router_wide = full_router.astype(F32)
    second_grads = row_grads + jnp.dot(logit_grads, router_wide.T, precision=HIGHEST)
    pulled = second_grads * gain_moe
    residual_grads = upstream + moe_factor * (
        pulled - residual_n * jnp.mean(pulled * residual_n, axis=-1, keepdims=True)
    )
    branch_low = residual_grads.astype(BF16)

    def sum_near(terms):
        mask = 2
        while mask < half_f:
            terms = {
                r: terms[r] + swap(terms[r | mask].astype(BF16), "fsdp", F, mask).astype(F32)
                for r in terms
                if not r & mask
            }
            mask *= 2
        (total,) = terms.values()
        return total

    def far_sum(n, *dep):
        terms = {
            r ^ 1: quarters(in_terms[r ^ 1], 1)[n].astype(F32) + far_got[n][r].astype(F32)
            for r in far_odd
        }
        return far_swap(sum_near(terms).astype(BF16), *dep)

    branch_first = gather_first(branch_low, S)
    far_sums = [far_sum(0, branch_low)]
    down_got = [send_down(0, branch_low)]
    for r in range(0, half_f, 2):
        down_products(r, branch_low)
    branch_first, far_sums[0], down_got[0], down_terms = tie(
        branch_first, far_sums[0], down_got[0], down_terms
    )
    branch_more = gather_more(branch_low, branch_first, S)
    far_sums.append(far_sum(1, branch_first))
    down_got.append(send_down(1, branch_first))
    branch_even, branch_odd = gather_end(branch_low, branch_first, branch_more, S)

    head_grads = jnp.concatenate(
        [matmul_t(branch_even, own_output), matmul_t(branch_odd, own_output)], 0
    ).astype(BF16)
    head_grads = absolute(head_grads.reshape(S, T, C), s).reshape(L, C)
    head_grads, far_sums[1], down_got[1] = tie(head_grads, far_sums[1], down_got[1])
    far_sums.append(far_sum(2, head_grads))
    down_got.append(send_down(2, head_grads))
    other_out_sums = sum_cores(other_parts[0], after(other_out_got, head_grads), S)
    come, head_grads = sum_first(other_out_sums, S, head_grads)
    query_back, key_back, value_back = attention_backward(
        query_low, key_low, value_low, head_grads, lse, seg_row, seg_col
    )
    query_back, key_back, value_back, far_sums[2], down_got[2], come = tie(
        query_back, key_back, value_back, far_sums[2], down_got[2], come
    )

    singles, other_total = sum_more(other_out_sums, come, S)
    come = sum_last(singles, S)
    far_sums.append(far_sum(3, query_back))
    attended_rel = relative(after(attended_blocks, singles), s).reshape(2, L // 2, C)
    output_term = t_matmul(attended_rel[0], branch_even) + t_matmul(attended_rel[1], branch_odd)
    output_term = by_index(output_term.astype(BF16).reshape(F, part, D), f, F)
    output_got = swap(output_term[: F // 2], "fsdp", F, 1)
    value_rel = relative(value_back.reshape(S, T, C), s).reshape(2, L // 2, C)

    def weight_term(even, odd):
        term = (t_matmul(normed_even, even) + t_matmul(normed_odd, odd)).astype(BF16)
        return by_index(term.reshape(S, F, part, -1).transpose(1, 0, 2, 3), f, F)

    means, gain_term = rope_means(
        query_back, key_back, query_pre, key_pre, squares, head_gain, cosine, sine
    )
    means = sum_all(means, "seq", S)
    value_term = weight_term(value_rel[0], value_rel[1])
    means, come, far_sums[3], output_got, value_term = tie(
        means, come, far_sums[3], output_got, value_term
    )
    other_outs = add_all(other_total, come).astype(BF16)
    outs_back = [far_swap(other_outs[:half_rows])]
    value_got = swap(value_term[: F // 2], "fsdp", F, 1)
    pre_rel = rope_back(
        (query_back, key_back, value_back),
        query_pre,
        key_pre,
        squares,
        means,
        head_gain,
        cosine,
        sine,
        me,
        T,
    ).reshape(2, L // 2, 3 * C)
    normed_got = swap(matmul_t(pre_rel[1], w_qkv).astype(BF16), "seq", S, 1)
    normed_kept = matmul_t(pre_rel[0], w_qkv).astype(BF16)
    normed_got, normed_kept, value_got, outs_back[0] = tie(
        normed_got, normed_kept, value_got, outs_back[0]
    )

    normed_sums = sum_cores(normed_kept, normed_got, S)
    come = sum_first(normed_sums, S)
    value_sum = sum_rest(sum_even(value_term, value_got, F), F)
    turned_term = weight_term(
        after(pre_rel[0][:, : 2 * C], normed_got), after(pre_rel[1][:, : 2 * C], normed_got)
    )
    late_grads, late_logits = after(second_grads, normed_got), after(logit_grads, normed_got)
    router_term = jnp.dot(second_low.astype(F32).T, late_logits, precision=HIGHEST)
    moe_gain_term = jnp.sum(late_grads * residual_n, axis=0)
    gain_terms = jnp.concatenate(
        [router_term.reshape(S * F, part * E), moe_gain_term.reshape(S * F, part)], 1
    )
    gain_terms = in_relative(gain_terms, S, F, s, f).reshape(S, F, -1)
    head_terms = gain_term.reshape(2, F, part).transpose(1, 0, 2).reshape(F, 2 * part)
    head_terms = in_relative(head_terms, 1, F, 0, f)
    gain_terms = jnp.concatenate([gain_terms.transpose(1, 0, 2).reshape(F, -1), head_terms], 1)
    own_out_sums = sum_cores(own_parts[0], after(own_out_got, normed_got), S)
    own_come = sum_first(own_out_sums, S)
    come, turned_term, value_sum, gain_terms, own_come = tie(
        come, turned_term, value_sum, gain_terms, own_come
    )
    turned_got = swap(turned_term[: F // 2], "fsdp", F, 1)
    singles, normed_total = sum_more(normed_sums, come, S)
    come = sum_last(singles, S)
    gain_got = swap(gain_terms[F // 2 :], "fsdp", F, half_f)
    for r in near_odd:
        in_products(r ^ 1, turned_term)
    come, turned_got, gain_got, in_terms = tie(come, turned_got, gain_got, in_terms)
    gain_terms = gain_terms[: F // 2] + gain_got
    normed_grads = add_all(normed_total, come)
    turned_sum = sum_rest(sum_even(turned_term, turned_got, F), F)
    middle = in_part // 2

    def send_near(first, dep):
        return {
            r: swap(after(in_terms[r][:, first : first + middle], dep), "fsdp", F, 1)
            for r in near_odd
        }

    near_got = [send_near(0, turned_got)]
    gain_terms = halve(after(gain_terms, turned_got), "fsdp", F, half_f // 2)
    singles, own_total = sum_more(after(own_out_sums, turned_got), own_come, S)
    own_come = sum_last(singles, S)
    turned_sum, own_come, near_got[0], gain_terms = tie(
        turned_sum, own_come, near_got[0], gain_terms
    )
    near_got.append(send_near(middle, turned_sum))
    outs_back.append(far_swap(other_outs[half_rows:], turned_sum))
    count = S * part * (E + 1)
    head_terms = gain_terms[0, count:]
    gain_terms = halve(gain_terms[0, :count].reshape(S, -1), "seq", S, S // 2)[0]
    own_outs = add_all(own_total, own_come)
    qkv_term = jnp.concatenate([turned_sum, value_sum], -1).astype(BF16)
    qkv_term = lax.all_to_all(qkv_term, "seq", split_axis=0, concat_axis=0, tiled=True)
    qkv_term, outs_back[1], near_got[1], gain_terms = tie(
        qkv_term, outs_back[1], near_got[1], gain_terms
    )
    outs_back = jnp.concatenate(outs_back, 0).astype(F32)
    mixed = (residual + own_outs + outs_back).astype(BF16)[None]
    qkv_term = [
        qkv_term[:, :, j * C : (j + 1) * C].transpose(1, 0, 2).reshape(part, D).astype(F32)
        for j in range(3)
    ]
    grad_output = sum_rest(sum_even(output_term, output_got, F), F)

    near_got = {r: jnp.concatenate([got[r] for got in near_got], 1) for r in near_odd}
    own_term = sum_near(
        {r ^ 1: in_terms[r ^ 1].astype(F32) + near_got[r].astype(F32) for r in near_odd}
    )
    far_term = jnp.concatenate(far_sums, 1).astype(F32)
    first_half = half_at == 0
    lower = jnp.where(first_half, own_term, far_term)
    upper = jnp.where(first_half, far_term, own_term)
    grad_gate, grad_up = (
        jnp.concatenate([lower[..., at], upper[..., at]], axis=-1)
        for at in (slice(0, hidden_half), slice(hidden_half, 2 * hidden_half))
    )
    down_got = after(down_got, turned_sum)
    down_got = {r: jnp.concatenate([got[r] for got in down_got], 1) for r in down_sent}
    grad_down = sum_near(
        {r ^ 1: down_terms[r ^ 1].astype(F32) + down_got[r].astype(F32) for r in down_sent}
    )

    attn_factor = rms_factor(inputs)
    inputs_n = inputs * attn_factor
    attn_pulled = normed_grads * gain_attn
    grad_tokens = residual_grads + attn_factor * (
        attn_pulled - inputs_n * jnp.mean(attn_pulled * inputs_n, axis=-1, keepdims=True)
    )
    grad_attn_gain = sum(
        jnp.sum(term * weight.astype(F32), axis=1)
        for term, weight in zip(qkv_term, (w_query, w_key, w_value))
    ) / attn_gain.astype(F32)
    return (
        mixed,
        grad_tokens[None],
        qkv_term[0],
        qkv_term[1],
        qkv_term[2],
        grad_output,
        gain_terms[: part * E].reshape(part, E),
        grad_attn_gain,
        gain_terms[part * E :],
        head_terms[:part],
        head_terms[part:],
        grad_gate,
        grad_up,
        grad_down,
    )


def solution(mesh):
    tokens_spec = P("fsdp", "seq", None)
    rows_spec = P(("seq", "fsdp"), None)
    gain_spec = P(("seq", "fsdp"))
    expert_spec = P("seq", "fsdp", None)
    in_specs = (
        (tokens_spec, P("fsdp", None), tokens_spec, tokens_spec)
        + (rows_spec,) * 5
        + (gain_spec,) * 4
        + (expert_spec,) * 3
    )
    out_specs = (tokens_spec,) * 2 + (rows_spec,) * 5 + (gain_spec,) * 4 + (expert_spec,) * 3
    return jax.shard_map(
        partial(per_device, mesh.shape["seq"], mesh.shape["fsdp"]),
        mesh=mesh,
        in_specs=in_specs,
        out_specs=out_specs,
        check_vma=False,
    )
```

```python
from functools import partial

import jax
import jax.numpy as jnp
from jax import lax
from jax.experimental import pallas as pl
from jax.experimental.pallas import tpu as pltpu
from jax.sharding import PartitionSpec as P

D = 2048
H = 16
DH = 128
E = 16
WINDOW = 1024
CAP = 144

EPSILON = 1e-06
ROPE_BASE = 50000.0
HIGHEST = lax.Precision.HIGHEST
BF16 = jnp.bfloat16
F32 = jnp.float32
MIB = 1024 * 1024


def matmul(left, right):
    return jnp.dot(left, right, preferred_element_type=F32)


def matmul_t(left, right):
    return lax.dot_general(left, right, (((1,), (1,)), ((), ())), preferred_element_type=F32)


def t_matmul(left, right):
    return lax.dot_general(left, right, (((0,), (0,)), ((), ())), preferred_element_type=F32)


def rms_factor(values):
    return lax.rsqrt(jnp.mean(values * values, axis=-1, keepdims=True) + EPSILON)


def swap(values, axis, size, mask):
    return lax.ppermute(values, axis, [(i, i ^ mask) for i in range(size)])


def high_bit(number):
    return 1 << (number.bit_length() - 1)


def low_bit(number):
    return number & -number


def after(values, *others):
    return lax.optimization_barrier((values, others))[0]


def tie(*values):
    return lax.optimization_barrier(values)


def gather_first(values, size):
    return {r: swap(values, "seq", size, r) for r in range(2, size, 2) if r == low_bit(r)}


def gather_more(values, first, size):
    rows = values.shape[0] // 2
    pieces = dict(first)
    for r in range(2, size, 2):
        if r not in pieces:
            up, down = high_bit(r), low_bit(r)
            upper, lower = pieces[r ^ up], pieces[r ^ down]
            upper = upper[0] if isinstance(upper, tuple) else upper[:rows]
            lower = lower[1] if isinstance(lower, tuple) else lower[rows:]
            pieces[r] = (swap(upper, "seq", size, up), swap(lower, "seq", size, down))
    return {r: piece for r, piece in pieces.items() if r not in first}


def gather_end(values, first, more, size):
    blocks = [values]
    for r in range(2, size, 2):
        blocks.extend([first[r]] if r in first else more[r])
    even = jnp.concatenate(blocks, 0)
    return even, swap(even, "seq", size, 1)


def relative(blocks, me):
    size = blocks.shape[0]
    order = list(range(0, size, 2)) + list(range(1, size, 2))
    return jnp.concatenate([lax.dynamic_slice_in_dim(blocks, me ^ r, 1, 0) for r in order], 0)


def absolute(blocks, me):
    size = blocks.shape[0]
    places = [((me ^ j) // 2) + ((me ^ j) % 2) * (size // 2) for j in range(size)]
    return jnp.concatenate([lax.dynamic_slice_in_dim(blocks, at, 1, 0) for at in places], 0)


def sum_cores(even, got, size):
    rows = even.shape[0] // (size // 2)
    half = rows // 2

    def part(r, first):
        at = slice(r // 2 * rows + first, r // 2 * rows + first + half)
        return even[at].astype(F32) + got[at].astype(F32)

    return {r: [part(r, 0), part(r, half)] for r in range(0, size, 2)}


def sum_first(sums, size, held=None):
    sums = {r: list(value) for r, value in sums.items()}
    come = {}
    for r in range(size - 2, 0, -2):
        if r != low_bit(r):
            up, down = high_bit(r), low_bit(r)
            for (goal, k, _), piece in come.items():
                if goal == r:
                    sums[r][k] += piece.astype(F32)
            upper, lower, held = tie(sums[r][0].astype(BF16), sums[r][1].astype(BF16), held)
            come[r ^ up, 0, r] = swap(upper, "seq", size, up)
            come[r ^ down, 1, r] = swap(lower, "seq", size, down)
    return come if held is None else (come, held)


def sum_more(sums, come, size):
    sums = {r: list(value) for r, value in sums.items() if r == 0 or r == low_bit(r)}
    for (goal, k, _), piece in come.items():
        if goal in sums:
            sums[goal][k] += piece.astype(F32)
    singles = {
        r: jnp.concatenate([v.astype(BF16) for v in value], 0) for r, value in sums.items() if r
    }
    return tie(singles)[0], jnp.concatenate(sums[0], 0)


def sum_last(singles, size):
    return {r: swap(value, "seq", size, r) for r, value in singles.items()}


def add_all(total, pieces):
    for piece in pieces.values():
        total += piece.astype(F32)
    return total


def quarters(values, axis):
    step = values.shape[axis] // 4
    return [lax.slice_in_dim(values, k * step, (k + 1) * step, axis=axis) for k in range(4)]


def sum_all(values, axis, size):
    mask = 1
    while mask < size:
        values = values + swap(values, axis, size, mask)
        mask *= 2
    return values


def fsdp_pieces(values, size):
    pieces = {0: values}
    for r in range(1, size):
        low = low_bit(r)
        pieces[r] = swap(pieces[r ^ low], "fsdp", size, low)
    return pieces


def place_fsdp(pieces, me, axis):
    size = len(pieces)
    shape = pieces[0].shape
    whole = jnp.zeros(shape[:axis] + (size,) + shape[axis:], pieces[0].dtype)
    for r, piece in pieces.items():
        whole = lax.dynamic_update_slice_in_dim(whole, jnp.expand_dims(piece, axis), me ^ r, axis)
    return whole


def near_pieces(values, size):
    pieces = {0: values}
    for r in range(1, size // 2):
        up = high_bit(r)
        pieces[r] = swap(pieces[r ^ up], "fsdp", size, up)
    return pieces


def double(values, axis, size):
    mask = 1
    while mask < size:
        values = jnp.concatenate([values, swap(values, axis, size, mask)], 0)
        mask *= 2
    return values


def halve(values, axis, size, mask):
    while mask:
        half = values.shape[0] // 2
        values = values[:half] + swap(values[half:], axis, size, mask)
        mask //= 2
    return values


def relative_pick(seq_size, fsdp_size, s, f):
    index = jnp.arange(seq_size * fsdp_size, dtype=jnp.int32)
    source = ((index // fsdp_size) ^ s) * fsdp_size + ((index % fsdp_size) ^ f)
    return source[:, None] == index[None, :]


def in_order(values, seq_size, fsdp_size, s, f):
    pick = relative_pick(seq_size, fsdp_size, s, f).astype(values.dtype)
    return matmul(pick, values).astype(values.dtype)


def in_relative(values, seq_size, fsdp_size, s, f):
    pick = relative_pick(seq_size, fsdp_size, s, f).astype(F32)
    return jnp.dot(pick, values, precision=HIGHEST)


def by_index(partial_sum, me, size):
    order = [r for r in range(size) if r & 1] + [r for r in range(size) if not r & 1]
    return jnp.concatenate([lax.dynamic_slice_in_dim(partial_sum, me ^ r, 1, 0) for r in order], 0)


def sum_even(stacked, got, size):
    return (stacked[size // 2 :].astype(F32) + got.astype(F32)).astype(BF16)


def sum_rest(stacked, size):
    mask = 2
    values = stacked.astype(F32)
    while mask < size:
        count = values.shape[0] // 2
        pairs = values.reshape((count, 2) + values.shape[1:])
        got = swap(pairs[:, 1].astype(BF16), "fsdp", size, mask)
        values = pairs[:, 0] + got.astype(F32)
        mask *= 2
    return values[0]


def allowed_keys(seg_row, seg_col, first_query, first_key, rows, span, half_window):
    query_at = first_query + lax.broadcasted_iota(jnp.int32, (span, rows), 1)
    key_at = first_key + lax.broadcasted_iota(jnp.int32, (span, rows), 0)
    return (jnp.abs(query_at - key_at) <= half_window) & (seg_col == seg_row)


def first_key_of(block, rows, span, length):
    start = jnp.clip(block * rows - (span - rows) // 2, 0, length - span)
    return pl.multiple_of(start, rows)


def forward_kernel(span, q_ref, k_ref, v_ref, seg_row_ref, seg_col_ref, o_ref, lse_ref):
    block = pl.program_id(1)
    rows, length = q_ref.shape[0], k_ref.shape[0]
    first_key = first_key_of(block, rows, span, length)
    keys = k_ref[pl.ds(first_key, span), :]
    values = v_ref[pl.ds(first_key, span), :]
    scores = matmul_t(keys, q_ref[...]) * DH ** (-0.5)
    allowed = allowed_keys(
        seg_row_ref[...],
        seg_col_ref[pl.ds(first_key, span), :],
        block * rows,
        first_key,
        rows,
        span,
        WINDOW // 2,
    )
    scores = jnp.where(allowed, scores, -1e30)
    peak = jnp.max(scores, axis=0, keepdims=True)
    expos = jnp.exp(scores - peak)
    totals = jnp.sum(expos, axis=0, keepdims=True)
    probs = (expos * (1.0 / totals)).astype(BF16)
    o_ref[...] = t_matmul(values, probs).T.astype(BF16)
    lse_ref[...] = (peak + jnp.log(totals))[None]


def backward_kernel(
    span,
    q_ref,
    k_ref,
    v_ref,
    do_ref,
    lse_ref,
    seg_row_ref,
    seg_col_ref,
    dq_ref,
    dk_ref,
    dv_ref,
    dk_sum,
    dv_sum,
):
    block = pl.program_id(1)
    rows, length = q_ref.shape[0], k_ref.shape[0]

    @pl.when(block == 0)
    def _():
        dk_sum[...] = jnp.zeros_like(dk_sum)
        dv_sum[...] = jnp.zeros_like(dv_sum)

    first_key = first_key_of(block, rows, span, length)
    at = pl.ds(first_key, span)
    keys = k_ref[at, :]
    values = v_ref[at, :]
    queries = q_ref[...]
    grads = do_ref[...]
    scores = matmul_t(keys, queries) * DH ** (-0.5)
    allowed = allowed_keys(
        seg_row_ref[...],
        seg_col_ref[at, :],
        block * rows,
        first_key,
        rows,
        span,
        WINDOW // 2,
    )
    probs = jnp.where(allowed, jnp.exp(scores - lse_ref[0]), 0.0)
    dv_sum[at, :] += matmul(probs.astype(BF16), grads)
    prob_grads = matmul_t(values, grads)
    center = jnp.sum(probs * prob_grads, axis=0, keepdims=True)
    score_grads = (probs * (prob_grads - center)).astype(BF16)
    dk_sum[at, :] += matmul(score_grads, queries)
    dq_ref[...] = (t_matmul(keys, score_grads) * DH ** (-0.5)).T.astype(BF16)

    @pl.when(block == length // rows - 1)
    def _():
        dk_ref[...] = (dk_sum[...] * DH ** (-0.5)).astype(BF16)
        dv_ref[...] = dv_sum[...].astype(BF16)


def attention_sizes(length):
    rows = 256
    return rows, min(length, rows + WINDOW)


def attention_forward(queries, keys, values, seg_row, seg_col):
    length, columns = queries.shape
    heads = columns // DH
    rows, span = attention_sizes(length)
    block = pl.BlockSpec((rows, DH), lambda h, i: (i, h))
    whole = pl.BlockSpec((length, DH), lambda h, i: (0, h))
    return pl.pallas_call(
        partial(forward_kernel, span),
        grid=(heads, length // rows),
        in_specs=[
            block,
            whole,
            whole,
            pl.BlockSpec((1, rows), lambda h, i: (0, i)),
            pl.BlockSpec((length, 1), lambda h, i: (0, 0)),
        ],
        out_specs=[block, pl.BlockSpec((1, 1, rows), lambda h, i: (h, 0, i))],
        out_shape=[
            jax.ShapeDtypeStruct((length, columns), BF16),
            jax.ShapeDtypeStruct((heads, 1, length), F32),
        ],
        compiler_params=pltpu.CompilerParams(vmem_limit_bytes=48 * MIB),
        cost_estimate=pl.CostEstimate(
            flops=4 * heads * length * span * DH,
            bytes_accessed=8 * length * columns,
            transcendentals=heads * length * span,
        ),
        name="attend",
    )(queries, keys, values, seg_row, seg_col)


def attention_backward(queries, keys, values, grads, lse, seg_row, seg_col):
    length, columns = queries.shape
    heads = columns // DH
    rows, span = attention_sizes(length)
    block = pl.BlockSpec((rows, DH), lambda h, i: (i, h))
    whole = pl.BlockSpec((length, DH), lambda h, i: (0, h))
    shape = jax.ShapeDtypeStruct((length, columns), BF16)
    return pl.pallas_call(
        partial(backward_kernel, span),
        grid=(heads, length // rows),
        in_specs=[
            block,
            whole,
            whole,
            block,
            pl.BlockSpec((1, 1, rows), lambda h, i: (h, 0, i)),
            pl.BlockSpec((1, rows), lambda h, i: (0, i)),
            pl.BlockSpec((length, 1), lambda h, i: (0, 0)),
        ],
        out_specs=[block, whole, whole],
        out_shape=[shape, shape, shape],
        scratch_shapes=[pltpu.VMEM((length, DH), F32), pltpu.VMEM((length, DH), F32)],
        compiler_params=pltpu.CompilerParams(vmem_limit_bytes=48 * MIB),
        cost_estimate=pl.CostEstimate(
            flops=10 * heads * length * span * DH,
            bytes_accessed=14 * length * columns,
            transcendentals=heads * length * span,
        ),
        name="attend_back",
    )(queries, keys, values, grads, lse, seg_row, seg_col)


def qkv_kernel(
    me_ref,
    even_ref,
    odd_ref,
    weight_ref,
    gain_ref,
    normed_even_ref,
    normed_odd_ref,
    q_ref,
    k_ref,
    v_ref,
    square_ref,
):
    turned = me_ref[0] % 2
    rows = even_ref.shape[0]
    columns = q_ref.shape[1]
    for k, (token_ref, normed_ref) in enumerate(
        ((even_ref, normed_even_ref), (odd_ref, normed_odd_ref))
    ):
        at = pl.ds(pl.multiple_of((turned ^ k) * rows, rows), rows)
        wide = token_ref[...].astype(F32)
        normed = (wide * rms_factor(wide) * gain_ref[...]).astype(BF16)
        normed_ref[...] = normed
        pre = matmul(normed, weight_ref[...])
        q_ref[at, :] = pre[:, :columns]
        k_ref[at, :] = pre[:, columns : 2 * columns]
        v_ref[at, :] = pre[:, 2 * columns :].astype(BF16)
        for j in range(2):
            squares = 0.0
            for c in range(j * columns, (j + 1) * columns, DH):
                squares += pre[:, c : c + DH] * pre[:, c : c + DH]
            square_ref[j : j + 1, at] = jnp.sum(squares.T, axis=0, keepdims=True)


def project(even, odd, weight, gain, me, rows):
    pairs = even.shape[0] // rows
    length = 2 * even.shape[0]
    depth, columns = weight.shape[0], weight.shape[1] // 3
    token = pl.BlockSpec((rows, depth), lambda i, me: (i, 0))

    def placed(shape):
        return pl.BlockSpec(shape, lambda i, me: (i ^ (me[0] // 2), 0))

    head = jax.ShapeDtypeStruct((length, columns), F32)
    return pl.pallas_call(
        qkv_kernel,
        grid_spec=pltpu.PrefetchScalarGridSpec(
            num_scalar_prefetch=1,
            grid=(pairs,),
            in_specs=[
                token,
                token,
                pl.BlockSpec(weight.shape, lambda i, me: (0, 0)),
                pl.BlockSpec((1, depth), lambda i, me: (0, 0)),
            ],
            out_specs=[
                token,
                token,
                placed((2 * rows, columns)),
                placed((2 * rows, columns)),
                placed((2 * rows, columns)),
                pl.BlockSpec((2, 2 * rows), lambda i, me: (0, i ^ (me[0] // 2))),
            ],
        ),
        out_shape=[
            jax.ShapeDtypeStruct((length // 2, depth), BF16),
            jax.ShapeDtypeStruct((length // 2, depth), BF16),
            head,
            head,
            jax.ShapeDtypeStruct((length, columns), BF16),
            jax.ShapeDtypeStruct((2, length), F32),
        ],
        compiler_params=pltpu.CompilerParams(vmem_limit_bytes=48 * MIB),
        cost_estimate=pl.CostEstimate(
            flops=6 * length * depth * columns,
            bytes_accessed=length * (4 * depth + 10 * columns) + 6 * depth * columns,
            transcendentals=length,
        ),
        name="project",
    )(me, even, odd, weight, gain)


def split_kernel(q_ref, k_ref, v_ref, out_ref):
    columns = q_ref.shape[1]
    for j, ref in enumerate((q_ref, k_ref, v_ref)):
        out_ref[0, :, j * columns : (j + 1) * columns] = ref[...]


def split_heads(w_query, w_key, w_value, parts):
    rows, columns = w_query.shape[0], w_query.shape[1] // parts
    block = pl.BlockSpec((rows, columns), lambda i: (0, i))
    return pl.pallas_call(
        split_kernel,
        grid=(parts,),
        in_specs=[block] * 3,
        out_specs=pl.BlockSpec((1, rows, 3 * columns), lambda i: (i, 0, 0)),
        out_shape=jax.ShapeDtypeStruct((parts, rows, 3 * columns), BF16),
        name="split_heads",
    )(w_query, w_key, w_value)


def spread(row, columns):
    return jnp.broadcast_to(row, (columns, row.shape[1])).T


def factor_of(square_row):
    return lax.rsqrt(square_row / D + EPSILON)


def turn(values, cosine, sine):
    return values * cosine + pltpu.roll(values, DH // 2, 1) * sine


def rope_kernel(q_ref, k_ref, square_ref, gain_ref, cos_ref, sin_ref, q_out, k_out):
    cosine, sine = cos_ref[...], sin_ref[...]
    for j, (pre_ref, out_ref) in enumerate(((q_ref, q_out), (k_ref, k_out))):
        factor = spread(factor_of(square_ref[j : j + 1, :]), DH)
        for c in range(0, pre_ref.shape[1], DH):
            at = slice(c, c + DH)
            normed = pre_ref[:, at] * factor * gain_ref[j : j + 1, at]
            out_ref[:, at] = turn(normed, cosine, sine).astype(BF16)


def rope(query_pre, key_pre, squares, gains, cosine, sine):
    length, columns = query_pre.shape
    rows = min(512, length)
    block = pl.BlockSpec((rows, columns), lambda i: (i, 0))
    table = pl.BlockSpec((rows, DH), lambda i: (i, 0))
    return pl.pallas_call(
        rope_kernel,
        grid=(length // rows,),
        in_specs=[
            block,
            block,
            pl.BlockSpec((2, rows), lambda i: (0, i)),
            pl.BlockSpec((2, columns), lambda i: (0, 0)),
            table,
            table,
        ],
        out_specs=[block, block],
        out_shape=[jax.ShapeDtypeStruct((length, columns), BF16)] * 2,
        compiler_params=pltpu.CompilerParams(vmem_limit_bytes=32 * MIB),
        name="rope",
    )(query_pre, key_pre, squares, gains, cosine, sine)


def pulled_of(grad_ref, pre_ref, factor, gain_ref, cosine, sine, j, at):
    turned = turn(grad_ref[:, at].astype(F32), cosine, -sine)
    return turned, turned * gain_ref[j : j + 1, at], pre_ref[:, at] * factor


def rope_mean_kernel(
    dq_ref, dk_ref, q_ref, k_ref, square_ref, gain_ref, cos_ref, sin_ref, mean_ref, term_ref
):
    @pl.when(pl.program_id(0) == 0)
    def _():
        term_ref[...] = jnp.zeros_like(term_ref)

    cosine, sine = cos_ref[...], sin_ref[...]
    for j, (grad_ref, pre_ref) in enumerate(((dq_ref, q_ref), (dk_ref, k_ref))):
        factor = spread(factor_of(square_ref[j : j + 1, :]), DH)
        total = 0.0
        for c in range(0, pre_ref.shape[1], DH):
            at = slice(c, c + DH)
            turned, pulled, normed = pulled_of(
                grad_ref, pre_ref, factor, gain_ref, cosine, sine, j, at
            )
            term_ref[j : j + 1, at] += jnp.sum(turned * normed, axis=0, keepdims=True)
            total += pulled * normed
        mean_ref[j : j + 1, :] = jnp.sum(total.T, axis=0, keepdims=True)


def rope_means(query_back, key_back, query_pre, key_pre, squares, gains, cosine, sine):
    length, columns = query_pre.shape
    rows = min(512, length)
    block = pl.BlockSpec((rows, columns), lambda i: (i, 0))
    table = pl.BlockSpec((rows, DH), lambda i: (i, 0))
    row = pl.BlockSpec((2, rows), lambda i: (0, i))
    fixed = pl.BlockSpec((2, columns), lambda i: (0, 0))
    return pl.pallas_call(
        rope_mean_kernel,
        grid=(length // rows,),
        in_specs=[block, block, block, block, row, fixed, table, table],
        out_specs=[row, fixed],
        out_shape=[
            jax.ShapeDtypeStruct((2, length), F32),
            jax.ShapeDtypeStruct((2, columns), F32),
        ],
        compiler_params=pltpu.CompilerParams(vmem_limit_bytes=32 * MIB),
        name="rope_means",
    )(query_back, key_back, query_pre, key_pre, squares, gains, cosine, sine)


def rope_back_kernel(
    me_ref,
    dq_ref,
    dk_ref,
    dv_ref,
    q_ref,
    k_ref,
    square_ref,
    mean_ref,
    gain_ref,
    cos_ref,
    sin_ref,
    out_ref,
):
    cosine, sine = cos_ref[...], sin_ref[...]
    columns = q_ref.shape[1]
    for j, (grad_ref, pre_ref) in enumerate(((dq_ref, q_ref), (dk_ref, k_ref))):
        factor = spread(factor_of(square_ref[j : j + 1, :]), DH)
        mean = spread(mean_ref[j : j + 1, :] / D, DH)
        for c in range(0, columns, DH):
            at = slice(c, c + DH)
            _, pulled, normed = pulled_of(grad_ref, pre_ref, factor, gain_ref, cosine, sine, j, at)
            out_ref[:, j * columns + c : j * columns + c + DH] = (
                factor * (pulled - normed * mean)
            ).astype(BF16)
    out_ref[:, 2 * columns :] = dv_ref[...]


def rope_back(grads, query_pre, key_pre, squares, means, gains, cosine, sine, me, rows):
    length, columns = query_pre.shape
    half = length // rows // 2

    def source(p, me):
        return me[0] ^ (p % half * 2 + p // half)

    block = pl.BlockSpec((rows, columns), lambda p, me: (source(p, me), 0))
    table = pl.BlockSpec((rows, DH), lambda p, me: (source(p, me), 0))
    row = pl.BlockSpec((2, rows), lambda p, me: (0, source(p, me)))
    return pl.pallas_call(
        rope_back_kernel,
        grid_spec=pltpu.PrefetchScalarGridSpec(
            num_scalar_prefetch=1,
            grid=(2 * half,),
            in_specs=[block] * 5
            + [row, row, pl.BlockSpec((2, columns), lambda p, me: (0, 0)), table, table],
            out_specs=pl.BlockSpec((rows, 3 * columns), lambda p, me: (p, 0)),
        ),
        out_shape=jax.ShapeDtypeStruct((length, 3 * columns), BF16),
        compiler_params=pltpu.CompilerParams(vmem_limit_bytes=32 * MIB),
        name="rope_back",
    )(me, *grads, query_pre, key_pre, squares, means, gains, cosine, sine)


def expert_kernel(
    in_places, down_places, first_ref, xa_ref, xb_ref, ua_ref, ub_ref, ra_ref, rb_ref, router_ref, *refs
):
    weight_refs = refs[: len(in_places) + len(down_places)]
    (ya_ref, yb_ref, za_ref, zb_ref, ga_ref, gb_ref, xc_ref, uc_ref, dg_ref, hid_ref) = refs[-13:-3]
    wi_ref, wd_ref, sems = refs[-3:]
    experts, _, hidden = hid_ref.shape
    rows = xa_ref.shape[0]

    @pl.when(pl.program_id(0) == 0)
    def _():
        copies = []
        for n, (ref, (r, first, part)) in enumerate(zip(weight_refs, in_places + down_places)):
            goal = wi_ref if n < len(in_places) else wd_ref
            place = lax.rem(first_ref[1] ^ r, goal.shape[1] // part)
            at = pl.ds(pl.multiple_of(place * part + first, ref.shape[1]), ref.shape[1])
            copies.append(pltpu.make_async_copy(ref, goal.at[:, at, :], sems.at[n]))
        for copy in copies:
            copy.start()
        for copy in copies:
            copy.wait()

    slot = lax.broadcasted_iota(jnp.int32, (CAP, rows), 0)
    blocks = (
        (xa_ref, ua_ref, ra_ref, ya_ref, za_ref, ga_ref),
        (xb_ref, ub_ref, rb_ref, yb_ref, zb_ref, gb_ref),
    )
    picks = []
    for k, (x_ref, u_ref, rank_ref, _, _, _) in enumerate(blocks):
        hits = jnp.concatenate([slot == rank_ref[0, e : e + 1, :] for e in range(experts)], 0)
        pick = hits.astype(F32).astype(BF16)
        picks.append(pick)
        x_rows = matmul(pick, x_ref[...]).astype(BF16)
        u_rows = matmul(pick, u_ref[...]).astype(BF16)
        for e in range(experts):
            xc_ref[e, k * CAP : (k + 1) * CAP, :] = x_rows[e * CAP : (e + 1) * CAP]
            uc_ref[e, k * CAP : (k + 1) * CAP, :] = u_rows[e * CAP : (e + 1) * CAP]
    outs, backs, gate_grads = [], [], []
    for e in range(experts):
        x_rows, u_rows = xc_ref[e], uc_ref[e]
        logits = matmul(x_rows, router_ref[...])
        lane = lax.broadcasted_iota(jnp.int32, logits.shape, 1)
        logits = jnp.where(lane < E, logits, -1e30)
        expos = jnp.exp(logits - jnp.max(logits, axis=-1, keepdims=True))
        own = jnp.sum(jnp.where(lane == first_ref[0] + e, expos, 0.0), axis=-1, keepdims=True)
        gate = own / jnp.sum(expos, axis=-1, keepdims=True)
        gated = matmul(x_rows, wi_ref[e, :, :hidden])
        upward = matmul(x_rows, wi_ref[e, :, hidden:])
        pulled = matmul_t(u_rows, wd_ref[e])
        sig = jax.nn.sigmoid(gated)
        silu = gated * sig
        acts = silu * upward
        gate_grads.append(jnp.sum(acts * pulled, axis=-1, keepdims=True))
        hidden_gate = (acts * gate).astype(BF16)
        hidden_grads = pulled * gate
        hid_ref[e] = hidden_gate
        dg_ref[e, :, :hidden] = (hidden_grads * upward * sig * (1.0 + gated * (1.0 - sig))).astype(BF16)
        dg_ref[e, :, hidden:] = (hidden_grads * silu).astype(BF16)
        outs.append(matmul(hidden_gate, wd_ref[e]).astype(BF16))
        backs.append(matmul_t(dg_ref[e], wi_ref[e]).astype(BF16))
    for k, (_, _, rank_ref, y_ref, z_ref, g_ref) in enumerate(blocks):
        at = slice(k * CAP, (k + 1) * CAP)
        y_ref[...] = t_matmul(picks[k], jnp.concatenate([v[at] for v in outs], 0)).astype(BF16)
        z_ref[...] = t_matmul(picks[k], jnp.concatenate([v[at] for v in backs], 0)).astype(BF16)
        for e in range(experts):
            hit = slot == rank_ref[0, e : e + 1, :]
            g_ref[0, e : e + 1, :] = jnp.sum(
                jnp.where(hit, gate_grads[e][at], 0.0), axis=0, keepdims=True
            )


def run_experts(x, u, ranks, in_pieces, down_pieces, router, places, which, compact, parts):
    experts, _, hidden = in_pieces[0][2].shape
    hidden = hidden // 2
    depth = x[0].shape[1]
    in_places = [(r, at, parts[0]) for r, at, _ in in_pieces]
    down_places = [(r, at, parts[1]) for r, at, _ in down_pieces]
    pieces = [array for _, _, array in in_pieces + down_pieces]
    rows = ranks[0].shape[2]
    steps = x[0].shape[0] // rows
    token = pl.BlockSpec((rows, depth), lambda i: (i, 0))
    rank = pl.BlockSpec((1, experts, rows), lambda i: (i, 0, 0))
    anywhere = pl.BlockSpec(memory_space=pl.ANY)

    def slots(columns):
        return pl.BlockSpec((experts, 2 * CAP, columns), lambda i: (0, i + which * steps, 0))

    shape = jax.ShapeDtypeStruct
    tokens = shape(x[0].shape, BF16)
    gates = shape((steps, experts, rows), F32)
    count = 4 * steps * CAP
    wide = shape((experts, count, depth), BF16)
    inputs = [places, *x, *u, *ranks, router, *pieces]
    return pl.pallas_call(
        partial(expert_kernel, in_places, down_places),
        grid=(steps,),
        in_specs=[pl.BlockSpec(memory_space=pltpu.SMEM)]
        + [token] * 4
        + [rank] * 2
        + [pl.BlockSpec(router.shape, lambda i: (0, 0), pipeline_mode=pl.Buffered(1))]
        + [anywhere] * (len(pieces) + len(compact)),
        out_specs=[token] * 4 + [rank] * 2 + [slots(depth)] * 2 + [slots(2 * hidden), slots(hidden)],
        out_shape=[tokens] * 4
        + [gates] * 2
        + [wide] * 2
        + [shape((experts, count, 2 * hidden), BF16), shape((experts, count, hidden), BF16)],
        scratch_shapes=[
            pltpu.VMEM((experts, depth, 2 * hidden), BF16),
            pltpu.VMEM((experts, hidden, depth), BF16),
            pltpu.SemaphoreType.DMA((len(pieces),)),
        ],
        input_output_aliases={len(inputs) + i: 6 + i for i in range(len(compact))},
        compiler_params=pltpu.CompilerParams(vmem_limit_bytes=60 * MIB),
        cost_estimate=pl.CostEstimate(
            flops=4 * steps * CAP * experts * depth * (7 * hidden + 2 * rows),
            bytes_accessed=60 * MIB,
            transcendentals=2 * steps * CAP * experts * hidden,
        ),
        name="experts",
    )(*inputs, *compact)


def product_kernel(me_ref, left_ref, right_ref, out_ref):
    out_ref[0] = t_matmul(left_ref[0], right_ref[0]).astype(BF16)


def products(left, right, part, r, count, me, name):
    experts, rows, _ = left.shape
    columns = right.shape[2]
    wide = min(columns, 1024)
    return pl.pallas_call(
        product_kernel,
        grid_spec=pltpu.PrefetchScalarGridSpec(
            num_scalar_prefetch=1,
            grid=(experts, columns // wide),
            in_specs=[
                pl.BlockSpec((1, rows, part), lambda e, j, me: (e, 0, lax.rem(me[0] ^ r, count))),
                pl.BlockSpec((1, rows, wide), lambda e, j, me: (e, 0, j)),
            ],
            out_specs=pl.BlockSpec((1, part, wide), lambda e, j, me: (e, 0, j)),
        ),
        out_shape=jax.ShapeDtypeStruct((experts, part, columns), BF16),
        compiler_params=pltpu.CompilerParams(vmem_limit_bytes=56 * MIB),
        cost_estimate=pl.CostEstimate(
            flops=2 * experts * rows * part * columns,
            bytes_accessed=2 * experts * rows * (part + columns),
            transcendentals=0,
        ),
        name=name,
    )(me, left, right)


def per_device(
    S,
    F,
    tokens,
    segments,
    routes,
    cotangent,
    w_query,
    w_key,
    w_value,
    w_output,
    router,
    attn_gain,
    moe_gain,
    query_gain,
    key_gain,
    w_gate,
    w_up,
    w_down,
):
    s = lax.axis_index("seq")
    f = lax.axis_index("fsdp")
    T = tokens.shape[1]
    L = S * T
    heads = H // S
    C = heads * DH
    experts = E // S
    part = w_query.shape[0]
    half_f = F // 2
    hidden_half = w_gate.shape[2] // 2

    me = s.reshape(1).astype(jnp.int32)
    f_at = f.reshape(1).astype(jnp.int32)
    half_at = f // half_f
    tokens_low = tokens[0]
    upstream_low = cotangent[0]
    inputs = tokens_low.astype(F32)
    half_rows = T // 2
    in_part, down_part = w_gate.shape[1], w_down.shape[1]
    quarter = in_part // 4

    def hidden_part(which, first, count):
        return jnp.concatenate(
            [
                lax.dynamic_slice(
                    weight, (0, first, which * hidden_half), (experts, count, hidden_half)
                )
                for weight in (w_gate, w_up)
            ],
            2,
        )

    def far_swap(values, *dep):
        return swap(after(values, dep), "fsdp", F, half_f)

    def near_swap(values, *dep):
        return near_pieces(after(values, dep), F)

    named = routes[0].T[None] == jnp.arange(E, dtype=jnp.int32)[:, None, None]
    chosen = jnp.any(named, axis=1)
    index = jnp.arange(T, dtype=jnp.int32)
    before = (index[:, None] <= index[None, :]).astype(BF16)
    ranks = jnp.where(chosen, matmul(chosen.astype(BF16), before) - 1.0, -1.0)
    small = jnp.concatenate(
        [
            router.reshape(-1),
            attn_gain,
            moe_gain,
            query_gain,
            key_gain,
            ranks.astype(BF16).reshape(-1),
        ]
    )[None]
    crossed = split_heads(w_query, w_key, w_value, S)
    small = double(after(small, crossed), "fsdp", F)
    crossed = lax.all_to_all(crossed, "seq", split_axis=0, concat_axis=0, tiled=True)
    near_own = [near_swap(hidden_part(half_at, 0, 2 * quarter), small)]
    out_dep = small
    small = double(small, "seq", S)
    out_far = far_swap(w_output, out_dep)
    crossed, near_own[0], small, out_far = tie(crossed, near_own[0], small, out_far)

    held = after((w_gate, w_up, w_down, upstream_low), crossed)

    def held_part(which, first, count):
        return jnp.concatenate(
            [
                lax.dynamic_slice(
                    weight, (0, first, which * hidden_half), (experts, count, hidden_half)
                )
                for weight in held[:2]
            ],
            2,
        )

    own_quarters = {n: held_part(half_at, n * quarter, quarter) for n in (2, 3)}
    far_quarters = [held_part(1 - half_at, n * quarter, quarter) for n in range(4)]
    down_rows = quarters(held[2], 1)
    upstream_halves = [held[3][:half_rows], held[3][half_rows:]]
    small = in_order(small, S, F, s, f).reshape(S, F, -1)
    prepared = (own_quarters, far_quarters, down_rows, upstream_halves, small)
    token_first = gather_first(after(tokens_low, crossed), S)
    qkv_pieces = {0: crossed}
    for r in range(1, F):
        low = low_bit(r)
        qkv_pieces[r] = swap(qkv_pieces[r ^ low], "fsdp", F, low)
        if r == half_f:
            qkv_pieces, token_first, prepared = tie(qkv_pieces, token_first, prepared)
            own_quarters, far_quarters, down_rows, upstream_halves, small = prepared
            partner_up = [far_swap(upstream_halves[0])]
    token_more = gather_more(tokens_low, token_first, S)
    qkv_pieces, partner_up[0], token_more = tie(qkv_pieces, partner_up[0], token_more)
    tokens_even, tokens_odd = gather_end(tokens_low, token_first, token_more, S)
    w_qkv = place_fsdp(qkv_pieces, f, 1).reshape(D, 3 * C)

    full_router = small[:, :, : part * E].reshape(D, E)
    gains = [
        small[:, :, part * (E + i) : part * (E + i + 1)].reshape(D).astype(F32) for i in range(4)
    ]
    gain_attn, gain_moe = gains[0], gains[1]
    head_gain = lax.dynamic_slice(jnp.stack(gains[2:], 0), (0, s * C), (2, C))
    places = jnp.arange(L, dtype=jnp.int32).astype(F32)
    freqs = ROPE_BASE ** (-(jnp.arange(DH // 2, dtype=F32) * 2.0 / DH))
    angles = places[:, None] * freqs[None, :]
    cosine, sine = jnp.cos(angles), jnp.sin(angles)
    cosine = jnp.concatenate([cosine, cosine], 1)
    sine = jnp.concatenate([-sine, sine], 1)

    def far_part(n, *dep):
        return far_swap(far_quarters[n], *dep)

    partner_up.append(far_swap(upstream_halves[1], w_qkv))
    out_pieces = {0: after(w_output, w_qkv), half_f: after(out_far, w_qkv)}
    for r in range(1, F):
        if r != half_f:
            low = low_bit(r)
            out_pieces[r] = swap(out_pieces[r ^ low], "fsdp", F, low)
    own_up_first = gather_first(after(upstream_low, w_qkv), S)
    normed_even, normed_odd, query_pre, key_pre, value_low, squares = project(
        tokens_even, tokens_odd, w_qkv, gain_attn[None], me, T
    )
    squares, partner_up[1], out_pieces, own_up_first = tie(
        squares, partner_up[1], out_pieces, own_up_first
    )
    partner_up = jnp.concatenate(partner_up, 0)
    own_output = place_fsdp(out_pieces, f, 0).reshape(C, D)

    out_first = gather_first(own_output, S)
    far = [far_part(0, squares)]
    near_own.append(near_swap(own_quarters[2], squares))
    squares = sum_all(squares, "seq", S)
    query_low, key_low = rope(query_pre, key_pre, squares, head_gain, cosine, sine)
    query_low, out_first, far[0], near_own[1] = tie(query_low, out_first, far[0], near_own[1])

    seg_row = segments
    seg_col = segments.reshape(L, 1)
    out_more = gather_more(own_output, out_first, S)
    far.append(far_part(1, query_low))
    near_own.append(near_swap(own_quarters[3], query_low))
    down = [near_swap(down_rows[0], query_low)]
    attended, lse = attention_forward(query_low, key_low, value_low, seg_row, seg_col)
    attended, out_more, far[1], near_own[2], down[0] = tie(
        attended, out_more, far[1], near_own[2], down[0]
    )
    attended_blocks = attended.reshape(S, T, C)
    come = lax.all_to_all(attended_blocks, "seq", split_axis=0, concat_axis=0, tiled=True)
    out_even, out_odd = gather_end(own_output, out_first, out_more, S)
    far.append(far_part(2, attended))
    near_far = [near_swap(far[0], attended)]
    own_up_more = gather_more(after(upstream_low, attended), own_up_first, S)
    come, far[2], near_far[0], own_up_more = tie(come, far[2], near_far[0], own_up_more)
    own_u = gather_end(upstream_low, own_up_first, own_up_more, S)
    near_far.append(near_swap(far[1], come))
    down.append(near_swap(down_rows[1], come))
    partner_up_first = gather_first(after(partner_up, come), S)
    come = relative(come, s).transpose(1, 0, 2).reshape(T, D)
    residual = inputs + matmul(come[:, : D // 2], out_even) + matmul(come[:, D // 2 :], out_odd)
    moe_factor = rms_factor(residual)
    residual_n = residual * moe_factor
    second_low = (residual_n * gain_moe).astype(BF16)
    second_low, down[1], near_far[1], partner_up_first, own_u = tie(
        second_low, down[1], near_far[1], partner_up_first, own_u
    )

    own_first = gather_first(second_low, S)
    partner_low = [far_swap(second_low[:half_rows])]
    near_far.append(near_swap(far[2], second_low))
    rank_part = after(small, second_low)[:, :, part * (E + 4) :].reshape(S, F, E, T)

    def ranks_of(index):
        ranks = lax.dynamic_slice(rank_part, (0, index, s * experts, 0), (S, 1, experts, T))
        ranks = relative(ranks[:, 0], s).astype(jnp.int32)
        return ranks[: S // 2], ranks[S // 2 :]

    own_ranks, other_ranks = ranks_of(f), ranks_of(f ^ half_f)
    own_first, partner_low[0], near_far[2], own_ranks, other_ranks = tie(
        own_first, partner_low[0], near_far[2], own_ranks, other_ranks
    )
    own_more = gather_more(second_low, own_first, S)
    partner_low.append(far_swap(second_low[half_rows:], own_first))
    down.append(near_swap(down_rows[2], own_first))
    partner_up_more = gather_more(after(partner_up, own_first), partner_up_first, S)
    own_more, partner_low[1], down[2], partner_up_more = tie(
        own_more, partner_low[1], down[2], partner_up_more
    )
    partner_low = jnp.concatenate(partner_low, 0)
    own_x = gather_end(second_low, own_first, own_more, S)
    partner_first = gather_first(after(partner_low, own_more), S)
    down.append(near_swap(down_rows[3], own_more))
    far.append(far_part(3, own_more))
    partner_first, down[3], own_x, far[3] = tie(partner_first, down[3], own_x, far[3])
    other_u = gather_end(after(partner_up, partner_first), partner_up_first, partner_up_more, S)
    partner_more = gather_more(partner_low, partner_first, S)
    near_far.append(near_swap(far[3], partner_first))
    partner_more, other_u, near_far[3] = tie(partner_more, other_u, near_far[3])
    other_x = gather_end(partner_low, partner_first, partner_more, S)
    in_pieces = []
    for r in range(F):
        for n, rows in enumerate(near_own if r < half_f else near_far):
            first = (0, 2, 3)[n] if r < half_f else n
            in_pieces.append((r, first * quarter, rows[r % half_f]))
    down_pieces = [
        (r, n * (down_part // 4), down[n][r]) for r in range(half_f) for n in range(4)
    ]
    wide_router = jnp.pad(full_router, ((0, 0), (0, 128 - E)))
    expert_places = jnp.stack([s * experts, f]).astype(jnp.int32)
    parts = (in_part, down_part)
    own_parts = run_experts(
        own_x, own_u, own_ranks, in_pieces, down_pieces, wide_router, expert_places, 0, (), parts
    )
    own_parts, other_x = tie(own_parts, other_x)
    own_got = swap(own_parts[3], "seq", S, 1)
    own_out_got = swap(own_parts[1], "seq", S, 1)
    other_parts = run_experts(
        other_x,
        other_u,
        other_ranks,
        in_pieces,
        down_pieces,
        wide_router,
        expert_places,
        1,
        own_parts[6:],
        parts,
    )
    other_parts, own_got, own_out_got = tie(other_parts, own_got, own_out_got)
    logits = matmul(second_low, full_router)
    router_probs = jax.nn.softmax(logits, axis=-1)

    x_rows, u_rows, in_grads, hidden_gate = other_parts[6:]
    in_terms, down_terms = {}, {}

    def in_products(r, *dep):
        in_terms[r] = products(
            x_rows, after(in_grads, dep), in_part, r, F, f_at, "in_products"
        )

    odd = [r for r in range(F) if r & 1]
    far_odd = [r for r in odd if r & half_f]
    near_odd = [r for r in odd if not r & half_f]

    def to_home(even, odd):
        return absolute(jnp.concatenate([even, odd], 0).transpose(0, 2, 1), s)

    gate_grads = jnp.stack(
        [to_home(own_parts[4], own_parts[5]), to_home(other_parts[4], other_parts[5])], 1
    ).reshape(S, -1)
    other_got = swap(other_parts[3], "seq", S, 1)
    gate_grads = lax.all_to_all(gate_grads, "seq", split_axis=0, concat_axis=0, tiled=True)
    other_got, gate_grads = tie(other_got, gate_grads)
    for r in far_odd:
        in_products(r, other_got)

    def send_in(n, *dep):
        return {r: swap(after(sent[r][n], dep), "fsdp", F, 1) for r in sent}

    other_sums = sum_cores(other_parts[2], other_got, S)
    come = sum_first(other_sums, S)
    other_out_got = swap(after(other_parts[1], other_got), "seq", S, 1)
    gate_grads = gate_grads.reshape(S, 2, T * experts)
    partner_grads = far_swap(gate_grads[:, 1])
    come, in_terms, other_out_got, partner_grads = tie(
        come, in_terms, other_out_got, partner_grads
    )
    sent = {r: quarters(in_terms[r], 1) for r in far_odd}
    singles, other_total = sum_more(other_sums, come, S)
    come = sum_last(singles, S)
    start_got = {r: swap(in_terms[r][:, : 2 * quarter], "fsdp", F, 1) for r in far_odd}

    def down_products(r, dep):
        down_terms[r] = products(
            after(hidden_gate, dep), u_rows, down_part, r, half_f, f_at, "down_products"
        )

    for r in range(1, half_f, 2):
        down_products(r, singles)
    come, start_got, down_terms = tie(come, start_got, down_terms)
    far_got = [
        {r: got[:, n * quarter : (n + 1) * quarter] for r, got in start_got.items()}
        for n in range(2)
    ]
    other_rows = add_all(other_total, come).astype(BF16)
    gate_grads = gate_grads[:, 0] + partner_grads
    gate_grads = gate_grads.reshape(S, T, experts).transpose(1, 0, 2).reshape(T, E)
    back = [far_swap(other_rows[:half_rows])]
    own_sums = sum_cores(own_parts[2], after(own_got, other_rows), S)
    come = sum_first(own_sums, S)
    far_got.append(send_in(2, other_rows))
    for r in far_odd:
        in_products(r ^ 1, other_rows)
    come, back[0], far_got[2], in_terms = tie(come, back[0], far_got[2], in_terms)
    back.append(far_swap(other_rows[half_rows:], come))
    singles, own_total = sum_more(own_sums, come, S)
    come = sum_last(singles, S)
    down_sent = {r: quarters(down_terms[r], 1) for r in range(1, half_f, 2)}
    for r in down_sent:
        down_sent[r] = down_sent[r][:2] + [jnp.concatenate(down_sent[r][2:], 1)]

    def send_down(n, *dep):
        return {r: swap(after(down_sent[r][n], dep), "fsdp", F, 1) for r in down_sent}

    far_got.append(send_in(3, singles))
    for r in near_odd:
        in_products(r, singles)
    come, back[1], far_got[3], in_terms = tie(come, back[1], far_got[3], in_terms)
    row_grads = add_all(own_total, come) + jnp.concatenate(back, 0).astype(F32)

    upstream = upstream_low.astype(F32)
    logit_grads = router_probs * (
        gate_grads - jnp.sum(router_probs * gate_grads, axis=-1, keepdims=True)
    )
    router_wide = full_router.astype(F32)
    second_grads = row_grads + jnp.dot(logit_grads, router_wide.T, precision=HIGHEST)
    pulled = second_grads * gain_moe
    residual_grads = upstream + moe_factor * (
        pulled - residual_n * jnp.mean(pulled * residual_n, axis=-1, keepdims=True)
    )
    branch_low = residual_grads.astype(BF16)

    def sum_near(terms):
        mask = 2
        while mask < half_f:
            terms = {
                r: terms[r] + swap(terms[r | mask].astype(BF16), "fsdp", F, mask).astype(F32)
                for r in terms
                if not r & mask
            }
            mask *= 2
        (total,) = terms.values()
        return total

    def far_sum(n, *dep):
        terms = {
            r ^ 1: quarters(in_terms[r ^ 1], 1)[n].astype(F32) + far_got[n][r].astype(F32)
            for r in far_odd
        }
        return far_swap(sum_near(terms).astype(BF16), *dep)

    branch_first = gather_first(branch_low, S)
    far_sums = [far_sum(0, branch_low)]
    down_got = [send_down(0, branch_low)]
    for r in range(0, half_f, 2):
        down_products(r, branch_low)
    branch_first, far_sums[0], down_got[0], down_terms = tie(
        branch_first, far_sums[0], down_got[0], down_terms
    )
    branch_more = gather_more(branch_low, branch_first, S)
    far_sums.append(far_sum(1, branch_first))
    down_got.append(send_down(1, branch_first))
    branch_even, branch_odd = gather_end(branch_low, branch_first, branch_more, S)

    head_grads = jnp.concatenate(
        [matmul_t(branch_even, own_output), matmul_t(branch_odd, own_output)], 0
    ).astype(BF16)
    head_grads = absolute(head_grads.reshape(S, T, C), s).reshape(L, C)
    head_grads, far_sums[1], down_got[1] = tie(head_grads, far_sums[1], down_got[1])
    far_sums.append(far_sum(2, head_grads))
    down_got.append(send_down(2, head_grads))
    other_out_sums = sum_cores(other_parts[0], after(other_out_got, head_grads), S)
    come, head_grads = sum_first(other_out_sums, S, head_grads)
    query_back, key_back, value_back = attention_backward(
        query_low, key_low, value_low, head_grads, lse, seg_row, seg_col
    )
    query_back, key_back, value_back, far_sums[2], down_got[2], come = tie(
        query_back, key_back, value_back, far_sums[2], down_got[2], come
    )

    singles, other_total = sum_more(other_out_sums, come, S)
    come = sum_last(singles, S)
    far_sums.append(far_sum(3, query_back))
    attended_rel = relative(after(attended_blocks, singles), s).reshape(2, L // 2, C)
    output_term = t_matmul(attended_rel[0], branch_even) + t_matmul(attended_rel[1], branch_odd)
    output_term = by_index(output_term.astype(BF16).reshape(F, part, D), f, F)
    output_got = swap(output_term[: F // 2], "fsdp", F, 1)
    value_rel = relative(value_back.reshape(S, T, C), s).reshape(2, L // 2, C)

    def weight_term(even, odd):
        term = (t_matmul(normed_even, even) + t_matmul(normed_odd, odd)).astype(BF16)
        return by_index(term.reshape(S, F, part, -1).transpose(1, 0, 2, 3), f, F)

    means, gain_term = rope_means(
        query_back, key_back, query_pre, key_pre, squares, head_gain, cosine, sine
    )
    means = sum_all(means, "seq", S)
    value_term = weight_term(value_rel[0], value_rel[1])
    means, come, far_sums[3], output_got, value_term = tie(
        means, come, far_sums[3], output_got, value_term
    )
    other_outs = add_all(other_total, come).astype(BF16)
    outs_back = [far_swap(other_outs[:half_rows])]
    value_got = swap(value_term[: F // 2], "fsdp", F, 1)
    pre_rel = rope_back(
        (query_back, key_back, value_back),
        query_pre,
        key_pre,
        squares,
        means,
        head_gain,
        cosine,
        sine,
        me,
        T,
    ).reshape(2, L // 2, 3 * C)
    normed_got = swap(matmul_t(pre_rel[1], w_qkv).astype(BF16), "seq", S, 1)
    normed_kept = matmul_t(pre_rel[0], w_qkv).astype(BF16)
    normed_got, normed_kept, value_got, outs_back[0] = tie(
        normed_got, normed_kept, value_got, outs_back[0]
    )

    normed_sums = sum_cores(normed_kept, normed_got, S)
    come = sum_first(normed_sums, S)
    value_sum = sum_rest(sum_even(value_term, value_got, F), F)
    turned_term = weight_term(
        after(pre_rel[0][:, : 2 * C], normed_got), after(pre_rel[1][:, : 2 * C], normed_got)
    )
    late_grads, late_logits = after(second_grads, normed_got), after(logit_grads, normed_got)
    router_term = jnp.dot(second_low.astype(F32).T, late_logits, precision=HIGHEST)
    moe_gain_term = jnp.sum(late_grads * residual_n, axis=0)
    gain_terms = jnp.concatenate(
        [router_term.reshape(S * F, part * E), moe_gain_term.reshape(S * F, part)], 1
    )
    gain_terms = in_relative(gain_terms, S, F, s, f).reshape(S, F, -1)
    head_terms = gain_term.reshape(2, F, part).transpose(1, 0, 2).reshape(F, 2 * part)
    head_terms = in_relative(head_terms, 1, F, 0, f)
    gain_terms = jnp.concatenate([gain_terms.transpose(1, 0, 2).reshape(F, -1), head_terms], 1)
    own_out_sums = sum_cores(own_parts[0], after(own_out_got, normed_got), S)
    own_come = sum_first(own_out_sums, S)
    come, turned_term, value_sum, gain_terms, own_come = tie(
        come, turned_term, value_sum, gain_terms, own_come
    )
    turned_got = swap(turned_term[: F // 2], "fsdp", F, 1)
    singles, normed_total = sum_more(normed_sums, come, S)
    come = sum_last(singles, S)
    gain_got = swap(gain_terms[F // 2 :], "fsdp", F, half_f)
    for r in near_odd:
        in_products(r ^ 1, turned_term)
    come, turned_got, gain_got, in_terms = tie(come, turned_got, gain_got, in_terms)
    gain_terms = gain_terms[: F // 2] + gain_got
    normed_grads = add_all(normed_total, come)
    turned_sum = sum_rest(sum_even(turned_term, turned_got, F), F)
    middle = in_part // 2

    def send_near(first, dep):
        return {
            r: swap(after(in_terms[r][:, first : first + middle], dep), "fsdp", F, 1)
            for r in near_odd
        }

    near_got = [send_near(0, turned_got)]
    gain_terms = halve(after(gain_terms, turned_got), "fsdp", F, half_f // 2)
    singles, own_total = sum_more(after(own_out_sums, turned_got), own_come, S)
    own_come = sum_last(singles, S)
    turned_sum, own_come, near_got[0], gain_terms = tie(
        turned_sum, own_come, near_got[0], gain_terms
    )
    near_got.append(send_near(middle, turned_sum))
    outs_back.append(far_swap(other_outs[half_rows:], turned_sum))
    count = S * part * (E + 1)
    head_terms = gain_terms[0, count:]
    gain_terms = halve(gain_terms[0, :count].reshape(S, -1), "seq", S, S // 2)[0]
    own_outs = add_all(own_total, own_come)
    qkv_term = jnp.concatenate([turned_sum, value_sum], -1).astype(BF16)
    qkv_term = lax.all_to_all(qkv_term, "seq", split_axis=0, concat_axis=0, tiled=True)
    qkv_term, outs_back[1], near_got[1], gain_terms = tie(
        qkv_term, outs_back[1], near_got[1], gain_terms
    )
    outs_back = jnp.concatenate(outs_back, 0).astype(F32)
    mixed = (residual + own_outs + outs_back).astype(BF16)[None]
    qkv_term = [
        qkv_term[:, :, j * C : (j + 1) * C].transpose(1, 0, 2).reshape(part, D).astype(F32)
        for j in range(3)
    ]
    grad_output = sum_rest(sum_even(output_term, output_got, F), F)

    near_got = {r: jnp.concatenate([got[r] for got in near_got], 1) for r in near_odd}
    own_term = sum_near(
        {r ^ 1: in_terms[r ^ 1].astype(F32) + near_got[r].astype(F32) for r in near_odd}
    )
    far_term = jnp.concatenate(far_sums, 1).astype(F32)
    first_half = half_at == 0
    lower = jnp.where(first_half, own_term, far_term)
    upper = jnp.where(first_half, far_term, own_term)
    grad_gate, grad_up = (
        jnp.concatenate([lower[..., at], upper[..., at]], axis=-1)
        for at in (slice(0, hidden_half), slice(hidden_half, 2 * hidden_half))
    )
    down_got = after(down_got, turned_sum)
    down_got = {r: jnp.concatenate([got[r] for got in down_got], 1) for r in down_sent}
    grad_down = sum_near(
        {r ^ 1: down_terms[r ^ 1].astype(F32) + down_got[r].astype(F32) for r in down_sent}
    )

    attn_factor = rms_factor(inputs)
    inputs_n = inputs * attn_factor
    attn_pulled = normed_grads * gain_attn
    grad_tokens = residual_grads + attn_factor * (
        attn_pulled - inputs_n * jnp.mean(attn_pulled * inputs_n, axis=-1, keepdims=True)
    )
    grad_attn_gain = sum(
        jnp.sum(term * weight.astype(F32), axis=1)
        for term, weight in zip(qkv_term, (w_query, w_key, w_value))
    ) / attn_gain.astype(F32)
    return (
        mixed,
        grad_tokens[None],
        qkv_term[0],
        qkv_term[1],
        qkv_term[2],
        grad_output,
        gain_terms[: part * E].reshape(part, E),
        grad_attn_gain,
        gain_terms[part * E :],
        head_terms[:part],
        head_terms[part:],
        grad_gate,
        grad_up,
        grad_down,
    )


def solution(mesh):
    tokens_spec = P("fsdp", "seq", None)
    rows_spec = P(("seq", "fsdp"), None)
    gain_spec = P(("seq", "fsdp"))
    expert_spec = P("seq", "fsdp", None)
    in_specs = (
        (tokens_spec, P("fsdp", None), tokens_spec, tokens_spec)
        + (rows_spec,) * 5
        + (gain_spec,) * 4
        + (expert_spec,) * 3
    )
    out_specs = (tokens_spec,) * 2 + (rows_spec,) * 5 + (gain_spec,) * 4 + (expert_spec,) * 3
    return jax.shard_map(
        partial(per_device, mesh.shape["seq"], mesh.shape["fsdp"]),
        mesh=mesh,
        in_specs=in_specs,
        out_specs=out_specs,
        check_vma=False,
    )
```
